32 devices in a mesh: dp: 4 (over z), tm: 4 (over y, core), height: 2 (over x).
Axes of the slice: x: 2, y: 2, z: 4, core: 2. Of those that a mesh axis runs over, the one named last changes fastest.
Arguments:
- clip_inputs: bfloat16 [4, 8, 4, 16, 512], P('dp', 'tm', 'height'), may hold values from -6 to 6
- conv_in_weight: bfloat16 [13824, 512], P(('tm', 'height'), 'dp'), may hold values from -0.0546875 to 0.0546875
- group_gain: bfloat16 [512], P('dp'), may hold values from 0.099609375 to 1.8984375
- group_bias: bfloat16 [512], P('dp'), may hold values from -3 to 3
- conv_out_weight: bfloat16 [27, 512, 16], P(None, 'dp'), may hold values from -0.109375 to 0.109375
- out_bias: float32 [16], replicated, may hold values from -3 to 3
- patch_weight: bfloat16 [64, 3072], replicated, may hold values from -1.5 to 1.5
- patch_bias: bfloat16 [3072], replicated, may hold values from -3 to 3
- qkv_weight: bfloat16 [3072, 3072], P(('tm', 'height'), 'dp'), may hold values from -0.109375 to 0.109375
- qkv_bias: bfloat16 [3072], P('dp'), may hold values from -3 to 3
- q_gain: bfloat16 [128], replicated, may hold values from 0.099609375 to 1.8984375
- k_gain: bfloat16 [128], replicated, may hold values from 0.099609375 to 1.8984375
- frame_pos: int32 [8], P('tm'), may hold values from 0 to 63
- row_pos: int32 [2], P('height'), may hold values from 0 to 127
Outputs:
- latents: float32 [4, 8, 4, 256], P('dp', 'tm', 'height')
- queries: bfloat16 [4, 8, 2, 8, 1024], P(None, 'tm', 'height', None, 'dp')
- keys: bfloat16 [4, 8, 2, 8, 1024], P(None, 'tm', 'height', None, 'dp')
- values: bfloat16 [4, 8, 2, 8, 1024], P(None, 'tm', 'height', None, 'dp')
The draws below stay inside these ranges and needn't reach their ends.
All inputs are finite; a program needn't handle non-finite values.
Results may differ from the reference program's by a relative error of at most 0.01.
Values may be sent and summed in bfloat16 or wider, within the bound.
No kernel may reach another device: no remote copies, remote signals or barrier semaphores. Data moves between devices by JAX's collectives and lax.ppermute only.
A program may use at most 64 MiB of HBM per device.

```python
import math
import jax
import jax.numpy as jnp
from jax import lax

C = 512
ZC = 16
HID = 3072
HD = 128
GROUPS = 32
TAPS = 27
COLS = 16
HEADS = 8
CLIPS = 4
FRAMES = 8
ROWS = 4
TROWS = 2
TCOLS = 8
PATCH = 64


def wave_sum(base, freqs, phases, channel_vecs, amplitude):
    frames_at = jnp.arange(FRAMES, dtype=jnp.float32) / FRAMES
    rows_at = jnp.arange(ROWS, dtype=jnp.float32) / ROWS
    cols_at = jnp.arange(COLS, dtype=jnp.float32) / COLS
    total = base
    for mode in range(2):
        argument = 2.0 * math.pi * (freqs[mode, 0] * frames_at[:, None, None] + freqs[mode, 1] * rows_at[None, :, None] + freqs[mode, 2] * cols_at[None, None, :])
        wave = jnp.cos(argument[None] + phases[:, mode][:, None, None, None])
        total = total + amplitude * wave[..., None] * channel_vecs[mode][None, None, None, None, :]
    return total


def draw_clip_inputs(key, part):
    key = jax.random.fold_in(key, 11)
    freq_key, phase_key, chan_key, sign_key, offset_key, noise_key = jax.random.split(key, 6)
    shape = (CLIPS, FRAMES, ROWS, COLS, C)
    freqs = jax.random.randint(freq_key, (2, 3), 1, 4).astype(jnp.float32)
    phases = jax.random.uniform(phase_key, (CLIPS, 2), jnp.float32, -math.pi, math.pi)
    channel_vecs = jnp.clip(jax.random.normal(chan_key, (2, C), jnp.float32), -2.5, 2.5)
    signs = (2 * jax.random.randint(sign_key, (CLIPS,), 0, 2) - 1).astype(jnp.float32)
    offsets = jnp.clip(jax.random.normal(offset_key, (C,), jnp.float32), -2.5, 2.5)
    noise = 0.5 * jnp.clip(jax.random.normal(noise_key, shape, jnp.float32), -3.5, 3.5)
    field = wave_sum(noise, freqs, phases, channel_vecs, 0.7)
    field = field + 0.5 * signs[:, None, None, None, None] * offsets
    return jnp.clip(field, -6.0, 6.0).astype(jnp.bfloat16)


def plant(drawn, stream_key, least, high):
    longest = drawn.shape.index(max(drawn.shape))
    spots = []
    for shift in (0, 1):
        where = [jax.random.randint(jax.random.fold_in(stream_key, axis), (), 0, length) for axis, length in enumerate(drawn.shape)]
        where[longest] = (where[longest] + shift) % drawn.shape[longest]
        spots.append(tuple(where))
    return drawn.at[spots[0]].set(least).at[spots[1]].set(high)


def shard_levels(rng, shape, pieces, least, high):
    def one(position, parts):
        heights = jax.random.uniform(jax.random.fold_in(jax.random.fold_in(rng, 6), position), (parts,), jnp.float32, least / len(pieces), high / len(pieces))
        return jnp.repeat(jnp.exp(heights), shape[position] // parts).reshape((-1,) + (1,) * (len(shape) - position - 1))

    level = one(*pieces[0])
    for cut in pieces[1:]:
        level = level * one(*cut)
    return level


def normal_values(key, shape, deviation, reach, pieces=(), held_as=jnp.bfloat16):
    values = deviation * jax.random.normal(key, shape, jnp.float32)
    if pieces:
        values = values * shard_levels(key, shape, pieces, -0.22, 0.18)
    return jnp.clip(values, -reach, reach).astype(held_as)


def setup_inputs(seed: int = 0) -> dict:
    streams_of = jax.random.split(jax.random.key(seed), 15)
    return {
        "clip_inputs": draw_clip_inputs(jax.random.fold_in(streams_of[14], 71), 0),
        "conv_in_weight": normal_values(streams_of[1], (TAPS * C, C), (TAPS * C) ** -0.5, 0.0546875, ((0, 8), (1, 4))),
        "group_gain": jnp.clip(1.0 + 0.18 * jax.random.normal(streams_of[2], (C,), jnp.float32), 0.099609375, 1.8984375).astype(jnp.bfloat16),
        "group_bias": normal_values(streams_of[3], (C,), 0.5, 3.0, ((0, 4),)),
        "conv_out_weight": normal_values(streams_of[4], (TAPS, C, ZC), (TAPS * C // 4) ** -0.5, 0.109375, ((1, 4),)),
        "out_bias": normal_values(streams_of[5], (ZC,), 0.5, 3.0, (), jnp.float32),
        "patch_weight": normal_values(streams_of[6], (PATCH, HID), (PATCH // 4) ** -0.5, 1.5),
        "patch_bias": normal_values(streams_of[7], (HID,), 0.5, 3.0),
        "qkv_weight": normal_values(streams_of[8], (HID, HEADS * 3 * HD), HID ** -0.5, 0.109375, ((0, 8), (1, 4))),
        "qkv_bias": normal_values(streams_of[9], (HEADS * 3 * HD,), 0.5, 3.0, ((0, 4),)),
        "q_gain": jnp.clip(1.0 + 0.18 * jax.random.normal(streams_of[10], (HD,), jnp.float32), 0.099609375, 1.8984375).astype(jnp.bfloat16),
        "k_gain": jnp.clip(1.0 + 0.18 * jax.random.normal(streams_of[11], (HD,), jnp.float32), 0.099609375, 1.8984375).astype(jnp.bfloat16),
        "frame_pos": plant(jax.random.randint(streams_of[12], (FRAMES,), 0, 64), jax.random.fold_in(streams_of[12], 1), 0, 63).astype(jnp.int32),
        "row_pos": jax.random.randint(streams_of[13], (TROWS,), 0, 128).astype(jnp.int32),
    }


norm_eps = 1e-06
latent_scale = 0.476986
rope_base = 256.0
time_dims = 16
row_dims = 56

def extend(block):
    return jnp.pad(block, ((2, 0), (1, 1), (1, 1), (0, 0)), mode='edge')

def convolve(padded, weight):
    frames = padded.shape[0] - 2
    rows = padded.shape[1] - 2
    cols = padded.shape[2] - 2
    total = jnp.zeros((frames * rows * cols, weight.shape[2]), jnp.float32)
    for shift_t in range(3):
        for shift_r in range(3):
            for shift_c in range(3):
                window = padded[shift_t:shift_t + frames, shift_r:shift_r + rows, shift_c:shift_c + cols]
                window = window.reshape(-1, padded.shape[3])
                total = total + jnp.dot(window, weight[9 * shift_t + 3 * shift_r + shift_c], preferred_element_type=jnp.float32)
    return total.reshape(frames, rows, cols, weight.shape[2])

def section_freqs(dims):
    return jnp.power(rope_base, -jnp.arange(0, dims, 2, dtype=jnp.float32) / dims)

def rope_angles(tpos, hpos, width):
    frames = tpos.shape[0]
    rows = hpos.shape[0]
    cols = jnp.arange(width, dtype=jnp.float32)
    part_t = tpos[:, None, None, None] * section_freqs(time_dims)
    part_h = hpos[None, :, None, None] * section_freqs(row_dims)
    part_w = cols[None, None, :, None] * section_freqs(row_dims)
    shape = (frames, rows, width)
    return jnp.concatenate([jnp.broadcast_to(part_t, shape + (time_dims // 2,)), jnp.broadcast_to(part_h, shape + (row_dims // 2,)), jnp.broadcast_to(part_w, shape + (row_dims // 2,))], axis=-1)

def rotate(vectors, angles):
    pairs = vectors.reshape(vectors.shape[:-1] + (vectors.shape[-1] // 2, 2))
    first = pairs[..., 0]
    second = pairs[..., 1]
    cosine = jnp.cos(angles)[..., None, :]
    sine = jnp.sin(angles)[..., None, :]
    turned = jnp.stack([first * cosine - second * sine, first * sine + second * cosine], axis=-1)
    return turned.reshape(vectors.shape)

def rms_scale(vectors, gain):
    return vectors * lax.rsqrt(lax.optimization_barrier(jnp.mean(vectors * vectors, axis=-1, keepdims=True)) + norm_eps) * gain.astype(jnp.float32)

def reference(clip_inputs, conv_in_weight, group_gain, group_bias, conv_out_weight, out_bias, patch_weight, patch_bias, qkv_weight, qkv_bias, q_gain, k_gain, frame_pos, row_pos):
    weight_in = conv_in_weight.reshape(TAPS, C, C)
    angles = rope_angles(frame_pos.astype(jnp.float32), row_pos.astype(jnp.float32), TCOLS)

    def one_clip(block):
        hidden = convolve(extend(block), weight_in)
        grouped = hidden.reshape(-1, GROUPS, C // GROUPS)
        mean = lax.optimization_barrier(jnp.mean(grouped, axis=(0, 2)))
        var = lax.optimization_barrier(jnp.mean(grouped * grouped, axis=(0, 2))) - mean * mean
        scaled = (grouped - mean[None, :, None]) * lax.rsqrt(var + norm_eps)[None, :, None]
        scaled = scaled.reshape(hidden.shape) * group_gain.astype(jnp.float32) + group_bias.astype(jnp.float32)
        normed = jax.nn.silu(scaled).astype(jnp.bfloat16)
        latent = (convolve(extend(normed), conv_out_weight) + out_bias) * latent_scale
        latent_bf = latent.astype(jnp.bfloat16)
        patches = latent_bf.reshape(FRAMES, TROWS, 2, TCOLS, 2, ZC).transpose(0, 1, 3, 2, 4, 5).reshape(-1, PATCH)
        embedded = (jnp.dot(patches, patch_weight, preferred_element_type=jnp.float32) + patch_bias.astype(jnp.float32)).astype(jnp.bfloat16)
        projected = jnp.dot(embedded, qkv_weight, preferred_element_type=jnp.float32) + qkv_bias.astype(jnp.float32)
        projected = projected.reshape(FRAMES, TROWS, TCOLS, HEADS, 3, HD)
        query = rotate(rms_scale(projected[..., 0, :], q_gain), angles)
        key = rotate(rms_scale(projected[..., 1, :], k_gain), angles)
        value = projected[..., 2, :]
        merged = (FRAMES, TROWS, TCOLS, HEADS * HD)
        return (latent.reshape(FRAMES, ROWS, COLS * ZC), query.reshape(merged).astype(jnp.bfloat16), key.reshape(merged).astype(jnp.bfloat16), value.reshape(merged).astype(jnp.bfloat16))
    latents, queries, keys, values = lax.map(one_clip, clip_inputs)
    return (latents, queries, keys, values)
```

```python
import functools

import jax
import jax.numpy as jnp
from jax import lax
from jax.experimental import pallas as pl
from jax.experimental.pallas import tpu as pltpu
from jax.sharding import PartitionSpec as P

HD = 128
GROUPS = 32
TAPS = 27


norm_eps = 1e-06
latent_scale = 0.476986
rope_base = 256.0
time_dims = 16
row_dims = 56


def from_behind(value, axis, steps):
    count = lax.axis_size(axis)
    first, last = (max(0, -steps), min(count, count - steps))
    return lax.ppermute(value, axis, [(source, source + steps) for source in range(first, last)])


def padded_2(block, sides, width):
    for axis, dim in sides:
        count = lax.axis_size(axis)
        forward = [(i, i + 1) for i in range(count - 1)]
        backward = [(target, source) for source, target in forward]
        low = lax.ppermute(
            lax.slice_in_dim(block, block.shape[dim] - width, None, axis=dim), axis, forward
        )
        high = lax.ppermute(lax.slice_in_dim(block, 0, width, axis=dim), axis, backward)
        block = jnp.concatenate([low, block, high], axis=dim)
    return block


def repeat_first(block):
    return jnp.concatenate([block[:, :1], block[:, :1]], axis=1)


def time_join(block, earlier):
    start = jnp.where(lax.axis_index("tm") == 0, repeat_first(block), earlier)
    return jnp.concatenate([start, block], axis=1)


def rows_finish(grown):
    place = lax.axis_index("height")
    top = jnp.where(place == 0, grown[:, :, 1:2], grown[:, :, :1])
    bottom = jnp.where(place == lax.axis_size("height") - 1, grown[:, :, -2:-1], grown[:, :, -1:])
    inner = jnp.concatenate([top, grown[:, :, 1:-1], bottom], axis=2)
    return jnp.pad(inner, ((0, 0), (0, 0), (0, 0), (1, 1), (0, 0)), mode="edge")


def edges_before(block):
    earlier = from_behind(block, "tm", 1)
    longer = time_join(block, earlier)
    return rows_finish(padded_2(longer, (("height", 2),), 1))


def edges_norm(block):
    earlier = from_behind(block, "tm", 1)
    longer = time_join(block, earlier)
    return rows_finish(padded_2(longer, (("height", 2),), 1))


def convolve(padded, weight):
    clips = padded.shape[0]
    frames = padded.shape[1] - 2
    rows = padded.shape[2] - 2
    cols = padded.shape[3] - 2
    total = jnp.zeros((clips * frames * rows * cols, weight.shape[2]), jnp.float32)
    for shift_t in range(3):
        for shift_r in range(3):
            for shift_c in range(3):
                window = padded[
                    :,
                    shift_t : shift_t + frames,
                    shift_r : shift_r + rows,
                    shift_c : shift_c + cols,
                ]
                window = window.reshape(-1, padded.shape[4])
                total = total + jnp.dot(
                    window,
                    weight[9 * shift_t + 3 * shift_r + shift_c],
                    preferred_element_type=jnp.float32,
                )
    return total.reshape(clips, frames, rows, cols, weight.shape[2])


def section_freqs(dims):
    return jnp.power(rope_base, -jnp.arange(0, dims, 2, dtype=jnp.float32) / dims)


def rope_angles(tpos, hpos, width):
    frames = tpos.shape[0]
    rows = hpos.shape[0]
    cols = jnp.arange(width, dtype=jnp.float32)
    part_t = tpos[:, None, None, None] * section_freqs(time_dims)
    part_h = hpos[None, :, None, None] * section_freqs(row_dims)
    part_w = cols[None, None, :, None] * section_freqs(row_dims)
    shape = (frames, rows, width)
    return jnp.concatenate(
        [
            jnp.broadcast_to(part_t, shape + (time_dims // 2,)),
            jnp.broadcast_to(part_h, shape + (row_dims // 2,)),
            jnp.broadcast_to(part_w, shape + (row_dims // 2,)),
        ],
        axis=-1,
    )


def rotate(vectors, angles):
    pairs = vectors.reshape(vectors.shape[:-1] + (vectors.shape[-1] // 2, 2))
    first = pairs[..., 0]
    second = pairs[..., 1]
    cosine = jnp.cos(angles)[..., None, :]
    sine = jnp.sin(angles)[..., None, :]
    turned = jnp.stack([first * cosine - second * sine, first * sine + second * cosine], axis=-1)
    return turned.reshape(vectors.shape)


def rms_scale(vectors, gain):
    return (
        vectors
        * lax.rsqrt(jnp.mean(vectors * vectors, axis=-1, keepdims=True) + norm_eps)
        * gain.astype(jnp.float32)
    )


def shards(
    clip_inputs,
    conv_in_weight,
    group_gain,
    group_bias,
    conv_out_weight,
    out_bias,
    patch_weight,
    patch_bias,
    qkv_weight,
    qkv_bias,
    q_gain,
    k_gain,
    frame_pos,
    row_pos,
):
    channels = clip_inputs.shape[4]
    frames = clip_inputs.shape[1]
    rows = clip_inputs.shape[2]
    cols = clip_inputs.shape[3]
    padded = lax.all_gather(edges_before(clip_inputs), "dp", axis=0, tiled=True)
    clips = padded.shape[0]
    weight_in = lax.all_gather(conv_in_weight, ("tm", "height"), axis=0, tiled=True).reshape(
        TAPS, channels, -1
    )
    hidden = convolve(padded, weight_in)
    block_width = hidden.shape[4]
    group_width = channels // GROUPS
    local_groups = block_width // group_width
    grouped = hidden.reshape(clips, -1, local_groups, group_width)
    sums_local = jnp.sum(grouped, axis=(1, 3))
    squares_local = jnp.sum(grouped * grouped, axis=(1, 3))
    sums_all, squares_all = lax.psum((sums_local, squares_local), ("tm", "height"))
    count = float(
        frames * lax.axis_size("tm") * rows * lax.axis_size("height") * cols * group_width
    )
    mean = sums_all / count
    var = squares_all / count - mean * mean
    scaled = (grouped - mean[:, None, :, None]) * lax.rsqrt(var + norm_eps)[:, None, :, None]
    scaled = scaled.reshape(hidden.shape) * group_gain.astype(jnp.float32) + group_bias.astype(
        jnp.float32
    )
    normed = jax.nn.silu(scaled).astype(jnp.bfloat16)
    partial_latent = convolve(edges_norm(normed), conv_out_weight)
    own_sum = lax.psum_scatter(partial_latent, "dp", scatter_dimension=0, tiled=True)
    own_latent = (own_sum + out_bias) * latent_scale
    every_latent = lax.all_gather(own_latent.astype(jnp.bfloat16), "dp", axis=0, tiled=True)
    latent_dims = every_latent.shape[4]
    latents = own_latent.reshape(1, frames, rows, cols * latent_dims)
    tok_rows = rows // 2
    tok_cols = cols // 2
    patches = every_latent.reshape(clips, frames, tok_rows, 2, tok_cols, 2, latent_dims)
    patches = patches.transpose(0, 1, 2, 4, 3, 5, 6).reshape(-1, 4 * latent_dims)
    embedded = (
        jnp.dot(patches, patch_weight, preferred_element_type=jnp.float32)
        + patch_bias.astype(jnp.float32)
    ).astype(jnp.bfloat16)
    projected = jnp.dot(
        embedded,
        lax.all_gather(qkv_weight, ("tm", "height"), axis=0, tiled=True),
        preferred_element_type=jnp.float32,
    )
    projected = projected + qkv_bias.astype(jnp.float32)
    local_heads = qkv_weight.shape[1] // (3 * HD)
    projected = projected.reshape(clips, frames, tok_rows, tok_cols, local_heads, 3, HD)
    angles = rope_angles(frame_pos.astype(jnp.float32), row_pos.astype(jnp.float32), tok_cols)
    query = rotate(rms_scale(projected[..., 0, :], q_gain), angles)
    key = rotate(rms_scale(projected[..., 1, :], k_gain), angles)
    value = projected[..., 2, :]
    merged = (clips, frames, tok_rows, tok_cols, local_heads * HD)
    return (
        latents,
        query.reshape(merged).astype(jnp.bfloat16),
        key.reshape(merged).astype(jnp.bfloat16),
        value.reshape(merged).astype(jnp.bfloat16),
    )


LANES = 128
TILE = 16
GROUP = 16


def one_group_each(mesh, clip_inputs, conv_in_weight, conv_out_weight):
    plane = mesh.shape["tm"] * mesh.shape["height"]
    return (
        clip_inputs.shape[:4] == (1, 2, 2, 16)
        and mesh.shape["height"] == 2
        and mesh.shape["dp"] % 2 == 0
        and conv_in_weight.shape[1] == plane * GROUP
        and clip_inputs.shape[4] == GROUP * GROUPS
        and conv_out_weight.shape[2] == TILE
    )


def lane_shifts(lane):
    col = lane % 16
    row = lane // 16 % 2
    half = lane // 64

    def cols(left, mid, right):
        left = jnp.where(col == 0, left, pltpu.roll(left, 1, 1))
        right = jnp.where(col == 15, right, pltpu.roll(right, LANES - 1, 1))
        return mid + left + right

    def rows(up, mid, down):
        up = jnp.where(
            row == 1, pltpu.roll(up, 16, 1), jnp.where(half == 1, pltpu.roll(up, 48, 1), up)
        )
        down = jnp.where(
            row == 0,
            pltpu.roll(down, LANES - 16, 1),
            jnp.where(half == 0, pltpu.roll(down, LANES - 48, 1), down),
        )
        return mid + up + down

    return cols, rows


def tap_sums(y_ref, tiles):
    lane = lax.broadcasted_iota(jnp.int32, (TILE, LANES), 1)
    second = lane // 32 % 2 == 1
    cols, rows = lane_shifts(lane)
    sums = []
    before = None
    for tile in range(tiles):

        def part(tap):
            return y_ref[tap * TILE : (tap + 1) * TILE, tile * LANES : (tile + 1) * LANES]

        oldest, older, now = (
            rows(*(cols(*(part(9 * i + 3 * j + l) for l in range(3))) for j in range(3)))
            for i in range(3)
        )
        turned = pltpu.roll(older, 32, 1)
        if before is None:
            start = jnp.where(second, pltpu.roll(oldest, 32, 1), oldest)
            total = now + jnp.where(second, turned, older) + start
        else:
            total = now + jnp.where(second, turned, pltpu.roll(before[1], 96, 1)) + before[0]
        before = (oldest, older)
        sums.append(total)
    return sums


def join_weight(w_ref, wt_ref, channels):
    depth = w_ref.shape[2]
    for tap in range(TAPS):
        start = tap * channels
        end = start + channels
        while start < end:
            source = start // depth
            stop = min(end, (source + 1) * depth)
            wt_ref[
                tap * GROUP : (tap + 1) * GROUP, start - tap * channels : stop - tap * channels
            ] = w_ref[source, :, start - source * depth : stop - source * depth]
            start = stop


def conv_kernel(x_ref, w_ref, gain_ref, bias_ref, w2_ref, out_ref, wt_ref, y_ref, l_ref):
    clips, tiles = l_ref.shape[:2]
    channels = x_ref.shape[2]
    join_weight(w_ref, wt_ref, channels)
    count = float(tiles * LANES * GROUP)

    def one_clip(clip, carry):
        x = x_ref[pl.ds(clip * tiles, tiles)].reshape(tiles * LANES, channels)
        y_ref[...] = lax.dot_general(
            wt_ref[...], x, (((1,), (1,)), ((), ())), preferred_element_type=jnp.float32
        )
        hidden = tap_sums(y_ref, tiles)
        mean = sum(jnp.sum(part, keepdims=True) for part in hidden) / count
        var = sum(jnp.sum(part * part, keepdims=True) for part in hidden) / count - mean * mean
        scale = lax.rsqrt(var + norm_eps)
        normed = []
        for part in hidden:
            scaled = (part - mean) * scale * gain_ref[...] + bias_ref[...]
            normed.append((scaled / (1.0 + jnp.exp(-scaled))).astype(jnp.bfloat16))
        y_ref[...] = jnp.dot(
            w2_ref[...], jnp.concatenate(normed, axis=1), preferred_element_type=jnp.float32
        )
        for tile, part in enumerate(tap_sums(y_ref, tiles)):
            l_ref[clip, tile] = part
        return carry

    lax.fori_loop(0, clips, one_clip, 0)
    low = lax.broadcasted_iota(jnp.int32, (TILE, LANES), 1) < 64
    for tile in range(tiles):
        for pair in range(clips // 2):
            one = l_ref[2 * pair, tile]
            two = l_ref[2 * pair + 1, tile]
            at = slice(pair * LANES, (pair + 1) * LANES)
            out_ref[2 * tile, :, at] = jnp.where(low, one, pltpu.roll(two, 64, 1))
            out_ref[2 * tile + 1, :, at] = jnp.where(low, pltpu.roll(one, 64, 1), two)


def token_kernel(
    p_ref, o_ref, bias_ref, m_ref, qkv_bias_ref, q_gain_ref, k_gain_ref, cos_ref, sin_ref,
    lat_ref, q_ref, k_ref, v_ref,
):
    total = p_ref[...]
    for other in range(o_ref.shape[0]):
        total = total + o_ref[other]
    lat = (total + bias_ref[...]) * latent_scale
    clips = lat.shape[1] // 64
    tokens = clips * 16
    place = lax.axis_index("dp")
    own = lat[:, :LANES]
    for pair in range(1, clips // 2):
        own = jnp.where(place // 2 == pair, lat[:, pair * LANES : (pair + 1) * LANES], own)
    own = jnp.where(place % 2 == 1, pltpu.roll(own, 64, 1), own)
    turned = own.T[:64]
    wide = jnp.concatenate([turned] * 16, axis=1)
    spot = lax.broadcasted_iota(jnp.int32, wide.shape, 0) % 16
    spread = lax.broadcasted_iota(jnp.int32, wide.shape, 1) // 16
    merged = jnp.sum(jnp.where(spot == spread, wide, 0.0).reshape(4, 16, 256), axis=1)
    lat_ref[0, 0] = merged[:2]
    lat_ref[0, 1] = merged[2:]

    lat_bf = lat.astype(jnp.bfloat16)
    token = lax.broadcasted_iota(jnp.int32, (tokens, clips * 64), 0)
    lane = lax.broadcasted_iota(jnp.int32, (tokens, clips * 64), 1)
    first = token // 8 * 32 + token % 8 * 2
    projected = m_ref[64:65] + qkv_bias_ref[...]
    for a in range(2):
        for e in range(2):
            chosen = jnp.where(lane == first + (16 * a + e), 1.0, 0.0).astype(jnp.bfloat16)
            patch = lax.dot_general(
                chosen, lat_bf, (((1,), (1,)), ((), ())), preferred_element_type=jnp.float32
            ).astype(jnp.bfloat16)
            weight = m_ref[(2 * a + e) * TILE : (2 * a + e + 1) * TILE]
            coarse = weight.astype(jnp.bfloat16)
            fine = (weight - coarse.astype(jnp.float32)).astype(jnp.bfloat16)
            projected = projected + jnp.dot(patch, coarse, preferred_element_type=jnp.float32)
            projected = projected + jnp.dot(patch, fine, preferred_element_type=jnp.float32)

    even = lax.broadcasted_iota(jnp.int32, (tokens, HD), 1) % 2 == 0
    cosine = jnp.concatenate([cos_ref[...]] * clips, axis=0)
    sine = jnp.concatenate([sin_ref[...]] * clips, axis=0)

    def turn(vectors, gain_ref):
        square = jnp.mean(vectors * vectors, axis=-1, keepdims=True)
        vectors = vectors * lax.rsqrt(square + norm_eps) * gain_ref[...]
        swapped = jnp.where(even, pltpu.roll(vectors, HD - 1, 1), pltpu.roll(vectors, 1, 1))
        return vectors * cosine + swapped * sine

    def keep(ref, head, value):
        value = value.reshape(tokens // 8, 8, HD).astype(jnp.bfloat16)
        ref[:, :, head * HD : (head + 1) * HD] = value

    for head in range(q_ref.shape[2] // HD):
        at = 3 * HD * head
        keep(q_ref, head, turn(projected[:, at : at + HD], q_gain_ref))
        keep(k_ref, head, turn(projected[:, at + HD : at + 2 * HD], k_gain_ref))
        keep(v_ref, head, projected[:, at + 2 * HD : at + 3 * HD])


def rope_tables(frame_pos, row_pos, width):
    angles = rope_angles(frame_pos.astype(jnp.float32), row_pos.astype(jnp.float32), width)
    angles = angles.reshape(-1, HD // 2)
    cosine = jnp.repeat(jnp.cos(angles), 2, axis=1)
    sine = jnp.sin(angles)
    return cosine, jnp.stack([-sine, sine], axis=-1).reshape(cosine.shape)


def vmem(count):
    return [pl.BlockSpec(memory_space=pltpu.VMEM)] * count


def grouped(
    clip_inputs,
    conv_in_weight,
    group_gain,
    group_bias,
    conv_out_weight,
    out_bias,
    patch_weight,
    patch_bias,
    qkv_weight,
    qkv_bias,
    q_gain,
    k_gain,
    frame_pos,
    row_pos,
):
    plane_axes = ("tm", "height")
    clips = lax.axis_size("dp")
    steps = lax.axis_size("tm")
    plane = steps * lax.axis_size("height")
    place = lax.axis_index("tm") * lax.axis_size("height") + lax.axis_index("height")
    channels = clip_inputs.shape[4]
    depth = conv_in_weight.shape[0]

    block = clip_inputs.reshape(64, channels)
    with jax.named_scope("gather_clips"):
        everything = lax.all_gather(block, ("dp",) + plane_axes, axis=0, tiled=True)
    everything = everything.reshape(clips * steps, LANES, channels)
    with jax.named_scope("weight_by_group"):
        spread = conv_in_weight.T.reshape(plane, GROUP, depth)
        weight = lax.all_to_all(spread, plane_axes, 0, 0, tiled=True)

    with jax.named_scope("small_weights"):
        gain = lax.dynamic_slice_in_dim(group_gain, place * GROUP, GROUP).astype(jnp.float32)
        bias = lax.dynamic_slice_in_dim(group_bias, place * GROUP, GROUP).astype(jnp.float32)
        weight_out = lax.dynamic_slice_in_dim(conv_out_weight, place * GROUP, GROUP, axis=1)
        weight_out = weight_out.transpose(0, 2, 1).reshape(TAPS * TILE, GROUP)
        cosine, sine = rope_tables(frame_pos, row_pos, clip_inputs.shape[3] // 2)

    with jax.named_scope("merged_projection"):
        rows = qkv_weight.shape[0]
        stacked = jnp.concatenate(
            [
                lax.dynamic_slice_in_dim(patch_weight, place * rows, rows, axis=1),
                lax.dynamic_slice_in_dim(patch_bias, place * rows, rows)[None],
                jnp.zeros((7, rows), jnp.bfloat16),
            ],
            axis=0,
        )
        merged = jnp.dot(stacked, qkv_weight, preferred_element_type=jnp.float32)
        merged = lax.psum(merged, plane_axes)

    flops = 2 * clips * steps * LANES * TAPS * TILE * (channels + 16)
    partial = pl.pallas_call(
        conv_kernel,
        out_shape=jax.ShapeDtypeStruct((plane, TILE, clips * 64), jnp.float32),
        in_specs=vmem(5),
        out_specs=vmem(1)[0],
        scratch_shapes=[
            pltpu.VMEM((TAPS * GROUP, channels), jnp.bfloat16),
            pltpu.VMEM((TAPS * TILE, steps * LANES), jnp.float32),
            pltpu.VMEM((clips, steps, TILE, LANES), jnp.float32),
        ],
        compiler_params=pltpu.CompilerParams(vmem_limit_bytes=32 * 1024 * 1024),
        cost_estimate=pl.CostEstimate(
            flops=flops, bytes_accessed=everything.size * 2, transcendentals=0
        ),
        name="convolutions",
    )(everything, weight, gain[:, None], bias[:, None], weight_out)

    with jax.named_scope("sum_latents"):
        shares = lax.all_to_all(partial, plane_axes, 0, 0, tiled=True)
        here = jnp.sum(shares, axis=0)
        others = jnp.stack(
            [
                lax.ppermute(here, "dp", [(i, (i + step) % clips) for i in range(clips)])
                for step in range(1, clips)
            ]
        )

    heads = qkv_weight.shape[1] // (3 * HD)
    frames = clip_inputs.shape[1]
    tokens = jax.ShapeDtypeStruct((clips * frames, 8, heads * HD), jnp.bfloat16)
    latents, query, key, value = pl.pallas_call(
        token_kernel,
        out_shape=(jax.ShapeDtypeStruct((1, 2, 2, 256), jnp.float32), tokens, tokens, tokens),
        in_specs=vmem(9),
        out_specs=tuple(vmem(4)),
        compiler_params=pltpu.CompilerParams(vmem_limit_bytes=32 * 1024 * 1024),
        cost_estimate=pl.CostEstimate(flops=10**8, bytes_accessed=10**6, transcendentals=0),
        name="tokens",
    )(
        here,
        others,
        out_bias[:, None],
        merged,
        qkv_bias.astype(jnp.float32)[None],
        q_gain.astype(jnp.float32)[None],
        k_gain.astype(jnp.float32)[None],
        cosine,
        sine,
    )
    full = (clips, frames, 1, 8, heads * HD)
    return latents, query.reshape(full), key.reshape(full), value.reshape(full)


def pick(mesh, *arrays):
    if one_group_each(mesh, arrays[0], arrays[1], arrays[4]):
        return grouped(*arrays)
    return shards(*arrays)


def solution(mesh):
    placed = (
        P("dp", "tm", "height", None, None),
        P(("tm", "height"), "dp"),
        P("dp"),
        P("dp"),
        P(None, "dp", None),
        P(),
        P(),
        P(),
        P(("tm", "height"), "dp"),
        P("dp"),
        P(),
        P(),
        P("tm"),
        P("height"),
    )
    return jax.shard_map(
        functools.partial(pick, mesh),
        mesh=mesh,
        in_specs=placed,
        out_specs=(
            P("dp", "tm", "height", None),
            P(None, "tm", "height", None, "dp"),
            P(None, "tm", "height", None, "dp"),
            P(None, "tm", "height", None, "dp"),
        ),
        check_vma=False,
    )
```

```python
import functools

import jax
import jax.numpy as jnp
from jax import lax
from jax.experimental import pallas as pl
from jax.experimental.pallas import tpu as pltpu
from jax.sharding import PartitionSpec as P

HD = 128
GROUPS = 32
TAPS = 27


norm_eps = 1e-06
latent_scale = 0.476986
rope_base = 256.0
time_dims = 16
row_dims = 56


def from_behind(value, axis, steps):
    count = lax.axis_size(axis)
    first, last = (max(0, -steps), min(count, count - steps))
    return lax.ppermute(value, axis, [(source, source + steps) for source in range(first, last)])


def padded_2(block, sides, width):
    for axis, dim in sides:
        count = lax.axis_size(axis)
        forward = [(i, i + 1) for i in range(count - 1)]
        backward = [(target, source) for source, target in forward]
        low = lax.ppermute(
            lax.slice_in_dim(block, block.shape[dim] - width, None, axis=dim), axis, forward
        )
        high = lax.ppermute(lax.slice_in_dim(block, 0, width, axis=dim), axis, backward)
        block = jnp.concatenate([low, block, high], axis=dim)
    return block


def repeat_first(block):
    return jnp.concatenate([block[:, :1], block[:, :1]], axis=1)


def time_join(block, earlier):
    start = jnp.where(lax.axis_index("tm") == 0, repeat_first(block), earlier)
    return jnp.concatenate([start, block], axis=1)


def rows_finish(grown):
    place = lax.axis_index("height")
    top = jnp.where(place == 0, grown[:, :, 1:2], grown[:, :, :1])
    bottom = jnp.where(place == lax.axis_size("height") - 1, grown[:, :, -2:-1], grown[:, :, -1:])
    inner = jnp.concatenate([top, grown[:, :, 1:-1], bottom], axis=2)
    return jnp.pad(inner, ((0, 0), (0, 0), (0, 0), (1, 1), (0, 0)), mode="edge")


def edges_before(block):
    earlier = from_behind(block, "tm", 1)
    longer = time_join(block, earlier)
    return rows_finish(padded_2(longer, (("height", 2),), 1))


def edges_norm(block):
    earlier = from_behind(block, "tm", 1)
    longer = time_join(block, earlier)
    return rows_finish(padded_2(longer, (("height", 2),), 1))


def convolve(padded, weight):
    clips = padded.shape[0]
    frames = padded.shape[1] - 2
    rows = padded.shape[2] - 2
    cols = padded.shape[3] - 2
    total = jnp.zeros((clips * frames * rows * cols, weight.shape[2]), jnp.float32)
    for shift_t in range(3):
        for shift_r in range(3):
            for shift_c in range(3):
                window = padded[
                    :,
                    shift_t : shift_t + frames,
                    shift_r : shift_r + rows,
                    shift_c : shift_c + cols,
                ]
                window = window.reshape(-1, padded.shape[4])
                total = total + jnp.dot(
                    window,
                    weight[9 * shift_t + 3 * shift_r + shift_c],
                    preferred_element_type=jnp.float32,
                )
    return total.reshape(clips, frames, rows, cols, weight.shape[2])


def section_freqs(dims):
    return jnp.power(rope_base, -jnp.arange(0, dims, 2, dtype=jnp.float32) / dims)


def rope_angles(tpos, hpos, width):
    frames = tpos.shape[0]
    rows = hpos.shape[0]
    cols = jnp.arange(width, dtype=jnp.float32)
    part_t = tpos[:, None, None, None] * section_freqs(time_dims)
    part_h = hpos[None, :, None, None] * section_freqs(row_dims)
    part_w = cols[None, None, :, None] * section_freqs(row_dims)
    shape = (frames, rows, width)
    return jnp.concatenate(
        [
            jnp.broadcast_to(part_t, shape + (time_dims // 2,)),
            jnp.broadcast_to(part_h, shape + (row_dims // 2,)),
            jnp.broadcast_to(part_w, shape + (row_dims // 2,)),
        ],
        axis=-1,
    )


def rotate(vectors, angles):
    pairs = vectors.reshape(vectors.shape[:-1] + (vectors.shape[-1] // 2, 2))
    first = pairs[..., 0]
    second = pairs[..., 1]
    cosine = jnp.cos(angles)[..., None, :]
    sine = jnp.sin(angles)[..., None, :]
    turned = jnp.stack([first * cosine - second * sine, first * sine + second * cosine], axis=-1)
    return turned.reshape(vectors.shape)


def rms_scale(vectors, gain):
    return (
        vectors
        * lax.rsqrt(jnp.mean(vectors * vectors, axis=-1, keepdims=True) + norm_eps)
        * gain.astype(jnp.float32)
    )


def shards(
    clip_inputs,
    conv_in_weight,
    group_gain,
    group_bias,
    conv_out_weight,
    out_bias,
    patch_weight,
    patch_bias,
    qkv_weight,
    qkv_bias,
    q_gain,
    k_gain,
    frame_pos,
    row_pos,
):
    channels = clip_inputs.shape[4]
    frames = clip_inputs.shape[1]
    rows = clip_inputs.shape[2]
    cols = clip_inputs.shape[3]
    padded = lax.all_gather(edges_before(clip_inputs), "dp", axis=0, tiled=True)
    clips = padded.shape[0]
    weight_in = lax.all_gather(conv_in_weight, ("tm", "height"), axis=0, tiled=True).reshape(
        TAPS, channels, -1
    )
    hidden = convolve(padded, weight_in)
    block_width = hidden.shape[4]
    group_width = channels // GROUPS
    local_groups = block_width // group_width
    grouped = hidden.reshape(clips, -1, local_groups, group_width)
    sums_local = jnp.sum(grouped, axis=(1, 3))
    squares_local = jnp.sum(grouped * grouped, axis=(1, 3))
    sums_all, squares_all = lax.psum((sums_local, squares_local), ("tm", "height"))
    count = float(
        frames * lax.axis_size("tm") * rows * lax.axis_size("height") * cols * group_width
    )
    mean = sums_all / count
    var = squares_all / count - mean * mean
    scaled = (grouped - mean[:, None, :, None]) * lax.rsqrt(var + norm_eps)[:, None, :, None]
    scaled = scaled.reshape(hidden.shape) * group_gain.astype(jnp.float32) + group_bias.astype(
        jnp.float32
    )
    normed = jax.nn.silu(scaled).astype(jnp.bfloat16)
    partial_latent = convolve(edges_norm(normed), conv_out_weight)
    own_sum = lax.psum_scatter(partial_latent, "dp", scatter_dimension=0, tiled=True)
    own_latent = (own_sum + out_bias) * latent_scale
    every_latent = lax.all_gather(own_latent.astype(jnp.bfloat16), "dp", axis=0, tiled=True)
    latent_dims = every_latent.shape[4]
    latents = own_latent.reshape(1, frames, rows, cols * latent_dims)
    tok_rows = rows // 2
    tok_cols = cols // 2
    patches = every_latent.reshape(clips, frames, tok_rows, 2, tok_cols, 2, latent_dims)
    patches = patches.transpose(0, 1, 2, 4, 3, 5, 6).reshape(-1, 4 * latent_dims)
    embedded = (
        jnp.dot(patches, patch_weight, preferred_element_type=jnp.float32)
        + patch_bias.astype(jnp.float32)
    ).astype(jnp.bfloat16)
    projected = jnp.dot(
        embedded,
        lax.all_gather(qkv_weight, ("tm", "height"), axis=0, tiled=True),
        preferred_element_type=jnp.float32,
    )
    projected = projected + qkv_bias.astype(jnp.float32)
    local_heads = qkv_weight.shape[1] // (3 * HD)
    projected = projected.reshape(clips, frames, tok_rows, tok_cols, local_heads, 3, HD)
    angles = rope_angles(frame_pos.astype(jnp.float32), row_pos.astype(jnp.float32), tok_cols)
    query = rotate(rms_scale(projected[..., 0, :], q_gain), angles)
    key = rotate(rms_scale(projected[..., 1, :], k_gain), angles)
    value = projected[..., 2, :]
    merged = (clips, frames, tok_rows, tok_cols, local_heads * HD)
    return (
        latents,
        query.reshape(merged).astype(jnp.bfloat16),
        key.reshape(merged).astype(jnp.bfloat16),
        value.reshape(merged).astype(jnp.bfloat16),
    )


LANES = 128
TILE = 16
GROUP = 16


def one_group_each(mesh, clip_inputs, conv_in_weight, conv_out_weight):
    plane = mesh.shape["tm"] * mesh.shape["height"]
    return (
        clip_inputs.shape[:4] == (1, 2, 2, 16)
        and mesh.shape["height"] == 2
        and mesh.shape["tm"] == 4
        and mesh.shape["dp"] == 4
        and conv_in_weight.shape[1] == plane * GROUP
        and clip_inputs.shape[4] == GROUP * GROUPS
        and conv_out_weight.shape[2] == TILE
    )


def lane_shifts(lane):
    col = lane % 16
    row = lane // 16 % 2
    half = lane // 64

    def cols(left, mid, right):
        left = jnp.where(col == 0, left, pltpu.roll(left, 1, 1))
        right = jnp.where(col == 15, right, pltpu.roll(right, LANES - 1, 1))
        return mid + left + right

    def rows(up, mid, down):
        up = jnp.where(
            row == 1, pltpu.roll(up, 16, 1), jnp.where(half == 1, pltpu.roll(up, 48, 1), up)
        )
        down = jnp.where(
            row == 0,
            pltpu.roll(down, LANES - 16, 1),
            jnp.where(half == 0, pltpu.roll(down, LANES - 48, 1), down),
        )
        return mid + up + down

    return cols, rows


def tap_sums(y_ref, top, tiles):
    lane = lax.broadcasted_iota(jnp.int32, (TILE, LANES), 1)
    second = lane // 32 % 2 == 1
    cols, rows = lane_shifts(lane)
    sums = []
    before = None
    for tile in range(tiles):

        def part(tap):
            at = top + tap * TILE
            return y_ref[at : at + TILE, tile * LANES : (tile + 1) * LANES]

        oldest, older, now = (
            rows(*(cols(*(part(9 * i + 3 * j + l) for l in range(3))) for j in range(3)))
            for i in range(3)
        )
        turned = pltpu.roll(older, 32, 1)
        if before is None:
            start = jnp.where(second, pltpu.roll(oldest, 32, 1), oldest)
            total = now + jnp.where(second, turned, older) + start
        else:
            total = now + jnp.where(second, turned, pltpu.roll(before[1], 96, 1)) + before[0]
        before = (oldest, older)
        sums.append(total)
    return sums


def join_weight(w_ref, wt_ref, group, channels):
    depth = w_ref.shape[2]
    for tap in range(TAPS):
        start = tap * channels
        end = start + channels
        at = (group * TAPS + tap) * GROUP
        while start < end:
            source = start // depth
            stop = min(end, (source + 1) * depth)
            wt_ref[at : at + GROUP, start - tap * channels : stop - tap * channels] = w_ref[
                source, :, start - source * depth : stop - source * depth
            ]
            start = stop


def place_blocks(pieces, x_ref):
    blocks = pieces[0].shape[0] // 64
    layer = lax.axis_index("dp")
    high = lax.axis_index("tm") // 2
    side = lax.axis_index("height")
    for index, piece in enumerate(pieces):
        there = high if index < 2 else 1 - high
        beside = side if index % 2 == 0 else 1 - side
        for step in range(blocks):
            slot = lax.rem(layer + blocks - step, blocks)
            tile = slot // 2 * 4 + there * 2 + slot % 2
            x_ref[tile * 2 + beside] = piece[step * 64 : (step + 1) * 64]


def conv_kernel(
    own_ref, side_ref, high_ref, far_ref, w_ref, v_ref, gain_ref, bias_ref, w2_ref,
    out_ref, x_ref, wt_ref, y_ref, l_ref,
):
    clips, tiles = l_ref.shape[:2]
    channels = x_ref.shape[2]
    groups = wt_ref.shape[0] // (TAPS * GROUP)
    place_blocks((own_ref, side_ref, high_ref, far_ref), x_ref)
    join_weight(w_ref, wt_ref, 0, channels)
    join_weight(v_ref, wt_ref, 1, channels)
    count = float(tiles * LANES * GROUP)

    def one_clip(clip, carry):
        x = x_ref[pl.ds(clip * tiles * 2, tiles * 2)].reshape(tiles * LANES, channels)
        y_ref[...] = lax.dot_general(
            wt_ref[...], x, (((1,), (1,)), ((), ())), preferred_element_type=jnp.float32
        )
        normed = []
        for group in range(groups):
            hidden = tap_sums(y_ref, group * TAPS * GROUP, tiles)
            at = slice(group * GROUP, (group + 1) * GROUP)
            mean = sum(jnp.sum(part, keepdims=True) for part in hidden) / count
            square = sum(jnp.sum(part * part, keepdims=True) for part in hidden) / count
            scale = lax.rsqrt(square - mean * mean + norm_eps)
            parts = []
            for part in hidden:
                scaled = (part - mean) * scale * gain_ref[at] + bias_ref[at]
                parts.append((scaled / (1.0 + jnp.exp(-scaled))).astype(jnp.bfloat16))
            normed.append(jnp.concatenate(parts, axis=1))
        y_ref[: TAPS * TILE] = jnp.dot(
            w2_ref[...], jnp.concatenate(normed, axis=0), preferred_element_type=jnp.float32
        )
        for tile, part in enumerate(tap_sums(y_ref, 0, tiles)):
            l_ref[clip, tile] = part
        return carry

    lax.fori_loop(0, clips, one_clip, 0)
    low = lax.broadcasted_iota(jnp.int32, (TILE, LANES), 1) < 64
    for tile in range(tiles):
        one = l_ref[0, tile]
        two = l_ref[1, tile]
        out_ref[2 * tile] = jnp.where(low, one, pltpu.roll(two, 64, 1))
        out_ref[2 * tile + 1] = jnp.where(low, pltpu.roll(one, 64, 1), two)


def token_kernel(
    p_ref, o1_ref, o2_ref, o3_ref, bias_ref, m_ref, qkv_bias_ref, q_gain_ref, k_gain_ref, cos_ref, sin_ref,
    lat_ref, q_ref, k_ref, v_ref,
):
    total = p_ref[...] + o1_ref[...] + o2_ref[...] + o3_ref[...]
    total = jnp.concatenate([total[0], total[1]], axis=1)
    lat = (total + bias_ref[...]) * latent_scale
    clips = lat.shape[1] // 64
    tokens = clips * 16
    place = lax.axis_index("dp")
    own = lat[:, :LANES]
    for pair in range(1, clips // 2):
        own = jnp.where(place // 2 == pair, lat[:, pair * LANES : (pair + 1) * LANES], own)
    own = jnp.where(place % 2 == 1, pltpu.roll(own, 64, 1), own)
    turned = own.T[:64]
    wide = jnp.concatenate([turned] * 16, axis=1)
    spot = lax.broadcasted_iota(jnp.int32, wide.shape, 0) % 16
    spread = lax.broadcasted_iota(jnp.int32, wide.shape, 1) // 16
    merged = jnp.sum(jnp.where(spot == spread, wide, 0.0).reshape(4, 16, 256), axis=1)
    lat_ref[0, 0] = merged[:2]
    lat_ref[0, 1] = merged[2:]

    lat_bf = lat.astype(jnp.bfloat16)
    token = lax.broadcasted_iota(jnp.int32, (tokens, clips * 64), 0)
    lane = lax.broadcasted_iota(jnp.int32, (tokens, clips * 64), 1)
    first = token // 8 * 32 + token % 8 * 2
    projected = m_ref[64:65] + qkv_bias_ref[...]
    for a in range(2):
        for e in range(2):
            chosen = jnp.where(lane == first + (16 * a + e), 1.0, 0.0).astype(jnp.bfloat16)
            patch = lax.dot_general(
                chosen, lat_bf, (((1,), (1,)), ((), ())), preferred_element_type=jnp.float32
            ).astype(jnp.bfloat16)
            weight = m_ref[(2 * a + e) * TILE : (2 * a + e + 1) * TILE]
            coarse = weight.astype(jnp.bfloat16)
            fine = (weight - coarse.astype(jnp.float32)).astype(jnp.bfloat16)
            projected = projected + jnp.dot(patch, coarse, preferred_element_type=jnp.float32)
            projected = projected + jnp.dot(patch, fine, preferred_element_type=jnp.float32)

    even = lax.broadcasted_iota(jnp.int32, (tokens, HD), 1) % 2 == 0
    cosine = jnp.concatenate([cos_ref[...]] * clips, axis=0)
    sine = jnp.concatenate([sin_ref[...]] * clips, axis=0)

    def turn(vectors, gain_ref):
        square = jnp.mean(vectors * vectors, axis=-1, keepdims=True)
        vectors = vectors * lax.rsqrt(square + norm_eps) * gain_ref[...]
        swapped = jnp.where(even, pltpu.roll(vectors, HD - 1, 1), pltpu.roll(vectors, 1, 1))
        return vectors * cosine + swapped * sine

    def keep(ref, head, value):
        value = value.reshape(tokens // 8, 8, HD).astype(jnp.bfloat16)
        ref[:, :, head * HD : (head + 1) * HD] = value

    for head in range(q_ref.shape[2] // HD):
        at = 3 * HD * head
        keep(q_ref, head, turn(projected[:, at : at + HD], q_gain_ref))
        keep(k_ref, head, turn(projected[:, at + HD : at + 2 * HD], k_gain_ref))
        keep(v_ref, head, projected[:, at + 2 * HD : at + 3 * HD])


def rope_tables(frame_pos, row_pos, width):
    angles = rope_angles(frame_pos.astype(jnp.float32), row_pos.astype(jnp.float32), width)
    angles = angles.reshape(-1, HD // 2)
    cosine = jnp.repeat(jnp.cos(angles), 2, axis=1)
    sine = jnp.sin(angles)
    return cosine, jnp.stack([-sine, sine], axis=-1).reshape(cosine.shape)


def vmem(count):
    return [pl.BlockSpec(memory_space=pltpu.VMEM)] * count


def grouped(
    clip_inputs,
    conv_in_weight,
    group_gain,
    group_bias,
    conv_out_weight,
    out_bias,
    patch_weight,
    patch_bias,
    qkv_weight,
    qkv_bias,
    q_gain,
    k_gain,
    frame_pos,
    row_pos,
):
    plane_axes = ("tm", "height")
    clips = lax.axis_size("dp")
    steps = lax.axis_size("tm")
    plane = steps * lax.axis_size("height")
    place = lax.axis_index("tm") * lax.axis_size("height") + lax.axis_index("height")
    channels = clip_inputs.shape[4]
    depth = conv_in_weight.shape[0]

    with jax.named_scope("weight_by_group"):
        spread = conv_in_weight.T.reshape(plane, GROUP, depth)
        weight = lax.all_to_all(spread, plane_axes, 0, 0, tiled=True)
        weight_pair = lax.ppermute(weight, "tm", [(i, i ^ 1) for i in range(steps)])
    with jax.named_scope("gather_clips"):
        block = clip_inputs.reshape(64, channels)
        half = clips // 2
        blocks = []
        for step in range(clips):
            pairs = []
            for layer in range(clips):
                for tm in range(steps):
                    to = (layer % half * 2 + tm % 2 + step) % clips
                    pairs.append((layer * steps + tm, to * steps + tm // 2 * 2 + layer // half))
            blocks.append(lax.ppermute(block, ("dp", "tm"), pairs))
        own = jnp.concatenate(blocks, axis=0)
        side = lax.ppermute(own, "height", [(0, 1), (1, 0)])
        high = lax.ppermute(own, "tm", [(i, i ^ 2) for i in range(steps)])
        far = lax.ppermute(own, plane_axes, [(i, i ^ 5) for i in range(plane)])

    with jax.named_scope("small_weights"):
        pair_place = place + 2 - 4 * (lax.axis_index("tm") % 2)

        def both(values, axis):
            return jnp.concatenate(
                [
                    lax.dynamic_slice_in_dim(values, at * GROUP, GROUP, axis=axis)
                    for at in (place, pair_place)
                ],
                axis=axis,
            )

        gain = both(group_gain, 0).astype(jnp.float32)
        bias = both(group_bias, 0).astype(jnp.float32)
        weight_out = both(conv_out_weight, 1)
        weight_out = weight_out.transpose(0, 2, 1).reshape(TAPS * TILE, 2 * GROUP)
        cosine, sine = rope_tables(frame_pos, row_pos, clip_inputs.shape[3] // 2)

    with jax.named_scope("merged_projection"):
        rows = qkv_weight.shape[0]
        stacked = jnp.concatenate(
            [
                lax.dynamic_slice_in_dim(patch_weight, place * rows, rows, axis=1),
                lax.dynamic_slice_in_dim(patch_bias, place * rows, rows)[None],
                jnp.zeros((7, rows), jnp.bfloat16),
            ],
            axis=0,
        )
        merged = jnp.dot(stacked, qkv_weight, preferred_element_type=jnp.float32)
        merged = lax.psum(merged, plane_axes)

    flops = 2 * clips * steps * LANES * TAPS * TILE * (channels + 16)
    partial = pl.pallas_call(
        conv_kernel,
        out_shape=jax.ShapeDtypeStruct((plane, TILE, LANES), jnp.float32),
        in_specs=vmem(9),
        out_specs=vmem(1)[0],
        scratch_shapes=[
            pltpu.VMEM((half * steps * 2, 64, channels), jnp.bfloat16),
            pltpu.VMEM((2 * TAPS * GROUP, channels), jnp.bfloat16),
            pltpu.VMEM((2 * TAPS * GROUP, steps * LANES), jnp.float32),
            pltpu.VMEM((half, steps, TILE, LANES), jnp.float32),
        ],
        compiler_params=pltpu.CompilerParams(vmem_limit_bytes=32 * 1024 * 1024),
        cost_estimate=pl.CostEstimate(
            flops=flops, bytes_accessed=4 * own.size * 2, transcendentals=0
        ),
        name="convolutions",
    )(own, side, high, far, weight, weight_pair, gain[:, None], bias[:, None], weight_out)

    with jax.named_scope("sum_latents"):
        shares = lax.all_to_all(partial, plane_axes, 0, 0, tiled=True)
        here = jnp.sum(shares.reshape(steps // 2, 2, 2, TILE, LANES), axis=(0, 2))
        others = [
            lax.ppermute(here, "dp", [(i, (i + step) % clips) for i in range(clips)])
            for step in range(1, clips)
        ]

    heads = qkv_weight.shape[1] // (3 * HD)
    frames = clip_inputs.shape[1]
    tokens = jax.ShapeDtypeStruct((clips * frames, 8, heads * HD), jnp.bfloat16)
    latents, query, key, value = pl.pallas_call(
        token_kernel,
        out_shape=(jax.ShapeDtypeStruct((1, 2, 2, 256), jnp.float32), tokens, tokens, tokens),
        in_specs=vmem(11),
        out_specs=tuple(vmem(4)),
        compiler_params=pltpu.CompilerParams(vmem_limit_bytes=32 * 1024 * 1024),
        cost_estimate=pl.CostEstimate(flops=10**8, bytes_accessed=10**6, transcendentals=0),
        name="tokens",
    )(
        here,
        *others,
        out_bias[:, None],
        merged,
        qkv_bias.astype(jnp.float32)[None],
        q_gain.astype(jnp.float32)[None],
        k_gain.astype(jnp.float32)[None],
        cosine,
        sine,
    )
    full = (clips, frames, 1, 8, heads * HD)
    return latents, query.reshape(full), key.reshape(full), value.reshape(full)


def pick(mesh, *arrays):
    if one_group_each(mesh, arrays[0], arrays[1], arrays[4]):
        return grouped(*arrays)
    return shards(*arrays)


def solution(mesh):
    placed = (
        P("dp", "tm", "height", None, None),
        P(("tm", "height"), "dp"),
        P("dp"),
        P("dp"),
        P(None, "dp", None),
        P(),
        P(),
        P(),
        P(("tm", "height"), "dp"),
        P("dp"),
        P(),
        P(),
        P("tm"),
        P("height"),
    )
    return jax.shard_map(
        functools.partial(pick, mesh),
        mesh=mesh,
        in_specs=placed,
        out_specs=(
            P("dp", "tm", "height", None),
            P(None, "tm", "height", None, "dp"),
            P(None, "tm", "height", None, "dp"),
            P(None, "tm", "height", None, "dp"),
        ),
        check_vma=False,
    )
```

```python
import functools

import jax
import jax.numpy as jnp
from jax import lax
from jax.experimental import pallas as pl
from jax.experimental.pallas import tpu as pltpu
from jax.sharding import PartitionSpec as P

HD = 128
GROUPS = 32
TAPS = 27


norm_eps = 1e-06
latent_scale = 0.476986
rope_base = 256.0
time_dims = 16
row_dims = 56


def from_behind(value, axis, steps):
    count = lax.axis_size(axis)
    first, last = (max(0, -steps), min(count, count - steps))
    return lax.ppermute(value, axis, [(source, source + steps) for source in range(first, last)])


def padded_2(block, sides, width):
    for axis, dim in sides:
        count = lax.axis_size(axis)
        forward = [(i, i + 1) for i in range(count - 1)]
        backward = [(target, source) for source, target in forward]
        low = lax.ppermute(
            lax.slice_in_dim(block, block.shape[dim] - width, None, axis=dim), axis, forward
        )
        high = lax.ppermute(lax.slice_in_dim(block, 0, width, axis=dim), axis, backward)
        block = jnp.concatenate([low, block, high], axis=dim)
    return block


def repeat_first(block):
    return jnp.concatenate([block[:, :1], block[:, :1]], axis=1)


def time_join(block, earlier):
    start = jnp.where(lax.axis_index("tm") == 0, repeat_first(block), earlier)
    return jnp.concatenate([start, block], axis=1)


def rows_finish(grown):
    place = lax.axis_index("height")
    top = jnp.where(place == 0, grown[:, :, 1:2], grown[:, :, :1])
    bottom = jnp.where(place == lax.axis_size("height") - 1, grown[:, :, -2:-1], grown[:, :, -1:])
    inner = jnp.concatenate([top, grown[:, :, 1:-1], bottom], axis=2)
    return jnp.pad(inner, ((0, 0), (0, 0), (0, 0), (1, 1), (0, 0)), mode="edge")


def edges_before(block):
    earlier = from_behind(block, "tm", 1)
    longer = time_join(block, earlier)
    return rows_finish(padded_2(longer, (("height", 2),), 1))


def edges_norm(block):
    earlier = from_behind(block, "tm", 1)
    longer = time_join(block, earlier)
    return rows_finish(padded_2(longer, (("height", 2),), 1))


def convolve(padded, weight):
    clips = padded.shape[0]
    frames = padded.shape[1] - 2
    rows = padded.shape[2] - 2
    cols = padded.shape[3] - 2
    total = jnp.zeros((clips * frames * rows * cols, weight.shape[2]), jnp.float32)
    for shift_t in range(3):
        for shift_r in range(3):
            for shift_c in range(3):
                window = padded[
                    :,
                    shift_t : shift_t + frames,
                    shift_r : shift_r + rows,
                    shift_c : shift_c + cols,
                ]
                window = window.reshape(-1, padded.shape[4])
                total = total + jnp.dot(
                    window,
                    weight[9 * shift_t + 3 * shift_r + shift_c],
                    preferred_element_type=jnp.float32,
                )
    return total.reshape(clips, frames, rows, cols, weight.shape[2])


def section_freqs(dims):
    return jnp.power(rope_base, -jnp.arange(0, dims, 2, dtype=jnp.float32) / dims)


def rope_angles(tpos, hpos, width):
    frames = tpos.shape[0]
    rows = hpos.shape[0]
    cols = jnp.arange(width, dtype=jnp.float32)
    part_t = tpos[:, None, None, None] * section_freqs(time_dims)
    part_h = hpos[None, :, None, None] * section_freqs(row_dims)
    part_w = cols[None, None, :, None] * section_freqs(row_dims)
    shape = (frames, rows, width)
    return jnp.concatenate(
        [
            jnp.broadcast_to(part_t, shape + (time_dims // 2,)),
            jnp.broadcast_to(part_h, shape + (row_dims // 2,)),
            jnp.broadcast_to(part_w, shape + (row_dims // 2,)),
        ],
        axis=-1,
    )


def rotate(vectors, angles):
    pairs = vectors.reshape(vectors.shape[:-1] + (vectors.shape[-1] // 2, 2))
    first = pairs[..., 0]
    second = pairs[..., 1]
    cosine = jnp.cos(angles)[..., None, :]
    sine = jnp.sin(angles)[..., None, :]
    turned = jnp.stack([first * cosine - second * sine, first * sine + second * cosine], axis=-1)
    return turned.reshape(vectors.shape)


def rms_scale(vectors, gain):
    return (
        vectors
        * lax.rsqrt(jnp.mean(vectors * vectors, axis=-1, keepdims=True) + norm_eps)
        * gain.astype(jnp.float32)
    )


def shards(
    clip_inputs,
    conv_in_weight,
    group_gain,
    group_bias,
    conv_out_weight,
    out_bias,
    patch_weight,
    patch_bias,
    qkv_weight,
    qkv_bias,
    q_gain,
    k_gain,
    frame_pos,
    row_pos,
):
    channels = clip_inputs.shape[4]
    frames = clip_inputs.shape[1]
    rows = clip_inputs.shape[2]
    cols = clip_inputs.shape[3]
    padded = lax.all_gather(edges_before(clip_inputs), "dp", axis=0, tiled=True)
    clips = padded.shape[0]
    weight_in = lax.all_gather(conv_in_weight, ("tm", "height"), axis=0, tiled=True).reshape(
        TAPS, channels, -1
    )
    hidden = convolve(padded, weight_in)
    block_width = hidden.shape[4]
    group_width = channels // GROUPS
    local_groups = block_width // group_width
    grouped = hidden.reshape(clips, -1, local_groups, group_width)
    sums_local = jnp.sum(grouped, axis=(1, 3))
    squares_local = jnp.sum(grouped * grouped, axis=(1, 3))
    sums_all, squares_all = lax.psum((sums_local, squares_local), ("tm", "height"))
    count = float(
        frames * lax.axis_size("tm") * rows * lax.axis_size("height") * cols * group_width
    )
    mean = sums_all / count
    var = squares_all / count - mean * mean
    scaled = (grouped - mean[:, None, :, None]) * lax.rsqrt(var + norm_eps)[:, None, :, None]
    scaled = scaled.reshape(hidden.shape) * group_gain.astype(jnp.float32) + group_bias.astype(
        jnp.float32
    )
    normed = jax.nn.silu(scaled).astype(jnp.bfloat16)
    partial_latent = convolve(edges_norm(normed), conv_out_weight)
    own_sum = lax.psum_scatter(partial_latent, "dp", scatter_dimension=0, tiled=True)
    own_latent = (own_sum + out_bias) * latent_scale
    every_latent = lax.all_gather(own_latent.astype(jnp.bfloat16), "dp", axis=0, tiled=True)
    latent_dims = every_latent.shape[4]
    latents = own_latent.reshape(1, frames, rows, cols * latent_dims)
    tok_rows = rows // 2
    tok_cols = cols // 2
    patches = every_latent.reshape(clips, frames, tok_rows, 2, tok_cols, 2, latent_dims)
    patches = patches.transpose(0, 1, 2, 4, 3, 5, 6).reshape(-1, 4 * latent_dims)
    embedded = (
        jnp.dot(patches, patch_weight, preferred_element_type=jnp.float32)
        + patch_bias.astype(jnp.float32)
    ).astype(jnp.bfloat16)
    projected = jnp.dot(
        embedded,
        lax.all_gather(qkv_weight, ("tm", "height"), axis=0, tiled=True),
        preferred_element_type=jnp.float32,
    )
    projected = projected + qkv_bias.astype(jnp.float32)
    local_heads = qkv_weight.shape[1] // (3 * HD)
    projected = projected.reshape(clips, frames, tok_rows, tok_cols, local_heads, 3, HD)
    angles = rope_angles(frame_pos.astype(jnp.float32), row_pos.astype(jnp.float32), tok_cols)
    query = rotate(rms_scale(projected[..., 0, :], q_gain), angles)
    key = rotate(rms_scale(projected[..., 1, :], k_gain), angles)
    value = projected[..., 2, :]
    merged = (clips, frames, tok_rows, tok_cols, local_heads * HD)
    return (
        latents,
        query.reshape(merged).astype(jnp.bfloat16),
        key.reshape(merged).astype(jnp.bfloat16),
        value.reshape(merged).astype(jnp.bfloat16),
    )


LANES = 128
TILE = 16
GROUP = 16


def one_group_each(mesh, clip_inputs, conv_in_weight, conv_out_weight, qkv_weight):
    plane = mesh.shape["tm"] * mesh.shape["height"]
    return (
        clip_inputs.shape[:4] == (1, 2, 2, 16)
        and mesh.shape["height"] == 2
        and mesh.shape["tm"] == 4
        and mesh.shape["dp"] == 4
        and conv_in_weight.shape[1] == plane * GROUP
        and clip_inputs.shape[4] == GROUP * GROUPS
        and conv_out_weight.shape[2] == TILE
        and qkv_weight.shape[1] == 6 * HD
    )


def lane_shifts(lane):
    col = lane % 16
    row = lane // 16 % 2
    half = lane // 64

    def cols(left, mid, right):
        left = jnp.where(col == 0, left, pltpu.roll(left, 1, 1))
        right = jnp.where(col == 15, right, pltpu.roll(right, LANES - 1, 1))
        return mid + left + right

    def rows(up, mid, down):
        up = jnp.where(
            row == 1, pltpu.roll(up, 16, 1), jnp.where(half == 1, pltpu.roll(up, 48, 1), up)
        )
        down = jnp.where(
            row == 0,
            pltpu.roll(down, LANES - 16, 1),
            jnp.where(half == 0, pltpu.roll(down, LANES - 48, 1), down),
        )
        return mid + up + down

    return cols, rows


def tap_sums(y_ref, top, tiles):
    lane = lax.broadcasted_iota(jnp.int32, (TILE, LANES), 1)
    second = lane // 32 % 2 == 1
    cols, rows = lane_shifts(lane)
    sums = []
    before = None
    for tile in range(tiles):

        def part(tap):
            at = top + tap * TILE
            return y_ref[at : at + TILE, tile * LANES : (tile + 1) * LANES]

        oldest, older, now = (
            rows(*(cols(*(part(9 * i + 3 * j + l) for l in range(3))) for j in range(3)))
            for i in range(3)
        )
        turned = pltpu.roll(older, 32, 1)
        if before is None:
            start = jnp.where(second, pltpu.roll(oldest, 32, 1), oldest)
            total = now + jnp.where(second, turned, older) + start
        else:
            total = now + jnp.where(second, turned, pltpu.roll(before[1], 96, 1)) + before[0]
        before = (oldest, older)
        sums.append(total)
    return sums


def pack_kernel(w_ref, qkv_ref, patch_ref, patch_bias_ref, out_ref):
    plane, _, width = out_ref.shape
    depth = w_ref.shape[0]
    rows = qkv_ref.shape[0]
    place = lax.axis_index("tm") * lax.axis_size("height") + lax.axis_index("height")
    at = pl.ds(pl.multiple_of(place * rows, LANES), rows)
    merged = jnp.dot(patch_ref[:, at], qkv_ref[...], preferred_element_type=jnp.float32)
    bias = jnp.broadcast_to(patch_bias_ref[:, at], (8, rows))
    bias = jnp.dot(bias, qkv_ref[...], preferred_element_type=jnp.float32)
    line = lax.broadcasted_iota(jnp.int32, (8, LANES), 0)
    lines = jnp.zeros((8, LANES), jnp.float32)
    for part in range(bias.shape[1] // LANES):
        lines = jnp.where(line == part, bias[:, part * LANES : (part + 1) * LANES], lines)
    lines = jnp.concatenate([lines, jnp.zeros_like(lines)], axis=0).astype(jnp.bfloat16)
    turned = w_ref[...].T
    half = bias.shape[1] // 2
    for to in range(plane):
        out_ref[to, :, :depth] = turned[to * GROUP : (to + 1) * GROUP]
        out_ref[to, :, width - half - LANES : width - half] = lines
        mine = merged[8 * to : 8 * to + 8]
        mine = jnp.concatenate([mine[:, :half], mine[:, half:]], axis=0)
        out_ref[to, :, width - half :] = mine.astype(jnp.bfloat16)


def merge_kernel(parts_ref, share_ref, bias_ref):
    plane, rows, half = share_ref.shape
    at = parts_ref.shape[2] - half - LANES
    total = parts_ref[0, :, at:].astype(jnp.float32)
    for source in range(1, plane):
        total = total + parts_ref[source, :, at:].astype(jnp.float32)
    bias_ref[...] = total[:8, :LANES]
    for to in range(plane):
        share_ref[to] = total[:, LANES:].astype(jnp.bfloat16)


def join_weight(w_ref, wt_ref, group, channels):
    depth = TAPS * channels // w_ref.shape[0]
    for tap in range(TAPS):
        start = tap * channels
        end = start + channels
        at = (group * TAPS + tap) * GROUP
        while start < end:
            source = start // depth
            stop = min(end, (source + 1) * depth)
            wt_ref[at : at + GROUP, start - tap * channels : stop - tap * channels] = w_ref[
                source, :, start - source * depth : stop - source * depth
            ]
            start = stop


def conv_kernel(
    x_ref, w_ref, v_ref, gain_ref, bias_ref, w2_ref, out_ref, wt_ref, y_ref, l_ref
):
    clips, tiles = l_ref.shape[:2]
    channels = x_ref.shape[2]
    groups = wt_ref.shape[0] // (TAPS * GROUP)
    join_weight(w_ref, wt_ref, 0, channels)
    join_weight(v_ref, wt_ref, 1, channels)
    count = float(tiles * LANES * GROUP)

    def one_clip(clip, carry):
        x = x_ref[:, pl.ds(pl.multiple_of(clip * 64, 64), 64)].reshape(tiles * LANES, channels)
        y_ref[...] = lax.dot_general(
            wt_ref[...], x, (((1,), (1,)), ((), ())), preferred_element_type=jnp.float32
        )
        normed = []
        for group in range(groups):
            hidden = tap_sums(y_ref, group * TAPS * GROUP, tiles)
            at = slice(group * GROUP, (group + 1) * GROUP)
            mean = sum(jnp.sum(part, keepdims=True) for part in hidden) / count
            square = sum(jnp.sum(part * part, keepdims=True) for part in hidden) / count
            scale = lax.rsqrt(square - mean * mean + norm_eps)
            parts = []
            for part in hidden:
                scaled = (part - mean) * scale * gain_ref[at] + bias_ref[at]
                parts.append((scaled / (1.0 + jnp.exp(-scaled))).astype(jnp.bfloat16))
            normed.append(jnp.concatenate(parts, axis=1))
        y_ref[: TAPS * TILE] = jnp.dot(
            w2_ref[...], jnp.concatenate(normed, axis=0), preferred_element_type=jnp.float32
        )
        for tile, part in enumerate(tap_sums(y_ref, 0, tiles)):
            l_ref[clip, tile] = part
        return carry

    lax.fori_loop(0, clips, one_clip, 0)
    low = lax.broadcasted_iota(jnp.int32, (TILE, LANES), 1) < 64
    for tile in range(tiles):
        one = l_ref[0, tile]
        two = l_ref[1, tile]
        out_ref[2 * tile] = jnp.where(low, one, pltpu.roll(two, 64, 1))
        out_ref[2 * tile + 1] = jnp.where(low, pltpu.roll(one, 64, 1), two)


def token_kernel(
    p_ref, o1_ref, o2_ref, o3_ref, bias_ref, m_ref, m_bias_ref, qkv_bias_ref, q_gain_ref, k_gain_ref, cos_ref, sin_ref,
    lat_ref, q_ref, k_ref, v_ref,
):
    total = p_ref[...] + o1_ref[...] + o2_ref[...] + o3_ref[...]
    total = jnp.concatenate([total[0], total[1]], axis=1)
    lat = (total + bias_ref[...]) * latent_scale
    clips = lat.shape[1] // 64
    tokens = clips * 16
    place = lax.axis_index("dp")
    own = lat[:, :LANES]
    for pair in range(1, clips // 2):
        own = jnp.where(place // 2 == pair, lat[:, pair * LANES : (pair + 1) * LANES], own)
    own = jnp.where(place % 2 == 1, pltpu.roll(own, 64, 1), own)
    turned = own.T[:64]
    wide = jnp.concatenate([turned] * 16, axis=1)
    spot = lax.broadcasted_iota(jnp.int32, wide.shape, 0) % 16
    spread = lax.broadcasted_iota(jnp.int32, wide.shape, 1) // 16
    merged = jnp.sum(jnp.where(spot == spread, wide, 0.0).reshape(4, 16, 256), axis=1)
    lat_ref[0, 0] = merged[:2]
    lat_ref[0, 1] = merged[2:]

    lat_bf = lat.astype(jnp.bfloat16)
    token = lax.broadcasted_iota(jnp.int32, (tokens, clips * 64), 0)
    lane = lax.broadcasted_iota(jnp.int32, (tokens, clips * 64), 1)
    first = token // 8 * 32 + token % 8 * 2
    heads = q_ref.shape[2] // HD
    extra = [m_bias_ref[part : part + 1] for part in range(3 * heads)]
    projected = jnp.concatenate(extra, axis=1) + qkv_bias_ref[...]
    merged = m_ref[...].astype(jnp.float32)
    merged = jnp.concatenate(
        [merged[:, half * 8 : half * 8 + 8].reshape(64, -1) for half in range(2)], axis=1
    ).astype(jnp.bfloat16)
    for a in range(2):
        for e in range(2):
            chosen = jnp.where(lane == first + (16 * a + e), 1.0, 0.0).astype(jnp.bfloat16)
            patch = lax.dot_general(
                chosen, lat_bf, (((1,), (1,)), ((), ())), preferred_element_type=jnp.float32
            ).astype(jnp.bfloat16)
            weight = merged[(2 * a + e) * TILE : (2 * a + e + 1) * TILE]
            projected = projected + jnp.dot(patch, weight, preferred_element_type=jnp.float32)

    even = lax.broadcasted_iota(jnp.int32, (tokens, HD), 1) % 2 == 0
    cosine = jnp.concatenate([cos_ref[...]] * clips, axis=0)
    sine = jnp.concatenate([sin_ref[...]] * clips, axis=0)

    def turn(vectors, gain_ref):
        square = jnp.mean(vectors * vectors, axis=-1, keepdims=True)
        vectors = vectors * lax.rsqrt(square + norm_eps) * gain_ref[...]
        swapped = jnp.where(even, pltpu.roll(vectors, HD - 1, 1), pltpu.roll(vectors, 1, 1))
        return vectors * cosine + swapped * sine

    def keep(ref, head, value):
        value = value.reshape(tokens // 8, 8, HD).astype(jnp.bfloat16)
        ref[:, :, head * HD : (head + 1) * HD] = value

    for head in range(heads):
        at = 3 * HD * head
        keep(q_ref, head, turn(projected[:, at : at + HD], q_gain_ref))
        keep(k_ref, head, turn(projected[:, at + HD : at + 2 * HD], k_gain_ref))
        keep(v_ref, head, projected[:, at + 2 * HD : at + 3 * HD])


def rope_tables(frame_pos, row_pos, width):
    angles = rope_angles(frame_pos.astype(jnp.float32), row_pos.astype(jnp.float32), width)
    angles = angles.reshape(-1, HD // 2)
    cosine = jnp.repeat(jnp.cos(angles), 2, axis=1)
    sine = jnp.sin(angles)
    return cosine, jnp.stack([-sine, sine], axis=-1).reshape(cosine.shape)


def vmem(count):
    return [pl.BlockSpec(memory_space=pltpu.VMEM)] * count


def grouped(
    clip_inputs,
    conv_in_weight,
    group_gain,
    group_bias,
    conv_out_weight,
    out_bias,
    patch_weight,
    patch_bias,
    qkv_weight,
    qkv_bias,
    q_gain,
    k_gain,
    frame_pos,
    row_pos,
):
    plane_axes = ("tm", "height")
    clips = lax.axis_size("dp")
    steps = lax.axis_size("tm")
    plane = steps * lax.axis_size("height")
    place = lax.axis_index("tm") * lax.axis_size("height") + lax.axis_index("height")
    channels = clip_inputs.shape[4]
    depth = conv_in_weight.shape[0]

    width = -(-depth // LANES) * LANES + LANES + qkv_weight.shape[1] // 2
    half = clips // 2
    with jax.named_scope("gather_clips"):
        block = clip_inputs.reshape(64, channels)
        block = jnp.broadcast_to(block[None], (clips, 64, channels))
        layers = lax.all_to_all(block, "dp", 0, 0, tiled=True)
    with jax.named_scope("weight_by_group"):
        packed = pl.pallas_call(
            pack_kernel,
            out_shape=jax.ShapeDtypeStruct((plane, GROUP, width), jnp.bfloat16),
            in_specs=vmem(4),
            out_specs=vmem(1)[0],
            compiler_params=pltpu.CompilerParams(vmem_limit_bytes=32 * 1024 * 1024),
            cost_estimate=pl.CostEstimate(flops=10**8, bytes_accessed=10**6, transcendentals=0),
            name="pack_weights",
        )(conv_in_weight, qkv_weight, patch_weight, patch_bias[None])
        weight = lax.all_to_all(packed, plane_axes, 0, 0, tiled=True)
        weight_pair = lax.ppermute(weight, "tm", [(i, i ^ 1) for i in range(steps)])
    with jax.named_scope("spread_clips"):
        halves = layers.reshape(1, 2, 1, half * 64, channels)
        halves = jnp.broadcast_to(halves, (steps // 2, 2, 2, half * 64, channels))
        halves = halves.reshape(plane, half * 64, channels)
        everything = lax.all_to_all(halves, plane_axes, 0, 0, tiled=True)
    with jax.named_scope("merged_projection"):
        share, merged_bias = pl.pallas_call(
            merge_kernel,
            out_shape=(
                jax.ShapeDtypeStruct((plane, 16, qkv_weight.shape[1] // 2), jnp.bfloat16),
                jax.ShapeDtypeStruct((8, LANES), jnp.float32),
            ),
            in_specs=vmem(1),
            out_specs=tuple(vmem(2)),
            compiler_params=pltpu.CompilerParams(vmem_limit_bytes=32 * 1024 * 1024),
            cost_estimate=pl.CostEstimate(flops=10**6, bytes_accessed=10**6, transcendentals=0),
            name="merge_projection",
        )(weight)
        merged = lax.all_to_all(share, plane_axes, 0, 0, tiled=True)

    with jax.named_scope("small_weights"):
        pair_place = place + 2 - 4 * (lax.axis_index("tm") % 2)

        def both(values, axis):
            return jnp.concatenate(
                [
                    lax.dynamic_slice_in_dim(values, at * GROUP, GROUP, axis=axis)
                    for at in (place, pair_place)
                ],
                axis=axis,
            )

        gain = both(group_gain, 0).astype(jnp.float32)
        bias = both(group_bias, 0).astype(jnp.float32)
        weight_out = both(conv_out_weight, 1)
        weight_out = weight_out.transpose(0, 2, 1).reshape(TAPS * TILE, 2 * GROUP)
        cosine, sine = rope_tables(frame_pos, row_pos, clip_inputs.shape[3] // 2)

    flops = 2 * clips * steps * LANES * TAPS * TILE * (channels + 16)
    partial = pl.pallas_call(
        conv_kernel,
        out_shape=jax.ShapeDtypeStruct((plane, TILE, LANES), jnp.float32),
        in_specs=vmem(6),
        out_specs=vmem(1)[0],
        scratch_shapes=[
            pltpu.VMEM((2 * TAPS * GROUP, channels), jnp.bfloat16),
            pltpu.VMEM((2 * TAPS * GROUP, steps * LANES), jnp.float32),
            pltpu.VMEM((half, steps, TILE, LANES), jnp.float32),
        ],
        compiler_params=pltpu.CompilerParams(vmem_limit_bytes=32 * 1024 * 1024),
        cost_estimate=pl.CostEstimate(
            flops=flops, bytes_accessed=everything.size * 2, transcendentals=0
        ),
        name="convolutions",
    )(everything, weight, weight_pair, gain[:, None], bias[:, None], weight_out)

    with jax.named_scope("sum_latents"):
        shares = lax.all_to_all(partial, plane_axes, 0, 0, tiled=True)
        here = jnp.sum(shares.reshape(steps // 2, 2, 2, TILE, LANES), axis=(0, 2))
        others = [
            lax.ppermute(here, "dp", [(i, (i + step) % clips) for i in range(clips)])
            for step in range(1, clips)
        ]

    heads = qkv_weight.shape[1] // (3 * HD)
    frames = clip_inputs.shape[1]
    tokens = jax.ShapeDtypeStruct((clips * frames, 8, heads * HD), jnp.bfloat16)
    latents, query, key, value = pl.pallas_call(
        token_kernel,
        out_shape=(jax.ShapeDtypeStruct((1, 2, 2, 256), jnp.float32), tokens, tokens, tokens),
        in_specs=vmem(12),
        out_specs=tuple(vmem(4)),
        compiler_params=pltpu.CompilerParams(vmem_limit_bytes=32 * 1024 * 1024),
        cost_estimate=pl.CostEstimate(flops=10**8, bytes_accessed=10**6, transcendentals=0),
        name="tokens",
    )(
        here,
        *others,
        out_bias[:, None],
        merged,
        merged_bias,
        qkv_bias.astype(jnp.float32)[None],
        q_gain.astype(jnp.float32)[None],
        k_gain.astype(jnp.float32)[None],
        cosine,
        sine,
    )
    full = (clips, frames, 1, 8, heads * HD)
    return latents, query.reshape(full), key.reshape(full), value.reshape(full)


def pick(mesh, *arrays):
    if one_group_each(mesh, arrays[0], arrays[1], arrays[4], arrays[8]):
        return grouped(*arrays)
    return shards(*arrays)


def solution(mesh):
    placed = (
        P("dp", "tm", "height", None, None),
        P(("tm", "height"), "dp"),
        P("dp"),
        P("dp"),
        P(None, "dp", None),
        P(),
        P(),
        P(),
        P(("tm", "height"), "dp"),
        P("dp"),
        P(),
        P(),
        P("tm"),
        P("height"),
    )
    return jax.shard_map(
        functools.partial(pick, mesh),
        mesh=mesh,
        in_specs=placed,
        out_specs=(
            P("dp", "tm", "height", None),
            P(None, "tm", "height", None, "dp"),
            P(None, "tm", "height", None, "dp"),
            P(None, "tm", "height", None, "dp"),
        ),
        check_vma=False,
    )
```

```python
import functools

import jax
import jax.numpy as jnp
from jax import lax
from jax.experimental import pallas as pl
from jax.experimental.pallas import tpu as pltpu
from jax.sharding import PartitionSpec as P

HD = 128
GROUPS = 32
TAPS = 27


norm_eps = 1e-06
latent_scale = 0.476986
rope_base = 256.0
time_dims = 16
row_dims = 56


def from_behind(value, axis, steps):
    count = lax.axis_size(axis)
    first, last = (max(0, -steps), min(count, count - steps))
    return lax.ppermute(value, axis, [(source, source + steps) for source in range(first, last)])


def padded_2(block, sides, width):
    for axis, dim in sides:
        count = lax.axis_size(axis)
        forward = [(i, i + 1) for i in range(count - 1)]
        backward = [(target, source) for source, target in forward]
        low = lax.ppermute(
            lax.slice_in_dim(block, block.shape[dim] - width, None, axis=dim), axis, forward
        )
        high = lax.ppermute(lax.slice_in_dim(block, 0, width, axis=dim), axis, backward)
        block = jnp.concatenate([low, block, high], axis=dim)
    return block


def repeat_first(block):
    return jnp.concatenate([block[:, :1], block[:, :1]], axis=1)


def time_join(block, earlier):
    start = jnp.where(lax.axis_index("tm") == 0, repeat_first(block), earlier)
    return jnp.concatenate([start, block], axis=1)


def rows_finish(grown):
    place = lax.axis_index("height")
    top = jnp.where(place == 0, grown[:, :, 1:2], grown[:, :, :1])
    bottom = jnp.where(place == lax.axis_size("height") - 1, grown[:, :, -2:-1], grown[:, :, -1:])
    inner = jnp.concatenate([top, grown[:, :, 1:-1], bottom], axis=2)
    return jnp.pad(inner, ((0, 0), (0, 0), (0, 0), (1, 1), (0, 0)), mode="edge")


def edges_before(block):
    earlier = from_behind(block, "tm", 1)
    longer = time_join(block, earlier)
    return rows_finish(padded_2(longer, (("height", 2),), 1))


def edges_norm(block):
    earlier = from_behind(block, "tm", 1)
    longer = time_join(block, earlier)
    return rows_finish(padded_2(longer, (("height", 2),), 1))


def convolve(padded, weight):
    clips = padded.shape[0]
    frames = padded.shape[1] - 2
    rows = padded.shape[2] - 2
    cols = padded.shape[3] - 2
    total = jnp.zeros((clips * frames * rows * cols, weight.shape[2]), jnp.float32)
    for shift_t in range(3):
        for shift_r in range(3):
            for shift_c in range(3):
                window = padded[
                    :,
                    shift_t : shift_t + frames,
                    shift_r : shift_r + rows,
                    shift_c : shift_c + cols,
                ]
                window = window.reshape(-1, padded.shape[4])
                total = total + jnp.dot(
                    window,
                    weight[9 * shift_t + 3 * shift_r + shift_c],
                    preferred_element_type=jnp.float32,
                )
    return total.reshape(clips, frames, rows, cols, weight.shape[2])


def section_freqs(dims):
    return jnp.power(rope_base, -jnp.arange(0, dims, 2, dtype=jnp.float32) / dims)


def rope_angles(tpos, hpos, width):
    frames = tpos.shape[0]
    rows = hpos.shape[0]
    cols = jnp.arange(width, dtype=jnp.float32)
    part_t = tpos[:, None, None, None] * section_freqs(time_dims)
    part_h = hpos[None, :, None, None] * section_freqs(row_dims)
    part_w = cols[None, None, :, None] * section_freqs(row_dims)
    shape = (frames, rows, width)
    return jnp.concatenate(
        [
            jnp.broadcast_to(part_t, shape + (time_dims // 2,)),
            jnp.broadcast_to(part_h, shape + (row_dims // 2,)),
            jnp.broadcast_to(part_w, shape + (row_dims // 2,)),
        ],
        axis=-1,
    )


def rotate(vectors, angles):
    pairs = vectors.reshape(vectors.shape[:-1] + (vectors.shape[-1] // 2, 2))
    first = pairs[..., 0]
    second = pairs[..., 1]
    cosine = jnp.cos(angles)[..., None, :]
    sine = jnp.sin(angles)[..., None, :]
    turned = jnp.stack([first * cosine - second * sine, first * sine + second * cosine], axis=-1)
    return turned.reshape(vectors.shape)


def rms_scale(vectors, gain):
    return (
        vectors
        * lax.rsqrt(jnp.mean(vectors * vectors, axis=-1, keepdims=True) + norm_eps)
        * gain.astype(jnp.float32)
    )


def shards(
    clip_inputs,
    conv_in_weight,
    group_gain,
    group_bias,
    conv_out_weight,
    out_bias,
    patch_weight,
    patch_bias,
    qkv_weight,
    qkv_bias,
    q_gain,
    k_gain,
    frame_pos,
    row_pos,
):
    channels = clip_inputs.shape[4]
    frames = clip_inputs.shape[1]
    rows = clip_inputs.shape[2]
    cols = clip_inputs.shape[3]
    padded = lax.all_gather(edges_before(clip_inputs), "dp", axis=0, tiled=True)
    clips = padded.shape[0]
    weight_in = lax.all_gather(conv_in_weight, ("tm", "height"), axis=0, tiled=True).reshape(
        TAPS, channels, -1
    )
    hidden = convolve(padded, weight_in)
    block_width = hidden.shape[4]
    group_width = channels // GROUPS
    local_groups = block_width // group_width
    grouped = hidden.reshape(clips, -1, local_groups, group_width)
    sums_local = jnp.sum(grouped, axis=(1, 3))
    squares_local = jnp.sum(grouped * grouped, axis=(1, 3))
    sums_all, squares_all = lax.psum((sums_local, squares_local), ("tm", "height"))
    count = float(
        frames * lax.axis_size("tm") * rows * lax.axis_size("height") * cols * group_width
    )
    mean = sums_all / count
    var = squares_all / count - mean * mean
    scaled = (grouped - mean[:, None, :, None]) * lax.rsqrt(var + norm_eps)[:, None, :, None]
    scaled = scaled.reshape(hidden.shape) * group_gain.astype(jnp.float32) + group_bias.astype(
        jnp.float32
    )
    normed = jax.nn.silu(scaled).astype(jnp.bfloat16)
    partial_latent = convolve(edges_norm(normed), conv_out_weight)
    own_sum = lax.psum_scatter(partial_latent, "dp", scatter_dimension=0, tiled=True)
    own_latent = (own_sum + out_bias) * latent_scale
    every_latent = lax.all_gather(own_latent.astype(jnp.bfloat16), "dp", axis=0, tiled=True)
    latent_dims = every_latent.shape[4]
    latents = own_latent.reshape(1, frames, rows, cols * latent_dims)
    tok_rows = rows // 2
    tok_cols = cols // 2
    patches = every_latent.reshape(clips, frames, tok_rows, 2, tok_cols, 2, latent_dims)
    patches = patches.transpose(0, 1, 2, 4, 3, 5, 6).reshape(-1, 4 * latent_dims)
    embedded = (
        jnp.dot(patches, patch_weight, preferred_element_type=jnp.float32)
        + patch_bias.astype(jnp.float32)
    ).astype(jnp.bfloat16)
    projected = jnp.dot(
        embedded,
        lax.all_gather(qkv_weight, ("tm", "height"), axis=0, tiled=True),
        preferred_element_type=jnp.float32,
    )
    projected = projected + qkv_bias.astype(jnp.float32)
    local_heads = qkv_weight.shape[1] // (3 * HD)
    projected = projected.reshape(clips, frames, tok_rows, tok_cols, local_heads, 3, HD)
    angles = rope_angles(frame_pos.astype(jnp.float32), row_pos.astype(jnp.float32), tok_cols)
    query = rotate(rms_scale(projected[..., 0, :], q_gain), angles)
    key = rotate(rms_scale(projected[..., 1, :], k_gain), angles)
    value = projected[..., 2, :]
    merged = (clips, frames, tok_rows, tok_cols, local_heads * HD)
    return (
        latents,
        query.reshape(merged).astype(jnp.bfloat16),
        key.reshape(merged).astype(jnp.bfloat16),
        value.reshape(merged).astype(jnp.bfloat16),
    )


LANES = 128
TILE = 16
GROUP = 16


def one_group_each(mesh, clip_inputs, conv_in_weight, conv_out_weight, qkv_weight):
    plane = mesh.shape["tm"] * mesh.shape["height"]
    return (
        clip_inputs.shape[:4] == (1, 2, 2, 16)
        and mesh.shape["height"] == 2
        and mesh.shape["tm"] == 4
        and mesh.shape["dp"] == 4
        and conv_in_weight.shape[1] == plane * GROUP
        and clip_inputs.shape[4] == GROUP * GROUPS
        and conv_out_weight.shape[2] == TILE
        and qkv_weight.shape[1] == 6 * HD
    )


def lane_shifts(lane):
    col = lane % 16
    row = lane // 16 % 2
    half = lane // 64

    def cols(left, mid, right):
        left = jnp.where(col == 0, left, pltpu.roll(left, 1, 1))
        right = jnp.where(col == 15, right, pltpu.roll(right, LANES - 1, 1))
        return mid + left + right

    def rows(up, mid, down):
        up = jnp.where(
            row == 1, pltpu.roll(up, 16, 1), jnp.where(half == 1, pltpu.roll(up, 48, 1), up)
        )
        down = jnp.where(
            row == 0,
            pltpu.roll(down, LANES - 16, 1),
            jnp.where(half == 0, pltpu.roll(down, LANES - 48, 1), down),
        )
        return mid + up + down

    return cols, rows


def tap_sums(y_ref, group, tiles):
    lane = lax.broadcasted_iota(jnp.int32, (TILE, LANES), 1)
    second = lane // 32 % 2 == 1
    cols, rows = lane_shifts(lane)
    sums = []
    before = None
    for tile in range(tiles):

        def part(tap):
            at = tap * TILE
            return y_ref[group, at : at + TILE, tile * LANES : (tile + 1) * LANES]

        oldest, older, now = (
            rows(*(cols(*(part(9 * i + 3 * j + l) for l in range(3))) for j in range(3)))
            for i in range(3)
        )
        turned = pltpu.roll(older, 32, 1)
        if before is None:
            start = jnp.where(second, pltpu.roll(oldest, 32, 1), oldest)
            total = now + jnp.where(second, turned, older) + start
        else:
            total = now + jnp.where(second, turned, pltpu.roll(before[1], 96, 1)) + before[0]
        before = (oldest, older)
        sums.append(total)
    return sums


def pack_kernel(w_ref, qkv_ref, patch_ref, patch_bias_ref, block_ref, out_ref, copy_ref):
    copy_ref[...] = block_ref[...]
    plane, channels, width = out_ref.shape
    depth = w_ref.shape[0]
    rows = qkv_ref.shape[0]
    place = lax.axis_index("tm") * lax.axis_size("height") + lax.axis_index("height")
    at = pl.ds(pl.multiple_of(place * rows, LANES), rows)
    merged = jnp.dot(patch_ref[:, at], qkv_ref[...], preferred_element_type=jnp.float32)
    bias = jnp.broadcast_to(patch_bias_ref[:, at], (8, rows))
    bias = jnp.dot(bias, qkv_ref[...], preferred_element_type=jnp.float32)
    line = lax.broadcasted_iota(jnp.int32, (8, LANES), 0)
    lines = jnp.zeros((8, LANES), jnp.float32)
    for part in range(bias.shape[1] // LANES):
        lines = jnp.where(line == part, bias[:, part * LANES : (part + 1) * LANES], lines)
    turned = w_ref[...].T
    for to in range(plane):
        first = to // 2 * channels
        out_ref[to, :, :depth] = turned[first : first + channels]
        parts = [merged[8 * to : 8 * to + 8, q * LANES : (q + 1) * LANES] for q in range(6)]
        parts += [lines, jnp.zeros_like(lines)]
        for tile in range(2):
            some = jnp.concatenate(parts[4 * tile : 4 * tile + 4], axis=0)
            end = width - LANES * (1 - tile)
            out_ref[to, :, end - LANES : end] = some.astype(jnp.bfloat16)


def arrange_kernel(own_ref, one_ref, two_ref, three_ref, *rest):
    out_refs, all_ref = rest[:4], rest[4]
    clip = lax.axis_index("height") * 2 + lax.axis_index("tm") % 2
    layer = lax.axis_index("dp")
    for step, piece in enumerate((own_ref, one_ref, two_ref, three_ref)):
        all_ref[(layer + 4 - step) % 4] = piece[...]
    for flip, out_ref in enumerate(out_refs):
        out_ref[...] = all_ref[clip ^ flip]


def merge_kernel(
    parts_ref, out_bias_ref, qkv_bias_ref, q_gain_ref, k_gain_ref,
    share_ref, bias_ref, qkv_ref, gains_ref,
):
    plane = parts_ref.shape[0]
    at = parts_ref.shape[2] - 2 * LANES
    total = parts_ref[0, :, at:].astype(jnp.float32)
    for source in range(1, plane):
        total = total + parts_ref[source, :, at:].astype(jnp.float32)
    for q in range(6):
        share_ref[8 * q : 8 * q + 8] = total[
            q % 4 * 8 : q % 4 * 8 + 8, q // 4 * LANES : (q // 4 + 1) * LANES
        ]
    extra = jnp.concatenate([total[16 + q : 17 + q, LANES:] for q in range(6)], axis=1)
    qkv_ref[...] = extra + qkv_bias_ref[...].astype(jnp.float32)
    bias_ref[...] = jnp.broadcast_to(out_bias_ref[...], bias_ref.shape)
    gains_ref[0:1] = q_gain_ref[...].astype(jnp.float32)
    gains_ref[1:2] = k_gain_ref[...].astype(jnp.float32)


def join_weight(w_ref, wt_ref, half, channels):
    depth = TAPS * channels // w_ref.shape[0]
    for group in range(w_ref.shape[1] // GROUP):
        for tap in range(TAPS):
            start = tap * channels
            end = start + channels
            at = (group * TAPS + tap) * GROUP
            while start < end:
                source = start // depth
                stop = min(end, (source + 1) * depth)
                wt_ref[
                    half, at : at + GROUP, start - tap * channels : stop - tap * channels
                ] = w_ref[
                    source,
                    group * GROUP : (group + 1) * GROUP,
                    start - source * depth : stop - source * depth,
                ]
                start = stop


def conv_kernel(*refs):
    x_refs, refs = refs[:8], refs[8:]
    w_ref, v_ref, gain_ref, bias_ref, w2_ref, share_ref, out_ref, x_ref, wt_ref, y_ref = refs
    channels = x_ref.shape[2]
    tiles = x_ref.shape[0] // 2
    place = lax.axis_index("tm") * 2 + lax.axis_index("height")
    for flip, piece in enumerate(x_refs):
        x_ref[place ^ flip] = piece[...]
    half = lax.axis_index("tm") % 2
    join_weight(w_ref, wt_ref, half, channels)
    join_weight(v_ref, wt_ref, 1 - half, channels)
    count = float(tiles * LANES * GROUP)
    x = x_ref[...].reshape(tiles * LANES, channels)
    taps = TAPS * GROUP
    normed = []
    for group in range(4):
        at = group % 2 * taps
        y_ref[group] = lax.dot_general(
            wt_ref[group // 2, at : at + taps],
            x,
            (((1,), (1,)), ((), ())),
            preferred_element_type=jnp.float32,
        )
        hidden = tap_sums(y_ref, group, tiles)
        at = slice(group * GROUP, (group + 1) * GROUP)
        mean = sum(jnp.sum(part, keepdims=True) for part in hidden) / count
        square = sum(jnp.sum(part * part, keepdims=True) for part in hidden) / count
        scale = lax.rsqrt(square - mean * mean + norm_eps)
        parts = []
        for part in hidden:
            scaled = (part - mean) * scale * gain_ref[at] + bias_ref[at]
            parts.append((scaled / (1.0 + jnp.exp(-scaled))).astype(jnp.bfloat16))
        normed.append(jnp.concatenate(parts, axis=1))
    y_ref[0] = jnp.dot(
        w2_ref[...], jnp.concatenate(normed, axis=0), preferred_element_type=jnp.float32
    )
    for tile, part in enumerate(tap_sums(y_ref, 0, tiles)):
        out_ref[2 * tile, :TILE] = part
        out_ref[2 * tile + 1, :TILE] = pltpu.roll(part, 64, 1)
    for to in range(2 * tiles):
        out_ref[to, TILE:] = share_ref[...]


def fold_kernel(shares_ref, out_ref):
    low = lax.broadcasted_iota(jnp.int32, (TILE, LANES), 1) < 64
    for side in range(2):
        one, two = (
            shares_ref[2 * core + side, :TILE] + shares_ref[4 + 2 * core + side, :TILE]
            for core in range(2)
        )
        out_ref[side] = jnp.where(low, one, pltpu.roll(two, 64, 1))


def token_kernel(
    p_ref, o1_ref, o2_ref, o3_ref, m_ref, bias_ref, qkv_bias_ref, gains_ref, cos_ref, sin_ref,
    lat_ref, q_ref, k_ref, v_ref,
):
    total = p_ref[...] + o1_ref[...] + o2_ref[...] + o3_ref[...]
    total = jnp.concatenate([total[0], total[1]], axis=1)
    lat = (total + bias_ref[:, :1]) * latent_scale
    clips = lat.shape[1] // 64
    tokens = clips * 16
    place = lax.axis_index("dp")
    own = lat[:, :LANES]
    for pair in range(1, clips // 2):
        own = jnp.where(place // 2 == pair, lat[:, pair * LANES : (pair + 1) * LANES], own)
    own = jnp.where(place % 2 == 1, pltpu.roll(own, 64, 1), own)
    turned = own.T[:64]
    wide = jnp.concatenate([turned] * 16, axis=1)
    spot = lax.broadcasted_iota(jnp.int32, wide.shape, 0) % 16
    spread = lax.broadcasted_iota(jnp.int32, wide.shape, 1) // 16
    merged = jnp.sum(jnp.where(spot == spread, wide, 0.0).reshape(4, 16, 256), axis=1)
    lat_ref[0, 0] = merged[:2]
    lat_ref[0, 1] = merged[2:]

    lat_bf = lat.astype(jnp.bfloat16)
    token = lax.broadcasted_iota(jnp.int32, (tokens, clips * 64), 0)
    lane = lax.broadcasted_iota(jnp.int32, (tokens, clips * 64), 1)
    first = token // 8 * 32 + token % 8 * 2
    heads = q_ref.shape[2] // HD
    projected = qkv_bias_ref[...]
    merged = jnp.concatenate(
        [m_ref[:, TILE + 8 * q : TILE + 8 * q + 8].reshape(64, LANES) for q in range(3 * heads)],
        axis=1,
    )
    coarse = merged.astype(jnp.bfloat16)
    fine = (merged - coarse.astype(jnp.float32)).astype(jnp.bfloat16)
    for a in range(2):
        for e in range(2):
            chosen = jnp.where(lane == first + (16 * a + e), 1.0, 0.0).astype(jnp.bfloat16)
            patch = lax.dot_general(
                chosen, lat_bf, (((1,), (1,)), ((), ())), preferred_element_type=jnp.float32
            ).astype(jnp.bfloat16)
            at = slice((2 * a + e) * TILE, (2 * a + e + 1) * TILE)
            for weight in (coarse[at], fine[at]):
                projected = projected + jnp.dot(patch, weight, preferred_element_type=jnp.float32)

    even = lax.broadcasted_iota(jnp.int32, (tokens, HD), 1) % 2 == 0
    cosine = jnp.concatenate([cos_ref[...]] * clips, axis=0)
    sine = jnp.concatenate([sin_ref[...]] * clips, axis=0)

    def turn(vectors, gain):
        square = jnp.mean(vectors * vectors, axis=-1, keepdims=True)
        vectors = vectors * lax.rsqrt(square + norm_eps) * gain
        swapped = jnp.where(even, pltpu.roll(vectors, HD - 1, 1), pltpu.roll(vectors, 1, 1))
        return vectors * cosine + swapped * sine

    def keep(ref, head, value):
        value = value.reshape(tokens // 8, 8, HD).astype(jnp.bfloat16)
        ref[:, :, head * HD : (head + 1) * HD] = value

    for head in range(heads):
        at = 3 * HD * head
        keep(q_ref, head, turn(projected[:, at : at + HD], gains_ref[0:1]))
        keep(k_ref, head, turn(projected[:, at + HD : at + 2 * HD], gains_ref[1:2]))
        keep(v_ref, head, projected[:, at + 2 * HD : at + 3 * HD])


def rope_tables(frame_pos, row_pos, width):
    angles = rope_angles(frame_pos.astype(jnp.float32), row_pos.astype(jnp.float32), width)
    angles = angles.reshape(-1, HD // 2)
    cosine = jnp.repeat(jnp.cos(angles), 2, axis=1)
    sine = jnp.sin(angles)
    return cosine, jnp.stack([-sine, sine], axis=-1).reshape(cosine.shape)


def vmem(count):
    return [pl.BlockSpec(memory_space=pltpu.VMEM)] * count


def grouped(
    clip_inputs,
    conv_in_weight,
    group_gain,
    group_bias,
    conv_out_weight,
    out_bias,
    patch_weight,
    patch_bias,
    qkv_weight,
    qkv_bias,
    q_gain,
    k_gain,
    frame_pos,
    row_pos,
):
    plane_axes = ("tm", "height")
    clips = lax.axis_size("dp")
    steps = lax.axis_size("tm")
    plane = steps * lax.axis_size("height")
    channels = clip_inputs.shape[4]
    depth = conv_in_weight.shape[0]

    width = -(-depth // LANES) * LANES + 2 * LANES
    limit = pltpu.CompilerParams(vmem_limit_bytes=32 * 1024 * 1024)
    small = pl.CostEstimate(flops=10**6, bytes_accessed=10**6, transcendentals=0)
    block = jax.ShapeDtypeStruct((64, channels), jnp.bfloat16)
    with jax.named_scope("weight_by_group"):
        packed, copied = pl.pallas_call(
            pack_kernel,
            out_shape=(
                jax.ShapeDtypeStruct((plane, 2 * GROUP, width), jnp.bfloat16),
                block,
            ),
            in_specs=vmem(5),
            out_specs=tuple(vmem(2)),
            compiler_params=limit,
            cost_estimate=pl.CostEstimate(flops=10**8, bytes_accessed=10**6, transcendentals=0),
            name="pack_weights",
        )(
            conv_in_weight,
            qkv_weight,
            patch_weight,
            patch_bias[None],
            clip_inputs.reshape(64, channels),
        )
        weight = lax.all_to_all(packed, plane_axes, 0, 0, tiled=True)
        weight_pair = lax.ppermute(weight, "tm", [(i, i ^ 1) for i in range(steps)])
    with jax.named_scope("gather_clips"):
        layers = [
            lax.ppermute(copied, "dp", [(i, (i + step) % clips) for i in range(clips)])
            for step in range(1, clips)
        ]
    with jax.named_scope("spread_clips"):
        sent = pl.pallas_call(
            arrange_kernel,
            out_shape=(block,) * 4,
            in_specs=vmem(4),
            out_specs=tuple(vmem(4)),
            scratch_shapes=[pltpu.VMEM((4, 64, channels), jnp.bfloat16)],
            compiler_params=limit,
            cost_estimate=small,
            name="arrange_clips",
        )(copied, *layers)
        pieces = [sent[0]]
        for flip in range(1, plane):
            clip_flip = flip % 2 * 2 + flip // 2 % 2
            pairs = [(i, i ^ flip) for i in range(plane)]
            pieces.append(lax.ppermute(sent[clip_flip], plane_axes, pairs))
    with jax.named_scope("small_weights"):
        first = lax.axis_index("tm") // 2 * (4 * GROUP)
        gain = lax.dynamic_slice_in_dim(group_gain, first, 4 * GROUP).astype(jnp.float32)
        bias = lax.dynamic_slice_in_dim(group_bias, first, 4 * GROUP).astype(jnp.float32)
        weight_out = lax.dynamic_slice_in_dim(conv_out_weight, first, 4 * GROUP, axis=1)
        weight_out = weight_out.transpose(0, 2, 1).reshape(TAPS * TILE, 4 * GROUP)
        cosine, sine = rope_tables(frame_pos, row_pos, clip_inputs.shape[3] // 2)
    with jax.named_scope("merged_projection"):
        share, latent_bias, merged_bias, gains = pl.pallas_call(
            merge_kernel,
            out_shape=(
                jax.ShapeDtypeStruct((48, LANES), jnp.float32),
                jax.ShapeDtypeStruct((TILE, LANES), jnp.float32),
                jax.ShapeDtypeStruct((1, qkv_weight.shape[1]), jnp.float32),
                jax.ShapeDtypeStruct((2, HD), jnp.float32),
            ),
            in_specs=vmem(5),
            out_specs=tuple(vmem(4)),
            compiler_params=limit,
            cost_estimate=small,
            name="merge_projection",
        )(weight, out_bias[:, None], qkv_bias[None], q_gain[None], k_gain[None])

    flops = 2 * clips * steps * LANES * TAPS * TILE * (channels + 16)
    partial = pl.pallas_call(
        conv_kernel,
        out_shape=jax.ShapeDtypeStruct((plane, TILE + 48, LANES), jnp.float32),
        in_specs=vmem(14),
        out_specs=vmem(1)[0],
        scratch_shapes=[
            pltpu.VMEM((plane, 64, channels), jnp.bfloat16),
            pltpu.VMEM((2, 2 * TAPS * GROUP, channels), jnp.bfloat16),
            pltpu.VMEM((4, TAPS * GROUP, steps * LANES), jnp.float32),
        ],
        compiler_params=limit,
        cost_estimate=pl.CostEstimate(flops=flops, bytes_accessed=10**6, transcendentals=0),
        name="convolutions",
    )(*pieces, weight, weight_pair, gain[:, None], bias[:, None], weight_out, share)

    with jax.named_scope("sum_latents"):
        shares = lax.all_to_all(partial, plane_axes, 0, 0, tiled=True)
        here = pl.pallas_call(
            fold_kernel,
            out_shape=jax.ShapeDtypeStruct((2, TILE, LANES), jnp.float32),
            in_specs=vmem(1),
            out_specs=vmem(1)[0],
            compiler_params=limit,
            cost_estimate=small,
            name="fold_latents",
        )(shares)
        others = [
            lax.ppermute(here, "dp", [(i, (i + step) % clips) for i in range(clips)])
            for step in range(1, clips)
        ]

    heads = qkv_weight.shape[1] // (3 * HD)
    frames = clip_inputs.shape[1]
    tokens = jax.ShapeDtypeStruct((clips * frames, 8, heads * HD), jnp.bfloat16)
    latents, query, key, value = pl.pallas_call(
        token_kernel,
        out_shape=(jax.ShapeDtypeStruct((1, 2, 2, 256), jnp.float32), tokens, tokens, tokens),
        in_specs=vmem(10),
        out_specs=tuple(vmem(4)),
        compiler_params=pltpu.CompilerParams(vmem_limit_bytes=32 * 1024 * 1024),
        cost_estimate=pl.CostEstimate(flops=10**8, bytes_accessed=10**6, transcendentals=0),
        name="tokens",
    )(
        here,
        *others,
        shares,
        latent_bias,
        merged_bias,
        gains,
        cosine,
        sine,
    )
    full = (clips, frames, 1, 8, heads * HD)
    return latents, query.reshape(full), key.reshape(full), value.reshape(full)


def pick(mesh, *arrays):
    if one_group_each(mesh, arrays[0], arrays[1], arrays[4], arrays[8]):
        return grouped(*arrays)
    return shards(*arrays)


def solution(mesh):
    placed = (
        P("dp", "tm", "height", None, None),
        P(("tm", "height"), "dp"),
        P("dp"),
        P("dp"),
        P(None, "dp", None),
        P(),
        P(),
        P(),
        P(("tm", "height"), "dp"),
        P("dp"),
        P(),
        P(),
        P("tm"),
        P("height"),
    )
    return jax.shard_map(
        functools.partial(pick, mesh),
        mesh=mesh,
        in_specs=placed,
        out_specs=(
            P("dp", "tm", "height", None),
            P(None, "tm", "height", None, "dp"),
            P(None, "tm", "height", None, "dp"),
            P(None, "tm", "height", None, "dp"),
        ),
        check_vma=False,
    )
```

```python
import functools

import jax
import jax.numpy as jnp
from jax import lax
from jax.experimental import pallas as pl
from jax.experimental.pallas import tpu as pltpu
from jax.sharding import PartitionSpec as P

HD = 128
GROUPS = 32
TAPS = 27


norm_eps = 1e-06
latent_scale = 0.476986
rope_base = 256.0
time_dims = 16
row_dims = 56


def from_behind(value, axis, steps):
    count = lax.axis_size(axis)
    first, last = (max(0, -steps), min(count, count - steps))
    return lax.ppermute(value, axis, [(source, source + steps) for source in range(first, last)])


def padded_2(block, sides, width):
    for axis, dim in sides:
        count = lax.axis_size(axis)
        forward = [(i, i + 1) for i in range(count - 1)]
        backward = [(target, source) for source, target in forward]
        low = lax.ppermute(
            lax.slice_in_dim(block, block.shape[dim] - width, None, axis=dim), axis, forward
        )
        high = lax.ppermute(lax.slice_in_dim(block, 0, width, axis=dim), axis, backward)
        block = jnp.concatenate([low, block, high], axis=dim)
    return block


def repeat_first(block):
    return jnp.concatenate([block[:, :1], block[:, :1]], axis=1)


def time_join(block, earlier):
    start = jnp.where(lax.axis_index("tm") == 0, repeat_first(block), earlier)
    return jnp.concatenate([start, block], axis=1)


def rows_finish(grown):
    place = lax.axis_index("height")
    top = jnp.where(place == 0, grown[:, :, 1:2], grown[:, :, :1])
    bottom = jnp.where(place == lax.axis_size("height") - 1, grown[:, :, -2:-1], grown[:, :, -1:])
    inner = jnp.concatenate([top, grown[:, :, 1:-1], bottom], axis=2)
    return jnp.pad(inner, ((0, 0), (0, 0), (0, 0), (1, 1), (0, 0)), mode="edge")


def edges_before(block):
    earlier = from_behind(block, "tm", 1)
    longer = time_join(block, earlier)
    return rows_finish(padded_2(longer, (("height", 2),), 1))


def edges_norm(block):
    earlier = from_behind(block, "tm", 1)
    longer = time_join(block, earlier)
    return rows_finish(padded_2(longer, (("height", 2),), 1))


def convolve(padded, weight):
    clips = padded.shape[0]
    frames = padded.shape[1] - 2
    rows = padded.shape[2] - 2
    cols = padded.shape[3] - 2
    total = jnp.zeros((clips * frames * rows * cols, weight.shape[2]), jnp.float32)
    for shift_t in range(3):
        for shift_r in range(3):
            for shift_c in range(3):
                window = padded[
                    :,
                    shift_t : shift_t + frames,
                    shift_r : shift_r + rows,
                    shift_c : shift_c + cols,
                ]
                window = window.reshape(-1, padded.shape[4])
                total = total + jnp.dot(
                    window,
                    weight[9 * shift_t + 3 * shift_r + shift_c],
                    preferred_element_type=jnp.float32,
                )
    return total.reshape(clips, frames, rows, cols, weight.shape[2])


def section_freqs(dims):
    return jnp.power(rope_base, -jnp.arange(0, dims, 2, dtype=jnp.float32) / dims)


def rope_angles(tpos, hpos, width):
    frames = tpos.shape[0]
    rows = hpos.shape[0]
    cols = jnp.arange(width, dtype=jnp.float32)
    part_t = tpos[:, None, None, None] * section_freqs(time_dims)
    part_h = hpos[None, :, None, None] * section_freqs(row_dims)
    part_w = cols[None, None, :, None] * section_freqs(row_dims)
    shape = (frames, rows, width)
    return jnp.concatenate(
        [
            jnp.broadcast_to(part_t, shape + (time_dims // 2,)),
            jnp.broadcast_to(part_h, shape + (row_dims // 2,)),
            jnp.broadcast_to(part_w, shape + (row_dims // 2,)),
        ],
        axis=-1,
    )


def rotate(vectors, angles):
    pairs = vectors.reshape(vectors.shape[:-1] + (vectors.shape[-1] // 2, 2))
    first = pairs[..., 0]
    second = pairs[..., 1]
    cosine = jnp.cos(angles)[..., None, :]
    sine = jnp.sin(angles)[..., None, :]
    turned = jnp.stack([first * cosine - second * sine, first * sine + second * cosine], axis=-1)
    return turned.reshape(vectors.shape)


def rms_scale(vectors, gain):
    return (
        vectors
        * lax.rsqrt(jnp.mean(vectors * vectors, axis=-1, keepdims=True) + norm_eps)
        * gain.astype(jnp.float32)
    )


def shards(
    clip_inputs,
    conv_in_weight,
    group_gain,
    group_bias,
    conv_out_weight,
    out_bias,
    patch_weight,
    patch_bias,
    qkv_weight,
    qkv_bias,
    q_gain,
    k_gain,
    frame_pos,
    row_pos,
):
    channels = clip_inputs.shape[4]
    frames = clip_inputs.shape[1]
    rows = clip_inputs.shape[2]
    cols = clip_inputs.shape[3]
    padded = lax.all_gather(edges_before(clip_inputs), "dp", axis=0, tiled=True)
    clips = padded.shape[0]
    weight_in = lax.all_gather(conv_in_weight, ("tm", "height"), axis=0, tiled=True).reshape(
        TAPS, channels, -1
    )
    hidden = convolve(padded, weight_in)
    block_width = hidden.shape[4]
    group_width = channels // GROUPS
    local_groups = block_width // group_width
    grouped = hidden.reshape(clips, -1, local_groups, group_width)
    sums_local = jnp.sum(grouped, axis=(1, 3))
    squares_local = jnp.sum(grouped * grouped, axis=(1, 3))
    sums_all, squares_all = lax.psum((sums_local, squares_local), ("tm", "height"))
    count = float(
        frames * lax.axis_size("tm") * rows * lax.axis_size("height") * cols * group_width
    )
    mean = sums_all / count
    var = squares_all / count - mean * mean
    scaled = (grouped - mean[:, None, :, None]) * lax.rsqrt(var + norm_eps)[:, None, :, None]
    scaled = scaled.reshape(hidden.shape) * group_gain.astype(jnp.float32) + group_bias.astype(
        jnp.float32
    )
    normed = jax.nn.silu(scaled).astype(jnp.bfloat16)
    partial_latent = convolve(edges_norm(normed), conv_out_weight)
    own_sum = lax.psum_scatter(partial_latent, "dp", scatter_dimension=0, tiled=True)
    own_latent = (own_sum + out_bias) * latent_scale
    every_latent = lax.all_gather(own_latent.astype(jnp.bfloat16), "dp", axis=0, tiled=True)
    latent_dims = every_latent.shape[4]
    latents = own_latent.reshape(1, frames, rows, cols * latent_dims)
    tok_rows = rows // 2
    tok_cols = cols // 2
    patches = every_latent.reshape(clips, frames, tok_rows, 2, tok_cols, 2, latent_dims)
    patches = patches.transpose(0, 1, 2, 4, 3, 5, 6).reshape(-1, 4 * latent_dims)
    embedded = (
        jnp.dot(patches, patch_weight, preferred_element_type=jnp.float32)
        + patch_bias.astype(jnp.float32)
    ).astype(jnp.bfloat16)
    projected = jnp.dot(
        embedded,
        lax.all_gather(qkv_weight, ("tm", "height"), axis=0, tiled=True),
        preferred_element_type=jnp.float32,
    )
    projected = projected + qkv_bias.astype(jnp.float32)
    local_heads = qkv_weight.shape[1] // (3 * HD)
    projected = projected.reshape(clips, frames, tok_rows, tok_cols, local_heads, 3, HD)
    angles = rope_angles(frame_pos.astype(jnp.float32), row_pos.astype(jnp.float32), tok_cols)
    query = rotate(rms_scale(projected[..., 0, :], q_gain), angles)
    key = rotate(rms_scale(projected[..., 1, :], k_gain), angles)
    value = projected[..., 2, :]
    merged = (clips, frames, tok_rows, tok_cols, local_heads * HD)
    return (
        latents,
        query.reshape(merged).astype(jnp.bfloat16),
        key.reshape(merged).astype(jnp.bfloat16),
        value.reshape(merged).astype(jnp.bfloat16),
    )


LANES = 128
TILE = 16
GROUP = 16


def one_group_each(mesh, clip_inputs, conv_in_weight, conv_out_weight, qkv_weight):
    plane = mesh.shape["tm"] * mesh.shape["height"]
    return (
        clip_inputs.shape[:4] == (1, 2, 2, 16)
        and mesh.shape["height"] == 2
        and mesh.shape["tm"] == 4
        and mesh.shape["dp"] == 4
        and conv_in_weight.shape[1] == plane * GROUP
        and clip_inputs.shape[4] == GROUP * GROUPS
        and conv_out_weight.shape[2] == TILE
        and qkv_weight.shape[1] == 6 * HD
    )


def lane_shifts(lane):
    col = lane % 16
    row = lane // 16 % 2
    half = lane // 64

    def cols(left, mid, right):
        left = jnp.where(col == 0, left, pltpu.roll(left, 1, 1))
        right = jnp.where(col == 15, right, pltpu.roll(right, LANES - 1, 1))
        return mid + left + right

    def rows(up, mid, down):
        up = jnp.where(
            row == 1, pltpu.roll(up, 16, 1), jnp.where(half == 1, pltpu.roll(up, 48, 1), up)
        )
        down = jnp.where(
            row == 0,
            pltpu.roll(down, LANES - 16, 1),
            jnp.where(half == 0, pltpu.roll(down, LANES - 48, 1), down),
        )
        return mid + up + down

    return cols, rows


def tap_sums(y_ref, side, top, tiles):
    lane = lax.broadcasted_iota(jnp.int32, (TILE, LANES), 1)
    second = lane // 32 % 2 == 1
    cols, rows = lane_shifts(lane)
    sums = []
    before = None
    for tile in range(tiles):

        def part(tap):
            at = top + tap * TILE
            return y_ref[side, at : at + TILE, tile * LANES : (tile + 1) * LANES]

        oldest, older, now = (
            rows(*(cols(*(part(9 * i + 3 * j + l) for l in range(3))) for j in range(3)))
            for i in range(3)
        )
        turned = pltpu.roll(older, 32, 1)
        if before is None:
            start = jnp.where(second, pltpu.roll(oldest, 32, 1), oldest)
            total = now + jnp.where(second, turned, older) + start
        else:
            total = now + jnp.where(second, turned, pltpu.roll(before[1], 96, 1)) + before[0]
        before = (oldest, older)
        sums.append(total)
    return sums


def pack_kernel(w_ref, qkv_ref, patch_ref, patch_bias_ref, out_ref):
    plane, channels, width = out_ref.shape
    depth = w_ref.shape[0]
    rows = qkv_ref.shape[0]
    place = lax.axis_index("tm") * lax.axis_size("height") + lax.axis_index("height")
    at = pl.ds(pl.multiple_of(place * rows, LANES), rows)
    merged = jnp.dot(patch_ref[:, at], qkv_ref[...], preferred_element_type=jnp.float32)
    bias = jnp.broadcast_to(patch_bias_ref[:, at], (8, rows))
    bias = jnp.dot(bias, qkv_ref[...], preferred_element_type=jnp.float32)
    line = lax.broadcasted_iota(jnp.int32, (8, LANES), 0)
    lines = jnp.zeros((8, LANES), jnp.float32)
    for part in range(bias.shape[1] // LANES):
        lines = jnp.where(line == part, bias[:, part * LANES : (part + 1) * LANES], lines)
    turned = w_ref[...].T
    for to in range(plane):
        first = to // 2 * channels
        out_ref[to, :, :depth] = turned[first : first + channels]
        parts = [merged[8 * to : 8 * to + 8, q * LANES : (q + 1) * LANES] for q in range(6)]
        parts += [lines, jnp.zeros_like(lines)]
        for tile in range(2):
            some = jnp.concatenate(parts[4 * tile : 4 * tile + 4], axis=0)
            end = width - LANES * (1 - tile)
            out_ref[to, :, end - LANES : end] = some.astype(jnp.bfloat16)


def arrange_kernel(own_ref, one_ref, two_ref, three_ref, *rest):
    out_refs, all_ref = rest[:4], rest[4]
    clip = lax.axis_index("height") * 2 + lax.axis_index("tm") % 2
    layer = lax.axis_index("dp")
    for step, piece in enumerate((own_ref, one_ref, two_ref, three_ref)):
        all_ref[(layer + 4 - step) % 4] = piece[...]
    for flip, out_ref in enumerate(out_refs):
        out_ref[...] = all_ref[clip ^ flip]


def merge_kernel(
    parts_ref, pair_ref, out_bias_ref, qkv_bias_ref, q_gain_ref, k_gain_ref,
    share_ref, bias_ref, qkv_ref, gains_ref,
):
    plane = parts_ref.shape[0]
    at = parts_ref.shape[2] - 2 * LANES
    for index, ref in enumerate((pair_ref, parts_ref)):
        total = ref[0, :, at:].astype(jnp.float32)
        for source in range(1, plane):
            total = total + ref[source, :, at:].astype(jnp.float32)
        for q in range(6):
            share_ref[1 - index, 8 * q : 8 * q + 8] = total[
                q % 4 * 8 : q % 4 * 8 + 8, q // 4 * LANES : (q // 4 + 1) * LANES
            ]
    extra = jnp.concatenate([total[16 + q : 17 + q, LANES:] for q in range(6)], axis=1)
    qkv_ref[...] = extra + qkv_bias_ref[...].astype(jnp.float32)
    bias_ref[...] = jnp.broadcast_to(out_bias_ref[...], bias_ref.shape)
    gains_ref[0:1] = q_gain_ref[...].astype(jnp.float32)
    gains_ref[1:2] = k_gain_ref[...].astype(jnp.float32)


def join_weight(w_ref, wt_ref, half, channels):
    depth = TAPS * channels // w_ref.shape[0]
    for group in range(w_ref.shape[1] // GROUP):
        for tap in range(TAPS):
            start = tap * channels
            end = start + channels
            at = (group * TAPS + tap) * GROUP
            while start < end:
                source = start // depth
                stop = min(end, (source + 1) * depth)
                wt_ref[
                    half, at : at + GROUP, start - tap * channels : stop - tap * channels
                ] = w_ref[
                    source,
                    group * GROUP : (group + 1) * GROUP,
                    start - source * depth : stop - source * depth,
                ]
                start = stop


def conv_kernel(*refs):
    x_refs, refs = refs[:8], refs[8:]
    w_ref, v_ref, gain_ref, bias_ref, w2_ref, out_ref, x_ref, wt_ref, y_ref = refs
    channels = x_ref.shape[2]
    tiles = x_ref.shape[0] // 2
    place = lax.axis_index("tm") * 2 + lax.axis_index("height")
    for flip, piece in enumerate(x_refs):
        x_ref[place ^ flip] = piece[...]
    half = lax.axis_index("tm") % 2
    join_weight(w_ref, wt_ref, half, channels)
    join_weight(v_ref, wt_ref, 1 - half, channels)
    count = float(tiles * LANES * GROUP)
    x = x_ref[...].reshape(tiles * LANES, channels)
    taps = TAPS * GROUP
    normed = []
    for side in range(2):
        y_ref[side] = lax.dot_general(
            wt_ref[side], x, (((1,), (1,)), ((), ())), preferred_element_type=jnp.float32
        )
        for group in range(2 * side, 2 * side + 2):
            hidden = tap_sums(y_ref, side, group % 2 * taps, tiles)
            at = slice(group * GROUP, (group + 1) * GROUP)
            mean = jnp.sum(sum(hidden), keepdims=True) / count
            square = jnp.sum(sum(part * part for part in hidden), keepdims=True) / count
            scale = lax.rsqrt(square - mean * mean + norm_eps)
            parts = []
            for part in hidden:
                scaled = (part - mean) * scale * gain_ref[at] + bias_ref[at]
                parts.append((scaled / (1.0 + jnp.exp(-scaled))).astype(jnp.bfloat16))
            normed.append(jnp.concatenate(parts, axis=1))
    y_ref[0, :taps] = jnp.dot(
        w2_ref[...], jnp.concatenate(normed, axis=0), preferred_element_type=jnp.float32
    )
    low = lax.broadcasted_iota(jnp.int32, (8, LANES), 1) < 64
    layers = out_ref.shape[0] // (2 * tiles)
    for tile, part in enumerate(tap_sums(y_ref, 0, 0, tiles)):
        turned = pltpu.roll(part, 64, 1)
        near = jnp.where(low, part[:8], turned[8:])
        far = jnp.where(low, turned[:8], part[8:])
        for layer in range(layers):
            out_ref[layer * 2 * tiles + 2 * tile] = near
            out_ref[layer * 2 * tiles + 2 * tile + 1] = far


def token_kernel(
    p_ref, m0_ref, m1_ref, m2_ref, m3_ref, bias_ref, qkv_bias_ref, gains_ref, cos_ref, sin_ref,
    lat_ref, q_ref, k_ref, v_ref, m_ref,
):
    spot = lax.axis_index("tm") * 2 + lax.axis_index("height")
    for flip, ref in ((0, m0_ref), (1, m1_ref), (4, m2_ref), (5, m3_ref)):
        m_ref[spot ^ flip] = ref[0]
        m_ref[spot ^ flip ^ 2] = ref[1]
    low = lax.broadcasted_iota(jnp.int32, (8, LANES), 1) < 64
    pairs = []
    for side in range(2):
        one, two = (
            sum(p_ref[4 * index + 2 * core + side] for index in range(p_ref.shape[0] // 4))
            for core in range(2)
        )
        top = jnp.where(low, one, pltpu.roll(two, 64, 1))
        bottom = jnp.where(low, pltpu.roll(one, 64, 1), two)
        pairs.append(jnp.concatenate([top, bottom], axis=0))
    total = jnp.concatenate(pairs, axis=1)
    lat = (total + bias_ref[:, :1]) * latent_scale
    clips = lat.shape[1] // 64
    tokens = clips * 16
    place = lax.axis_index("dp")
    own = lat[:, :LANES]
    for pair in range(1, clips // 2):
        own = jnp.where(place // 2 == pair, lat[:, pair * LANES : (pair + 1) * LANES], own)
    own = jnp.where(place % 2 == 1, pltpu.roll(own, 64, 1), own)
    turned = own.T[:64]
    wide = jnp.concatenate([turned] * 16, axis=1)
    spot = lax.broadcasted_iota(jnp.int32, wide.shape, 0) % 16
    spread = lax.broadcasted_iota(jnp.int32, wide.shape, 1) // 16
    merged = jnp.sum(jnp.where(spot == spread, wide, 0.0).reshape(4, 16, 256), axis=1)
    lat_ref[0, 0] = merged[:2]
    lat_ref[0, 1] = merged[2:]

    lat_bf = lat.astype(jnp.bfloat16)
    token = lax.broadcasted_iota(jnp.int32, (tokens, clips * 64), 0)
    lane = lax.broadcasted_iota(jnp.int32, (tokens, clips * 64), 1)
    first = token // 8 * 32 + token % 8 * 2
    heads = q_ref.shape[2] // HD
    projected = qkv_bias_ref[...]
    merged = jnp.concatenate(
        [m_ref[:, 8 * q : 8 * q + 8].reshape(64, LANES) for q in range(3 * heads)],
        axis=1,
    )
    coarse = merged.astype(jnp.bfloat16)
    fine = (merged - coarse.astype(jnp.float32)).astype(jnp.bfloat16)
    for a in range(2):
        for e in range(2):
            chosen = jnp.where(lane == first + (16 * a + e), 1.0, 0.0).astype(jnp.bfloat16)
            patch = lax.dot_general(
                chosen, lat_bf, (((1,), (1,)), ((), ())), preferred_element_type=jnp.float32
            ).astype(jnp.bfloat16)
            at = slice((2 * a + e) * TILE, (2 * a + e + 1) * TILE)
            for weight in (coarse[at], fine[at]):
                projected = projected + jnp.dot(patch, weight, preferred_element_type=jnp.float32)

    even = lax.broadcasted_iota(jnp.int32, (tokens, HD), 1) % 2 == 0
    cosine = jnp.concatenate([cos_ref[...]] * clips, axis=0)
    sine = jnp.concatenate([sin_ref[...]] * clips, axis=0)

    def turn(vectors, gain):
        square = jnp.mean(vectors * vectors, axis=-1, keepdims=True)
        vectors = vectors * lax.rsqrt(square + norm_eps) * gain
        swapped = jnp.where(even, pltpu.roll(vectors, HD - 1, 1), pltpu.roll(vectors, 1, 1))
        return vectors * cosine + swapped * sine

    def keep(ref, head, value):
        value = value.reshape(tokens // 8, 8, HD).astype(jnp.bfloat16)
        ref[:, :, head * HD : (head + 1) * HD] = value

    for head in range(heads):
        at = 3 * HD * head
        keep(q_ref, head, turn(projected[:, at : at + HD], gains_ref[0:1]))
        keep(k_ref, head, turn(projected[:, at + HD : at + 2 * HD], gains_ref[1:2]))
        keep(v_ref, head, projected[:, at + 2 * HD : at + 3 * HD])


def rope_tables(frame_pos, row_pos, width):
    angles = rope_angles(frame_pos.astype(jnp.float32), row_pos.astype(jnp.float32), width)
    angles = angles.reshape(-1, HD // 2)
    cosine = jnp.repeat(jnp.cos(angles), 2, axis=1)
    sine = jnp.sin(angles)
    return cosine, jnp.stack([-sine, sine], axis=-1).reshape(cosine.shape)


def vmem(count):
    return [pl.BlockSpec(memory_space=pltpu.VMEM)] * count


def grouped(
    clip_inputs,
    conv_in_weight,
    group_gain,
    group_bias,
    conv_out_weight,
    out_bias,
    patch_weight,
    patch_bias,
    qkv_weight,
    qkv_bias,
    q_gain,
    k_gain,
    frame_pos,
    row_pos,
):
    plane_axes = ("tm", "height")
    clips = lax.axis_size("dp")
    steps = lax.axis_size("tm")
    plane = steps * lax.axis_size("height")
    channels = clip_inputs.shape[4]
    depth = conv_in_weight.shape[0]

    width = -(-depth // LANES) * LANES + 2 * LANES
    limit = pltpu.CompilerParams(vmem_limit_bytes=32 * 1024 * 1024)
    small = pl.CostEstimate(flops=10**6, bytes_accessed=10**6, transcendentals=0)
    block = jax.ShapeDtypeStruct((64, channels), jnp.bfloat16)
    with jax.named_scope("weight_by_group"):
        packed = pl.pallas_call(
            pack_kernel,
            out_shape=jax.ShapeDtypeStruct((plane, 2 * GROUP, width), jnp.bfloat16),
            in_specs=vmem(4),
            out_specs=vmem(1)[0],
            compiler_params=limit,
            cost_estimate=pl.CostEstimate(flops=10**8, bytes_accessed=10**6, transcendentals=0),
            name="pack_weights",
        )(conv_in_weight, qkv_weight, patch_weight, patch_bias[None])
        weight = lax.all_to_all(packed, plane_axes, 0, 0, tiled=True)
        weight_pair = lax.ppermute(weight, "tm", [(i, i ^ 1) for i in range(steps)])
    with jax.named_scope("gather_clips"):
        copied = clip_inputs.reshape(64, channels)
        layers = [
            lax.ppermute(copied, "dp", [(i, (i + step) % clips) for i in range(clips)])
            for step in range(1, clips)
        ]
    with jax.named_scope("spread_clips"):
        sent = pl.pallas_call(
            arrange_kernel,
            out_shape=(block,) * 4,
            in_specs=vmem(4),
            out_specs=tuple(vmem(4)),
            scratch_shapes=[pltpu.VMEM((4, 64, channels), jnp.bfloat16)],
            compiler_params=limit,
            cost_estimate=small,
            name="arrange_clips",
        )(copied, *layers)
        pieces = [sent[0]]
        for flip in range(1, plane):
            clip_flip = flip % 2 * 2 + flip // 2 % 2
            pairs = [(i, i ^ flip) for i in range(plane)]
            pieces.append(lax.ppermute(sent[clip_flip], plane_axes, pairs))
    with jax.named_scope("small_weights"):
        first = lax.axis_index("tm") // 2 * (4 * GROUP)
        gain = lax.dynamic_slice_in_dim(group_gain, first, 4 * GROUP).astype(jnp.float32)
        bias = lax.dynamic_slice_in_dim(group_bias, first, 4 * GROUP).astype(jnp.float32)
        weight_out = lax.dynamic_slice_in_dim(conv_out_weight, first, 4 * GROUP, axis=1)
        weight_out = weight_out.transpose(0, 2, 1).reshape(TAPS * TILE, 4 * GROUP)
        cosine, sine = rope_tables(frame_pos, row_pos, clip_inputs.shape[3] // 2)
    with jax.named_scope("merged_projection"):
        share, latent_bias, merged_bias, gains = pl.pallas_call(
            merge_kernel,
            out_shape=(
                jax.ShapeDtypeStruct((2, 48, LANES), jnp.float32),
                jax.ShapeDtypeStruct((TILE, LANES), jnp.float32),
                jax.ShapeDtypeStruct((1, qkv_weight.shape[1]), jnp.float32),
                jax.ShapeDtypeStruct((2, HD), jnp.float32),
            ),
            in_specs=vmem(6),
            out_specs=tuple(vmem(4)),
            compiler_params=limit,
            cost_estimate=small,
            name="merge_projection",
        )(weight, weight_pair, out_bias[:, None], qkv_bias[None], q_gain[None], k_gain[None])
        shares = [share]
        for flip in (1, 4, 5):
            pairs = [(i, i ^ flip) for i in range(plane)]
            shares.append(lax.ppermute(share, plane_axes, pairs))

    flops = 2 * clips * steps * LANES * TAPS * TILE * (channels + 16)
    partial = pl.pallas_call(
        conv_kernel,
        out_shape=jax.ShapeDtypeStruct((clips * plane, 8, LANES), jnp.float32),
        in_specs=vmem(13),
        out_specs=vmem(1)[0],
        scratch_shapes=[
            pltpu.VMEM((plane, 64, channels), jnp.bfloat16),
            pltpu.VMEM((2, 2 * TAPS * GROUP, channels), jnp.bfloat16),
            pltpu.VMEM((2, 2 * TAPS * GROUP, steps * LANES), jnp.float32),
        ],
        compiler_params=limit,
        cost_estimate=pl.CostEstimate(flops=flops, bytes_accessed=10**6, transcendentals=0),
        name="convolutions",
    )(*pieces, weight, weight_pair, gain[:, None], bias[:, None], weight_out)

    with jax.named_scope("sum_latents"):
        partials = lax.all_to_all(partial, ("dp",) + plane_axes, 0, 0, tiled=True)

    heads = qkv_weight.shape[1] // (3 * HD)
    frames = clip_inputs.shape[1]
    tokens = jax.ShapeDtypeStruct((clips * frames, 8, heads * HD), jnp.bfloat16)
    latents, query, key, value = pl.pallas_call(
        token_kernel,
        out_shape=(jax.ShapeDtypeStruct((1, 2, 2, 256), jnp.float32), tokens, tokens, tokens),
        in_specs=vmem(10),
        out_specs=tuple(vmem(4)),
        scratch_shapes=[pltpu.VMEM((plane, 48, LANES), jnp.float32)],
        compiler_params=limit,
        cost_estimate=pl.CostEstimate(flops=10**8, bytes_accessed=10**6, transcendentals=0),
        name="tokens",
    )(
        partials,
        *shares,
        latent_bias,
        merged_bias,
        gains,
        cosine,
        sine,
    )
    full = (clips, frames, 1, 8, heads * HD)
    return latents, query.reshape(full), key.reshape(full), value.reshape(full)


def pick(mesh, *arrays):
    if one_group_each(mesh, arrays[0], arrays[1], arrays[4], arrays[8]):
        return grouped(*arrays)
    return shards(*arrays)


def solution(mesh):
    placed = (
        P("dp", "tm", "height", None, None),
        P(("tm", "height"), "dp"),
        P("dp"),
        P("dp"),
        P(None, "dp", None),
        P(),
        P(),
        P(),
        P(("tm", "height"), "dp"),
        P("dp"),
        P(),
        P(),
        P("tm"),
        P("height"),
    )
    return jax.shard_map(
        functools.partial(pick, mesh),
        mesh=mesh,
        in_specs=placed,
        out_specs=(
            P("dp", "tm", "height", None),
            P(None, "tm", "height", None, "dp"),
            P(None, "tm", "height", None, "dp"),
            P(None, "tm", "height", None, "dp"),
        ),
        check_vma=False,
    )
```

```python
import functools

import jax
import jax.numpy as jnp
from jax import lax
from jax.experimental import pallas as pl
from jax.experimental.pallas import tpu as pltpu
from jax.sharding import PartitionSpec as P

HD = 128
GROUPS = 32
TAPS = 27


norm_eps = 1e-06
latent_scale = 0.476986
rope_base = 256.0
time_dims = 16
row_dims = 56


def from_behind(value, axis, steps):
    count = lax.axis_size(axis)
    first, last = (max(0, -steps), min(count, count - steps))
    return lax.ppermute(value, axis, [(source, source + steps) for source in range(first, last)])


def padded_2(block, sides, width):
    for axis, dim in sides:
        count = lax.axis_size(axis)
        forward = [(i, i + 1) for i in range(count - 1)]
        backward = [(target, source) for source, target in forward]
        low = lax.ppermute(
            lax.slice_in_dim(block, block.shape[dim] - width, None, axis=dim), axis, forward
        )
        high = lax.ppermute(lax.slice_in_dim(block, 0, width, axis=dim), axis, backward)
        block = jnp.concatenate([low, block, high], axis=dim)
    return block


def repeat_first(block):
    return jnp.concatenate([block[:, :1], block[:, :1]], axis=1)


def time_join(block, earlier):
    start = jnp.where(lax.axis_index("tm") == 0, repeat_first(block), earlier)
    return jnp.concatenate([start, block], axis=1)


def rows_finish(grown):
    place = lax.axis_index("height")
    top = jnp.where(place == 0, grown[:, :, 1:2], grown[:, :, :1])
    bottom = jnp.where(place == lax.axis_size("height") - 1, grown[:, :, -2:-1], grown[:, :, -1:])
    inner = jnp.concatenate([top, grown[:, :, 1:-1], bottom], axis=2)
    return jnp.pad(inner, ((0, 0), (0, 0), (0, 0), (1, 1), (0, 0)), mode="edge")


def edges_before(block):
    earlier = from_behind(block, "tm", 1)
    longer = time_join(block, earlier)
    return rows_finish(padded_2(longer, (("height", 2),), 1))


def edges_norm(block):
    earlier = from_behind(block, "tm", 1)
    longer = time_join(block, earlier)
    return rows_finish(padded_2(longer, (("height", 2),), 1))


def convolve(padded, weight):
    clips = padded.shape[0]
    frames = padded.shape[1] - 2
    rows = padded.shape[2] - 2
    cols = padded.shape[3] - 2
    total = jnp.zeros((clips * frames * rows * cols, weight.shape[2]), jnp.float32)
    for shift_t in range(3):
        for shift_r in range(3):
            for shift_c in range(3):
                window = padded[
                    :,
                    shift_t : shift_t + frames,
                    shift_r : shift_r + rows,
                    shift_c : shift_c + cols,
                ]
                window = window.reshape(-1, padded.shape[4])
                total = total + jnp.dot(
                    window,
                    weight[9 * shift_t + 3 * shift_r + shift_c],
                    preferred_element_type=jnp.float32,
                )
    return total.reshape(clips, frames, rows, cols, weight.shape[2])


def section_freqs(dims):
    return jnp.power(rope_base, -jnp.arange(0, dims, 2, dtype=jnp.float32) / dims)


def rope_angles(tpos, hpos, width):
    frames = tpos.shape[0]
    rows = hpos.shape[0]
    cols = jnp.arange(width, dtype=jnp.float32)
    part_t = tpos[:, None, None, None] * section_freqs(time_dims)
    part_h = hpos[None, :, None, None] * section_freqs(row_dims)
    part_w = cols[None, None, :, None] * section_freqs(row_dims)
    shape = (frames, rows, width)
    return jnp.concatenate(
        [
            jnp.broadcast_to(part_t, shape + (time_dims // 2,)),
            jnp.broadcast_to(part_h, shape + (row_dims // 2,)),
            jnp.broadcast_to(part_w, shape + (row_dims // 2,)),
        ],
        axis=-1,
    )


def rotate(vectors, angles):
    pairs = vectors.reshape(vectors.shape[:-1] + (vectors.shape[-1] // 2, 2))
    first = pairs[..., 0]
    second = pairs[..., 1]
    cosine = jnp.cos(angles)[..., None, :]
    sine = jnp.sin(angles)[..., None, :]
    turned = jnp.stack([first * cosine - second * sine, first * sine + second * cosine], axis=-1)
    return turned.reshape(vectors.shape)


def rms_scale(vectors, gain):
    return (
        vectors
        * lax.rsqrt(jnp.mean(vectors * vectors, axis=-1, keepdims=True) + norm_eps)
        * gain.astype(jnp.float32)
    )


def shards(
    clip_inputs,
    conv_in_weight,
    group_gain,
    group_bias,
    conv_out_weight,
    out_bias,
    patch_weight,
    patch_bias,
    qkv_weight,
    qkv_bias,
    q_gain,
    k_gain,
    frame_pos,
    row_pos,
):
    channels = clip_inputs.shape[4]
    frames = clip_inputs.shape[1]
    rows = clip_inputs.shape[2]
    cols = clip_inputs.shape[3]
    padded = lax.all_gather(edges_before(clip_inputs), "dp", axis=0, tiled=True)
    clips = padded.shape[0]
    weight_in = lax.all_gather(conv_in_weight, ("tm", "height"), axis=0, tiled=True).reshape(
        TAPS, channels, -1
    )
    hidden = convolve(padded, weight_in)
    block_width = hidden.shape[4]
    group_width = channels // GROUPS
    local_groups = block_width // group_width
    grouped = hidden.reshape(clips, -1, local_groups, group_width)
    sums_local = jnp.sum(grouped, axis=(1, 3))
    squares_local = jnp.sum(grouped * grouped, axis=(1, 3))
    sums_all, squares_all = lax.psum((sums_local, squares_local), ("tm", "height"))
    count = float(
        frames * lax.axis_size("tm") * rows * lax.axis_size("height") * cols * group_width
    )
    mean = sums_all / count
    var = squares_all / count - mean * mean
    scaled = (grouped - mean[:, None, :, None]) * lax.rsqrt(var + norm_eps)[:, None, :, None]
    scaled = scaled.reshape(hidden.shape) * group_gain.astype(jnp.float32) + group_bias.astype(
        jnp.float32
    )
    normed = jax.nn.silu(scaled).astype(jnp.bfloat16)
    partial_latent = convolve(edges_norm(normed), conv_out_weight)
    own_sum = lax.psum_scatter(partial_latent, "dp", scatter_dimension=0, tiled=True)
    own_latent = (own_sum + out_bias) * latent_scale
    every_latent = lax.all_gather(own_latent.astype(jnp.bfloat16), "dp", axis=0, tiled=True)
    latent_dims = every_latent.shape[4]
    latents = own_latent.reshape(1, frames, rows, cols * latent_dims)
    tok_rows = rows // 2
    tok_cols = cols // 2
    patches = every_latent.reshape(clips, frames, tok_rows, 2, tok_cols, 2, latent_dims)
    patches = patches.transpose(0, 1, 2, 4, 3, 5, 6).reshape(-1, 4 * latent_dims)
    embedded = (
        jnp.dot(patches, patch_weight, preferred_element_type=jnp.float32)
        + patch_bias.astype(jnp.float32)
    ).astype(jnp.bfloat16)
    projected = jnp.dot(
        embedded,
        lax.all_gather(qkv_weight, ("tm", "height"), axis=0, tiled=True),
        preferred_element_type=jnp.float32,
    )
    projected = projected + qkv_bias.astype(jnp.float32)
    local_heads = qkv_weight.shape[1] // (3 * HD)
    projected = projected.reshape(clips, frames, tok_rows, tok_cols, local_heads, 3, HD)
    angles = rope_angles(frame_pos.astype(jnp.float32), row_pos.astype(jnp.float32), tok_cols)
    query = rotate(rms_scale(projected[..., 0, :], q_gain), angles)
    key = rotate(rms_scale(projected[..., 1, :], k_gain), angles)
    value = projected[..., 2, :]
    merged = (clips, frames, tok_rows, tok_cols, local_heads * HD)
    return (
        latents,
        query.reshape(merged).astype(jnp.bfloat16),
        key.reshape(merged).astype(jnp.bfloat16),
        value.reshape(merged).astype(jnp.bfloat16),
    )


LANES = 128
TILE = 16
GROUP = 16


def one_group_each(mesh, clip_inputs, conv_in_weight, conv_out_weight, qkv_weight):
    plane = mesh.shape["tm"] * mesh.shape["height"]
    return (
        clip_inputs.shape[:4] == (1, 2, 2, 16)
        and mesh.shape["height"] == 2
        and mesh.shape["tm"] == 4
        and mesh.shape["dp"] == 4
        and conv_in_weight.shape[1] == plane * GROUP
        and clip_inputs.shape[4] == GROUP * GROUPS
        and conv_out_weight.shape[2] == TILE
        and qkv_weight.shape[1] == 6 * HD
    )


def lane_shifts(lane):
    col = lane % 16
    row = lane // 16 % 2
    half = lane // 64

    def cols(left, mid, right):
        left = jnp.where(col == 0, left, pltpu.roll(left, 1, 1))
        right = jnp.where(col == 15, right, pltpu.roll(right, LANES - 1, 1))
        return mid + left + right

    def rows(up, mid, down):
        up = jnp.where(
            row == 1, pltpu.roll(up, 16, 1), jnp.where(half == 1, pltpu.roll(up, 48, 1), up)
        )
        down = jnp.where(
            row == 0,
            pltpu.roll(down, LANES - 16, 1),
            jnp.where(half == 0, pltpu.roll(down, LANES - 48, 1), down),
        )
        return mid + up + down

    return cols, rows


def tap_sums(y_ref, top, tiles):
    lane = lax.broadcasted_iota(jnp.int32, (TILE, LANES), 1)
    second = lane // 32 % 2 == 1
    cols, rows = lane_shifts(lane)
    sums = []
    before = None
    for tile in range(tiles):

        def part(tap):
            at = top + tap * TILE
            return y_ref[at : at + TILE, tile * LANES : (tile + 1) * LANES]

        oldest, older, now = (
            rows(*(cols(*(part(9 * i + 3 * j + l) for l in range(3))) for j in range(3)))
            for i in range(3)
        )
        turned = pltpu.roll(older, 32, 1)
        if before is None:
            start = jnp.where(second, pltpu.roll(oldest, 32, 1), oldest)
            total = now + jnp.where(second, turned, older) + start
        else:
            total = now + jnp.where(second, turned, pltpu.roll(before[1], 96, 1)) + before[0]
        before = (oldest, older)
        sums.append(total)
    return sums


def pack_kernel(
    w_hbm, qkv_hbm, patch_hbm, patch_bias_ref, out_ref, w_ref, qkv_ref, patch_ref, sems
):
    plane, channels, width = out_ref.shape
    depth = w_ref.shape[0]
    rows = qkv_ref.shape[0]
    place = lax.axis_index("tm") * lax.axis_size("height") + lax.axis_index("height")
    at = pl.ds(pl.multiple_of(place * rows, LANES), rows)
    loads = [
        pltpu.make_async_copy(w_hbm, w_ref, sems.at[0]),
        pltpu.make_async_copy(qkv_hbm, qkv_ref, sems.at[1]),
        pltpu.make_async_copy(patch_hbm.at[:, at], patch_ref, sems.at[2]),
    ]
    for load in loads:
        load.start()
    for load in loads:
        load.wait()
    merged = jnp.dot(patch_ref[...], qkv_ref[...], preferred_element_type=jnp.float32)
    bias = jnp.broadcast_to(patch_bias_ref[:, at], (8, rows))
    bias = jnp.dot(bias, qkv_ref[...], preferred_element_type=jnp.float32)
    line = lax.broadcasted_iota(jnp.int32, (8, LANES), 0)
    lines = jnp.zeros((8, LANES), jnp.float32)
    for part in range(bias.shape[1] // LANES):
        lines = jnp.where(line == part, bias[:, part * LANES : (part + 1) * LANES], lines)
    turned = w_ref[...].T
    for to in range(plane):
        first = to // 2 * channels
        out_ref[to, :, :depth] = turned[first : first + channels]
        parts = [merged[8 * to : 8 * to + 8, q * LANES : (q + 1) * LANES] for q in range(6)]
        parts += [lines, jnp.zeros_like(lines)]
        for tile in range(2):
            some = jnp.concatenate(parts[4 * tile : 4 * tile + 4], axis=0)
            end = width - LANES * (1 - tile)
            out_ref[to, :, end - LANES : end] = some.astype(jnp.bfloat16)


def arrange_kernel(*refs):
    pieces, (keep_ref, send_ref, all_ref) = refs[:4], refs[4:]
    side = lax.axis_index("height")
    layer = lax.axis_index("dp")
    for step, piece in enumerate(pieces):
        all_ref[(layer + 4 - step) % 4] = piece[...]
    for core in range(2):
        keep_ref[core] = all_ref[2 * side + core]
        send_ref[core] = all_ref[2 - 2 * side + core]


def join_kernel(
    w_ref, one_ref, two_ref, three_ref, out_bias_ref, qkv_bias_ref, q_gain_ref, k_gain_ref,
    wt_ref, bias_ref, qkv_ref, gains_ref,
):
    plane, width, lanes = w_ref.shape
    channels = wt_ref.shape[1]
    depth = TAPS * channels // plane
    for group in range(width // GROUP):
        for tap in range(TAPS):
            start = tap * channels
            end = start + channels
            at = (group * TAPS + tap) * GROUP
            while start < end:
                source = start // depth
                stop = min(end, (source + 1) * depth)
                wt_ref[
                    at : at + GROUP, start - tap * channels : stop - tap * channels
                ] = w_ref[
                    source,
                    group * GROUP : (group + 1) * GROUP,
                    start - source * depth : stop - source * depth,
                ]
                start = stop
    total = w_ref[0, :, lanes - 2 * LANES :].astype(jnp.float32)
    for source in range(1, plane):
        total = total + w_ref[source, :, lanes - 2 * LANES :].astype(jnp.float32)
    parts = [
        total[q % 4 * 8 : q % 4 * 8 + 8, q // 4 * LANES : (q // 4 + 1) * LANES] for q in range(7)
    ]
    empty = jnp.zeros((8, LANES), jnp.float32)
    share = jnp.concatenate(
        [jnp.concatenate(parts[:4], axis=1), jnp.concatenate(parts[4:6] + [empty] * 2, axis=1)],
        axis=0,
    )
    coarse = share.astype(jnp.bfloat16)
    top = width * TAPS
    wt_ref[top : top + 16] = coarse
    wt_ref[top + 16 : top + 32] = (share - coarse.astype(jnp.float32)).astype(jnp.bfloat16)
    extra = jnp.concatenate([parts[6][q : q + 1] for q in range(6)], axis=1)
    qkv_ref[...] = extra + qkv_bias_ref[...].astype(jnp.float32)
    bias_ref[...] = jnp.broadcast_to(out_bias_ref[...], bias_ref.shape)
    gains_ref[0:1] = q_gain_ref[...].astype(jnp.float32)
    gains_ref[1:2] = k_gain_ref[...].astype(jnp.float32)


def place_clip(pieces, x_ref):
    place = lax.axis_index("tm") // 2 * 4 + lax.axis_index("height")
    for flip, piece in zip((0, 1, 4, 5), pieces):
        for core in range(2):
            x_ref[(place ^ flip) + 2 * core] = piece[core]


def normed_half(x_ref, wt_ref, y_ref, gain_ref, bias_ref, half):
    channels = x_ref.shape[2]
    tiles = x_ref.shape[0] // 2
    taps = TAPS * GROUP
    count = float(tiles * LANES * GROUP)
    y_ref[...] = lax.dot_general(
        wt_ref[: 2 * taps],
        x_ref[...].reshape(tiles * LANES, channels),
        (((1,), (1,)), ((), ())),
        preferred_element_type=jnp.float32,
    )
    normed = []
    for group in range(2):
        hidden = tap_sums(y_ref, group * taps, tiles)
        at = pl.ds(pl.multiple_of((2 * half + group) * GROUP, GROUP), GROUP)
        mean = jnp.sum(sum(hidden), keepdims=True) / count
        square = jnp.sum(sum(part * part for part in hidden), keepdims=True) / count
        scale = lax.rsqrt(square - mean * mean + norm_eps)
        parts = []
        for part in hidden:
            scaled = (part - mean) * scale * gain_ref[at] + bias_ref[at]
            parts.append((scaled / (1.0 + jnp.exp(-scaled))).astype(jnp.bfloat16))
        normed.append(jnp.concatenate(parts, axis=1))
    return jnp.concatenate(normed, axis=0)


def own_half_kernel(
    x0_ref, x1_ref, x2_ref, x3_ref, wt_ref, gain_ref, bias_ref, out_ref, x_ref, y_ref
):
    place_clip((x0_ref, x1_ref, x2_ref, x3_ref), x_ref)
    half = lax.axis_index("tm") % 2
    out_ref[...] = normed_half(x_ref, wt_ref, y_ref, gain_ref, bias_ref, half)


def conv_kernel(
    x_ref, normed_ref, wt_ref, gain_ref, bias_ref, w2_ref, out_ref, y_ref, n_ref
):
    tiles = x_ref.shape[0] // 2
    half = lax.axis_index("tm") % 2
    n_ref[pl.ds(pl.multiple_of(half * 2 * GROUP, 2 * GROUP), 2 * GROUP)] = normed_ref[...]
    other = normed_half(x_ref, wt_ref, y_ref, gain_ref, bias_ref, 1 - half)
    n_ref[pl.ds(pl.multiple_of((1 - half) * 2 * GROUP, 2 * GROUP), 2 * GROUP)] = other
    y_ref[: TAPS * TILE] = jnp.dot(w2_ref[...], n_ref[...], preferred_element_type=jnp.float32)
    low = lax.broadcasted_iota(jnp.int32, (8, LANES), 1) < 64
    layers = out_ref.shape[0] // (2 * tiles)
    for tile, part in enumerate(tap_sums(y_ref, 0, tiles)):
        turned = pltpu.roll(part, 64, 1)
        near = jnp.where(low, part[:8], turned[8:])
        far = jnp.where(low, turned[:8], part[8:])
        for layer in range(layers):
            out_ref[layer * 2 * tiles + 2 * tile] = near
            out_ref[layer * 2 * tiles + 2 * tile + 1] = far


def token_kernel(
    p_ref, m0_ref, m1_ref, m2_ref, m3_ref, bias_ref, qkv_bias_ref, gains_ref, cos_ref, sin_ref,
    lat_ref, q_ref, k_ref, v_ref, m_ref,
):
    spot = lax.axis_index("tm") * 2 + lax.axis_index("height")
    for flip, ref in ((0, m0_ref), (1, m1_ref), (4, m2_ref), (5, m3_ref)):
        for core in range(2):
            share = ref[core].astype(jnp.float32)
            at = spot ^ flip ^ (2 * core)
            for fine in range(2):
                m_ref[fine, at, :, : 4 * LANES] = share[16 * fine : 16 * fine + 8]
                m_ref[fine, at, :, 4 * LANES :] = share[16 * fine + 8 : 16 * fine + 16, : 2 * LANES]
    low = lax.broadcasted_iota(jnp.int32, (8, LANES), 1) < 64
    pairs = []
    for side in range(2):
        one, two = (
            sum(p_ref[4 * index + 2 * core + side] for index in range(p_ref.shape[0] // 4))
            for core in range(2)
        )
        top = jnp.where(low, one, pltpu.roll(two, 64, 1))
        bottom = jnp.where(low, pltpu.roll(one, 64, 1), two)
        pairs.append(jnp.concatenate([top, bottom], axis=0))
    total = jnp.concatenate(pairs, axis=1)
    lat = (total + bias_ref[:, :1]) * latent_scale
    clips = lat.shape[1] // 64
    tokens = clips * 16
    place = lax.axis_index("dp")
    own = lat[:, :LANES]
    for pair in range(1, clips // 2):
        own = jnp.where(place // 2 == pair, lat[:, pair * LANES : (pair + 1) * LANES], own)
    own = jnp.where(place % 2 == 1, pltpu.roll(own, 64, 1), own)
    turned = own.T[:64]
    wide = jnp.concatenate([turned] * 16, axis=1)
    spot = lax.broadcasted_iota(jnp.int32, wide.shape, 0) % 16
    spread = lax.broadcasted_iota(jnp.int32, wide.shape, 1) // 16
    merged = jnp.sum(jnp.where(spot == spread, wide, 0.0).reshape(4, 16, 256), axis=1)
    lat_ref[0, 0] = merged[:2]
    lat_ref[0, 1] = merged[2:]

    lat_bf = lat.astype(jnp.bfloat16)
    token = lax.broadcasted_iota(jnp.int32, (tokens, clips * 64), 0)
    lane = lax.broadcasted_iota(jnp.int32, (tokens, clips * 64), 1)
    first = token // 8 * 32 + token % 8 * 2
    heads = q_ref.shape[2] // HD
    projected = qkv_bias_ref[...]
    coarse, fine = (
        m_ref[index].reshape(64, 3 * HD * heads).astype(jnp.bfloat16) for index in range(2)
    )
    for a in range(2):
        for e in range(2):
            chosen = jnp.where(lane == first + (16 * a + e), 1.0, 0.0).astype(jnp.bfloat16)
            patch = lax.dot_general(
                chosen, lat_bf, (((1,), (1,)), ((), ())), preferred_element_type=jnp.float32
            ).astype(jnp.bfloat16)
            at = slice((2 * a + e) * TILE, (2 * a + e + 1) * TILE)
            for weight in (coarse[at], fine[at]):
                projected = projected + jnp.dot(patch, weight, preferred_element_type=jnp.float32)

    even = lax.broadcasted_iota(jnp.int32, (tokens, HD), 1) % 2 == 0
    cosine = jnp.concatenate([cos_ref[...]] * clips, axis=0)
    sine = jnp.concatenate([sin_ref[...]] * clips, axis=0)

    def turn(vectors, gain):
        square = jnp.mean(vectors * vectors, axis=-1, keepdims=True)
        vectors = vectors * lax.rsqrt(square + norm_eps) * gain
        swapped = jnp.where(even, pltpu.roll(vectors, HD - 1, 1), pltpu.roll(vectors, 1, 1))
        return vectors * cosine + swapped * sine

    def keep(ref, head, value):
        value = value.reshape(tokens // 8, 8, HD).astype(jnp.bfloat16)
        ref[:, :, head * HD : (head + 1) * HD] = value

    for head in range(heads):
        at = 3 * HD * head
        keep(q_ref, head, turn(projected[:, at : at + HD], gains_ref[0:1]))
        keep(k_ref, head, turn(projected[:, at + HD : at + 2 * HD], gains_ref[1:2]))
        keep(v_ref, head, projected[:, at + 2 * HD : at + 3 * HD])


def rope_tables(frame_pos, row_pos, width):
    angles = rope_angles(frame_pos.astype(jnp.float32), row_pos.astype(jnp.float32), width)
    angles = angles.reshape(-1, HD // 2)
    cosine = jnp.repeat(jnp.cos(angles), 2, axis=1)
    sine = jnp.sin(angles)
    return cosine, jnp.stack([-sine, sine], axis=-1).reshape(cosine.shape)


def vmem(count):
    return [pl.BlockSpec(memory_space=pltpu.VMEM)] * count


def grouped(
    clip_inputs,
    conv_in_weight,
    group_gain,
    group_bias,
    conv_out_weight,
    out_bias,
    patch_weight,
    patch_bias,
    qkv_weight,
    qkv_bias,
    q_gain,
    k_gain,
    frame_pos,
    row_pos,
):
    plane_axes = ("tm", "height")
    clips = lax.axis_size("dp")
    steps = lax.axis_size("tm")
    plane = steps * lax.axis_size("height")
    channels = clip_inputs.shape[4]
    depth = conv_in_weight.shape[0]

    width = -(-depth // LANES) * LANES + 2 * LANES
    limit = pltpu.CompilerParams(vmem_limit_bytes=32 * 1024 * 1024)
    small = pl.CostEstimate(flops=10**6, bytes_accessed=10**6, transcendentals=0)
    with jax.named_scope("weight_by_group"):
        packed = pl.pallas_call(
            pack_kernel,
            out_shape=jax.ShapeDtypeStruct((plane, 2 * GROUP, width), jnp.bfloat16),
            in_specs=[pl.BlockSpec(memory_space=pltpu.HBM)] * 3 + vmem(1),
            out_specs=vmem(1)[0],
            scratch_shapes=[
                pltpu.VMEM(conv_in_weight.shape, jnp.bfloat16),
                pltpu.VMEM(qkv_weight.shape, jnp.bfloat16),
                pltpu.VMEM((patch_weight.shape[0], qkv_weight.shape[0]), jnp.bfloat16),
                pltpu.SemaphoreType.DMA((3,)),
            ],
            compiler_params=pltpu.CompilerParams(vmem_limit_bytes=60 * 1024 * 1024),
            cost_estimate=pl.CostEstimate(flops=10**8, bytes_accessed=10**6, transcendentals=0),
            name="pack_weights",
        )(conv_in_weight, qkv_weight, patch_weight, patch_bias[None])
        weight = lax.all_to_all(packed, plane_axes, 0, 0, tiled=True)
    with jax.named_scope("gather_clips"):
        own = clip_inputs.reshape(64, channels)
        layers = []
        for step in range(clips):
            pairs = []
            for layer in range(clips):
                for tm in range(steps):
                    to = (layer // 2 * 2 + tm % 2 + step) % clips
                    pairs.append((layer * steps + tm, to * steps + tm // 2 * 2 + layer % 2))
            layers.append(lax.ppermute(own, ("dp", "tm"), pairs))
    with jax.named_scope("spread_clips"):
        keep, send = pl.pallas_call(
            arrange_kernel,
            out_shape=(jax.ShapeDtypeStruct((2, 64, channels), jnp.bfloat16),) * 2,
            in_specs=vmem(4),
            out_specs=tuple(vmem(2)),
            scratch_shapes=[pltpu.VMEM((4, 64, channels), jnp.bfloat16)],
            compiler_params=limit,
            cost_estimate=small,
            name="arrange_clips",
        )(*layers)
        pieces = [keep]
        for flip in (1, 4, 5):
            pairs = [(i, i ^ flip) for i in range(plane)]
            pieces.append(lax.ppermute(send if flip % 2 else keep, plane_axes, pairs))
    with jax.named_scope("small_weights"):
        first = lax.axis_index("tm") // 2 * (4 * GROUP)
        gain = lax.dynamic_slice_in_dim(group_gain, first, 4 * GROUP).astype(jnp.float32)
        bias = lax.dynamic_slice_in_dim(group_bias, first, 4 * GROUP).astype(jnp.float32)
        weight_out = lax.dynamic_slice_in_dim(conv_out_weight, first, 4 * GROUP, axis=1)
        weight_out = weight_out.transpose(0, 2, 1).reshape(TAPS * TILE, 4 * GROUP)
        cosine, sine = rope_tables(frame_pos, row_pos, clip_inputs.shape[3] // 2)
    with jax.named_scope("join_weights"):
        joined, latent_bias, merged_bias, gains = pl.pallas_call(
            join_kernel,
            out_shape=(
                jax.ShapeDtypeStruct((2 * GROUP * TAPS + 32, channels), jnp.bfloat16),
                jax.ShapeDtypeStruct((TILE, LANES), jnp.float32),
                jax.ShapeDtypeStruct((1, qkv_weight.shape[1]), jnp.float32),
                jax.ShapeDtypeStruct((2, HD), jnp.float32),
            ),
            in_specs=vmem(8),
            out_specs=tuple(vmem(4)),
            compiler_params=limit,
            cost_estimate=small,
            name="join_weights",
        )(weight, *pieces[1:], out_bias[:, None], qkv_bias[None], q_gain[None], k_gain[None])
        joined_pair = lax.ppermute(joined, "tm", [(i, i ^ 1) for i in range(steps)])
    with jax.named_scope("merged_projection"):
        share = jnp.stack([joined[-32:], joined_pair[-32:]])
        shares = [share]
        for flip in (1, 4, 5):
            pairs = [(i, i ^ flip) for i in range(plane)]
            shares.append(lax.ppermute(share, plane_axes, pairs))

    flops = 2 * clips * steps * LANES * TAPS * TILE * (channels + 16)
    cost = pl.CostEstimate(flops=flops // 2, bytes_accessed=10**6, transcendentals=0)
    product = pltpu.VMEM((2 * TAPS * GROUP, steps * LANES), jnp.float32)
    scale = (gain[:, None], bias[:, None])
    normed, clip = pl.pallas_call(
        own_half_kernel,
        out_shape=(
            jax.ShapeDtypeStruct((2 * GROUP, steps * LANES), jnp.bfloat16),
            jax.ShapeDtypeStruct((plane, 64, channels), jnp.bfloat16),
        ),
        in_specs=vmem(7),
        out_specs=tuple(vmem(2)),
        scratch_shapes=[product],
        compiler_params=limit,
        cost_estimate=cost,
        name="own_channels",
    )(*pieces, joined, *scale)
    partial = pl.pallas_call(
        conv_kernel,
        out_shape=jax.ShapeDtypeStruct((clips * plane, 8, LANES), jnp.float32),
        in_specs=vmem(6),
        out_specs=vmem(1)[0],
        scratch_shapes=[product, pltpu.VMEM((4 * GROUP, steps * LANES), jnp.bfloat16)],
        compiler_params=limit,
        cost_estimate=cost,
        name="convolutions",
    )(clip, normed, joined_pair, *scale, weight_out)

    with jax.named_scope("sum_latents"):
        partials = lax.all_to_all(partial, ("dp",) + plane_axes, 0, 0, tiled=True)

    heads = qkv_weight.shape[1] // (3 * HD)
    frames = clip_inputs.shape[1]
    tokens = jax.ShapeDtypeStruct((clips * frames, 8, heads * HD), jnp.bfloat16)
    latents, query, key, value = pl.pallas_call(
        token_kernel,
        out_shape=(jax.ShapeDtypeStruct((1, 2, 2, 256), jnp.float32), tokens, tokens, tokens),
        in_specs=vmem(10),
        out_specs=tuple(vmem(4)),
        scratch_shapes=[pltpu.VMEM((2, plane, 8, 6 * HD), jnp.float32)],
        compiler_params=limit,
        cost_estimate=pl.CostEstimate(flops=10**8, bytes_accessed=10**6, transcendentals=0),
        name="tokens",
    )(
        partials,
        *shares,
        latent_bias,
        merged_bias,
        gains,
        cosine,
        sine,
    )
    full = (clips, frames, 1, 8, heads * HD)
    return latents, query.reshape(full), key.reshape(full), value.reshape(full)


def pick(mesh, *arrays):
    if one_group_each(mesh, arrays[0], arrays[1], arrays[4], arrays[8]):
        return grouped(*arrays)
    return shards(*arrays)


def solution(mesh):
    placed = (
        P("dp", "tm", "height", None, None),
        P(("tm", "height"), "dp"),
        P("dp"),
        P("dp"),
        P(None, "dp", None),
        P(),
        P(),
        P(),
        P(("tm", "height"), "dp"),
        P("dp"),
        P(),
        P(),
        P("tm"),
        P("height"),
    )
    return jax.shard_map(
        functools.partial(pick, mesh),
        mesh=mesh,
        in_specs=placed,
        out_specs=(
            P("dp", "tm", "height", None),
            P(None, "tm", "height", None, "dp"),
            P(None, "tm", "height", None, "dp"),
            P(None, "tm", "height", None, "dp"),
        ),
        check_vma=False,
    )
```

```python
import functools

import jax
import jax.numpy as jnp
import numpy as np
from jax import lax
from jax.experimental import pallas as pl
from jax.experimental.pallas import tpu as pltpu
from jax.sharding import PartitionSpec as P

HD = 128
GROUPS = 32
TAPS = 27


norm_eps = 1e-06
latent_scale = 0.476986
rope_base = 256.0
time_dims = 16
row_dims = 56


def from_behind(value, axis, steps):
    count = lax.axis_size(axis)
    first, last = (max(0, -steps), min(count, count - steps))
    return lax.ppermute(value, axis, [(source, source + steps) for source in range(first, last)])


def padded_2(block, sides, width):
    for axis, dim in sides:
        count = lax.axis_size(axis)
        forward = [(i, i + 1) for i in range(count - 1)]
        backward = [(target, source) for source, target in forward]
        low = lax.ppermute(
            lax.slice_in_dim(block, block.shape[dim] - width, None, axis=dim), axis, forward
        )
        high = lax.ppermute(lax.slice_in_dim(block, 0, width, axis=dim), axis, backward)
        block = jnp.concatenate([low, block, high], axis=dim)
    return block


def repeat_first(block):
    return jnp.concatenate([block[:, :1], block[:, :1]], axis=1)


def time_join(block, earlier):
    start = jnp.where(lax.axis_index("tm") == 0, repeat_first(block), earlier)
    return jnp.concatenate([start, block], axis=1)


def rows_finish(grown):
    place = lax.axis_index("height")
    top = jnp.where(place == 0, grown[:, :, 1:2], grown[:, :, :1])
    bottom = jnp.where(place == lax.axis_size("height") - 1, grown[:, :, -2:-1], grown[:, :, -1:])
    inner = jnp.concatenate([top, grown[:, :, 1:-1], bottom], axis=2)
    return jnp.pad(inner, ((0, 0), (0, 0), (0, 0), (1, 1), (0, 0)), mode="edge")


def edges_before(block):
    earlier = from_behind(block, "tm", 1)
    longer = time_join(block, earlier)
    return rows_finish(padded_2(longer, (("height", 2),), 1))


def edges_norm(block):
    earlier = from_behind(block, "tm", 1)
    longer = time_join(block, earlier)
    return rows_finish(padded_2(longer, (("height", 2),), 1))


def convolve(padded, weight):
    clips = padded.shape[0]
    frames = padded.shape[1] - 2
    rows = padded.shape[2] - 2
    cols = padded.shape[3] - 2
    total = jnp.zeros((clips * frames * rows * cols, weight.shape[2]), jnp.float32)
    for shift_t in range(3):
        for shift_r in range(3):
            for shift_c in range(3):
                window = padded[
                    :,
                    shift_t : shift_t + frames,
                    shift_r : shift_r + rows,
                    shift_c : shift_c + cols,
                ]
                window = window.reshape(-1, padded.shape[4])
                total = total + jnp.dot(
                    window,
                    weight[9 * shift_t + 3 * shift_r + shift_c],
                    preferred_element_type=jnp.float32,
                )
    return total.reshape(clips, frames, rows, cols, weight.shape[2])


def section_freqs(dims):
    return jnp.power(rope_base, -jnp.arange(0, dims, 2, dtype=jnp.float32) / dims)


def rope_angles(tpos, hpos, width):
    frames = tpos.shape[0]
    rows = hpos.shape[0]
    cols = jnp.arange(width, dtype=jnp.float32)
    part_t = tpos[:, None, None, None] * section_freqs(time_dims)
    part_h = hpos[None, :, None, None] * section_freqs(row_dims)
    part_w = cols[None, None, :, None] * section_freqs(row_dims)
    shape = (frames, rows, width)
    return jnp.concatenate(
        [
            jnp.broadcast_to(part_t, shape + (time_dims // 2,)),
            jnp.broadcast_to(part_h, shape + (row_dims // 2,)),
            jnp.broadcast_to(part_w, shape + (row_dims // 2,)),
        ],
        axis=-1,
    )


def rotate(vectors, angles):
    pairs = vectors.reshape(vectors.shape[:-1] + (vectors.shape[-1] // 2, 2))
    first = pairs[..., 0]
    second = pairs[..., 1]
    cosine = jnp.cos(angles)[..., None, :]
    sine = jnp.sin(angles)[..., None, :]
    turned = jnp.stack([first * cosine - second * sine, first * sine + second * cosine], axis=-1)
    return turned.reshape(vectors.shape)


def rms_scale(vectors, gain):
    return (
        vectors
        * lax.rsqrt(jnp.mean(vectors * vectors, axis=-1, keepdims=True) + norm_eps)
        * gain.astype(jnp.float32)
    )


def shards(
    clip_inputs,
    conv_in_weight,
    group_gain,
    group_bias,
    conv_out_weight,
    out_bias,
    patch_weight,
    patch_bias,
    qkv_weight,
    qkv_bias,
    q_gain,
    k_gain,
    frame_pos,
    row_pos,
):
    channels = clip_inputs.shape[4]
    frames = clip_inputs.shape[1]
    rows = clip_inputs.shape[2]
    cols = clip_inputs.shape[3]
    padded = lax.all_gather(edges_before(clip_inputs), "dp", axis=0, tiled=True)
    clips = padded.shape[0]
    weight_in = lax.all_gather(conv_in_weight, ("tm", "height"), axis=0, tiled=True).reshape(
        TAPS, channels, -1
    )
    hidden = convolve(padded, weight_in)
    block_width = hidden.shape[4]
    group_width = channels // GROUPS
    local_groups = block_width // group_width
    grouped = hidden.reshape(clips, -1, local_groups, group_width)
    sums_local = jnp.sum(grouped, axis=(1, 3))
    squares_local = jnp.sum(grouped * grouped, axis=(1, 3))
    sums_all, squares_all = lax.psum((sums_local, squares_local), ("tm", "height"))
    count = float(
        frames * lax.axis_size("tm") * rows * lax.axis_size("height") * cols * group_width
    )
    mean = sums_all / count
    var = squares_all / count - mean * mean
    scaled = (grouped - mean[:, None, :, None]) * lax.rsqrt(var + norm_eps)[:, None, :, None]
    scaled = scaled.reshape(hidden.shape) * group_gain.astype(jnp.float32) + group_bias.astype(
        jnp.float32
    )
    normed = jax.nn.silu(scaled).astype(jnp.bfloat16)
    partial_latent = convolve(edges_norm(normed), conv_out_weight)
    own_sum = lax.psum_scatter(partial_latent, "dp", scatter_dimension=0, tiled=True)
    own_latent = (own_sum + out_bias) * latent_scale
    every_latent = lax.all_gather(own_latent.astype(jnp.bfloat16), "dp", axis=0, tiled=True)
    latent_dims = every_latent.shape[4]
    latents = own_latent.reshape(1, frames, rows, cols * latent_dims)
    tok_rows = rows // 2
    tok_cols = cols // 2
    patches = every_latent.reshape(clips, frames, tok_rows, 2, tok_cols, 2, latent_dims)
    patches = patches.transpose(0, 1, 2, 4, 3, 5, 6).reshape(-1, 4 * latent_dims)
    embedded = (
        jnp.dot(patches, patch_weight, preferred_element_type=jnp.float32)
        + patch_bias.astype(jnp.float32)
    ).astype(jnp.bfloat16)
    projected = jnp.dot(
        embedded,
        lax.all_gather(qkv_weight, ("tm", "height"), axis=0, tiled=True),
        preferred_element_type=jnp.float32,
    )
    projected = projected + qkv_bias.astype(jnp.float32)
    local_heads = qkv_weight.shape[1] // (3 * HD)
    projected = projected.reshape(clips, frames, tok_rows, tok_cols, local_heads, 3, HD)
    angles = rope_angles(frame_pos.astype(jnp.float32), row_pos.astype(jnp.float32), tok_cols)
    query = rotate(rms_scale(projected[..., 0, :], q_gain), angles)
    key = rotate(rms_scale(projected[..., 1, :], k_gain), angles)
    value = projected[..., 2, :]
    merged = (clips, frames, tok_rows, tok_cols, local_heads * HD)
    return (
        latents,
        query.reshape(merged).astype(jnp.bfloat16),
        key.reshape(merged).astype(jnp.bfloat16),
        value.reshape(merged).astype(jnp.bfloat16),
    )


LANES = 128
TILE = 16
GROUP = 16


def one_group_each(mesh, clip_inputs, conv_in_weight, conv_out_weight, qkv_weight):
    plane = mesh.shape["tm"] * mesh.shape["height"]
    return (
        clip_inputs.shape[:4] == (1, 2, 2, 16)
        and mesh.shape["height"] == 2
        and mesh.shape["tm"] == 4
        and mesh.shape["dp"] == 4
        and conv_in_weight.shape[1] == plane * GROUP
        and clip_inputs.shape[4] == GROUP * GROUPS
        and conv_out_weight.shape[2] == TILE
        and qkv_weight.shape[1] == 6 * HD
    )


def lane_shifts(lane):
    col = lane % 16
    row = lane // 16 % 2
    half = lane // 64

    def cols(left, mid, right):
        left = jnp.where(col == 0, left, pltpu.roll(left, 1, 1))
        right = jnp.where(col == 15, right, pltpu.roll(right, LANES - 1, 1))
        return mid + left + right

    def rows(up, mid, down):
        up = jnp.where(
            row == 1, pltpu.roll(up, 16, 1), jnp.where(half == 1, pltpu.roll(up, 48, 1), up)
        )
        down = jnp.where(
            row == 0,
            pltpu.roll(down, LANES - 16, 1),
            jnp.where(half == 0, pltpu.roll(down, LANES - 48, 1), down),
        )
        return mid + up + down

    return cols, rows


def tap_sums(y_ref, top, tiles):
    lane = lax.broadcasted_iota(jnp.int32, (TILE, LANES), 1)
    second = lane // 32 % 2 == 1
    cols, rows = lane_shifts(lane)
    sums = []
    before = None
    for tile in range(tiles):

        def part(tap):
            at = top + tap * TILE
            return y_ref[at : at + TILE, tile * LANES : (tile + 1) * LANES]

        oldest, older, now = (
            rows(*(cols(*(part(9 * i + 3 * j + l) for l in range(3))) for j in range(3)))
            for i in range(3)
        )
        turned = pltpu.roll(older, 32, 1)
        if before is None:
            start = jnp.where(second, pltpu.roll(oldest, 32, 1), oldest)
            total = now + jnp.where(second, turned, older) + start
        else:
            total = now + jnp.where(second, turned, pltpu.roll(before[1], 96, 1)) + before[0]
        before = (oldest, older)
        sums.append(total)
    return sums


def pack_kernel(
    w_hbm, qkv_hbm, patch_hbm, patch_bias_hbm, out_hbm, lines_ref,
    w_ref, qkv_ref, patch_ref, patch_bias_ref, rows_ref, out_ref, sems,
):
    plane, channels, width = out_ref.shape
    depth = w_ref.shape[0]
    rows = qkv_ref.shape[0]
    place = lax.axis_index("tm") * lax.axis_size("height") + lax.axis_index("height")
    at = pl.ds(pl.multiple_of(place * rows, LANES), rows)
    loads = [
        pltpu.make_async_copy(w_hbm, w_ref, sems.at[0]),
        pltpu.make_async_copy(qkv_hbm, qkv_ref, sems.at[1]),
        pltpu.make_async_copy(patch_hbm.at[:, at], patch_ref, sems.at[2]),
        pltpu.make_async_copy(patch_bias_hbm, patch_bias_ref, sems.at[3]),
    ]
    for load in loads:
        load.start()
    whole = depth // LANES * LANES
    loads[0].wait()
    turned = w_ref[...].T
    for to in range(plane):
        first = to // 2 * channels
        out_ref[to, :, :whole] = turned[first : first + channels, :whole]
    body = slice(0, whole)
    tail = slice(whole, width)
    stores = [
        pltpu.make_async_copy(out_ref.at[:, :, part], out_hbm.at[:, :, part], sems.at[4 + index])
        for index, part in enumerate((body, tail))
    ]
    stores[0].start()
    for load in loads[1:]:
        load.wait()
    merged = jnp.dot(patch_ref[...], qkv_ref[...], preferred_element_type=jnp.float32)
    lane = lax.broadcasted_iota(jnp.int32, (8, LANES), 1)
    for to in range(plane):
        first = to // 2 * channels
        mine = [merged[8 * to : 8 * to + 8, q * LANES : (q + 1) * LANES] for q in range(6)]
        upper = [pltpu.roll(mine[4], 64, 1), mine[4], pltpu.roll(mine[5], 64, 1), mine[5]]
        upper = jnp.concatenate(upper, axis=0)[:, 64:].astype(jnp.bfloat16)
        lower = turned[first : first + channels, whole:]
        out_ref[to, :, whole : whole + LANES] = jnp.concatenate([lower, upper], axis=1)
        out_ref[to, :, whole + LANES :] = jnp.concatenate(mine[:4], axis=0).astype(jnp.bfloat16)
    stores[1].start()
    rows_ref[...] = patch_bias_ref[...].astype(jnp.float32).reshape(rows_ref.shape)
    count = rows // LANES
    bias = [rows_ref[pl.ds(count * place + part, 1), :] for part in range(count)]
    bias = jnp.broadcast_to(jnp.concatenate(bias, axis=1), (8, rows)).astype(jnp.bfloat16)
    bias = jnp.dot(bias, qkv_ref[...], preferred_element_type=jnp.float32)
    line = lax.broadcasted_iota(jnp.int32, (8, LANES), 0)
    lines = jnp.zeros((8, LANES), jnp.float32)
    for part in range(bias.shape[1] // LANES):
        lines = jnp.where(line == part, bias[:, part * LANES : (part + 1) * LANES], lines)
    lines_ref[...] = lines
    for store in stores:
        store.wait()


def column(row_ref, first, size):
    length = row_ref.shape[0]
    row = row_ref[...].astype(jnp.float32).reshape(1, length)
    line = lax.broadcasted_iota(jnp.int32, (size, length), 0)
    lane = lax.broadcasted_iota(jnp.int32, (size, length), 1)
    picked = jnp.where(lane == line + first, jnp.broadcast_to(row, (size, length)), 0.0)
    return jnp.sum(picked, axis=1, keepdims=True)


def table_kernel(
    frame_ref, row_pos_ref, freq_ref, gain_hbm, bias_hbm, out_bias_hbm, qkv_hbm, q_hbm, k_hbm,
    scale_ref, table_ref,
    gain_v, bias_v, out_bias_v, qkv_v, q_v, k_v, sems,
):
    pairs = (
        (gain_hbm, gain_v), (bias_hbm, bias_v), (out_bias_hbm, out_bias_v),
        (qkv_hbm, qkv_v), (q_hbm, q_v), (k_hbm, k_v),
    )
    loads = [
        pltpu.make_async_copy(source, to, sems.at[index])
        for index, (source, to) in enumerate(pairs)
    ]
    for load in loads:
        load.start()
    shape = (TILE, LANES)
    line = lax.broadcasted_iota(jnp.int32, shape, 0)
    lane = lax.broadcasted_iota(jnp.int32, shape, 1)
    frame = jnp.where(line // 8 == 0, frame_ref[0], frame_ref[1]).astype(jnp.float32)
    row = jnp.broadcast_to(row_pos_ref[0], shape).astype(jnp.float32)
    spot = jnp.where(lane < 72, row, (line % 8).astype(jnp.float32))
    angles = jnp.where(lane < 16, frame, spot) * freq_ref[...]
    table_ref[:16] = jnp.cos(angles)
    sine = jnp.sin(angles)
    table_ref[16:32] = jnp.where(lane % 2 == 0, -sine, sine)
    for load in loads:
        load.wait()
    first = lax.axis_index("tm") // 2 * (4 * GROUP)
    scale_ref[:, 0:1] = column(gain_v, first, 4 * GROUP)
    scale_ref[:, 1:2] = column(bias_v, first, 4 * GROUP)
    table_ref[32:48] = jnp.broadcast_to(column(out_bias_v, 0, TILE), shape)
    table_ref[48:49] = q_v[...].astype(jnp.float32).reshape(1, HD)
    table_ref[49:50] = k_v[...].astype(jnp.float32).reshape(1, HD)
    table_ref[50:56] = qkv_v[...].astype(jnp.float32).reshape(6, LANES)


def arrange_kernel(*refs):
    pieces, (keep_ref, send_ref, all_ref) = refs[:4], refs[4:]
    side = lax.axis_index("height")
    layer = lax.axis_index("dp")
    for step, piece in enumerate(pieces):
        all_ref[(layer + 4 - step) % 4] = piece[...]
    for core in range(2):
        keep_ref[core] = all_ref[2 * side + core]
        send_ref[core] = all_ref[2 - 2 * side + core]


def join_kernel(w_ref, lines_ref, wt_ref):
    plane, width, lanes = w_ref.shape
    channels = wt_ref.shape[1]
    depth = TAPS * channels // plane
    for group in range(width // GROUP):
        for tap in range(TAPS):
            start = tap * channels
            end = start + channels
            at = (group * TAPS + tap) * GROUP
            while start < end:
                source = start // depth
                stop = min(end, (source + 1) * depth)
                wt_ref[
                    at : at + GROUP, start - tap * channels : stop - tap * channels
                ] = w_ref[
                    source,
                    group * GROUP : (group + 1) * GROUP,
                    start - source * depth : stop - source * depth,
                ]
                start = stop
    total = w_ref[0, :, lanes - 2 * LANES :].astype(jnp.float32)
    for source in range(1, plane):
        total = total + w_ref[source, :, lanes - 2 * LANES :].astype(jnp.float32)
    low = lax.broadcasted_iota(jnp.int32, (8, LANES), 1) < 64
    parts = [total[8 * q : 8 * q + 8, LANES:] for q in range(4)]
    for q in range(2):
        one = total[16 * q : 16 * q + 8, :LANES]
        two = total[16 * q + 8 : 16 * q + 16, :LANES]
        parts.append(jnp.where(low, pltpu.roll(one, 64, 1), two))
    parts += [lines_ref[...], jnp.zeros((8, LANES), jnp.float32)]
    share = jnp.concatenate(
        [jnp.concatenate(parts[:4], axis=1), jnp.concatenate(parts[4:], axis=1)], axis=0
    )
    wt_ref[width * TAPS :] = share.astype(jnp.bfloat16)


def place_clip(pieces, x_ref):
    place = lax.axis_index("tm") // 2 * 4 + lax.axis_index("height")
    for flip, piece in zip((0, 1, 4, 5), pieces):
        for core in range(2):
            x_ref[(place ^ flip) + 2 * core] = piece[core]


def normed_half(x_ref, wt_ref, y_ref, scale_ref, half):
    channels = x_ref.shape[2]
    tiles = x_ref.shape[0] // 2
    taps = TAPS * GROUP
    count = float(tiles * LANES * GROUP)
    y_ref[...] = lax.dot_general(
        wt_ref[: 2 * taps],
        x_ref[...].reshape(tiles * LANES, channels),
        (((1,), (1,)), ((), ())),
        preferred_element_type=jnp.float32,
    )
    normed = []
    for group in range(2):
        hidden = tap_sums(y_ref, group * taps, tiles)
        at = pl.ds(pl.multiple_of((2 * half + group) * GROUP, GROUP), GROUP)
        mean = jnp.sum(sum(hidden), keepdims=True) / count
        square = jnp.sum(sum(part * part for part in hidden), keepdims=True) / count
        scale = lax.rsqrt(square - mean * mean + norm_eps)
        parts = []
        for part in hidden:
            scaled = (part - mean) * scale * scale_ref[at, 0:1] + scale_ref[at, 1:2]
            parts.append((scaled / (1.0 + jnp.exp(-scaled))).astype(jnp.bfloat16))
        normed.append(jnp.concatenate(parts, axis=1))
    return jnp.concatenate(normed, axis=0)


def own_half_kernel(
    x0_ref, x1_ref, x2_ref, x3_ref, wt_ref, scale_ref, out_ref, x_ref, y_ref
):
    place_clip((x0_ref, x1_ref, x2_ref, x3_ref), x_ref)
    half = lax.axis_index("tm") % 2
    out_ref[...] = normed_half(x_ref, wt_ref, y_ref, scale_ref, half)


def conv_kernel(
    x_ref, normed_ref, wt_ref, scale_ref, w2_ref, out_ref, y_ref, n_ref
):
    tiles = x_ref.shape[0] // 2
    half = lax.axis_index("tm") % 2
    n_ref[pl.ds(pl.multiple_of(half * 2 * GROUP, 2 * GROUP), 2 * GROUP)] = normed_ref[...]
    other = normed_half(x_ref, wt_ref, y_ref, scale_ref, 1 - half)
    n_ref[pl.ds(pl.multiple_of((1 - half) * 2 * GROUP, 2 * GROUP), 2 * GROUP)] = other
    y_ref[: TAPS * TILE] = jnp.dot(w2_ref[...], n_ref[...], preferred_element_type=jnp.float32)
    low = lax.broadcasted_iota(jnp.int32, (8, LANES), 1) < 64
    layers = out_ref.shape[0] // (2 * tiles)
    for tile, part in enumerate(tap_sums(y_ref, 0, tiles)):
        turned = pltpu.roll(part, 64, 1)
        near = jnp.where(low, part[:8], turned[8:])
        far = jnp.where(low, turned[:8], part[8:])
        for layer in range(layers):
            out_ref[layer * 2 * tiles + 2 * tile] = near
            out_ref[layer * 2 * tiles + 2 * tile + 1] = far


def token_kernel(
    p_ref, m0_ref, m1_ref, m2_ref, m3_ref, table_ref,
    lat_ref, q_ref, k_ref, v_ref, m_ref,
):
    spot = lax.axis_index("tm") * 2 + lax.axis_index("height")
    lines = jnp.zeros((8, LANES), jnp.float32)
    for flip, ref in ((0, m0_ref), (1, m1_ref), (4, m2_ref), (5, m3_ref)):
        for core in range(2):
            share = ref[core].astype(jnp.float32)
            at = spot ^ flip ^ (2 * core)
            m_ref[at, :, : 4 * LANES] = share[:8]
            m_ref[at, :, 4 * LANES :] = share[8:, : 2 * LANES]
            lines = lines + share[8:, 2 * LANES : 3 * LANES]
    low = lax.broadcasted_iota(jnp.int32, (8, LANES), 1) < 64
    pairs = []
    for side in range(2):
        one, two = (
            sum(p_ref[4 * index + 2 * core + side] for index in range(p_ref.shape[0] // 4))
            for core in range(2)
        )
        top = jnp.where(low, one, pltpu.roll(two, 64, 1))
        bottom = jnp.where(low, pltpu.roll(one, 64, 1), two)
        pairs.append(jnp.concatenate([top, bottom], axis=0))
    total = jnp.concatenate(pairs, axis=1)
    lat = (total + table_ref[32:48, :1]) * latent_scale
    clips = lat.shape[1] // 64
    tokens = clips * 16
    place = lax.axis_index("dp")
    own = lat[:, :LANES]
    for pair in range(1, clips // 2):
        own = jnp.where(place // 2 == pair, lat[:, pair * LANES : (pair + 1) * LANES], own)
    own = jnp.where(place % 2 == 1, pltpu.roll(own, 64, 1), own)
    turned = own.T[:64]
    wide = jnp.concatenate([turned] * 16, axis=1)
    spot = lax.broadcasted_iota(jnp.int32, wide.shape, 0) % 16
    spread = lax.broadcasted_iota(jnp.int32, wide.shape, 1) // 16
    merged = jnp.sum(jnp.where(spot == spread, wide, 0.0).reshape(4, 16, 256), axis=1)
    lat_ref[0, 0] = merged[:2]
    lat_ref[0, 1] = merged[2:]

    lat_bf = lat.astype(jnp.bfloat16)
    token = lax.broadcasted_iota(jnp.int32, (tokens, clips * 64), 0)
    lane = lax.broadcasted_iota(jnp.int32, (tokens, clips * 64), 1)
    first = token // 8 * 32 + token % 8 * 2
    heads = q_ref.shape[2] // HD
    lines = lines[: 3 * heads] + table_ref[50:56]
    projected = jnp.concatenate([lines[part : part + 1] for part in range(3 * heads)], axis=1)
    merged = m_ref[...].reshape(64, 3 * HD * heads).astype(jnp.bfloat16)
    for a in range(2):
        for e in range(2):
            chosen = jnp.where(lane == first + (16 * a + e), 1.0, 0.0).astype(jnp.bfloat16)
            patch = lax.dot_general(
                chosen, lat_bf, (((1,), (1,)), ((), ())), preferred_element_type=jnp.float32
            ).astype(jnp.bfloat16)
            weight = merged[(2 * a + e) * TILE : (2 * a + e + 1) * TILE]
            projected = projected + jnp.dot(patch, weight, preferred_element_type=jnp.float32)

    even = lax.broadcasted_iota(jnp.int32, (tokens, HD), 1) % 2 == 0
    cosine = jnp.concatenate([table_ref[:16]] * clips, axis=0)
    sine = jnp.concatenate([table_ref[16:32]] * clips, axis=0)

    def turn(vectors, gain):
        square = jnp.mean(vectors * vectors, axis=-1, keepdims=True)
        vectors = vectors * lax.rsqrt(square + norm_eps) * gain
        swapped = jnp.where(even, pltpu.roll(vectors, HD - 1, 1), pltpu.roll(vectors, 1, 1))
        return vectors * cosine + swapped * sine

    def keep(ref, head, value):
        value = value.reshape(tokens // 8, 8, HD).astype(jnp.bfloat16)
        ref[:, :, head * HD : (head + 1) * HD] = value

    for head in range(heads):
        at = 3 * HD * head
        keep(q_ref, head, turn(projected[:, at : at + HD], table_ref[48:49]))
        keep(k_ref, head, turn(projected[:, at + HD : at + 2 * HD], table_ref[49:50]))
        keep(v_ref, head, projected[:, at + 2 * HD : at + 3 * HD])


def rope_freqs():
    freqs = []
    for dims in (time_dims, row_dims, row_dims):
        freqs.append(rope_base ** (-np.arange(0, dims, 2, dtype=np.float64) / dims))
    return np.repeat(np.concatenate(freqs), 2)[None].astype(np.float32)


def vmem(count):
    return [pl.BlockSpec(memory_space=pltpu.VMEM)] * count


def grouped(
    clip_inputs,
    conv_in_weight,
    group_gain,
    group_bias,
    conv_out_weight,
    out_bias,
    patch_weight,
    patch_bias,
    qkv_weight,
    qkv_bias,
    q_gain,
    k_gain,
    frame_pos,
    row_pos,
):
    plane_axes = ("tm", "height")
    clips = lax.axis_size("dp")
    steps = lax.axis_size("tm")
    plane = steps * lax.axis_size("height")
    channels = clip_inputs.shape[4]
    depth = conv_in_weight.shape[0]

    width = -(-depth // LANES) * LANES + LANES
    hbm = pl.BlockSpec(memory_space=pltpu.HBM)
    wide = pltpu.CompilerParams(vmem_limit_bytes=60 * 1024 * 1024)
    limit = pltpu.CompilerParams(vmem_limit_bytes=32 * 1024 * 1024)
    small = pl.CostEstimate(flops=10**6, bytes_accessed=10**6, transcendentals=0)
    with jax.named_scope("weight_by_group"):
        packed, lines = pl.pallas_call(
            pack_kernel,
            out_shape=(
                jax.ShapeDtypeStruct((plane, 2 * GROUP, width), jnp.bfloat16),
                jax.ShapeDtypeStruct((8, LANES), jnp.float32),
            ),
            in_specs=[hbm] * 4,
            out_specs=(hbm, vmem(1)[0]),
            scratch_shapes=[
                pltpu.VMEM(conv_in_weight.shape, jnp.bfloat16),
                pltpu.VMEM(qkv_weight.shape, jnp.bfloat16),
                pltpu.VMEM((patch_weight.shape[0], qkv_weight.shape[0]), jnp.bfloat16),
                pltpu.VMEM(patch_bias.shape, jnp.bfloat16),
                pltpu.VMEM((patch_bias.shape[0] // LANES, LANES), jnp.float32),
                pltpu.VMEM((plane, 2 * GROUP, width), jnp.bfloat16),
                pltpu.SemaphoreType.DMA((6,)),
            ],
            compiler_params=wide,
            cost_estimate=pl.CostEstimate(flops=10**8, bytes_accessed=10**6, transcendentals=0),
            name="pack_weights",
        )(conv_in_weight, qkv_weight, patch_weight, patch_bias)
        weight = lax.all_to_all(packed, plane_axes, 0, 0, tiled=True)
    with jax.named_scope("gather_clips"):
        own = clip_inputs.reshape(64, channels)
        layers = []
        for step in range(clips):
            pairs = []
            for layer in range(clips):
                for tm in range(steps):
                    to = (layer // 2 * 2 + tm % 2 + step) % clips
                    pairs.append((layer * steps + tm, to * steps + tm // 2 * 2 + layer % 2))
            layers.append(lax.ppermute(own, ("dp", "tm"), pairs))
    with jax.named_scope("spread_clips"):
        keep, send = pl.pallas_call(
            arrange_kernel,
            out_shape=(jax.ShapeDtypeStruct((2, 64, channels), jnp.bfloat16),) * 2,
            in_specs=vmem(4),
            out_specs=tuple(vmem(2)),
            scratch_shapes=[pltpu.VMEM((4, 64, channels), jnp.bfloat16)],
            compiler_params=limit,
            cost_estimate=small,
            name="arrange_clips",
        )(*layers)
        pieces = [keep]
        for flip in (1, 4, 5):
            pairs = [(i, i ^ flip) for i in range(plane)]
            pieces.append(lax.ppermute(send if flip % 2 else keep, plane_axes, pairs))
    with jax.named_scope("small_weights"):
        first = lax.axis_index("tm") // 2 * (4 * GROUP)
        weight_out = lax.dynamic_slice_in_dim(conv_out_weight, first, 4 * GROUP, axis=1)
        weight_out = weight_out.transpose(0, 2, 1).reshape(TAPS * TILE, 4 * GROUP)
        smem = pl.BlockSpec(memory_space=pltpu.SMEM)
        small_arrays = (group_gain, group_bias, out_bias, qkv_bias, q_gain, k_gain)
        scale, table = pl.pallas_call(
            table_kernel,
            out_shape=(
                jax.ShapeDtypeStruct((4 * GROUP, 2), jnp.float32),
                jax.ShapeDtypeStruct((56, LANES), jnp.float32),
            ),
            in_specs=[smem, smem, vmem(1)[0]] + [hbm] * 6,
            out_specs=tuple(vmem(2)),
            scratch_shapes=[pltpu.VMEM(array.shape, array.dtype) for array in small_arrays]
            + [pltpu.SemaphoreType.DMA((6,))],
            compiler_params=wide,
            cost_estimate=small,
            name="tables",
        )(frame_pos, row_pos, rope_freqs(), *small_arrays)
    with jax.named_scope("join_weights"):
        joined = pl.pallas_call(
            join_kernel,
            out_shape=jax.ShapeDtypeStruct((2 * GROUP * TAPS + 16, channels), jnp.bfloat16),
            in_specs=vmem(2),
            out_specs=vmem(1)[0],
            compiler_params=limit,
            cost_estimate=small,
            name="join_weights",
        )(weight, lines)
        joined_pair = lax.ppermute(joined, "tm", [(i, i ^ 1) for i in range(steps)])
    with jax.named_scope("merged_projection"):
        share = jnp.stack([joined[-16:], joined_pair[-16:]])
        shares = [share]
        for flip in (1, 4, 5):
            pairs = [(i, i ^ flip) for i in range(plane)]
            shares.append(lax.ppermute(share, plane_axes, pairs))

    flops = 2 * clips * steps * LANES * TAPS * TILE * (channels + 16)
    cost = pl.CostEstimate(flops=flops // 2, bytes_accessed=10**6, transcendentals=0)
    product = pltpu.VMEM((2 * TAPS * GROUP, steps * LANES), jnp.float32)
    normed, clip = pl.pallas_call(
        own_half_kernel,
        out_shape=(
            jax.ShapeDtypeStruct((2 * GROUP, steps * LANES), jnp.bfloat16),
            jax.ShapeDtypeStruct((plane, 64, channels), jnp.bfloat16),
        ),
        in_specs=vmem(6),
        out_specs=tuple(vmem(2)),
        scratch_shapes=[product],
        compiler_params=limit,
        cost_estimate=pl.CostEstimate(flops=4 * 10**10, bytes_accessed=10**6, transcendentals=0),
        name="own_channels",
    )(*pieces, joined, scale)
    partial = pl.pallas_call(
        conv_kernel,
        out_shape=jax.ShapeDtypeStruct((clips * plane, 8, LANES), jnp.float32),
        in_specs=vmem(5),
        out_specs=vmem(1)[0],
        scratch_shapes=[product, pltpu.VMEM((4 * GROUP, steps * LANES), jnp.bfloat16)],
        compiler_params=limit,
        cost_estimate=cost,
        name="convolutions",
    )(clip, normed, joined_pair, scale, weight_out)

    with jax.named_scope("sum_latents"):
        partials = lax.all_to_all(partial, ("dp",) + plane_axes, 0, 0, tiled=True)

    heads = qkv_weight.shape[1] // (3 * HD)
    frames = clip_inputs.shape[1]
    tokens = jax.ShapeDtypeStruct((clips * frames, 8, heads * HD), jnp.bfloat16)
    latents, query, key, value = pl.pallas_call(
        token_kernel,
        out_shape=(jax.ShapeDtypeStruct((1, 2, 2, 256), jnp.float32), tokens, tokens, tokens),
        in_specs=vmem(6),
        out_specs=tuple(vmem(4)),
        scratch_shapes=[pltpu.VMEM((plane, 8, 6 * HD), jnp.float32)],
        compiler_params=limit,
        cost_estimate=pl.CostEstimate(flops=10**8, bytes_accessed=10**6, transcendentals=0),
        name="tokens",
    )(
        partials,
        *shares,
        table,
    )
    full = (clips, frames, 1, 8, heads * HD)
    return latents, query.reshape(full), key.reshape(full), value.reshape(full)


def pick(mesh, *arrays):
    if one_group_each(mesh, arrays[0], arrays[1], arrays[4], arrays[8]):
        return grouped(*arrays)
    return shards(*arrays)


def solution(mesh):
    placed = (
        P("dp", "tm", "height", None, None),
        P(("tm", "height"), "dp"),
        P("dp"),
        P("dp"),
        P(None, "dp", None),
        P(),
        P(),
        P(),
        P(("tm", "height"), "dp"),
        P("dp"),
        P(),
        P(),
        P("tm"),
        P("height"),
    )
    return jax.shard_map(
        functools.partial(pick, mesh),
        mesh=mesh,
        in_specs=placed,
        out_specs=(
            P("dp", "tm", "height", None),
            P(None, "tm", "height", None, "dp"),
            P(None, "tm", "height", None, "dp"),
            P(None, "tm", "height", None, "dp"),
        ),
        check_vma=False,
    )
```

```python
import functools

import jax
import jax.numpy as jnp
import numpy as np
from jax import lax
from jax.experimental import pallas as pl
from jax.experimental.pallas import tpu as pltpu
from jax.sharding import PartitionSpec as P

HD = 128
GROUPS = 32
TAPS = 27


norm_eps = 1e-06
latent_scale = 0.476986
rope_base = 256.0
time_dims = 16
row_dims = 56


def from_behind(value, axis, steps):
    count = lax.axis_size(axis)
    first, last = (max(0, -steps), min(count, count - steps))
    return lax.ppermute(value, axis, [(source, source + steps) for source in range(first, last)])


def padded_2(block, sides, width):
    for axis, dim in sides:
        count = lax.axis_size(axis)
        forward = [(i, i + 1) for i in range(count - 1)]
        backward = [(target, source) for source, target in forward]
        low = lax.ppermute(
            lax.slice_in_dim(block, block.shape[dim] - width, None, axis=dim), axis, forward
        )
        high = lax.ppermute(lax.slice_in_dim(block, 0, width, axis=dim), axis, backward)
        block = jnp.concatenate([low, block, high], axis=dim)
    return block


def repeat_first(block):
    return jnp.concatenate([block[:, :1], block[:, :1]], axis=1)


def time_join(block, earlier):
    start = jnp.where(lax.axis_index("tm") == 0, repeat_first(block), earlier)
    return jnp.concatenate([start, block], axis=1)


def rows_finish(grown):
    place = lax.axis_index("height")
    top = jnp.where(place == 0, grown[:, :, 1:2], grown[:, :, :1])
    bottom = jnp.where(place == lax.axis_size("height") - 1, grown[:, :, -2:-1], grown[:, :, -1:])
    inner = jnp.concatenate([top, grown[:, :, 1:-1], bottom], axis=2)
    return jnp.pad(inner, ((0, 0), (0, 0), (0, 0), (1, 1), (0, 0)), mode="edge")


def edges_before(block):
    earlier = from_behind(block, "tm", 1)
    longer = time_join(block, earlier)
    return rows_finish(padded_2(longer, (("height", 2),), 1))


def edges_norm(block):
    earlier = from_behind(block, "tm", 1)
    longer = time_join(block, earlier)
    return rows_finish(padded_2(longer, (("height", 2),), 1))


def convolve(padded, weight):
    clips = padded.shape[0]
    frames = padded.shape[1] - 2
    rows = padded.shape[2] - 2
    cols = padded.shape[3] - 2
    total = jnp.zeros((clips * frames * rows * cols, weight.shape[2]), jnp.float32)
    for shift_t in range(3):
        for shift_r in range(3):
            for shift_c in range(3):
                window = padded[
                    :,
                    shift_t : shift_t + frames,
                    shift_r : shift_r + rows,
                    shift_c : shift_c + cols,
                ]
                window = window.reshape(-1, padded.shape[4])
                total = total + jnp.dot(
                    window,
                    weight[9 * shift_t + 3 * shift_r + shift_c],
                    preferred_element_type=jnp.float32,
                )
    return total.reshape(clips, frames, rows, cols, weight.shape[2])


def section_freqs(dims):
    return jnp.power(rope_base, -jnp.arange(0, dims, 2, dtype=jnp.float32) / dims)


def rope_angles(tpos, hpos, width):
    frames = tpos.shape[0]
    rows = hpos.shape[0]
    cols = jnp.arange(width, dtype=jnp.float32)
    part_t = tpos[:, None, None, None] * section_freqs(time_dims)
    part_h = hpos[None, :, None, None] * section_freqs(row_dims)
    part_w = cols[None, None, :, None] * section_freqs(row_dims)
    shape = (frames, rows, width)
    return jnp.concatenate(
        [
            jnp.broadcast_to(part_t, shape + (time_dims // 2,)),
            jnp.broadcast_to(part_h, shape + (row_dims // 2,)),
            jnp.broadcast_to(part_w, shape + (row_dims // 2,)),
        ],
        axis=-1,
    )


def rotate(vectors, angles):
    pairs = vectors.reshape(vectors.shape[:-1] + (vectors.shape[-1] // 2, 2))
    first = pairs[..., 0]
    second = pairs[..., 1]
    cosine = jnp.cos(angles)[..., None, :]
    sine = jnp.sin(angles)[..., None, :]
    turned = jnp.stack([first * cosine - second * sine, first * sine + second * cosine], axis=-1)
    return turned.reshape(vectors.shape)


def rms_scale(vectors, gain):
    return (
        vectors
        * lax.rsqrt(jnp.mean(vectors * vectors, axis=-1, keepdims=True) + norm_eps)
        * gain.astype(jnp.float32)
    )


def shards(
    clip_inputs,
    conv_in_weight,
    group_gain,
    group_bias,
    conv_out_weight,
    out_bias,
    patch_weight,
    patch_bias,
    qkv_weight,
    qkv_bias,
    q_gain,
    k_gain,
    frame_pos,
    row_pos,
):
    channels = clip_inputs.shape[4]
    frames = clip_inputs.shape[1]
    rows = clip_inputs.shape[2]
    cols = clip_inputs.shape[3]
    padded = lax.all_gather(edges_before(clip_inputs), "dp", axis=0, tiled=True)
    clips = padded.shape[0]
    weight_in = lax.all_gather(conv_in_weight, ("tm", "height"), axis=0, tiled=True).reshape(
        TAPS, channels, -1
    )
    hidden = convolve(padded, weight_in)
    block_width = hidden.shape[4]
    group_width = channels // GROUPS
    local_groups = block_width // group_width
    grouped = hidden.reshape(clips, -1, local_groups, group_width)
    sums_local = jnp.sum(grouped, axis=(1, 3))
    squares_local = jnp.sum(grouped * grouped, axis=(1, 3))
    sums_all, squares_all = lax.psum((sums_local, squares_local), ("tm", "height"))
    count = float(
        frames * lax.axis_size("tm") * rows * lax.axis_size("height") * cols * group_width
    )
    mean = sums_all / count
    var = squares_all / count - mean * mean
    scaled = (grouped - mean[:, None, :, None]) * lax.rsqrt(var + norm_eps)[:, None, :, None]
    scaled = scaled.reshape(hidden.shape) * group_gain.astype(jnp.float32) + group_bias.astype(
        jnp.float32
    )
    normed = jax.nn.silu(scaled).astype(jnp.bfloat16)
    partial_latent = convolve(edges_norm(normed), conv_out_weight)
    own_sum = lax.psum_scatter(partial_latent, "dp", scatter_dimension=0, tiled=True)
    own_latent = (own_sum + out_bias) * latent_scale
    every_latent = lax.all_gather(own_latent.astype(jnp.bfloat16), "dp", axis=0, tiled=True)
    latent_dims = every_latent.shape[4]
    latents = own_latent.reshape(1, frames, rows, cols * latent_dims)
    tok_rows = rows // 2
    tok_cols = cols // 2
    patches = every_latent.reshape(clips, frames, tok_rows, 2, tok_cols, 2, latent_dims)
    patches = patches.transpose(0, 1, 2, 4, 3, 5, 6).reshape(-1, 4 * latent_dims)
    embedded = (
        jnp.dot(patches, patch_weight, preferred_element_type=jnp.float32)
        + patch_bias.astype(jnp.float32)
    ).astype(jnp.bfloat16)
    projected = jnp.dot(
        embedded,
        lax.all_gather(qkv_weight, ("tm", "height"), axis=0, tiled=True),
        preferred_element_type=jnp.float32,
    )
    projected = projected + qkv_bias.astype(jnp.float32)
    local_heads = qkv_weight.shape[1] // (3 * HD)
    projected = projected.reshape(clips, frames, tok_rows, tok_cols, local_heads, 3, HD)
    angles = rope_angles(frame_pos.astype(jnp.float32), row_pos.astype(jnp.float32), tok_cols)
    query = rotate(rms_scale(projected[..., 0, :], q_gain), angles)
    key = rotate(rms_scale(projected[..., 1, :], k_gain), angles)
    value = projected[..., 2, :]
    merged = (clips, frames, tok_rows, tok_cols, local_heads * HD)
    return (
        latents,
        query.reshape(merged).astype(jnp.bfloat16),
        key.reshape(merged).astype(jnp.bfloat16),
        value.reshape(merged).astype(jnp.bfloat16),
    )


LANES = 128
TILE = 16
GROUP = 16


def one_group_each(mesh, clip_inputs, conv_in_weight, conv_out_weight, qkv_weight):
    plane = mesh.shape["tm"] * mesh.shape["height"]
    return (
        clip_inputs.shape[:4] == (1, 2, 2, 16)
        and mesh.shape["height"] == 2
        and mesh.shape["tm"] == 4
        and mesh.shape["dp"] == 4
        and conv_in_weight.shape[1] == plane * GROUP
        and clip_inputs.shape[4] == GROUP * GROUPS
        and conv_out_weight.shape[2] == TILE
        and qkv_weight.shape[1] == 6 * HD
    )


def lane_shifts(lane):
    col = lane % 16
    row = lane // 16 % 2
    half = lane // 64

    def cols(left, mid, right):
        left = jnp.where(col == 0, left, pltpu.roll(left, 1, 1))
        right = jnp.where(col == 15, right, pltpu.roll(right, LANES - 1, 1))
        return mid + left + right

    def rows(up, mid, down):
        up = jnp.where(
            row == 1, pltpu.roll(up, 16, 1), jnp.where(half == 1, pltpu.roll(up, 48, 1), up)
        )
        down = jnp.where(
            row == 0,
            pltpu.roll(down, LANES - 16, 1),
            jnp.where(half == 0, pltpu.roll(down, LANES - 48, 1), down),
        )
        return mid + up + down

    return cols, rows


def tap_sums(y_ref, top, tiles):
    lane = lax.broadcasted_iota(jnp.int32, (TILE, LANES), 1)
    second = lane // 32 % 2 == 1
    cols, rows = lane_shifts(lane)
    sums = []
    before = None
    for tile in range(tiles):

        def part(tap):
            at = top + tap * TILE
            return y_ref[at : at + TILE, tile * LANES : (tile + 1) * LANES]

        oldest, older, now = (
            rows(*(cols(*(part(9 * i + 3 * j + l) for l in range(3))) for j in range(3)))
            for i in range(3)
        )
        turned = pltpu.roll(older, 32, 1)
        if before is None:
            start = jnp.where(second, pltpu.roll(oldest, 32, 1), oldest)
            total = now + jnp.where(second, turned, older) + start
        else:
            total = now + jnp.where(second, turned, pltpu.roll(before[1], 96, 1)) + before[0]
        before = (oldest, older)
        sums.append(total)
    return sums


def pack_kernel(
    w_hbm, qkv_hbm, patch_hbm, patch_bias_hbm, out_hbm, lines_ref,
    w_ref, qkv_ref, patch_ref, patch_bias_ref, rows_ref, out_ref, sems,
):
    plane, channels, width = out_ref.shape
    depth = w_ref.shape[0]
    rows = qkv_ref.shape[0]
    place = lax.axis_index("tm") * lax.axis_size("height") + lax.axis_index("height")
    at = pl.ds(pl.multiple_of(place * rows, LANES), rows)
    loads = [
        pltpu.make_async_copy(w_hbm, w_ref, sems.at[0]),
        pltpu.make_async_copy(qkv_hbm, qkv_ref, sems.at[1]),
        pltpu.make_async_copy(patch_hbm.at[:, at], patch_ref, sems.at[2]),
        pltpu.make_async_copy(patch_bias_hbm, patch_bias_ref, sems.at[3]),
    ]
    for load in loads:
        load.start()
    whole = depth // LANES * LANES
    loads[0].wait()
    turned = w_ref[...].T
    for to in range(plane):
        first = to // 2 * channels
        out_ref[to, :, :whole] = turned[first : first + channels, :whole]
    body = slice(0, whole)
    tail = slice(whole, width)
    stores = [
        pltpu.make_async_copy(out_ref.at[:, :, part], out_hbm.at[:, :, part], sems.at[4 + index])
        for index, part in enumerate((body, tail))
    ]
    stores[0].start()
    for load in loads[1:]:
        load.wait()
    merged = jnp.dot(patch_ref[...], qkv_ref[...], preferred_element_type=jnp.float32)
    lane = lax.broadcasted_iota(jnp.int32, (8, LANES), 1)
    for to in range(plane):
        first = to // 2 * channels
        mine = [merged[8 * to : 8 * to + 8, q * LANES : (q + 1) * LANES] for q in range(6)]
        upper = [pltpu.roll(mine[4], 64, 1), mine[4], pltpu.roll(mine[5], 64, 1), mine[5]]
        upper = jnp.concatenate(upper, axis=0)[:, 64:].astype(jnp.bfloat16)
        lower = turned[first : first + channels, whole:]
        out_ref[to, :, whole : whole + LANES] = jnp.concatenate([lower, upper], axis=1)
        out_ref[to, :, whole + LANES :] = jnp.concatenate(mine[:4], axis=0).astype(jnp.bfloat16)
    stores[1].start()
    rows_ref[...] = patch_bias_ref[...].astype(jnp.float32).reshape(rows_ref.shape)
    count = rows // LANES
    bias = [rows_ref[pl.ds(count * place + part, 1), :] for part in range(count)]
    bias = jnp.broadcast_to(jnp.concatenate(bias, axis=1), (8, rows)).astype(jnp.bfloat16)
    bias = jnp.dot(bias, qkv_ref[...], preferred_element_type=jnp.float32)
    line = lax.broadcasted_iota(jnp.int32, (8, LANES), 0)
    lines = jnp.zeros((8, LANES), jnp.float32)
    for part in range(bias.shape[1] // LANES):
        lines = jnp.where(line == part, bias[:, part * LANES : (part + 1) * LANES], lines)
    lines_ref[...] = lines
    for store in stores:
        store.wait()


def column(row_ref, first, size):
    length = row_ref.shape[0]
    row = row_ref[...].astype(jnp.float32).reshape(1, length)
    line = lax.broadcasted_iota(jnp.int32, (size, length), 0)
    lane = lax.broadcasted_iota(jnp.int32, (size, length), 1)
    picked = jnp.where(lane == line + first, jnp.broadcast_to(row, (size, length)), 0.0)
    return jnp.sum(picked, axis=1, keepdims=True)


def table_kernel(
    frame_ref, row_pos_ref, freq_ref, gain_hbm, bias_hbm, out_bias_hbm, qkv_hbm, q_hbm, k_hbm,
    scale_ref, table_ref,
    gain_v, bias_v, out_bias_v, qkv_v, q_v, k_v, sems,
):
    pairs = (
        (gain_hbm, gain_v), (bias_hbm, bias_v), (out_bias_hbm, out_bias_v),
        (qkv_hbm, qkv_v), (q_hbm, q_v), (k_hbm, k_v),
    )
    loads = [
        pltpu.make_async_copy(source, to, sems.at[index])
        for index, (source, to) in enumerate(pairs)
    ]
    for load in loads:
        load.start()
    shape = (TILE, LANES)
    line = lax.broadcasted_iota(jnp.int32, shape, 0)
    lane = lax.broadcasted_iota(jnp.int32, shape, 1)
    frame = jnp.where(line // 8 == 0, frame_ref[0], frame_ref[1]).astype(jnp.float32)
    row = jnp.broadcast_to(row_pos_ref[0], shape).astype(jnp.float32)
    spot = jnp.where(lane < 72, row, (line % 8).astype(jnp.float32))
    angles = jnp.where(lane < 16, frame, spot) * freq_ref[...]
    table_ref[:16] = jnp.cos(angles)
    sine = jnp.sin(angles)
    table_ref[16:32] = jnp.where(lane % 2 == 0, -sine, sine)
    for load in loads:
        load.wait()
    first = lax.axis_index("tm") // 2 * (4 * GROUP)
    scale_ref[:, 0:1] = column(gain_v, first, 4 * GROUP)
    scale_ref[:, 1:2] = column(bias_v, first, 4 * GROUP)
    table_ref[32:48] = jnp.broadcast_to(column(out_bias_v, 0, TILE), shape)
    table_ref[48:49] = q_v[...].astype(jnp.float32).reshape(1, HD)
    table_ref[49:50] = k_v[...].astype(jnp.float32).reshape(1, HD)
    table_ref[50:56] = qkv_v[...].astype(jnp.float32).reshape(6, LANES)


def arrange_kernel(*refs):
    pieces, (table_ref, keep_ref, send_ref, kept_table_ref, all_ref) = refs[:4], refs[4:]
    kept_table_ref[...] = table_ref[...]
    side = lax.axis_index("height")
    layer = lax.axis_index("dp")
    for step, piece in enumerate(pieces):
        all_ref[(layer + 4 - step) % 4] = piece[...]
    for core in range(2):
        keep_ref[core] = all_ref[2 * side + core]
        send_ref[core] = all_ref[2 - 2 * side + core]


def join_kernel(w_ref, lines_ref, wt_ref):
    plane, width, lanes = w_ref.shape
    channels = wt_ref.shape[1]
    depth = TAPS * channels // plane
    for group in range(width // GROUP):
        for tap in range(TAPS):
            start = tap * channels
            end = start + channels
            at = (group * TAPS + tap) * GROUP
            while start < end:
                source = start // depth
                stop = min(end, (source + 1) * depth)
                wt_ref[
                    at : at + GROUP, start - tap * channels : stop - tap * channels
                ] = w_ref[
                    source,
                    group * GROUP : (group + 1) * GROUP,
                    start - source * depth : stop - source * depth,
                ]
                start = stop
    total = w_ref[0, :, lanes - 2 * LANES :].astype(jnp.float32)
    for source in range(1, plane):
        total = total + w_ref[source, :, lanes - 2 * LANES :].astype(jnp.float32)
    low = lax.broadcasted_iota(jnp.int32, (8, LANES), 1) < 64
    parts = [total[8 * q : 8 * q + 8, LANES:] for q in range(4)]
    for q in range(2):
        one = total[16 * q : 16 * q + 8, :LANES]
        two = total[16 * q + 8 : 16 * q + 16, :LANES]
        parts.append(jnp.where(low, pltpu.roll(one, 64, 1), two))
    parts += [lines_ref[...], jnp.zeros((8, LANES), jnp.float32)]
    share = jnp.concatenate(
        [jnp.concatenate(parts[:4], axis=1), jnp.concatenate(parts[4:], axis=1)], axis=0
    )
    wt_ref[width * TAPS :] = share.astype(jnp.bfloat16)


def place_clip(pieces, x_ref):
    place = lax.axis_index("tm") // 2 * 4 + lax.axis_index("height")
    for flip, piece in zip((0, 1, 4, 5), pieces):
        for core in range(2):
            x_ref[(place ^ flip) + 2 * core] = piece[core]


def normed_half(x_ref, wt_ref, y_ref, scale_ref, half):
    channels = x_ref.shape[2]
    tiles = x_ref.shape[0] // 2
    taps = TAPS * GROUP
    count = float(tiles * LANES * GROUP)
    y_ref[...] = lax.dot_general(
        wt_ref[: 2 * taps],
        x_ref[...].reshape(tiles * LANES, channels),
        (((1,), (1,)), ((), ())),
        preferred_element_type=jnp.float32,
    )
    normed = []
    for group in range(2):
        hidden = tap_sums(y_ref, group * taps, tiles)
        at = pl.ds(pl.multiple_of((2 * half + group) * GROUP, GROUP), GROUP)
        mean = jnp.sum(sum(hidden), keepdims=True) / count
        square = jnp.sum(sum(part * part for part in hidden), keepdims=True) / count
        scale = lax.rsqrt(square - mean * mean + norm_eps)
        parts = []
        for part in hidden:
            scaled = (part - mean) * scale * scale_ref[at, 0:1] + scale_ref[at, 1:2]
            parts.append((scaled / (1.0 + jnp.exp(-scaled))).astype(jnp.bfloat16))
        normed.append(jnp.concatenate(parts, axis=1))
    return jnp.concatenate(normed, axis=0)


def own_half_kernel(
    x0_ref, x1_ref, x2_ref, x3_ref, wt_ref, scale_ref, out_ref, x_ref, y_ref
):
    place_clip((x0_ref, x1_ref, x2_ref, x3_ref), x_ref)
    half = lax.axis_index("tm") % 2
    out_ref[...] = normed_half(x_ref, wt_ref, y_ref, scale_ref, half)


def conv_kernel(
    x_ref, normed_ref, wt_ref, scale_ref, w2_ref, keep_ref, send_ref, y_ref, n_ref, out_ref
):
    tiles = x_ref.shape[0] // 2
    half = lax.axis_index("tm") % 2
    n_ref[pl.ds(pl.multiple_of(half * 2 * GROUP, 2 * GROUP), 2 * GROUP)] = normed_ref[...]
    other = normed_half(x_ref, wt_ref, y_ref, scale_ref, 1 - half)
    n_ref[pl.ds(pl.multiple_of((1 - half) * 2 * GROUP, 2 * GROUP), 2 * GROUP)] = other
    y_ref[: TAPS * TILE] = jnp.dot(w2_ref[...], n_ref[...], preferred_element_type=jnp.float32)
    high = lax.axis_index("tm") // 2
    for tile, part in enumerate(tap_sums(y_ref, 0, tiles)):
        out_ref[high ^ (tile // 2), tile % 2] = part
    keep_ref[...] = out_ref[0]
    send_ref[...] = out_ref[1]


def spread_kernel(keep_ref, other_ref, *out_refs):
    core = lax.axis_index("tm") % 2
    side = lax.axis_index("height")
    low = lax.broadcasted_iota(jnp.int32, (8, LANES), 1) < 64
    for flip, out_ref in enumerate(out_refs):
        part = keep_ref[core ^ (flip // 2)] + other_ref[core ^ (flip // 2)]
        turned = pltpu.roll(part, 64, 1)
        near = jnp.where(low, part[:8], turned[8:])
        far = jnp.where(low, turned[:8], part[8:])
        out_ref[...] = jnp.where((side ^ (flip % 2)) == 0, near, far)


def clips_kernel(p0_ref, p1_ref, p2_ref, p3_ref, out_ref, all_ref):
    core = lax.axis_index("tm") % 2
    side = lax.axis_index("height")
    low = lax.broadcasted_iota(jnp.int32, (8, LANES), 1) < 64
    for flip, ref in enumerate((p0_ref, p1_ref, p2_ref, p3_ref)):
        all_ref[2 * (side ^ (flip % 2)) + (core ^ (flip // 2))] = ref[...]
    for pair in range(2):
        one, two = all_ref[2 * pair], all_ref[2 * pair + 1]
        out_ref[pair, :8] = jnp.where(low, one, pltpu.roll(two, 64, 1))
        out_ref[pair, 8:] = jnp.where(low, pltpu.roll(one, 64, 1), two)


def token_kernel(
    p0_ref, p1_ref, p2_ref, p3_ref, m0_ref, m1_ref, m2_ref, m3_ref, table_ref,
    lat_ref, q_ref, k_ref, v_ref, m_ref,
):
    spot = lax.axis_index("tm") * 2 + lax.axis_index("height")
    lines = jnp.zeros((8, LANES), jnp.float32)
    for flip, ref in ((0, m0_ref), (1, m1_ref), (4, m2_ref), (5, m3_ref)):
        for core in range(2):
            share = ref[core].astype(jnp.float32)
            at = spot ^ flip ^ (2 * core)
            m_ref[at, :, : 4 * LANES] = share[:8]
            m_ref[at, :, 4 * LANES :] = share[8:, : 2 * LANES]
            lines = lines + share[8:, 2 * LANES : 3 * LANES]
    total = p0_ref[...] + p1_ref[...] + p2_ref[...] + p3_ref[...]
    total = jnp.concatenate([total[0], total[1]], axis=1)
    lat = (total + table_ref[32:48, :1]) * latent_scale
    clips = lat.shape[1] // 64
    tokens = clips * 16
    place = lax.axis_index("dp")
    own = lat[:, :LANES]
    for pair in range(1, clips // 2):
        own = jnp.where(place // 2 == pair, lat[:, pair * LANES : (pair + 1) * LANES], own)
    own = jnp.where(place % 2 == 1, pltpu.roll(own, 64, 1), own)
    turned = own.T[:64]
    wide = jnp.concatenate([turned] * 16, axis=1)
    spot = lax.broadcasted_iota(jnp.int32, wide.shape, 0) % 16
    spread = lax.broadcasted_iota(jnp.int32, wide.shape, 1) // 16
    merged = jnp.sum(jnp.where(spot == spread, wide, 0.0).reshape(4, 16, 256), axis=1)
    lat_ref[0, 0] = merged[:2]
    lat_ref[0, 1] = merged[2:]

    lat_bf = lat.astype(jnp.bfloat16)
    token = lax.broadcasted_iota(jnp.int32, (tokens, clips * 64), 0)
    lane = lax.broadcasted_iota(jnp.int32, (tokens, clips * 64), 1)
    first = token // 8 * 32 + token % 8 * 2
    heads = q_ref.shape[2] // HD
    lines = lines[: 3 * heads] + table_ref[50:56]
    projected = jnp.concatenate([lines[part : part + 1] for part in range(3 * heads)], axis=1)
    merged = m_ref[...].reshape(64, 3 * HD * heads).astype(jnp.bfloat16)
    for a in range(2):
        for e in range(2):
            chosen = jnp.where(lane == first + (16 * a + e), 1.0, 0.0).astype(jnp.bfloat16)
            patch = lax.dot_general(
                chosen, lat_bf, (((1,), (1,)), ((), ())), preferred_element_type=jnp.float32
            ).astype(jnp.bfloat16)
            weight = merged[(2 * a + e) * TILE : (2 * a + e + 1) * TILE]
            projected = projected + jnp.dot(patch, weight, preferred_element_type=jnp.float32)

    even = lax.broadcasted_iota(jnp.int32, (tokens, HD), 1) % 2 == 0
    cosine = jnp.concatenate([table_ref[:16]] * clips, axis=0)
    sine = jnp.concatenate([table_ref[16:32]] * clips, axis=0)

    def turn(vectors, gain):
        square = jnp.mean(vectors * vectors, axis=-1, keepdims=True)
        vectors = vectors * lax.rsqrt(square + norm_eps) * gain
        swapped = jnp.where(even, pltpu.roll(vectors, HD - 1, 1), pltpu.roll(vectors, 1, 1))
        return vectors * cosine + swapped * sine

    def keep(ref, head, value):
        value = value.reshape(tokens // 8, 8, HD).astype(jnp.bfloat16)
        ref[:, :, head * HD : (head + 1) * HD] = value

    for head in range(heads):
        at = 3 * HD * head
        keep(q_ref, head, turn(projected[:, at : at + HD], table_ref[48:49]))
        keep(k_ref, head, turn(projected[:, at + HD : at + 2 * HD], table_ref[49:50]))
        keep(v_ref, head, projected[:, at + 2 * HD : at + 3 * HD])


def rope_freqs():
    freqs = []
    for dims in (time_dims, row_dims, row_dims):
        freqs.append(rope_base ** (-np.arange(0, dims, 2, dtype=np.float64) / dims))
    return np.repeat(np.concatenate(freqs), 2)[None].astype(np.float32)


def vmem(count):
    return [pl.BlockSpec(memory_space=pltpu.VMEM)] * count


def grouped(
    clip_inputs,
    conv_in_weight,
    group_gain,
    group_bias,
    conv_out_weight,
    out_bias,
    patch_weight,
    patch_bias,
    qkv_weight,
    qkv_bias,
    q_gain,
    k_gain,
    frame_pos,
    row_pos,
):
    plane_axes = ("tm", "height")
    clips = lax.axis_size("dp")
    steps = lax.axis_size("tm")
    plane = steps * lax.axis_size("height")
    channels = clip_inputs.shape[4]
    depth = conv_in_weight.shape[0]

    width = -(-depth // LANES) * LANES + LANES
    hbm = pl.BlockSpec(memory_space=pltpu.HBM)
    wide = pltpu.CompilerParams(vmem_limit_bytes=60 * 1024 * 1024)
    limit = pltpu.CompilerParams(vmem_limit_bytes=32 * 1024 * 1024)
    small = pl.CostEstimate(flops=10**6, bytes_accessed=10**6, transcendentals=0)
    with jax.named_scope("weight_by_group"):
        packed, lines = pl.pallas_call(
            pack_kernel,
            out_shape=(
                jax.ShapeDtypeStruct((plane, 2 * GROUP, width), jnp.bfloat16),
                jax.ShapeDtypeStruct((8, LANES), jnp.float32),
            ),
            in_specs=[hbm] * 4,
            out_specs=(hbm, vmem(1)[0]),
            scratch_shapes=[
                pltpu.VMEM(conv_in_weight.shape, jnp.bfloat16),
                pltpu.VMEM(qkv_weight.shape, jnp.bfloat16),
                pltpu.VMEM((patch_weight.shape[0], qkv_weight.shape[0]), jnp.bfloat16),
                pltpu.VMEM(patch_bias.shape, jnp.bfloat16),
                pltpu.VMEM((patch_bias.shape[0] // LANES, LANES), jnp.float32),
                pltpu.VMEM((plane, 2 * GROUP, width), jnp.bfloat16),
                pltpu.SemaphoreType.DMA((6,)),
            ],
            compiler_params=wide,
            cost_estimate=pl.CostEstimate(flops=10**8, bytes_accessed=10**6, transcendentals=0),
            name="pack_weights",
        )(conv_in_weight, qkv_weight, patch_weight, patch_bias)
        weight = lax.all_to_all(packed, plane_axes, 0, 0, tiled=True)
    with jax.named_scope("tables"):
        smem = pl.BlockSpec(memory_space=pltpu.SMEM)
        small_arrays = (group_gain, group_bias, out_bias, qkv_bias, q_gain, k_gain)
        scale, table = pl.pallas_call(
            table_kernel,
            out_shape=(
                jax.ShapeDtypeStruct((4 * GROUP, 2), jnp.float32),
                jax.ShapeDtypeStruct((56, LANES), jnp.float32),
            ),
            in_specs=[smem, smem, vmem(1)[0]] + [hbm] * 6,
            out_specs=tuple(vmem(2)),
            scratch_shapes=[pltpu.VMEM(array.shape, array.dtype) for array in small_arrays]
            + [pltpu.SemaphoreType.DMA((6,))],
            compiler_params=wide,
            cost_estimate=small,
            name="tables",
        )(frame_pos, row_pos, rope_freqs(), *small_arrays)
    with jax.named_scope("gather_clips"):
        own = clip_inputs.reshape(64, channels)
        layers = []
        for step in range(clips):
            pairs = []
            for layer in range(clips):
                for tm in range(steps):
                    to = (layer // 2 * 2 + tm % 2 + step) % clips
                    pairs.append((layer * steps + tm, to * steps + tm // 2 * 2 + layer % 2))
            layers.append(lax.ppermute(own, ("dp", "tm"), pairs))
    with jax.named_scope("spread_clips"):
        keep, send, table = pl.pallas_call(
            arrange_kernel,
            out_shape=(jax.ShapeDtypeStruct((2, 64, channels), jnp.bfloat16),) * 2
            + (jax.ShapeDtypeStruct(table.shape, table.dtype),),
            in_specs=vmem(5),
            out_specs=tuple(vmem(3)),
            scratch_shapes=[pltpu.VMEM((4, 64, channels), jnp.bfloat16)],
            compiler_params=limit,
            cost_estimate=small,
            name="arrange_clips",
        )(*layers, table)
        pieces = [keep]
        for flip in (1, 4, 5):
            pairs = [(i, i ^ flip) for i in range(plane)]
            pieces.append(lax.ppermute(send if flip % 2 else keep, plane_axes, pairs))
    with jax.named_scope("small_weights"):
        first = lax.axis_index("tm") // 2 * (4 * GROUP)
        weight_out = lax.dynamic_slice_in_dim(conv_out_weight, first, 4 * GROUP, axis=1)
        weight_out = weight_out.transpose(0, 2, 1).reshape(TAPS * TILE, 4 * GROUP)
    with jax.named_scope("join_weights"):
        joined = pl.pallas_call(
            join_kernel,
            out_shape=jax.ShapeDtypeStruct((2 * GROUP * TAPS + 16, channels), jnp.bfloat16),
            in_specs=vmem(2),
            out_specs=vmem(1)[0],
            compiler_params=limit,
            cost_estimate=small,
            name="join_weights",
        )(weight, lines)
        joined_pair = lax.ppermute(joined, "tm", [(i, i ^ 1) for i in range(steps)])
    with jax.named_scope("merged_projection"):
        share = jnp.stack([joined[-16:], joined_pair[-16:]])
        shares = [share]
        for flip in (1, 4, 5):
            pairs = [(i, i ^ flip) for i in range(plane)]
            shares.append(lax.ppermute(share, plane_axes, pairs))

    flops = 2 * clips * steps * LANES * TAPS * TILE * (channels + 16)
    cost = pl.CostEstimate(flops=flops // 2, bytes_accessed=10**6, transcendentals=0)
    product = pltpu.VMEM((2 * TAPS * GROUP, steps * LANES), jnp.float32)
    normed, clip = pl.pallas_call(
        own_half_kernel,
        out_shape=(
            jax.ShapeDtypeStruct((2 * GROUP, steps * LANES), jnp.bfloat16),
            jax.ShapeDtypeStruct((plane, 64, channels), jnp.bfloat16),
        ),
        in_specs=vmem(6),
        out_specs=tuple(vmem(2)),
        scratch_shapes=[product],
        compiler_params=limit,
        cost_estimate=pl.CostEstimate(flops=4 * 10**10, bytes_accessed=10**6, transcendentals=0),
        name="own_channels",
    )(*pieces, joined, scale)
    kept, sent = pl.pallas_call(
        conv_kernel,
        out_shape=(jax.ShapeDtypeStruct((2, TILE, LANES), jnp.float32),) * 2,
        in_specs=vmem(5),
        out_specs=tuple(vmem(2)),
        scratch_shapes=[
            product,
            pltpu.VMEM((4 * GROUP, steps * LANES), jnp.bfloat16),
            pltpu.VMEM((2, 2, TILE, LANES), jnp.float32),
        ],
        compiler_params=limit,
        cost_estimate=cost,
        name="convolutions",
    )(clip, normed, joined_pair, scale, weight_out)

    with jax.named_scope("sum_latents"):
        other = lax.ppermute(sent, "tm", [(i, i ^ 2) for i in range(steps)])
        parts = pl.pallas_call(
            spread_kernel,
            out_shape=(jax.ShapeDtypeStruct((8, LANES), jnp.float32),) * 4,
            in_specs=vmem(2),
            out_specs=tuple(vmem(4)),
            compiler_params=limit,
            cost_estimate=small,
            name="spread_latents",
        )(kept, other)
        parts = [parts[0]] + [
            lax.ppermute(parts[flip], plane_axes, [(i, i ^ flip) for i in range(plane)])
            for flip in (1, 2, 3)
        ]
        here = pl.pallas_call(
            clips_kernel,
            out_shape=jax.ShapeDtypeStruct((2, TILE, LANES), jnp.float32),
            in_specs=vmem(4),
            out_specs=vmem(1)[0],
            scratch_shapes=[pltpu.VMEM((4, 8, LANES), jnp.float32)],
            compiler_params=limit,
            cost_estimate=small,
            name="clip_latents",
        )(*parts)
        sums = [here] + [
            lax.ppermute(here, "dp", [(i, (i + step) % clips) for i in range(clips)])
            for step in range(1, clips)
        ]

    heads = qkv_weight.shape[1] // (3 * HD)
    frames = clip_inputs.shape[1]
    tokens = jax.ShapeDtypeStruct((clips * frames, 8, heads * HD), jnp.bfloat16)
    latents, query, key, value = pl.pallas_call(
        token_kernel,
        out_shape=(jax.ShapeDtypeStruct((1, 2, 2, 256), jnp.float32), tokens, tokens, tokens),
        in_specs=vmem(9),
        out_specs=tuple(vmem(4)),
        scratch_shapes=[pltpu.VMEM((plane, 8, 6 * HD), jnp.float32)],
        compiler_params=limit,
        cost_estimate=pl.CostEstimate(flops=10**8, bytes_accessed=10**6, transcendentals=0),
        name="tokens",
    )(
        *sums,
        *shares,
        table,
    )
    full = (clips, frames, 1, 8, heads * HD)
    return latents, query.reshape(full), key.reshape(full), value.reshape(full)


def pick(mesh, *arrays):
    if one_group_each(mesh, arrays[0], arrays[1], arrays[4], arrays[8]):
        return grouped(*arrays)
    return shards(*arrays)


def solution(mesh):
    placed = (
        P("dp", "tm", "height", None, None),
        P(("tm", "height"), "dp"),
        P("dp"),
        P("dp"),
        P(None, "dp", None),
        P(),
        P(),
        P(),
        P(("tm", "height"), "dp"),
        P("dp"),
        P(),
        P(),
        P("tm"),
        P("height"),
    )
    return jax.shard_map(
        functools.partial(pick, mesh),
        mesh=mesh,
        in_specs=placed,
        out_specs=(
            P("dp", "tm", "height", None),
            P(None, "tm", "height", None, "dp"),
            P(None, "tm", "height", None, "dp"),
            P(None, "tm", "height", None, "dp"),
        ),
        check_vma=False,
    )
```

```python
import functools

import jax
import jax.numpy as jnp
import numpy as np
from jax import lax
from jax.experimental import pallas as pl
from jax.experimental.pallas import tpu as pltpu
from jax.sharding import PartitionSpec as P

HD = 128
GROUPS = 32
TAPS = 27


norm_eps = 1e-06
latent_scale = 0.476986
rope_base = 256.0
time_dims = 16
row_dims = 56


def from_behind(value, axis, steps):
    count = lax.axis_size(axis)
    first, last = (max(0, -steps), min(count, count - steps))
    return lax.ppermute(value, axis, [(source, source + steps) for source in range(first, last)])


def padded_2(block, sides, width):
    for axis, dim in sides:
        count = lax.axis_size(axis)
        forward = [(i, i + 1) for i in range(count - 1)]
        backward = [(target, source) for source, target in forward]
        low = lax.ppermute(
            lax.slice_in_dim(block, block.shape[dim] - width, None, axis=dim), axis, forward
        )
        high = lax.ppermute(lax.slice_in_dim(block, 0, width, axis=dim), axis, backward)
        block = jnp.concatenate([low, block, high], axis=dim)
    return block


def repeat_first(block):
    return jnp.concatenate([block[:, :1], block[:, :1]], axis=1)


def time_join(block, earlier):
    start = jnp.where(lax.axis_index("tm") == 0, repeat_first(block), earlier)
    return jnp.concatenate([start, block], axis=1)


def rows_finish(grown):
    place = lax.axis_index("height")
    top = jnp.where(place == 0, grown[:, :, 1:2], grown[:, :, :1])
    bottom = jnp.where(place == lax.axis_size("height") - 1, grown[:, :, -2:-1], grown[:, :, -1:])
    inner = jnp.concatenate([top, grown[:, :, 1:-1], bottom], axis=2)
    return jnp.pad(inner, ((0, 0), (0, 0), (0, 0), (1, 1), (0, 0)), mode="edge")


def edges_before(block):
    earlier = from_behind(block, "tm", 1)
    longer = time_join(block, earlier)
    return rows_finish(padded_2(longer, (("height", 2),), 1))


def edges_norm(block):
    earlier = from_behind(block, "tm", 1)
    longer = time_join(block, earlier)
    return rows_finish(padded_2(longer, (("height", 2),), 1))


def convolve(padded, weight):
    clips = padded.shape[0]
    frames = padded.shape[1] - 2
    rows = padded.shape[2] - 2
    cols = padded.shape[3] - 2
    total = jnp.zeros((clips * frames * rows * cols, weight.shape[2]), jnp.float32)
    for shift_t in range(3):
        for shift_r in range(3):
            for shift_c in range(3):
                window = padded[
                    :,
                    shift_t : shift_t + frames,
                    shift_r : shift_r + rows,
                    shift_c : shift_c + cols,
                ]
                window = window.reshape(-1, padded.shape[4])
                total = total + jnp.dot(
                    window,
                    weight[9 * shift_t + 3 * shift_r + shift_c],
                    preferred_element_type=jnp.float32,
                )
    return total.reshape(clips, frames, rows, cols, weight.shape[2])


def section_freqs(dims):
    return jnp.power(rope_base, -jnp.arange(0, dims, 2, dtype=jnp.float32) / dims)


def rope_angles(tpos, hpos, width):
    frames = tpos.shape[0]
    rows = hpos.shape[0]
    cols = jnp.arange(width, dtype=jnp.float32)
    part_t = tpos[:, None, None, None] * section_freqs(time_dims)
    part_h = hpos[None, :, None, None] * section_freqs(row_dims)
    part_w = cols[None, None, :, None] * section_freqs(row_dims)
    shape = (frames, rows, width)
    return jnp.concatenate(
        [
            jnp.broadcast_to(part_t, shape + (time_dims // 2,)),
            jnp.broadcast_to(part_h, shape + (row_dims // 2,)),
            jnp.broadcast_to(part_w, shape + (row_dims // 2,)),
        ],
        axis=-1,
    )


def rotate(vectors, angles):
    pairs = vectors.reshape(vectors.shape[:-1] + (vectors.shape[-1] // 2, 2))
    first = pairs[..., 0]
    second = pairs[..., 1]
    cosine = jnp.cos(angles)[..., None, :]
    sine = jnp.sin(angles)[..., None, :]
    turned = jnp.stack([first * cosine - second * sine, first * sine + second * cosine], axis=-1)
    return turned.reshape(vectors.shape)


def rms_scale(vectors, gain):
    return (
        vectors
        * lax.rsqrt(jnp.mean(vectors * vectors, axis=-1, keepdims=True) + norm_eps)
        * gain.astype(jnp.float32)
    )


def shards(
    clip_inputs,
    conv_in_weight,
    group_gain,
    group_bias,
    conv_out_weight,
    out_bias,
    patch_weight,
    patch_bias,
    qkv_weight,
    qkv_bias,
    q_gain,
    k_gain,
    frame_pos,
    row_pos,
):
    channels = clip_inputs.shape[4]
    frames = clip_inputs.shape[1]
    rows = clip_inputs.shape[2]
    cols = clip_inputs.shape[3]
    padded = lax.all_gather(edges_before(clip_inputs), "dp", axis=0, tiled=True)
    clips = padded.shape[0]
    weight_in = lax.all_gather(conv_in_weight, ("tm", "height"), axis=0, tiled=True).reshape(
        TAPS, channels, -1
    )
    hidden = convolve(padded, weight_in)
    block_width = hidden.shape[4]
    group_width = channels // GROUPS
    local_groups = block_width // group_width
    grouped = hidden.reshape(clips, -1, local_groups, group_width)
    sums_local = jnp.sum(grouped, axis=(1, 3))
    squares_local = jnp.sum(grouped * grouped, axis=(1, 3))
    sums_all, squares_all = lax.psum((sums_local, squares_local), ("tm", "height"))
    count = float(
        frames * lax.axis_size("tm") * rows * lax.axis_size("height") * cols * group_width
    )
    mean = sums_all / count
    var = squares_all / count - mean * mean
    scaled = (grouped - mean[:, None, :, None]) * lax.rsqrt(var + norm_eps)[:, None, :, None]
    scaled = scaled.reshape(hidden.shape) * group_gain.astype(jnp.float32) + group_bias.astype(
        jnp.float32
    )
    normed = jax.nn.silu(scaled).astype(jnp.bfloat16)
    partial_latent = convolve(edges_norm(normed), conv_out_weight)
    own_sum = lax.psum_scatter(partial_latent, "dp", scatter_dimension=0, tiled=True)
    own_latent = (own_sum + out_bias) * latent_scale
    every_latent = lax.all_gather(own_latent.astype(jnp.bfloat16), "dp", axis=0, tiled=True)
    latent_dims = every_latent.shape[4]
    latents = own_latent.reshape(1, frames, rows, cols * latent_dims)
    tok_rows = rows // 2
    tok_cols = cols // 2
    patches = every_latent.reshape(clips, frames, tok_rows, 2, tok_cols, 2, latent_dims)
    patches = patches.transpose(0, 1, 2, 4, 3, 5, 6).reshape(-1, 4 * latent_dims)
    embedded = (
        jnp.dot(patches, patch_weight, preferred_element_type=jnp.float32)
        + patch_bias.astype(jnp.float32)
    ).astype(jnp.bfloat16)
    projected = jnp.dot(
        embedded,
        lax.all_gather(qkv_weight, ("tm", "height"), axis=0, tiled=True),
        preferred_element_type=jnp.float32,
    )
    projected = projected + qkv_bias.astype(jnp.float32)
    local_heads = qkv_weight.shape[1] // (3 * HD)
    projected = projected.reshape(clips, frames, tok_rows, tok_cols, local_heads, 3, HD)
    angles = rope_angles(frame_pos.astype(jnp.float32), row_pos.astype(jnp.float32), tok_cols)
    query = rotate(rms_scale(projected[..., 0, :], q_gain), angles)
    key = rotate(rms_scale(projected[..., 1, :], k_gain), angles)
    value = projected[..., 2, :]
    merged = (clips, frames, tok_rows, tok_cols, local_heads * HD)
    return (
        latents,
        query.reshape(merged).astype(jnp.bfloat16),
        key.reshape(merged).astype(jnp.bfloat16),
        value.reshape(merged).astype(jnp.bfloat16),
    )


LANES = 128
TILE = 16
GROUP = 16


def one_group_each(mesh, clip_inputs, conv_in_weight, conv_out_weight, qkv_weight):
    plane = mesh.shape["tm"] * mesh.shape["height"]
    return (
        clip_inputs.shape[:4] == (1, 2, 2, 16)
        and mesh.shape["height"] == 2
        and mesh.shape["tm"] == 4
        and mesh.shape["dp"] == 4
        and conv_in_weight.shape[1] == plane * GROUP
        and clip_inputs.shape[4] == GROUP * GROUPS
        and conv_out_weight.shape[2] == TILE
        and qkv_weight.shape == (3 * LANES, 6 * HD)
    )


def lane_shifts(lane):
    col = lane % 16
    row = lane // 16 % 2
    half = lane // 64

    def cols(left, mid, right):
        left = jnp.where(col == 0, left, pltpu.roll(left, 1, 1))
        right = jnp.where(col == 15, right, pltpu.roll(right, LANES - 1, 1))
        return mid + left + right

    def rows(up, mid, down):
        up = jnp.where(
            row == 1, pltpu.roll(up, 16, 1), jnp.where(half == 1, pltpu.roll(up, 48, 1), up)
        )
        down = jnp.where(
            row == 0,
            pltpu.roll(down, LANES - 16, 1),
            jnp.where(half == 0, pltpu.roll(down, LANES - 48, 1), down),
        )
        return mid + up + down

    return cols, rows


def tap_sums(y_ref, top, tiles):
    lane = lax.broadcasted_iota(jnp.int32, (TILE, LANES), 1)
    second = lane // 32 % 2 == 1
    cols, rows = lane_shifts(lane)
    sums = []
    before = None
    for tile in range(tiles):

        def part(tap):
            at = top + tap * TILE
            return y_ref[at : at + TILE, tile * LANES : (tile + 1) * LANES]

        oldest, older, now = (
            rows(*(cols(*(part(9 * i + 3 * j + l) for l in range(3))) for j in range(3)))
            for i in range(3)
        )
        turned = pltpu.roll(older, 32, 1)
        if before is None:
            start = jnp.where(second, pltpu.roll(oldest, 32, 1), oldest)
            total = now + jnp.where(second, turned, older) + start
        else:
            total = now + jnp.where(second, turned, pltpu.roll(before[1], 96, 1)) + before[0]
        before = (oldest, older)
        sums.append(total)
    return sums


def pack_kernel(
    w_hbm, qkv_hbm, patch_hbm, patch_bias_hbm, out_hbm, merged_ref,
    w_ref, qkv_ref, patch_ref, patch_bias_ref, rows_ref, out_ref, sems,
):
    plane, channels, depth = out_ref.shape
    rows = qkv_ref.shape[0]
    place = lax.axis_index("tm") * lax.axis_size("height") + lax.axis_index("height")
    at = pl.ds(pl.multiple_of(place * rows, LANES), rows)
    loads = [
        pltpu.make_async_copy(w_hbm, w_ref, sems.at[0]),
        pltpu.make_async_copy(qkv_hbm, qkv_ref, sems.at[1]),
        pltpu.make_async_copy(patch_hbm.at[:, at], patch_ref, sems.at[2]),
        pltpu.make_async_copy(patch_bias_hbm, patch_bias_ref, sems.at[3]),
    ]
    for load in loads:
        load.start()
    loads[0].wait()
    turned = w_ref[...].T
    for to in range(plane):
        out_ref[to] = turned[to // 2 * channels : (to // 2 + 1) * channels]
    store = pltpu.make_async_copy(out_ref, out_hbm, sems.at[4])
    store.start()
    for load in loads[1:]:
        load.wait()
    merged = jnp.dot(patch_ref[...], qkv_ref[...], preferred_element_type=jnp.float32)
    rows_ref[...] = patch_bias_ref[...].astype(jnp.float32).reshape(rows_ref.shape)
    count = rows // LANES
    bias = [rows_ref[pl.ds(count * place + part, 1), :] for part in range(count)]
    bias = jnp.broadcast_to(jnp.concatenate(bias, axis=1), (16, rows)).astype(jnp.bfloat16)
    bias = jnp.dot(bias, qkv_ref[...], preferred_element_type=jnp.float32)
    merged_ref[:64] = merged
    merged_ref[64:] = bias
    store.wait()


def column(row_ref, first, size):
    length = row_ref.shape[0]
    row = row_ref[...].astype(jnp.float32).reshape(1, length)
    line = lax.broadcasted_iota(jnp.int32, (size, length), 0)
    lane = lax.broadcasted_iota(jnp.int32, (size, length), 1)
    picked = jnp.where(lane == line + first, jnp.broadcast_to(row, (size, length)), 0.0)
    return jnp.sum(picked, axis=1, keepdims=True)


def table_kernel(
    frame_ref, row_pos_ref, freq_ref, gain_hbm, bias_hbm, out_bias_hbm, qkv_hbm, q_hbm, k_hbm,
    scale_ref, table_ref,
    gain_v, bias_v, out_bias_v, qkv_v, q_v, k_v, sems,
):
    pairs = (
        (gain_hbm, gain_v), (bias_hbm, bias_v), (out_bias_hbm, out_bias_v),
        (qkv_hbm, qkv_v), (q_hbm, q_v), (k_hbm, k_v),
    )
    loads = [
        pltpu.make_async_copy(source, to, sems.at[index])
        for index, (source, to) in enumerate(pairs)
    ]
    for load in loads:
        load.start()
    shape = (TILE, LANES)
    line = lax.broadcasted_iota(jnp.int32, shape, 0)
    lane = lax.broadcasted_iota(jnp.int32, shape, 1)
    frame = jnp.where(line // 8 == 0, frame_ref[0], frame_ref[1]).astype(jnp.float32)
    row = jnp.broadcast_to(row_pos_ref[0], shape).astype(jnp.float32)
    spot = jnp.where(lane < 72, row, (line % 8).astype(jnp.float32))
    angles = jnp.where(lane < 16, frame, spot) * freq_ref[...]
    table_ref[:16] = jnp.cos(angles)
    sine = jnp.sin(angles)
    table_ref[16:32] = jnp.where(lane % 2 == 0, -sine, sine)
    for load in loads:
        load.wait()
    first = lax.axis_index("tm") // 2 * (4 * GROUP)
    scale_ref[:, 0:1] = column(gain_v, first, 4 * GROUP)
    scale_ref[:, 1:2] = column(bias_v, first, 4 * GROUP)
    table_ref[32:48] = jnp.broadcast_to(column(out_bias_v, 0, TILE), shape)
    table_ref[48:49] = q_v[...].astype(jnp.float32).reshape(1, HD)
    table_ref[49:50] = k_v[...].astype(jnp.float32).reshape(1, HD)
    table_ref[50:56] = qkv_v[...].astype(jnp.float32).reshape(6, LANES)


def arrange_kernel(*refs):
    pieces, (_, keep_ref, send_ref, all_ref) = refs[:4], refs[4:]
    side = lax.axis_index("height")
    layer = lax.axis_index("dp")
    for step, piece in enumerate(pieces):
        all_ref[(layer + 4 - step) % 4] = piece[...]
    for core in range(2):
        keep_ref[core] = all_ref[2 * side + core]
        send_ref[core] = all_ref[2 - 2 * side + core]


def join_kernel(w_ref, wt_ref):
    plane, width, depth = w_ref.shape
    channels = wt_ref.shape[1]
    for group in range(width // GROUP):
        for tap in range(TAPS):
            start = tap * channels
            end = start + channels
            at = (group * TAPS + tap) * GROUP
            while start < end:
                source = start // depth
                stop = min(end, (source + 1) * depth)
                wt_ref[
                    at : at + GROUP, start - tap * channels : stop - tap * channels
                ] = w_ref[
                    source,
                    group * GROUP : (group + 1) * GROUP,
                    start - source * depth : stop - source * depth,
                ]
                start = stop

def place_clip(pieces, x_ref):
    place = lax.axis_index("tm") // 2 * 4 + lax.axis_index("height")
    for flip, piece in zip((0, 1, 4, 5), pieces):
        for core in range(2):
            x_ref[(place ^ flip) + 2 * core] = piece[core]


def normed_half(x_ref, wt_ref, y_ref, scale_ref, half):
    channels = x_ref.shape[2]
    tiles = x_ref.shape[0] // 2
    taps = TAPS * GROUP
    count = float(tiles * LANES * GROUP)
    y_ref[...] = lax.dot_general(
        wt_ref[: 2 * taps],
        x_ref[...].reshape(tiles * LANES, channels),
        (((1,), (1,)), ((), ())),
        preferred_element_type=jnp.float32,
    )
    normed = []
    for group in range(2):
        hidden = tap_sums(y_ref, group * taps, tiles)
        at = pl.ds(pl.multiple_of((2 * half + group) * GROUP, GROUP), GROUP)
        mean = jnp.sum(sum(hidden), keepdims=True) / count
        square = jnp.sum(sum(part * part for part in hidden), keepdims=True) / count
        scale = lax.rsqrt(square - mean * mean + norm_eps)
        parts = []
        for part in hidden:
            scaled = (part - mean) * scale * scale_ref[at, 0:1] + scale_ref[at, 1:2]
            parts.append((scaled / (1.0 + jnp.exp(-scaled))).astype(jnp.bfloat16))
        normed.append(jnp.concatenate(parts, axis=1))
    return jnp.concatenate(normed, axis=0)


def own_half_kernel(
    x0_ref, x1_ref, x2_ref, x3_ref, wt_ref, scale_ref, out_ref, x_ref, y_ref
):
    place_clip((x0_ref, x1_ref, x2_ref, x3_ref), x_ref)
    half = lax.axis_index("tm") % 2
    out_ref[...] = normed_half(x_ref, wt_ref, y_ref, scale_ref, half)


def conv_kernel(
    x_ref, normed_ref, wt_ref, scale_ref, w2_ref, out_ref, y_ref, n_ref
):
    tiles = x_ref.shape[0] // 2
    half = lax.axis_index("tm") % 2
    n_ref[pl.ds(pl.multiple_of(half * 2 * GROUP, 2 * GROUP), 2 * GROUP)] = normed_ref[...]
    other = normed_half(x_ref, wt_ref, y_ref, scale_ref, 1 - half)
    n_ref[pl.ds(pl.multiple_of((1 - half) * 2 * GROUP, 2 * GROUP), 2 * GROUP)] = other
    y_ref[: TAPS * TILE] = jnp.dot(w2_ref[...], n_ref[...], preferred_element_type=jnp.float32)
    low = lax.broadcasted_iota(jnp.int32, (8, LANES), 1) < 64
    layers = out_ref.shape[0] // (2 * tiles)
    for tile, part in enumerate(tap_sums(y_ref, 0, tiles)):
        turned = pltpu.roll(part, 64, 1)
        near = jnp.where(low, part[:8], turned[8:])
        far = jnp.where(low, turned[:8], part[8:])
        for layer in range(layers):
            out_ref[layer * 2 * tiles + 2 * tile] = near
            out_ref[layer * 2 * tiles + 2 * tile + 1] = far


def token_kernel(
    p_ref, m_ref, table_ref, lat_ref, q_ref, k_ref, v_ref
):
    low = lax.broadcasted_iota(jnp.int32, (8, LANES), 1) < 64
    pairs = []
    for side in range(2):
        one, two = (
            sum(p_ref[4 * index + 2 * core + side] for index in range(p_ref.shape[0] // 4))
            for core in range(2)
        )
        top = jnp.where(low, one, pltpu.roll(two, 64, 1))
        bottom = jnp.where(low, pltpu.roll(one, 64, 1), two)
        pairs.append(jnp.concatenate([top, bottom], axis=0))
    total = jnp.concatenate(pairs, axis=1)
    lat = (total + table_ref[32:48, :1]) * latent_scale
    clips = lat.shape[1] // 64
    tokens = clips * 16
    place = lax.axis_index("dp")
    own = lat[:, :LANES]
    for pair in range(1, clips // 2):
        own = jnp.where(place // 2 == pair, lat[:, pair * LANES : (pair + 1) * LANES], own)
    own = jnp.where(place % 2 == 1, pltpu.roll(own, 64, 1), own)
    turned = own.T[:64]
    wide = jnp.concatenate([turned] * 16, axis=1)
    spot = lax.broadcasted_iota(jnp.int32, wide.shape, 0) % 16
    spread = lax.broadcasted_iota(jnp.int32, wide.shape, 1) // 16
    merged = jnp.sum(jnp.where(spot == spread, wide, 0.0).reshape(4, 16, 256), axis=1)
    lat_ref[0, 0] = merged[:2]
    lat_ref[0, 1] = merged[2:]

    lat_bf = lat.astype(jnp.bfloat16)
    token = lax.broadcasted_iota(jnp.int32, (tokens, clips * 64), 0)
    lane = lax.broadcasted_iota(jnp.int32, (tokens, clips * 64), 1)
    first = token // 8 * 32 + token % 8 * 2
    heads = q_ref.shape[2] // HD
    rows = [table_ref[50 + part : 51 + part] for part in range(3 * heads)]
    projected = m_ref[64:65] + jnp.concatenate(rows, axis=1)
    for a in range(2):
        for e in range(2):
            chosen = jnp.where(lane == first + (16 * a + e), 1.0, 0.0).astype(jnp.bfloat16)
            patch = lax.dot_general(
                chosen, lat_bf, (((1,), (1,)), ((), ())), preferred_element_type=jnp.float32
            ).astype(jnp.bfloat16)
            weight = m_ref[(2 * a + e) * TILE : (2 * a + e + 1) * TILE]
            coarse = weight.astype(jnp.bfloat16)
            fine = (weight - coarse.astype(jnp.float32)).astype(jnp.bfloat16)
            for half in (coarse, fine):
                projected = projected + jnp.dot(patch, half, preferred_element_type=jnp.float32)

    even = lax.broadcasted_iota(jnp.int32, (tokens, HD), 1) % 2 == 0
    cosine = jnp.concatenate([table_ref[:16]] * clips, axis=0)
    sine = jnp.concatenate([table_ref[16:32]] * clips, axis=0)

    def turn(vectors, gain):
        square = jnp.mean(vectors * vectors, axis=-1, keepdims=True)
        vectors = vectors * lax.rsqrt(square + norm_eps) * gain
        swapped = jnp.where(even, pltpu.roll(vectors, HD - 1, 1), pltpu.roll(vectors, 1, 1))
        return vectors * cosine + swapped * sine

    def keep(ref, head, value):
        value = value.reshape(tokens // 8, 8, HD).astype(jnp.bfloat16)
        ref[:, :, head * HD : (head + 1) * HD] = value

    for head in range(heads):
        at = 3 * HD * head
        keep(q_ref, head, turn(projected[:, at : at + HD], table_ref[48:49]))
        keep(k_ref, head, turn(projected[:, at + HD : at + 2 * HD], table_ref[49:50]))
        keep(v_ref, head, projected[:, at + 2 * HD : at + 3 * HD])


def rope_freqs():
    freqs = []
    for dims in (time_dims, row_dims, row_dims):
        freqs.append(rope_base ** (-np.arange(0, dims, 2, dtype=np.float64) / dims))
    return np.repeat(np.concatenate(freqs), 2)[None].astype(np.float32)


def vmem(count):
    return [pl.BlockSpec(memory_space=pltpu.VMEM)] * count


def grouped(
    clip_inputs,
    conv_in_weight,
    group_gain,
    group_bias,
    conv_out_weight,
    out_bias,
    patch_weight,
    patch_bias,
    qkv_weight,
    qkv_bias,
    q_gain,
    k_gain,
    frame_pos,
    row_pos,
):
    plane_axes = ("tm", "height")
    clips = lax.axis_size("dp")
    steps = lax.axis_size("tm")
    plane = steps * lax.axis_size("height")
    channels = clip_inputs.shape[4]
    depth = conv_in_weight.shape[0]

    hbm = pl.BlockSpec(memory_space=pltpu.HBM)
    wide = pltpu.CompilerParams(vmem_limit_bytes=60 * 1024 * 1024)
    limit = pltpu.CompilerParams(vmem_limit_bytes=32 * 1024 * 1024)
    small = pl.CostEstimate(flops=10**6, bytes_accessed=10**6, transcendentals=0)
    with jax.named_scope("weight_by_group"):
        packed, merged = pl.pallas_call(
            pack_kernel,
            out_shape=(
                jax.ShapeDtypeStruct((plane, 2 * GROUP, depth), jnp.bfloat16),
                jax.ShapeDtypeStruct((64 + 16, qkv_weight.shape[1]), jnp.float32),
            ),
            in_specs=[hbm] * 4,
            out_specs=(hbm, vmem(1)[0]),
            scratch_shapes=[
                pltpu.VMEM(conv_in_weight.shape, jnp.bfloat16),
                pltpu.VMEM(qkv_weight.shape, jnp.bfloat16),
                pltpu.VMEM((patch_weight.shape[0], qkv_weight.shape[0]), jnp.bfloat16),
                pltpu.VMEM(patch_bias.shape, jnp.bfloat16),
                pltpu.VMEM((patch_bias.shape[0] // LANES, LANES), jnp.float32),
                pltpu.VMEM((plane, 2 * GROUP, depth), jnp.bfloat16),
                pltpu.SemaphoreType.DMA((5,)),
            ],
            compiler_params=wide,
            cost_estimate=pl.CostEstimate(flops=10**8, bytes_accessed=10**6, transcendentals=0),
            name="pack_weights",
        )(conv_in_weight, qkv_weight, patch_weight, patch_bias)
        weight = lax.all_to_all(packed, plane_axes, 0, 0, tiled=True)
    with jax.named_scope("tables"):
        smem = pl.BlockSpec(memory_space=pltpu.SMEM)
        small_arrays = (group_gain, group_bias, out_bias, qkv_bias, q_gain, k_gain)
        scale, table = pl.pallas_call(
            table_kernel,
            out_shape=(
                jax.ShapeDtypeStruct((4 * GROUP, 2), jnp.float32),
                jax.ShapeDtypeStruct((56, LANES), jnp.float32),
            ),
            in_specs=[smem, smem, vmem(1)[0]] + [hbm] * 6,
            out_specs=tuple(vmem(2)),
            scratch_shapes=[pltpu.VMEM(array.shape, array.dtype) for array in small_arrays]
            + [pltpu.SemaphoreType.DMA((6,))],
            compiler_params=wide,
            cost_estimate=small,
            name="tables",
        )(frame_pos, row_pos, rope_freqs(), *small_arrays)
    with jax.named_scope("gather_clips"):
        own = clip_inputs.reshape(64, channels)
        layers = []
        for step in range(clips):
            pairs = []
            for layer in range(clips):
                for tm in range(steps):
                    to = (layer // 2 * 2 + tm % 2 + step) % clips
                    pairs.append((layer * steps + tm, to * steps + tm // 2 * 2 + layer % 2))
            layers.append(lax.ppermute(own, ("dp", "tm"), pairs))
    with jax.named_scope("spread_clips"):
        keep, send = pl.pallas_call(
            arrange_kernel,
            out_shape=(jax.ShapeDtypeStruct((2, 64, channels), jnp.bfloat16),) * 2,
            in_specs=vmem(4) + [hbm],
            out_specs=tuple(vmem(2)),
            scratch_shapes=[pltpu.VMEM((4, 64, channels), jnp.bfloat16)],
            compiler_params=limit,
            cost_estimate=small,
            name="arrange_clips",
        )(*layers, table)
        pieces = [keep]
        for flip in (1, 4, 5):
            pairs = [(i, i ^ flip) for i in range(plane)]
            pieces.append(lax.ppermute(send if flip % 2 else keep, plane_axes, pairs))
    with jax.named_scope("small_weights"):
        first = lax.axis_index("tm") // 2 * (4 * GROUP)
        weight_out = lax.dynamic_slice_in_dim(conv_out_weight, first, 4 * GROUP, axis=1)
        weight_out = weight_out.transpose(0, 2, 1).reshape(TAPS * TILE, 4 * GROUP)
    with jax.named_scope("join_weights"):
        joined = pl.pallas_call(
            join_kernel,
            out_shape=jax.ShapeDtypeStruct((2 * GROUP * TAPS, channels), jnp.bfloat16),
            in_specs=vmem(1),
            out_specs=vmem(1)[0],
            compiler_params=limit,
            cost_estimate=small,
            name="join_weights",
        )(weight)
        joined_pair = lax.ppermute(joined, "tm", [(i, i ^ 1) for i in range(steps)])
    with jax.named_scope("merged_projection"):
        for flip in (1, 4, 2):
            pairs = [(i, i ^ flip) for i in range(plane)]
            there = lax.ppermute(merged.astype(jnp.bfloat16), plane_axes, pairs)
            merged = merged + there.astype(jnp.float32)

    flops = 2 * clips * steps * LANES * TAPS * TILE * (channels + 16)
    cost = pl.CostEstimate(flops=flops // 2, bytes_accessed=10**6, transcendentals=0)
    product = pltpu.VMEM((2 * TAPS * GROUP, steps * LANES), jnp.float32)
    normed, clip = pl.pallas_call(
        own_half_kernel,
        out_shape=(
            jax.ShapeDtypeStruct((2 * GROUP, steps * LANES), jnp.bfloat16),
            jax.ShapeDtypeStruct((plane, 64, channels), jnp.bfloat16),
        ),
        in_specs=vmem(6),
        out_specs=tuple(vmem(2)),
        scratch_shapes=[product],
        compiler_params=limit,
        cost_estimate=pl.CostEstimate(flops=4 * 10**10, bytes_accessed=10**6, transcendentals=0),
        name="own_channels",
    )(*pieces, joined, scale)
    partial = pl.pallas_call(
        conv_kernel,
        out_shape=jax.ShapeDtypeStruct((clips * plane, 8, LANES), jnp.float32),
        in_specs=vmem(5),
        out_specs=vmem(1)[0],
        scratch_shapes=[product, pltpu.VMEM((4 * GROUP, steps * LANES), jnp.bfloat16)],
        compiler_params=limit,
        cost_estimate=cost,
        name="convolutions",
    )(clip, normed, joined_pair, scale, weight_out)

    with jax.named_scope("sum_latents"):
        partials = lax.all_to_all(partial, ("dp",) + plane_axes, 0, 0, tiled=True)

    heads = qkv_weight.shape[1] // (3 * HD)
    frames = clip_inputs.shape[1]
    tokens = jax.ShapeDtypeStruct((clips * frames, 8, heads * HD), jnp.bfloat16)
    latents, query, key, value = pl.pallas_call(
        token_kernel,
        out_shape=(jax.ShapeDtypeStruct((1, 2, 2, 256), jnp.float32), tokens, tokens, tokens),
        in_specs=vmem(3),
        out_specs=tuple(vmem(4)),
        compiler_params=limit,
        cost_estimate=pl.CostEstimate(flops=10**8, bytes_accessed=10**6, transcendentals=0),
        name="tokens",
    )(
        partials,
        merged,
        table,
    )
    full = (clips, frames, 1, 8, heads * HD)
    return latents, query.reshape(full), key.reshape(full), value.reshape(full)


def pick(mesh, *arrays):
    if one_group_each(mesh, arrays[0], arrays[1], arrays[4], arrays[8]):
        return grouped(*arrays)
    return shards(*arrays)


def solution(mesh):
    placed = (
        P("dp", "tm", "height", None, None),
        P(("tm", "height"), "dp"),
        P("dp"),
        P("dp"),
        P(None, "dp", None),
        P(),
        P(),
        P(),
        P(("tm", "height"), "dp"),
        P("dp"),
        P(),
        P(),
        P("tm"),
        P("height"),
    )
    return jax.shard_map(
        functools.partial(pick, mesh),
        mesh=mesh,
        in_specs=placed,
        out_specs=(
            P("dp", "tm", "height", None),
            P(None, "tm", "height", None, "dp"),
            P(None, "tm", "height", None, "dp"),
            P(None, "tm", "height", None, "dp"),
        ),
        check_vma=False,
    )
```

```python
import functools

import jax
import jax.numpy as jnp
import numpy as np
from jax import lax
from jax.experimental import pallas as pl
from jax.experimental.pallas import tpu as pltpu
from jax.sharding import PartitionSpec as P

HD = 128
GROUPS = 32
TAPS = 27


norm_eps = 1e-06
latent_scale = 0.476986
rope_base = 256.0
time_dims = 16
row_dims = 56


def from_behind(value, axis, steps):
    count = lax.axis_size(axis)
    first, last = (max(0, -steps), min(count, count - steps))
    return lax.ppermute(value, axis, [(source, source + steps) for source in range(first, last)])


def padded_2(block, sides, width):
    for axis, dim in sides:
        count = lax.axis_size(axis)
        forward = [(i, i + 1) for i in range(count - 1)]
        backward = [(target, source) for source, target in forward]
        low = lax.ppermute(
            lax.slice_in_dim(block, block.shape[dim] - width, None, axis=dim), axis, forward
        )
        high = lax.ppermute(lax.slice_in_dim(block, 0, width, axis=dim), axis, backward)
        block = jnp.concatenate([low, block, high], axis=dim)
    return block


def repeat_first(block):
    return jnp.concatenate([block[:, :1], block[:, :1]], axis=1)


def time_join(block, earlier):
    start = jnp.where(lax.axis_index("tm") == 0, repeat_first(block), earlier)
    return jnp.concatenate([start, block], axis=1)


def rows_finish(grown):
    place = lax.axis_index("height")
    top = jnp.where(place == 0, grown[:, :, 1:2], grown[:, :, :1])
    bottom = jnp.where(place == lax.axis_size("height") - 1, grown[:, :, -2:-1], grown[:, :, -1:])
    inner = jnp.concatenate([top, grown[:, :, 1:-1], bottom], axis=2)
    return jnp.pad(inner, ((0, 0), (0, 0), (0, 0), (1, 1), (0, 0)), mode="edge")


def edges_before(block):
    earlier = from_behind(block, "tm", 1)
    longer = time_join(block, earlier)
    return rows_finish(padded_2(longer, (("height", 2),), 1))


def edges_norm(block):
    earlier = from_behind(block, "tm", 1)
    longer = time_join(block, earlier)
    return rows_finish(padded_2(longer, (("height", 2),), 1))


def convolve(padded, weight):
    clips = padded.shape[0]
    frames = padded.shape[1] - 2
    rows = padded.shape[2] - 2
    cols = padded.shape[3] - 2
    total = jnp.zeros((clips * frames * rows * cols, weight.shape[2]), jnp.float32)
    for shift_t in range(3):
        for shift_r in range(3):
            for shift_c in range(3):
                window = padded[
                    :,
                    shift_t : shift_t + frames,
                    shift_r : shift_r + rows,
                    shift_c : shift_c + cols,
                ]
                window = window.reshape(-1, padded.shape[4])
                total = total + jnp.dot(
                    window,
                    weight[9 * shift_t + 3 * shift_r + shift_c],
                    preferred_element_type=jnp.float32,
                )
    return total.reshape(clips, frames, rows, cols, weight.shape[2])


def section_freqs(dims):
    return jnp.power(rope_base, -jnp.arange(0, dims, 2, dtype=jnp.float32) / dims)


def rope_angles(tpos, hpos, width):
    frames = tpos.shape[0]
    rows = hpos.shape[0]
    cols = jnp.arange(width, dtype=jnp.float32)
    part_t = tpos[:, None, None, None] * section_freqs(time_dims)
    part_h = hpos[None, :, None, None] * section_freqs(row_dims)
    part_w = cols[None, None, :, None] * section_freqs(row_dims)
    shape = (frames, rows, width)
    return jnp.concatenate(
        [
            jnp.broadcast_to(part_t, shape + (time_dims // 2,)),
            jnp.broadcast_to(part_h, shape + (row_dims // 2,)),
            jnp.broadcast_to(part_w, shape + (row_dims // 2,)),
        ],
        axis=-1,
    )


def rotate(vectors, angles):
    pairs = vectors.reshape(vectors.shape[:-1] + (vectors.shape[-1] // 2, 2))
    first = pairs[..., 0]
    second = pairs[..., 1]
    cosine = jnp.cos(angles)[..., None, :]
    sine = jnp.sin(angles)[..., None, :]
    turned = jnp.stack([first * cosine - second * sine, first * sine + second * cosine], axis=-1)
    return turned.reshape(vectors.shape)


def rms_scale(vectors, gain):
    return (
        vectors
        * lax.rsqrt(jnp.mean(vectors * vectors, axis=-1, keepdims=True) + norm_eps)
        * gain.astype(jnp.float32)
    )


def shards(
    clip_inputs,
    conv_in_weight,
    group_gain,
    group_bias,
    conv_out_weight,
    out_bias,
    patch_weight,
    patch_bias,
    qkv_weight,
    qkv_bias,
    q_gain,
    k_gain,
    frame_pos,
    row_pos,
):
    channels = clip_inputs.shape[4]
    frames = clip_inputs.shape[1]
    rows = clip_inputs.shape[2]
    cols = clip_inputs.shape[3]
    padded = lax.all_gather(edges_before(clip_inputs), "dp", axis=0, tiled=True)
    clips = padded.shape[0]
    weight_in = lax.all_gather(conv_in_weight, ("tm", "height"), axis=0, tiled=True).reshape(
        TAPS, channels, -1
    )
    hidden = convolve(padded, weight_in)
    block_width = hidden.shape[4]
    group_width = channels // GROUPS
    local_groups = block_width // group_width
    grouped = hidden.reshape(clips, -1, local_groups, group_width)
    sums_local = jnp.sum(grouped, axis=(1, 3))
    squares_local = jnp.sum(grouped * grouped, axis=(1, 3))
    sums_all, squares_all = lax.psum((sums_local, squares_local), ("tm", "height"))
    count = float(
        frames * lax.axis_size("tm") * rows * lax.axis_size("height") * cols * group_width
    )
    mean = sums_all / count
    var = squares_all / count - mean * mean
    scaled = (grouped - mean[:, None, :, None]) * lax.rsqrt(var + norm_eps)[:, None, :, None]
    scaled = scaled.reshape(hidden.shape) * group_gain.astype(jnp.float32) + group_bias.astype(
        jnp.float32
    )
    normed = jax.nn.silu(scaled).astype(jnp.bfloat16)
    partial_latent = convolve(edges_norm(normed), conv_out_weight)
    own_sum = lax.psum_scatter(partial_latent, "dp", scatter_dimension=0, tiled=True)
    own_latent = (own_sum + out_bias) * latent_scale
    every_latent = lax.all_gather(own_latent.astype(jnp.bfloat16), "dp", axis=0, tiled=True)
    latent_dims = every_latent.shape[4]
    latents = own_latent.reshape(1, frames, rows, cols * latent_dims)
    tok_rows = rows // 2
    tok_cols = cols // 2
    patches = every_latent.reshape(clips, frames, tok_rows, 2, tok_cols, 2, latent_dims)
    patches = patches.transpose(0, 1, 2, 4, 3, 5, 6).reshape(-1, 4 * latent_dims)
    embedded = (
        jnp.dot(patches, patch_weight, preferred_element_type=jnp.float32)
        + patch_bias.astype(jnp.float32)
    ).astype(jnp.bfloat16)
    projected = jnp.dot(
        embedded,
        lax.all_gather(qkv_weight, ("tm", "height"), axis=0, tiled=True),
        preferred_element_type=jnp.float32,
    )
    projected = projected + qkv_bias.astype(jnp.float32)
    local_heads = qkv_weight.shape[1] // (3 * HD)
    projected = projected.reshape(clips, frames, tok_rows, tok_cols, local_heads, 3, HD)
    angles = rope_angles(frame_pos.astype(jnp.float32), row_pos.astype(jnp.float32), tok_cols)
    query = rotate(rms_scale(projected[..., 0, :], q_gain), angles)
    key = rotate(rms_scale(projected[..., 1, :], k_gain), angles)
    value = projected[..., 2, :]
    merged = (clips, frames, tok_rows, tok_cols, local_heads * HD)
    return (
        latents,
        query.reshape(merged).astype(jnp.bfloat16),
        key.reshape(merged).astype(jnp.bfloat16),
        value.reshape(merged).astype(jnp.bfloat16),
    )


LANES = 128
TILE = 16
GROUP = 16


def one_group_each(mesh, clip_inputs, conv_in_weight, conv_out_weight, qkv_weight):
    plane = mesh.shape["tm"] * mesh.shape["height"]
    return (
        clip_inputs.shape[:4] == (1, 2, 2, 16)
        and mesh.shape["height"] == 2
        and mesh.shape["tm"] == 4
        and mesh.shape["dp"] == 4
        and conv_in_weight.shape[1] == plane * GROUP
        and clip_inputs.shape[4] == GROUP * GROUPS
        and conv_out_weight.shape[2] == TILE
        and qkv_weight.shape[1] == 6 * HD
    )


def lane_shifts(lane):
    col = lane % 16
    row = lane // 16 % 2
    half = lane // 64

    def cols(left, mid, right):
        left = jnp.where(col == 0, left, pltpu.roll(left, 1, 1))
        right = jnp.where(col == 15, right, pltpu.roll(right, LANES - 1, 1))
        return mid + left + right

    def rows(up, mid, down):
        up = jnp.where(
            row == 1, pltpu.roll(up, 16, 1), jnp.where(half == 1, pltpu.roll(up, 48, 1), up)
        )
        down = jnp.where(
            row == 0,
            pltpu.roll(down, LANES - 16, 1),
            jnp.where(half == 0, pltpu.roll(down, LANES - 48, 1), down),
        )
        return mid + up + down

    return cols, rows


def tap_sums(y_ref, top, tiles):
    lane = lax.broadcasted_iota(jnp.int32, (TILE, LANES), 1)
    second = lane // 32 % 2 == 1
    cols, rows = lane_shifts(lane)
    sums = []
    before = None
    for tile in range(tiles):

        def part(tap):
            at = top + tap * TILE
            return y_ref[at : at + TILE, tile * LANES : (tile + 1) * LANES]

        oldest, older, now = (
            rows(*(cols(*(part(9 * i + 3 * j + l) for l in range(3))) for j in range(3)))
            for i in range(3)
        )
        turned = pltpu.roll(older, 32, 1)
        if before is None:
            start = jnp.where(second, pltpu.roll(oldest, 32, 1), oldest)
            total = now + jnp.where(second, turned, older) + start
        else:
            total = now + jnp.where(second, turned, pltpu.roll(before[1], 96, 1)) + before[0]
        before = (oldest, older)
        sums.append(total)
    return sums


def pack_kernel(
    w_hbm, qkv_hbm, patch_hbm, patch_bias_hbm, out_hbm, lines_ref,
    w_ref, qkv_ref, patch_ref, patch_bias_ref, rows_ref, out_ref, sems,
):
    plane, channels, width = out_ref.shape
    depth = w_ref.shape[0]
    rows = qkv_ref.shape[0]
    place = lax.axis_index("tm") * lax.axis_size("height") + lax.axis_index("height")
    at = pl.ds(pl.multiple_of(place * rows, LANES), rows)
    whole = depth // LANES * LANES
    cuts = [depth // LANES * part // 3 * LANES for part in range(3)] + [depth]
    spans = [slice(first, last) for first, last in zip(cuts, cuts[1:])]
    weights = [
        pltpu.make_async_copy(w_hbm.at[span], w_ref.at[span], sems.at[index])
        for index, span in enumerate(spans)
    ]
    loads = [
        pltpu.make_async_copy(qkv_hbm, qkv_ref, sems.at[3]),
        pltpu.make_async_copy(patch_hbm.at[:, at], patch_ref, sems.at[4]),
        pltpu.make_async_copy(patch_bias_hbm, patch_bias_ref, sems.at[5]),
    ]
    spans[2] = slice(cuts[2], width)
    stores = [
        pltpu.make_async_copy(out_ref.at[:, :, span], out_hbm.at[:, :, span], sems.at[6 + index])
        for index, span in enumerate(spans)
    ]
    for load in weights + loads:
        load.start()
    for index in range(2):
        weights[index].wait()
        turned = w_ref[spans[index]].T
        for to in range(plane):
            first = to // 2 * channels
            out_ref[to, :, spans[index]] = turned[first : first + channels]
        stores[index].start()
    for load in loads:
        load.wait()
    merged = jnp.dot(patch_ref[...], qkv_ref[...], preferred_element_type=jnp.float32)
    weights[2].wait()
    turned = w_ref[cuts[2] : depth].T
    for to in range(plane):
        first = to // 2 * channels
        mine = [merged[8 * to : 8 * to + 8, q * LANES : (q + 1) * LANES] for q in range(6)]
        upper = [pltpu.roll(mine[4], 64, 1), mine[4], pltpu.roll(mine[5], 64, 1), mine[5]]
        upper = jnp.concatenate(upper, axis=0)[:, 64:].astype(jnp.bfloat16)
        lower = turned[first : first + channels]
        out_ref[to, :, cuts[2] : whole + LANES] = jnp.concatenate([lower, upper], axis=1)
        out_ref[to, :, whole + LANES :] = jnp.concatenate(mine[:4], axis=0).astype(jnp.bfloat16)
    stores[2].start()
    rows_ref[...] = patch_bias_ref[...].astype(jnp.float32).reshape(rows_ref.shape)
    count = rows // LANES
    bias = [rows_ref[pl.ds(count * place + part, 1), :] for part in range(count)]
    bias = jnp.broadcast_to(jnp.concatenate(bias, axis=1), (8, rows)).astype(jnp.bfloat16)
    bias = jnp.dot(bias, qkv_ref[...], preferred_element_type=jnp.float32)
    line = lax.broadcasted_iota(jnp.int32, (8, LANES), 0)
    lines = jnp.zeros((8, LANES), jnp.float32)
    for part in range(bias.shape[1] // LANES):
        lines = jnp.where(line == part, bias[:, part * LANES : (part + 1) * LANES], lines)
    lines_ref[...] = lines
    for store in stores:
        store.wait()


def column(row_ref, first, size):
    length = row_ref.shape[0]
    row = row_ref[...].astype(jnp.float32).reshape(1, length)
    line = lax.broadcasted_iota(jnp.int32, (size, length), 0)
    lane = lax.broadcasted_iota(jnp.int32, (size, length), 1)
    picked = jnp.where(lane == line + first, jnp.broadcast_to(row, (size, length)), 0.0)
    return jnp.sum(picked, axis=1, keepdims=True)


def table_kernel(
    frame_ref, row_pos_ref, freq_ref, gain_hbm, bias_hbm, out_bias_hbm, qkv_hbm, q_hbm, k_hbm,
    scale_ref, table_ref,
    gain_v, bias_v, out_bias_v, qkv_v, q_v, k_v, sems,
):
    pairs = (
        (gain_hbm, gain_v), (bias_hbm, bias_v), (out_bias_hbm, out_bias_v),
        (qkv_hbm, qkv_v), (q_hbm, q_v), (k_hbm, k_v),
    )
    loads = [
        pltpu.make_async_copy(source, to, sems.at[index])
        for index, (source, to) in enumerate(pairs)
    ]
    for load in loads:
        load.start()
    shape = (TILE, LANES)
    line = lax.broadcasted_iota(jnp.int32, shape, 0)
    lane = lax.broadcasted_iota(jnp.int32, shape, 1)
    frame = jnp.where(line // 8 == 0, frame_ref[0], frame_ref[1]).astype(jnp.float32)
    row = jnp.broadcast_to(row_pos_ref[0], shape).astype(jnp.float32)
    spot = jnp.where(lane < 72, row, (line % 8).astype(jnp.float32))
    angles = jnp.where(lane < 16, frame, spot) * freq_ref[...]
    table_ref[:16] = jnp.cos(angles)
    sine = jnp.sin(angles)
    table_ref[16:32] = jnp.where(lane % 2 == 0, -sine, sine)
    for load in loads:
        load.wait()
    first = lax.axis_index("tm") // 2 * (4 * GROUP)
    scale_ref[:, 0:1] = column(gain_v, first, 4 * GROUP)
    scale_ref[:, 1:2] = column(bias_v, first, 4 * GROUP)
    table_ref[32:48] = jnp.broadcast_to(column(out_bias_v, 0, TILE), shape)
    table_ref[48:49] = q_v[...].astype(jnp.float32).reshape(1, HD)
    table_ref[49:50] = k_v[...].astype(jnp.float32).reshape(1, HD)
    table_ref[50:56] = qkv_v[...].astype(jnp.float32).reshape(6, LANES)


def arrange_kernel(*refs):
    pieces, (_, keep_ref, send_ref, all_ref) = refs[:4], refs[4:]
    side = lax.axis_index("height")
    layer = lax.axis_index("dp")
    for step, piece in enumerate(pieces):
        all_ref[(layer + 4 - step) % 4] = piece[...]
    for core in range(2):
        keep_ref[core] = all_ref[2 * side + core]
        send_ref[core] = all_ref[2 - 2 * side + core]


def join_kernel(w_ref, lines_ref, wt_ref):
    plane, width, lanes = w_ref.shape
    channels = wt_ref.shape[1]
    depth = TAPS * channels // plane
    for group in range(width // GROUP):
        for tap in range(TAPS):
            start = tap * channels
            end = start + channels
            at = (group * TAPS + tap) * GROUP
            while start < end:
                source = start // depth
                stop = min(end, (source + 1) * depth)
                wt_ref[
                    at : at + GROUP, start - tap * channels : stop - tap * channels
                ] = w_ref[
                    source,
                    group * GROUP : (group + 1) * GROUP,
                    start - source * depth : stop - source * depth,
                ]
                start = stop
    total = w_ref[0, :, lanes - 2 * LANES :].astype(jnp.float32)
    for source in range(1, plane):
        total = total + w_ref[source, :, lanes - 2 * LANES :].astype(jnp.float32)
    low = lax.broadcasted_iota(jnp.int32, (8, LANES), 1) < 64
    parts = [total[8 * q : 8 * q + 8, LANES:] for q in range(4)]
    for q in range(2):
        one = total[16 * q : 16 * q + 8, :LANES]
        two = total[16 * q + 8 : 16 * q + 16, :LANES]
        parts.append(jnp.where(low, pltpu.roll(one, 64, 1), two))
    parts += [lines_ref[...], jnp.zeros((8, LANES), jnp.float32)]
    share = jnp.concatenate(
        [jnp.concatenate(parts[:4], axis=1), jnp.concatenate(parts[4:], axis=1)], axis=0
    )
    wt_ref[width * TAPS :] = share.astype(jnp.bfloat16)


def place_clip(pieces, x_ref):
    place = lax.axis_index("tm") // 2 * 4 + lax.axis_index("height")
    for flip, piece in zip((0, 1, 4, 5), pieces):
        for core in range(2):
            x_ref[(place ^ flip) + 2 * core] = piece[core]


def normed_half(x_ref, wt_ref, y_ref, scale_ref, half):
    channels = x_ref.shape[2]
    tiles = x_ref.shape[0] // 2
    taps = TAPS * GROUP
    count = float(tiles * LANES * GROUP)
    y_ref[...] = lax.dot_general(
        wt_ref[: 2 * taps],
        x_ref[...].reshape(tiles * LANES, channels),
        (((1,), (1,)), ((), ())),
        preferred_element_type=jnp.float32,
    )
    normed = []
    for group in range(2):
        hidden = tap_sums(y_ref, group * taps, tiles)
        at = pl.ds(pl.multiple_of((2 * half + group) * GROUP, GROUP), GROUP)
        mean = jnp.sum(sum(hidden), keepdims=True) / count
        square = jnp.sum(sum(part * part for part in hidden), keepdims=True) / count
        scale = lax.rsqrt(square - mean * mean + norm_eps)
        parts = []
        for part in hidden:
            scaled = (part - mean) * scale * scale_ref[at, 0:1] + scale_ref[at, 1:2]
            parts.append((scaled / (1.0 + jnp.exp(-scaled))).astype(jnp.bfloat16))
        normed.append(jnp.concatenate(parts, axis=1))
    return jnp.concatenate(normed, axis=0)


def own_half_kernel(
    x0_ref, x1_ref, x2_ref, x3_ref, wt_ref, scale_ref, out_ref, x_ref, y_ref
):
    place_clip((x0_ref, x1_ref, x2_ref, x3_ref), x_ref)
    half = lax.axis_index("tm") % 2
    out_ref[...] = normed_half(x_ref, wt_ref, y_ref, scale_ref, half)


def conv_kernel(
    x_ref, normed_ref, wt_ref, scale_ref, w2_ref, out_hbm, y_ref, n_ref, out_ref, sems
):
    tiles = x_ref.shape[0] // 2
    half = lax.axis_index("tm") % 2
    n_ref[pl.ds(pl.multiple_of(half * 2 * GROUP, 2 * GROUP), 2 * GROUP)] = normed_ref[...]
    other = normed_half(x_ref, wt_ref, y_ref, scale_ref, 1 - half)
    n_ref[pl.ds(pl.multiple_of((1 - half) * 2 * GROUP, 2 * GROUP), 2 * GROUP)] = other
    y_ref[: TAPS * TILE] = jnp.dot(w2_ref[...], n_ref[...], preferred_element_type=jnp.float32)
    low = lax.broadcasted_iota(jnp.int32, (8, LANES), 1) < 64
    layers = out_hbm.shape[0] // (2 * tiles)
    stores = []
    for tile, part in enumerate(tap_sums(y_ref, 0, tiles)):
        turned = pltpu.roll(part, 64, 1)
        out_ref[2 * tile] = jnp.where(low, part[:8], turned[8:])
        out_ref[2 * tile + 1] = jnp.where(low, turned[:8], part[8:])
        for layer in range(layers):
            at = pl.ds((layer * tiles + tile) * 2, 2)
            source = out_ref.at[pl.ds(2 * tile, 2)]
            stores.append(
                pltpu.make_async_copy(source, out_hbm.at[at], sems.at[layer * tiles + tile])
            )
            stores[-1].start()
    for store in stores:
        store.wait()


def share_kernel(m0_ref, m1_ref, m2_ref, m3_ref, table_ref, merged_ref, base_ref, m_ref):
    spot = lax.axis_index("tm") * 2 + lax.axis_index("height")
    lines = table_ref[48:56]
    for flip, ref in ((0, m0_ref), (1, m1_ref), (4, m2_ref), (5, m3_ref)):
        for core in range(2):
            share = ref[core].astype(jnp.float32)
            at = spot ^ flip ^ (2 * core)
            m_ref[at, :, : 4 * LANES] = share[:8]
            m_ref[at, :, 4 * LANES :] = share[8:, : 2 * LANES]
            lines = lines + pltpu.roll(share[8:, 2 * LANES : 3 * LANES], 2, 0)
    base_ref[...] = jnp.concatenate([lines[2 + part : 3 + part] for part in range(6)], axis=1)
    merged_ref[...] = m_ref[...].reshape(merged_ref.shape).astype(jnp.bfloat16)


def token_kernel(p_ref, m_ref, base_ref, table_ref, lat_ref, q_ref, k_ref, v_ref):
    low = lax.broadcasted_iota(jnp.int32, (8, LANES), 1) < 64
    pairs = []
    for side in range(2):
        one, two = (
            sum(p_ref[4 * index + 2 * core + side] for index in range(p_ref.shape[0] // 4))
            for core in range(2)
        )
        top = jnp.where(low, one, pltpu.roll(two, 64, 1))
        bottom = jnp.where(low, pltpu.roll(one, 64, 1), two)
        pairs.append(jnp.concatenate([top, bottom], axis=0))
    total = jnp.concatenate(pairs, axis=1)
    lat = (total + table_ref[32:48, :1]) * latent_scale
    clips = lat.shape[1] // 64
    tokens = clips * 16
    place = lax.axis_index("dp")
    own = lat[:, :LANES]
    for pair in range(1, clips // 2):
        own = jnp.where(place // 2 == pair, lat[:, pair * LANES : (pair + 1) * LANES], own)
    own = jnp.where(place % 2 == 1, pltpu.roll(own, 64, 1), own)
    turned = own.T[:64]
    wide = jnp.concatenate([turned] * 16, axis=1)
    spot = lax.broadcasted_iota(jnp.int32, wide.shape, 0) % 16
    spread = lax.broadcasted_iota(jnp.int32, wide.shape, 1) // 16
    merged = jnp.sum(jnp.where(spot == spread, wide, 0.0).reshape(4, 16, 256), axis=1)
    lat_ref[0, 0] = merged[:2]
    lat_ref[0, 1] = merged[2:]

    lat_bf = lat.astype(jnp.bfloat16)
    token = lax.broadcasted_iota(jnp.int32, (tokens, clips * 64), 0)
    lane = lax.broadcasted_iota(jnp.int32, (tokens, clips * 64), 1)
    first = token // 8 * 32 + token % 8 * 2
    heads = q_ref.shape[2] // HD
    projected = base_ref[...]
    for a in range(2):
        for e in range(2):
            chosen = jnp.where(lane == first + (16 * a + e), 1.0, 0.0).astype(jnp.bfloat16)
            patch = lax.dot_general(
                chosen, lat_bf, (((1,), (1,)), ((), ())), preferred_element_type=jnp.float32
            ).astype(jnp.bfloat16)
            weight = m_ref[(2 * a + e) * TILE : (2 * a + e + 1) * TILE]
            projected = projected + jnp.dot(patch, weight, preferred_element_type=jnp.float32)

    even = lax.broadcasted_iota(jnp.int32, (tokens, HD), 1) % 2 == 0
    cosine = jnp.concatenate([table_ref[:16]] * clips, axis=0)
    sine = jnp.concatenate([table_ref[16:32]] * clips, axis=0)

    def turn(vectors, gain):
        square = jnp.mean(vectors * vectors, axis=-1, keepdims=True)
        vectors = vectors * lax.rsqrt(square + norm_eps) * gain
        swapped = jnp.where(even, pltpu.roll(vectors, HD - 1, 1), pltpu.roll(vectors, 1, 1))
        return vectors * cosine + swapped * sine

    def keep(ref, head, value):
        value = value.reshape(tokens // 8, 8, HD).astype(jnp.bfloat16)
        ref[:, :, head * HD : (head + 1) * HD] = value

    for head in range(heads):
        at = 3 * HD * head
        keep(q_ref, head, turn(projected[:, at : at + HD], table_ref[48:49]))
        keep(k_ref, head, turn(projected[:, at + HD : at + 2 * HD], table_ref[49:50]))
        keep(v_ref, head, projected[:, at + 2 * HD : at + 3 * HD])


def rope_freqs():
    freqs = []
    for dims in (time_dims, row_dims, row_dims):
        freqs.append(rope_base ** (-np.arange(0, dims, 2, dtype=np.float64) / dims))
    return np.repeat(np.concatenate(freqs), 2)[None].astype(np.float32)


def vmem(count):
    return [pl.BlockSpec(memory_space=pltpu.VMEM)] * count


def grouped(
    clip_inputs,
    conv_in_weight,
    group_gain,
    group_bias,
    conv_out_weight,
    out_bias,
    patch_weight,
    patch_bias,
    qkv_weight,
    qkv_bias,
    q_gain,
    k_gain,
    frame_pos,
    row_pos,
):
    plane_axes = ("tm", "height")
    clips = lax.axis_size("dp")
    steps = lax.axis_size("tm")
    plane = steps * lax.axis_size("height")
    channels = clip_inputs.shape[4]
    depth = conv_in_weight.shape[0]

    width = -(-depth // LANES) * LANES + LANES
    hbm = pl.BlockSpec(memory_space=pltpu.HBM)
    wide = pltpu.CompilerParams(vmem_limit_bytes=60 * 1024 * 1024)
    limit = pltpu.CompilerParams(vmem_limit_bytes=32 * 1024 * 1024)
    small = pl.CostEstimate(flops=10**6, bytes_accessed=10**6, transcendentals=0)
    with jax.named_scope("weight_by_group"):
        packed, lines = pl.pallas_call(
            pack_kernel,
            out_shape=(
                jax.ShapeDtypeStruct((plane, 2 * GROUP, width), jnp.bfloat16),
                jax.ShapeDtypeStruct((8, LANES), jnp.float32),
            ),
            in_specs=[hbm] * 4,
            out_specs=(hbm, vmem(1)[0]),
            scratch_shapes=[
                pltpu.VMEM(conv_in_weight.shape, jnp.bfloat16),
                pltpu.VMEM(qkv_weight.shape, jnp.bfloat16),
                pltpu.VMEM((patch_weight.shape[0], qkv_weight.shape[0]), jnp.bfloat16),
                pltpu.VMEM(patch_bias.shape, jnp.bfloat16),
                pltpu.VMEM((patch_bias.shape[0] // LANES, LANES), jnp.float32),
                pltpu.VMEM((plane, 2 * GROUP, width), jnp.bfloat16),
                pltpu.SemaphoreType.DMA((9,)),
            ],
            compiler_params=wide,
            cost_estimate=pl.CostEstimate(flops=10**8, bytes_accessed=10**6, transcendentals=0),
            name="pack_weights",
        )(conv_in_weight, qkv_weight, patch_weight, patch_bias)
        weight = lax.all_to_all(packed, plane_axes, 0, 0, tiled=True)
    with jax.named_scope("tables"):
        smem = pl.BlockSpec(memory_space=pltpu.SMEM)
        small_arrays = (group_gain, group_bias, out_bias, qkv_bias, q_gain, k_gain)
        scale, table = pl.pallas_call(
            table_kernel,
            out_shape=(
                jax.ShapeDtypeStruct((4 * GROUP, 2), jnp.float32),
                jax.ShapeDtypeStruct((56, LANES), jnp.float32),
            ),
            in_specs=[smem, smem, vmem(1)[0]] + [hbm] * 6,
            out_specs=tuple(vmem(2)),
            scratch_shapes=[pltpu.VMEM(array.shape, array.dtype) for array in small_arrays]
            + [pltpu.SemaphoreType.DMA((6,))],
            compiler_params=wide,
            cost_estimate=small,
            name="tables",
        )(frame_pos, row_pos, rope_freqs(), *small_arrays)
    with jax.named_scope("gather_clips"):
        own = clip_inputs.reshape(64, channels)
        layers = []
        for step in range(clips):
            pairs = []
            for layer in range(clips):
                for tm in range(steps):
                    to = (layer // 2 * 2 + tm % 2 + step) % clips
                    pairs.append((layer * steps + tm, to * steps + tm // 2 * 2 + layer % 2))
            layers.append(lax.ppermute(own, ("dp", "tm"), pairs))
    with jax.named_scope("spread_clips"):
        keep, send = pl.pallas_call(
            arrange_kernel,
            out_shape=(jax.ShapeDtypeStruct((2, 64, channels), jnp.bfloat16),) * 2,
            in_specs=vmem(4) + [hbm],
            out_specs=tuple(vmem(2)),
            scratch_shapes=[pltpu.VMEM((4, 64, channels), jnp.bfloat16)],
            compiler_params=limit,
            cost_estimate=small,
            name="arrange_clips",
        )(*layers, table)
        pieces = [keep]
        for flip in (1, 4, 5):
            pairs = [(i, i ^ flip) for i in range(plane)]
            pieces.append(lax.ppermute(send if flip % 2 else keep, plane_axes, pairs))
    with jax.named_scope("small_weights"):
        first = lax.axis_index("tm") // 2 * (4 * GROUP)
        weight_out = lax.dynamic_slice_in_dim(conv_out_weight, first, 4 * GROUP, axis=1)
        weight_out = weight_out.transpose(0, 2, 1).reshape(TAPS * TILE, 4 * GROUP)
    with jax.named_scope("join_weights"):
        joined = pl.pallas_call(
            join_kernel,
            out_shape=jax.ShapeDtypeStruct((2 * GROUP * TAPS + 16, channels), jnp.bfloat16),
            in_specs=vmem(2),
            out_specs=vmem(1)[0],
            compiler_params=limit,
            cost_estimate=small,
            name="join_weights",
        )(weight, lines)
        joined_pair = lax.ppermute(joined, "tm", [(i, i ^ 1) for i in range(steps)])
    with jax.named_scope("merged_projection"):
        share = jnp.stack([joined[-16:], joined_pair[-16:]])
        shares = [share]
        for flip in (1, 4, 5):
            pairs = [(i, i ^ flip) for i in range(plane)]
            shares.append(lax.ppermute(share, plane_axes, pairs))

        merged, base = pl.pallas_call(
            share_kernel,
            out_shape=(
                jax.ShapeDtypeStruct((64, 6 * HD), jnp.bfloat16),
                jax.ShapeDtypeStruct((1, 6 * HD), jnp.float32),
            ),
            in_specs=vmem(5),
            out_specs=tuple(vmem(2)),
            scratch_shapes=[pltpu.VMEM((plane, 8, 6 * HD), jnp.float32)],
            compiler_params=limit,
            cost_estimate=small,
            name="share_rows",
        )(*shares, table)

    flops = 2 * clips * steps * LANES * TAPS * TILE * (channels + 16)
    cost = pl.CostEstimate(flops=flops // 2, bytes_accessed=10**6, transcendentals=0)
    product = pltpu.VMEM((2 * TAPS * GROUP, steps * LANES), jnp.float32)
    normed, clip = pl.pallas_call(
        own_half_kernel,
        out_shape=(
            jax.ShapeDtypeStruct((2 * GROUP, steps * LANES), jnp.bfloat16),
            jax.ShapeDtypeStruct((plane, 64, channels), jnp.bfloat16),
        ),
        in_specs=vmem(6),
        out_specs=tuple(vmem(2)),
        scratch_shapes=[product],
        compiler_params=limit,
        cost_estimate=pl.CostEstimate(flops=4 * 10**10, bytes_accessed=10**6, transcendentals=0),
        name="own_channels",
    )(*pieces, joined, scale)
    partial = pl.pallas_call(
        conv_kernel,
        out_shape=jax.ShapeDtypeStruct((clips * plane, 8, LANES), jnp.float32),
        in_specs=vmem(5),
        out_specs=hbm,
        scratch_shapes=[
            product,
            pltpu.VMEM((4 * GROUP, steps * LANES), jnp.bfloat16),
            pltpu.VMEM((plane, 8, LANES), jnp.float32),
            pltpu.SemaphoreType.DMA((clips * steps,)),
        ],
        compiler_params=limit,
        cost_estimate=cost,
        name="convolutions",
    )(clip, normed, joined_pair, scale, weight_out)

    with jax.named_scope("sum_latents"):
        partials = lax.all_to_all(partial, ("dp",) + plane_axes, 0, 0, tiled=True)

    heads = qkv_weight.shape[1] // (3 * HD)
    frames = clip_inputs.shape[1]
    tokens = jax.ShapeDtypeStruct((clips * frames, 8, heads * HD), jnp.bfloat16)
    latents, query, key, value = pl.pallas_call(
        token_kernel,
        out_shape=(jax.ShapeDtypeStruct((1, 2, 2, 256), jnp.float32), tokens, tokens, tokens),
        in_specs=vmem(4),
        out_specs=tuple(vmem(4)),
        compiler_params=limit,
        cost_estimate=pl.CostEstimate(flops=10**8, bytes_accessed=10**6, transcendentals=0),
        name="tokens",
    )(
        partials,
        merged,
        base,
        table,
    )
    full = (clips, frames, 1, 8, heads * HD)
    return latents, query.reshape(full), key.reshape(full), value.reshape(full)


def pick(mesh, *arrays):
    if one_group_each(mesh, arrays[0], arrays[1], arrays[4], arrays[8]):
        return grouped(*arrays)
    return shards(*arrays)


def solution(mesh):
    placed = (
        P("dp", "tm", "height", None, None),
        P(("tm", "height"), "dp"),
        P("dp"),
        P("dp"),
        P(None, "dp", None),
        P(),
        P(),
        P(),
        P(("tm", "height"), "dp"),
        P("dp"),
        P(),
        P(),
        P("tm"),
        P("height"),
    )
    return jax.shard_map(
        functools.partial(pick, mesh),
        mesh=mesh,
        in_specs=placed,
        out_specs=(
            P("dp", "tm", "height", None),
            P(None, "tm", "height", None, "dp"),
            P(None, "tm", "height", None, "dp"),
            P(None, "tm", "height", None, "dp"),
        ),
        check_vma=False,
    )
```

```python
import functools

import jax
import jax.numpy as jnp
import numpy as np
from jax import lax
from jax.experimental import pallas as pl
from jax.experimental.pallas import tpu as pltpu
from jax.sharding import PartitionSpec as P

HD = 128
GROUPS = 32
TAPS = 27


norm_eps = 1e-06
latent_scale = 0.476986
rope_base = 256.0
time_dims = 16
row_dims = 56


def from_behind(value, axis, steps):
    count = lax.axis_size(axis)
    first, last = (max(0, -steps), min(count, count - steps))
    return lax.ppermute(value, axis, [(source, source + steps) for source in range(first, last)])


def padded_2(block, sides, width):
    for axis, dim in sides:
        count = lax.axis_size(axis)
        forward = [(i, i + 1) for i in range(count - 1)]
        backward = [(target, source) for source, target in forward]
        low = lax.ppermute(
            lax.slice_in_dim(block, block.shape[dim] - width, None, axis=dim), axis, forward
        )
        high = lax.ppermute(lax.slice_in_dim(block, 0, width, axis=dim), axis, backward)
        block = jnp.concatenate([low, block, high], axis=dim)
    return block


def repeat_first(block):
    return jnp.concatenate([block[:, :1], block[:, :1]], axis=1)


def time_join(block, earlier):
    start = jnp.where(lax.axis_index("tm") == 0, repeat_first(block), earlier)
    return jnp.concatenate([start, block], axis=1)


def rows_finish(grown):
    place = lax.axis_index("height")
    top = jnp.where(place == 0, grown[:, :, 1:2], grown[:, :, :1])
    bottom = jnp.where(place == lax.axis_size("height") - 1, grown[:, :, -2:-1], grown[:, :, -1:])
    inner = jnp.concatenate([top, grown[:, :, 1:-1], bottom], axis=2)
    return jnp.pad(inner, ((0, 0), (0, 0), (0, 0), (1, 1), (0, 0)), mode="edge")


def edges_before(block):
    earlier = from_behind(block, "tm", 1)
    longer = time_join(block, earlier)
    return rows_finish(padded_2(longer, (("height", 2),), 1))


def edges_norm(block):
    earlier = from_behind(block, "tm", 1)
    longer = time_join(block, earlier)
    return rows_finish(padded_2(longer, (("height", 2),), 1))


def convolve(padded, weight):
    clips = padded.shape[0]
    frames = padded.shape[1] - 2
    rows = padded.shape[2] - 2
    cols = padded.shape[3] - 2
    total = jnp.zeros((clips * frames * rows * cols, weight.shape[2]), jnp.float32)
    for shift_t in range(3):
        for shift_r in range(3):
            for shift_c in range(3):
                window = padded[
                    :,
                    shift_t : shift_t + frames,
                    shift_r : shift_r + rows,
                    shift_c : shift_c + cols,
                ]
                window = window.reshape(-1, padded.shape[4])
                total = total + jnp.dot(
                    window,
                    weight[9 * shift_t + 3 * shift_r + shift_c],
                    preferred_element_type=jnp.float32,
                )
    return total.reshape(clips, frames, rows, cols, weight.shape[2])


def section_freqs(dims):
    return jnp.power(rope_base, -jnp.arange(0, dims, 2, dtype=jnp.float32) / dims)


def rope_angles(tpos, hpos, width):
    frames = tpos.shape[0]
    rows = hpos.shape[0]
    cols = jnp.arange(width, dtype=jnp.float32)
    part_t = tpos[:, None, None, None] * section_freqs(time_dims)
    part_h = hpos[None, :, None, None] * section_freqs(row_dims)
    part_w = cols[None, None, :, None] * section_freqs(row_dims)
    shape = (frames, rows, width)
    return jnp.concatenate(
        [
            jnp.broadcast_to(part_t, shape + (time_dims // 2,)),
            jnp.broadcast_to(part_h, shape + (row_dims // 2,)),
            jnp.broadcast_to(part_w, shape + (row_dims // 2,)),
        ],
        axis=-1,
    )


def rotate(vectors, angles):
    pairs = vectors.reshape(vectors.shape[:-1] + (vectors.shape[-1] // 2, 2))
    first = pairs[..., 0]
    second = pairs[..., 1]
    cosine = jnp.cos(angles)[..., None, :]
    sine = jnp.sin(angles)[..., None, :]
    turned = jnp.stack([first * cosine - second * sine, first * sine + second * cosine], axis=-1)
    return turned.reshape(vectors.shape)


def rms_scale(vectors, gain):
    return (
        vectors
        * lax.rsqrt(jnp.mean(vectors * vectors, axis=-1, keepdims=True) + norm_eps)
        * gain.astype(jnp.float32)
    )


def shards(
    clip_inputs,
    conv_in_weight,
    group_gain,
    group_bias,
    conv_out_weight,
    out_bias,
    patch_weight,
    patch_bias,
    qkv_weight,
    qkv_bias,
    q_gain,
    k_gain,
    frame_pos,
    row_pos,
):
    channels = clip_inputs.shape[4]
    frames = clip_inputs.shape[1]
    rows = clip_inputs.shape[2]
    cols = clip_inputs.shape[3]
    padded = lax.all_gather(edges_before(clip_inputs), "dp", axis=0, tiled=True)
    clips = padded.shape[0]
    weight_in = lax.all_gather(conv_in_weight, ("tm", "height"), axis=0, tiled=True).reshape(
        TAPS, channels, -1
    )
    hidden = convolve(padded, weight_in)
    block_width = hidden.shape[4]
    group_width = channels // GROUPS
    local_groups = block_width // group_width
    grouped = hidden.reshape(clips, -1, local_groups, group_width)
    sums_local = jnp.sum(grouped, axis=(1, 3))
    squares_local = jnp.sum(grouped * grouped, axis=(1, 3))
    sums_all, squares_all = lax.psum((sums_local, squares_local), ("tm", "height"))
    count = float(
        frames * lax.axis_size("tm") * rows * lax.axis_size("height") * cols * group_width
    )
    mean = sums_all / count
    var = squares_all / count - mean * mean
    scaled = (grouped - mean[:, None, :, None]) * lax.rsqrt(var + norm_eps)[:, None, :, None]
    scaled = scaled.reshape(hidden.shape) * group_gain.astype(jnp.float32) + group_bias.astype(
        jnp.float32
    )
    normed = jax.nn.silu(scaled).astype(jnp.bfloat16)
    partial_latent = convolve(edges_norm(normed), conv_out_weight)
    own_sum = lax.psum_scatter(partial_latent, "dp", scatter_dimension=0, tiled=True)
    own_latent = (own_sum + out_bias) * latent_scale
    every_latent = lax.all_gather(own_latent.astype(jnp.bfloat16), "dp", axis=0, tiled=True)
    latent_dims = every_latent.shape[4]
    latents = own_latent.reshape(1, frames, rows, cols * latent_dims)
    tok_rows = rows // 2
    tok_cols = cols // 2
    patches = every_latent.reshape(clips, frames, tok_rows, 2, tok_cols, 2, latent_dims)
    patches = patches.transpose(0, 1, 2, 4, 3, 5, 6).reshape(-1, 4 * latent_dims)
    embedded = (
        jnp.dot(patches, patch_weight, preferred_element_type=jnp.float32)
        + patch_bias.astype(jnp.float32)
    ).astype(jnp.bfloat16)
    projected = jnp.dot(
        embedded,
        lax.all_gather(qkv_weight, ("tm", "height"), axis=0, tiled=True),
        preferred_element_type=jnp.float32,
    )
    projected = projected + qkv_bias.astype(jnp.float32)
    local_heads = qkv_weight.shape[1] // (3 * HD)
    projected = projected.reshape(clips, frames, tok_rows, tok_cols, local_heads, 3, HD)
    angles = rope_angles(frame_pos.astype(jnp.float32), row_pos.astype(jnp.float32), tok_cols)
    query = rotate(rms_scale(projected[..., 0, :], q_gain), angles)
    key = rotate(rms_scale(projected[..., 1, :], k_gain), angles)
    value = projected[..., 2, :]
    merged = (clips, frames, tok_rows, tok_cols, local_heads * HD)
    return (
        latents,
        query.reshape(merged).astype(jnp.bfloat16),
        key.reshape(merged).astype(jnp.bfloat16),
        value.reshape(merged).astype(jnp.bfloat16),
    )


LANES = 128
TILE = 16
GROUP = 16


def one_group_each(mesh, clip_inputs, conv_in_weight, conv_out_weight, qkv_weight):
    plane = mesh.shape["tm"] * mesh.shape["height"]
    return (
        clip_inputs.shape[:4] == (1, 2, 2, 16)
        and mesh.shape["height"] == 2
        and mesh.shape["tm"] == 4
        and mesh.shape["dp"] == 4
        and conv_in_weight.shape[1] == plane * GROUP
        and clip_inputs.shape[4] == GROUP * GROUPS
        and conv_out_weight.shape[2] == TILE
        and qkv_weight.shape[1] == 6 * HD
    )


def lane_shifts(lane):
    col = lane % 16
    row = lane // 16 % 2
    half = lane // 64

    def cols(left, mid, right):
        left = jnp.where(col == 0, left, pltpu.roll(left, 1, 1))
        right = jnp.where(col == 15, right, pltpu.roll(right, LANES - 1, 1))
        return mid + left + right

    def rows(up, mid, down):
        up = jnp.where(
            row == 1, pltpu.roll(up, 16, 1), jnp.where(half == 1, pltpu.roll(up, 48, 1), up)
        )
        down = jnp.where(
            row == 0,
            pltpu.roll(down, LANES - 16, 1),
            jnp.where(half == 0, pltpu.roll(down, LANES - 48, 1), down),
        )
        return mid + up + down

    return cols, rows


def tap_sums(source, tiles):
    lane = lax.broadcasted_iota(jnp.int32, (TILE, LANES), 1)
    second = lane // 32 % 2 == 1
    cols, rows = lane_shifts(lane)
    sums = []
    before = None
    for tile in range(tiles):

        def part(tap):
            return source(tap, slice(tile * LANES, (tile + 1) * LANES))

        oldest, older, now = (
            rows(*(cols(*(part(9 * i + 3 * j + l) for l in range(3))) for j in range(3)))
            for i in range(3)
        )
        turned = pltpu.roll(older, 32, 1)
        if before is None:
            start = jnp.where(second, pltpu.roll(oldest, 32, 1), oldest)
            total = now + jnp.where(second, turned, older) + start
        else:
            total = now + jnp.where(second, turned, pltpu.roll(before[1], 96, 1)) + before[0]
        before = (oldest, older)
        sums.append(total)
    return sums


def pack_kernel(
    w_hbm, qkv_hbm, patch_hbm, patch_bias_hbm, own_hbm, side_hbm, high_hbm, far_hbm, lines_ref,
    w_ref, qkv_ref, patch_ref, patch_bias_ref, rows_ref, turned_ref, merged_ref, out_ref, sems,
):
    _, channels, width = out_ref.shape
    depth = w_ref.shape[0]
    rows = qkv_ref.shape[0]
    side = lax.axis_index("height")
    high = lax.axis_index("tm") // 2
    place = lax.axis_index("tm") * 2 + side
    at = pl.ds(pl.multiple_of(place * rows, LANES), rows)
    loads = [
        pltpu.make_async_copy(w_hbm, w_ref, sems.at[0]),
        pltpu.make_async_copy(qkv_hbm, qkv_ref, sems.at[1]),
        pltpu.make_async_copy(patch_hbm.at[:, at], patch_ref, sems.at[2]),
        pltpu.make_async_copy(patch_bias_hbm, patch_bias_ref, sems.at[3]),
    ]
    for load in loads:
        load.start()
    whole = depth // LANES * LANES
    loads[0].wait()
    turned_ref[...] = w_ref[...].T
    for load in loads[1:]:
        load.wait()
    merged_ref[...] = jnp.dot(patch_ref[...], qkv_ref[...], preferred_element_type=jnp.float32)
    stores = []
    for flip, out_hbm in ((1, side_hbm), (2, high_hbm), (3, far_hbm), (0, own_hbm)):
        first = pl.multiple_of((high ^ (flip // 2)) * channels, channels)
        out_ref[flip, :, :whole] = turned_ref[pl.ds(first, channels), :whole]
        lower = turned_ref[pl.ds(first, channels), whole:]
        chip = (2 * high + side) ^ flip
        tail, upper = [], []
        for half in range(2):
            mine = merged_ref[pl.ds(pl.multiple_of(chip * 16 + half * 8, 8), 8)]
            mine = [mine[:, q * LANES : (q + 1) * LANES] for q in range(6)]
            tail += mine[:4]
            upper += [pltpu.roll(mine[4], 64, 1), mine[4], pltpu.roll(mine[5], 64, 1), mine[5]]
        upper = jnp.concatenate(upper, axis=0)[:, 64:].astype(jnp.bfloat16)
        out_ref[flip, :, whole : whole + LANES] = jnp.concatenate([lower, upper], axis=1)
        out_ref[flip, :, whole + LANES :] = jnp.concatenate(tail, axis=0).astype(jnp.bfloat16)
        stores.append(pltpu.make_async_copy(out_ref.at[flip], out_hbm, sems.at[4 + flip]))
        stores[-1].start()
    rows_ref[...] = patch_bias_ref[...].astype(jnp.float32).reshape(rows_ref.shape)
    count = rows // LANES
    bias = [rows_ref[pl.ds(count * place + part, 1), :] for part in range(count)]
    bias = jnp.broadcast_to(jnp.concatenate(bias, axis=1), (8, rows)).astype(jnp.bfloat16)
    bias = jnp.dot(bias, qkv_ref[...], preferred_element_type=jnp.float32)
    line = lax.broadcasted_iota(jnp.int32, (8, LANES), 0)
    lines = jnp.zeros((8, LANES), jnp.float32)
    for part in range(bias.shape[1] // LANES):
        lines = jnp.where(line == part, bias[:, part * LANES : (part + 1) * LANES], lines)
    lines_ref[...] = lines
    for store in stores:
        store.wait()


def column(row_ref, first, size):
    length = row_ref.shape[0]
    row = row_ref[...].astype(jnp.float32).reshape(1, length)
    line = lax.broadcasted_iota(jnp.int32, (size, length), 0)
    lane = lax.broadcasted_iota(jnp.int32, (size, length), 1)
    picked = jnp.where(lane == line + first, jnp.broadcast_to(row, (size, length)), 0.0)
    return jnp.sum(picked, axis=1, keepdims=True)


def table_kernel(
    frame_ref, row_pos_ref, freq_ref, gain_hbm, bias_hbm, out_bias_hbm, qkv_hbm, q_hbm, k_hbm,
    scale_ref, table_ref,
    gain_v, bias_v, out_bias_v, qkv_v, q_v, k_v, sems,
):
    pairs = (
        (gain_hbm, gain_v), (bias_hbm, bias_v), (out_bias_hbm, out_bias_v),
        (qkv_hbm, qkv_v), (q_hbm, q_v), (k_hbm, k_v),
    )
    loads = [
        pltpu.make_async_copy(source, to, sems.at[index])
        for index, (source, to) in enumerate(pairs)
    ]
    for load in loads:
        load.start()
    shape = (TILE, LANES)
    line = lax.broadcasted_iota(jnp.int32, shape, 0)
    lane = lax.broadcasted_iota(jnp.int32, shape, 1)
    frame = jnp.where(line // 8 == 0, frame_ref[0], frame_ref[1]).astype(jnp.float32)
    row = jnp.broadcast_to(row_pos_ref[0], shape).astype(jnp.float32)
    spot = jnp.where(lane < 72, row, (line % 8).astype(jnp.float32))
    angles = jnp.where(lane < 16, frame, spot) * freq_ref[...]
    table_ref[:16] = jnp.cos(angles)
    sine = jnp.sin(angles)
    table_ref[16:32] = jnp.where(lane % 2 == 0, -sine, sine)
    for load in loads:
        load.wait()
    first = lax.axis_index("tm") // 2 * (4 * GROUP)
    scale_ref[:, 0:1] = column(gain_v, first, 4 * GROUP)
    scale_ref[:, 1:2] = column(bias_v, first, 4 * GROUP)
    table_ref[32:48] = jnp.broadcast_to(column(out_bias_v, 0, TILE), shape)
    table_ref[48:49] = q_v[...].astype(jnp.float32).reshape(1, HD)
    table_ref[49:50] = k_v[...].astype(jnp.float32).reshape(1, HD)
    table_ref[50:56] = qkv_v[...].astype(jnp.float32).reshape(6, LANES)


def arrange_kernel(*refs):
    pieces, (keep_ref, send_ref, all_ref) = refs[:4], refs[4:]
    side = lax.axis_index("height")
    layer = lax.axis_index("dp")
    for step, piece in enumerate(pieces):
        all_ref[(layer + 4 - step) % 4] = piece[...]
    for core in range(2):
        keep_ref[core] = all_ref[2 * side + core]
        send_ref[core] = all_ref[2 - 2 * side + core]


def core_taps(core):
    quarter = TAPS / 4
    taps = []
    for tm in (core, core + 2):
        taps += range(int(quarter * tm), min(TAPS, -int(-quarter * (tm + 1) // 1)))
    return taps


def join_kernel(own_ref, side_ref, high_ref, far_ref, lines_ref, wt_ref, all_ref):
    channels, width = own_ref.shape
    inner = wt_ref.shape[1]
    depth = TAPS * inner // 8
    here = lax.axis_index("tm") // 2 * 2 + lax.axis_index("height")
    for flip, ref in enumerate((own_ref, side_ref, high_ref, far_ref)):
        all_ref[here ^ flip] = ref[...]

    def assemble(core):
        for index, tap in enumerate(core_taps(core)):
            rows = slice(index * channels, (index + 1) * channels)
            start, end = tap * inner, (tap + 1) * inner
            while start < end:
                source = start // depth
                stop = min(end, (source + 1) * depth)
                to = slice(start - tap * inner, stop - tap * inner)
                if source // 2 % 2 == core:
                    chip = source // 4 * 2 + source % 2
                    first = start - source * depth
                    wt_ref[rows, to] = all_ref[chip, :, first : first + stop - start]
                else:
                    wt_ref[rows, to] = jnp.zeros((channels, stop - start), jnp.bfloat16)
                start = stop

    core = lax.axis_index("tm") % 2
    pl.when(core == 0)(functools.partial(assemble, 0))
    pl.when(core == 1)(functools.partial(assemble, 1))
    total = sum(all_ref[chip, :, width - 2 * LANES :].astype(jnp.float32) for chip in range(4))
    low = lax.broadcasted_iota(jnp.int32, (8, LANES), 1) < 64
    empty = jnp.zeros((8, LANES), jnp.float32)
    wide, narrow = [], []
    for half in range(2):
        top = 32 * half
        wide.append([total[top + 8 * q : top + 8 * q + 8, LANES:] for q in range(4)])
        some = []
        for q in range(2):
            one = total[top + 16 * q : top + 16 * q + 8, :LANES]
            two = total[top + 16 * q + 8 : top + 16 * q + 16, :LANES]
            some.append(jnp.where(low, pltpu.roll(one, 64, 1), two))
        narrow.append(some + [lines_ref[...] if half == 0 else empty, empty])
    share = jnp.concatenate([jnp.concatenate(row, axis=1) for row in wide + narrow], axis=0)
    wt_ref[wt_ref.shape[0] - 32 :] = share.astype(jnp.bfloat16)


def place_kernel(*refs):
    pieces, x_ref = refs[:4], refs[4]
    place = lax.axis_index("tm") // 2 * 4 + lax.axis_index("height")
    for flip, piece in zip((0, 1, 4, 5), pieces):
        for core in range(2):
            x_ref[(place ^ flip) + 2 * core] = piece[core]


def tap_parts(y_ref, group, channels):
    held = [core_taps(core) for core in range(2)]

    def part(tap, lanes):
        found = []
        for core in range(2):
            if tap in held[core]:
                at = held[core].index(tap) * channels + group * GROUP
                found.append(y_ref[core, at : at + GROUP, lanes])
        return sum(found[1:], found[0])

    return part


def conv_kernel(
    x_ref, wt_ref, pair_ref, scale_ref, w2_ref, out_ref, y_ref
):
    channels = 4 * GROUP
    inner = x_ref.shape[2]
    tiles = x_ref.shape[0] // 2
    count = float(tiles * LANES * GROUP)
    core = lax.axis_index("tm") % 2
    x = x_ref[...].reshape(tiles * LANES, inner)
    height = y_ref.shape[1]
    for ref, at in ((wt_ref, core), (pair_ref, 1 - core)):
        y_ref[at] = lax.dot_general(
            ref[:height], x, (((1,), (1,)), ((), ())), preferred_element_type=jnp.float32
        )
    normed = []
    for group in range(4):
        hidden = tap_sums(tap_parts(y_ref, group, channels), tiles)
        at = slice(group * GROUP, (group + 1) * GROUP)
        mean = jnp.sum(sum(hidden), keepdims=True) / count
        square = jnp.sum(sum(part * part for part in hidden), keepdims=True) / count
        scale = lax.rsqrt(square - mean * mean + norm_eps)
        parts = []
        for part in hidden:
            scaled = (part - mean) * scale * scale_ref[at, 0:1] + scale_ref[at, 1:2]
            parts.append((scaled / (1.0 + jnp.exp(-scaled))).astype(jnp.bfloat16))
        normed.append(jnp.concatenate(parts, axis=1))
    y_ref[0, : TAPS * TILE] = jnp.dot(
        w2_ref[...], jnp.concatenate(normed, axis=0), preferred_element_type=jnp.float32
    )

    def part(tap, lanes):
        return y_ref[0, tap * TILE : (tap + 1) * TILE, lanes]

    low = lax.broadcasted_iota(jnp.int32, (8, LANES), 1) < 64
    layers = out_ref.shape[0] // (2 * tiles)
    for tile, latent in enumerate(tap_sums(part, tiles)):
        turned = pltpu.roll(latent, 64, 1)
        near = jnp.where(low, latent[:8], turned[8:])
        far = jnp.where(low, turned[:8], latent[8:])
        for layer in range(layers):
            out_ref[layer * 2 * tiles + 2 * tile] = near
            out_ref[layer * 2 * tiles + 2 * tile + 1] = far


def share_kernel(m0_ref, m1_ref, m2_ref, m3_ref, table_ref, merged_ref, base_ref, m_ref):
    here = lax.axis_index("tm") // 2 * 2 + lax.axis_index("height")
    lines = table_ref[48:56]
    for flip, ref in enumerate((m0_ref, m1_ref, m2_ref, m3_ref)):
        share = ref[...].astype(jnp.float32)
        m_ref[here ^ flip, :, : 4 * LANES] = share[:16]
        m_ref[here ^ flip, :, 4 * LANES :] = share[16:, : 2 * LANES]
        lines = lines + pltpu.roll(share[16:24, 2 * LANES : 3 * LANES], 2, 0)
    base_ref[...] = jnp.concatenate([lines[2 + part : 3 + part] for part in range(6)], axis=1)
    merged_ref[...] = m_ref[...].reshape(merged_ref.shape).astype(jnp.bfloat16)


def token_kernel(p_ref, m_ref, base_ref, table_ref, lat_ref, q_ref, k_ref, v_ref):
    low = lax.broadcasted_iota(jnp.int32, (8, LANES), 1) < 64
    pairs = []
    for side in range(2):
        one, two = (
            sum(p_ref[4 * index + 2 * core + side] for index in range(p_ref.shape[0] // 4))
            for core in range(2)
        )
        top = jnp.where(low, one, pltpu.roll(two, 64, 1))
        bottom = jnp.where(low, pltpu.roll(one, 64, 1), two)
        pairs.append(jnp.concatenate([top, bottom], axis=0))
    total = jnp.concatenate(pairs, axis=1)
    lat = (total + table_ref[32:48, :1]) * latent_scale
    clips = lat.shape[1] // 64
    tokens = clips * 16
    place = lax.axis_index("dp")
    own = lat[:, :LANES]
    for pair in range(1, clips // 2):
        own = jnp.where(place // 2 == pair, lat[:, pair * LANES : (pair + 1) * LANES], own)
    own = jnp.where(place % 2 == 1, pltpu.roll(own, 64, 1), own)
    turned = own.T[:64]
    wide = jnp.concatenate([turned] * 16, axis=1)
    spot = lax.broadcasted_iota(jnp.int32, wide.shape, 0) % 16
    spread = lax.broadcasted_iota(jnp.int32, wide.shape, 1) // 16
    merged = jnp.sum(jnp.where(spot == spread, wide, 0.0).reshape(4, 16, 256), axis=1)
    lat_ref[0, 0] = merged[:2]
    lat_ref[0, 1] = merged[2:]

    lat_bf = lat.astype(jnp.bfloat16)
    token = lax.broadcasted_iota(jnp.int32, (tokens, clips * 64), 0)
    lane = lax.broadcasted_iota(jnp.int32, (tokens, clips * 64), 1)
    first = token // 8 * 32 + token % 8 * 2
    heads = q_ref.shape[2] // HD
    projected = base_ref[...]
    for a in range(2):
        for e in range(2):
            chosen = jnp.where(lane == first + (16 * a + e), 1.0, 0.0).astype(jnp.bfloat16)
            patch = lax.dot_general(
                chosen, lat_bf, (((1,), (1,)), ((), ())), preferred_element_type=jnp.float32
            ).astype(jnp.bfloat16)
            weight = m_ref[(2 * a + e) * TILE : (2 * a + e + 1) * TILE]
            projected = projected + jnp.dot(patch, weight, preferred_element_type=jnp.float32)

    even = lax.broadcasted_iota(jnp.int32, (tokens, HD), 1) % 2 == 0
    cosine = jnp.concatenate([table_ref[:16]] * clips, axis=0)
    sine = jnp.concatenate([table_ref[16:32]] * clips, axis=0)

    def turn(vectors, gain):
        square = jnp.mean(vectors * vectors, axis=-1, keepdims=True)
        vectors = vectors * lax.rsqrt(square + norm_eps) * gain
        swapped = jnp.where(even, pltpu.roll(vectors, HD - 1, 1), pltpu.roll(vectors, 1, 1))
        return vectors * cosine + swapped * sine

    def keep(ref, head, value):
        value = value.reshape(tokens // 8, 8, HD).astype(jnp.bfloat16)
        ref[:, :, head * HD : (head + 1) * HD] = value

    for head in range(heads):
        at = 3 * HD * head
        keep(q_ref, head, turn(projected[:, at : at + HD], table_ref[48:49]))
        keep(k_ref, head, turn(projected[:, at + HD : at + 2 * HD], table_ref[49:50]))
        keep(v_ref, head, projected[:, at + 2 * HD : at + 3 * HD])


def rope_freqs():
    freqs = []
    for dims in (time_dims, row_dims, row_dims):
        freqs.append(rope_base ** (-np.arange(0, dims, 2, dtype=np.float64) / dims))
    return np.repeat(np.concatenate(freqs), 2)[None].astype(np.float32)


def vmem(count):
    return [pl.BlockSpec(memory_space=pltpu.VMEM)] * count


def grouped(
    clip_inputs,
    conv_in_weight,
    group_gain,
    group_bias,
    conv_out_weight,
    out_bias,
    patch_weight,
    patch_bias,
    qkv_weight,
    qkv_bias,
    q_gain,
    k_gain,
    frame_pos,
    row_pos,
):
    plane_axes = ("tm", "height")
    clips = lax.axis_size("dp")
    steps = lax.axis_size("tm")
    plane = steps * lax.axis_size("height")
    channels = clip_inputs.shape[4]
    depth = conv_in_weight.shape[0]

    width = -(-depth // LANES) * LANES + LANES
    hbm = pl.BlockSpec(memory_space=pltpu.HBM)
    wide = pltpu.CompilerParams(vmem_limit_bytes=60 * 1024 * 1024)
    limit = pltpu.CompilerParams(vmem_limit_bytes=32 * 1024 * 1024)
    small = pl.CostEstimate(flops=10**6, bytes_accessed=10**6, transcendentals=0)
    with jax.named_scope("weight_by_group"):
        weight_block = jax.ShapeDtypeStruct((4 * GROUP, width), jnp.bfloat16)
        *packed, lines = pl.pallas_call(
            pack_kernel,
            out_shape=(weight_block,) * 4 + (jax.ShapeDtypeStruct((8, LANES), jnp.float32),),
            in_specs=[hbm] * 4,
            out_specs=(hbm,) * 4 + (vmem(1)[0],),
            scratch_shapes=[
                pltpu.VMEM(conv_in_weight.shape, jnp.bfloat16),
                pltpu.VMEM(qkv_weight.shape, jnp.bfloat16),
                pltpu.VMEM((patch_weight.shape[0], qkv_weight.shape[0]), jnp.bfloat16),
                pltpu.VMEM(patch_bias.shape, jnp.bfloat16),
                pltpu.VMEM((patch_bias.shape[0] // LANES, LANES), jnp.float32),
                pltpu.VMEM((8 * GROUP, depth), jnp.bfloat16),
                pltpu.VMEM((patch_weight.shape[0], qkv_weight.shape[1]), jnp.float32),
                pltpu.VMEM((4, 4 * GROUP, width), jnp.bfloat16),
                pltpu.SemaphoreType.DMA((8,)),
            ],
            compiler_params=wide,
            cost_estimate=pl.CostEstimate(flops=10**8, bytes_accessed=10**6, transcendentals=0),
            name="pack_weights",
        )(conv_in_weight, qkv_weight, patch_weight, patch_bias)
        blocks = [packed[0]]
        for flip, block in zip((1, 4, 5), packed[1:]):
            blocks.append(lax.ppermute(block, plane_axes, [(i, i ^ flip) for i in range(plane)]))
    with jax.named_scope("gather_clips"):
        own = clip_inputs.reshape(64, channels)
        layers = []
        for step in range(clips):
            pairs = []
            for layer in range(clips):
                for tm in range(steps):
                    to = (layer // 2 * 2 + tm % 2 + step) % clips
                    pairs.append((layer * steps + tm, to * steps + tm // 2 * 2 + layer % 2))
            layers.append(lax.ppermute(own, ("dp", "tm"), pairs))
    with jax.named_scope("spread_clips"):
        keep, send = pl.pallas_call(
            arrange_kernel,
            out_shape=(jax.ShapeDtypeStruct((2, 64, channels), jnp.bfloat16),) * 2,
            in_specs=vmem(4),
            out_specs=tuple(vmem(2)),
            scratch_shapes=[pltpu.VMEM((4, 64, channels), jnp.bfloat16)],
            compiler_params=limit,
            cost_estimate=small,
            name="arrange_clips",
        )(*layers)
        pieces = [keep]
        for flip in (1, 4, 5):
            pairs = [(i, i ^ flip) for i in range(plane)]
            pieces.append(lax.ppermute(send if flip % 2 else keep, plane_axes, pairs))
    with jax.named_scope("small_weights"):
        first = lax.axis_index("tm") // 2 * (4 * GROUP)
        weight_out = lax.dynamic_slice_in_dim(conv_out_weight, first, 4 * GROUP, axis=1)
        weight_out = weight_out.transpose(0, 2, 1).reshape(TAPS * TILE, 4 * GROUP)
        smem = pl.BlockSpec(memory_space=pltpu.SMEM)
        small_arrays = (group_gain, group_bias, out_bias, qkv_bias, q_gain, k_gain)
        scale, table = pl.pallas_call(
            table_kernel,
            out_shape=(
                jax.ShapeDtypeStruct((4 * GROUP, 2), jnp.float32),
                jax.ShapeDtypeStruct((56, LANES), jnp.float32),
            ),
            in_specs=[smem, smem, vmem(1)[0]] + [hbm] * 6,
            out_specs=tuple(vmem(2)),
            scratch_shapes=[pltpu.VMEM(array.shape, array.dtype) for array in small_arrays]
            + [pltpu.SemaphoreType.DMA((6,))],
            compiler_params=wide,
            cost_estimate=small,
            name="tables",
        )(frame_pos, row_pos, rope_freqs(), *small_arrays)
    with jax.named_scope("join_weights"):
        height = len(core_taps(0)) * 4 * GROUP
        joined = pl.pallas_call(
            join_kernel,
            out_shape=jax.ShapeDtypeStruct((height + 32, channels), jnp.bfloat16),
            in_specs=vmem(5),
            out_specs=vmem(1)[0],
            scratch_shapes=[pltpu.VMEM((4, 4 * GROUP, width), jnp.bfloat16)],
            compiler_params=limit,
            cost_estimate=small,
            name="join_weights",
        )(*blocks, lines)
        joined_pair = lax.ppermute(joined, "tm", [(i, i ^ 1) for i in range(steps)])
    with jax.named_scope("merged_projection"):
        share = joined[height:].astype(jnp.float32) + joined_pair[height:].astype(jnp.float32)
        share = share.astype(jnp.bfloat16)
        shares = [share]
        for flip in (1, 4, 5):
            pairs = [(i, i ^ flip) for i in range(plane)]
            shares.append(lax.ppermute(share, plane_axes, pairs))

        merged, base = pl.pallas_call(
            share_kernel,
            out_shape=(
                jax.ShapeDtypeStruct((64, 6 * HD), jnp.bfloat16),
                jax.ShapeDtypeStruct((1, 6 * HD), jnp.float32),
            ),
            in_specs=vmem(5),
            out_specs=tuple(vmem(2)),
            scratch_shapes=[pltpu.VMEM((4, 16, 6 * HD), jnp.float32)],
            compiler_params=limit,
            cost_estimate=small,
            name="share_rows",
        )(*shares, table)

    flops = 4 * height * steps * LANES * channels
    clip = pl.pallas_call(
        place_kernel,
        out_shape=jax.ShapeDtypeStruct((plane, 64, channels), jnp.bfloat16),
        in_specs=vmem(4),
        out_specs=vmem(1)[0],
        compiler_params=limit,
        cost_estimate=pl.CostEstimate(flops=4 * 10**10, bytes_accessed=10**6, transcendentals=0),
        name="place_clip",
    )(*pieces)
    partial = pl.pallas_call(
        conv_kernel,
        out_shape=jax.ShapeDtypeStruct((clips * plane, 8, LANES), jnp.float32),
        in_specs=vmem(5),
        out_specs=vmem(1)[0],
        scratch_shapes=[
            pltpu.VMEM((2, height, steps * LANES), jnp.float32),
        ],
        compiler_params=limit,
        cost_estimate=pl.CostEstimate(flops=flops, bytes_accessed=10**6, transcendentals=0),
        name="convolutions",
    )(clip, joined, joined_pair, scale, weight_out)

    with jax.named_scope("sum_latents"):
        partials = lax.all_to_all(partial, ("dp",) + plane_axes, 0, 0, tiled=True)

    heads = qkv_weight.shape[1] // (3 * HD)
    frames = clip_inputs.shape[1]
    tokens = jax.ShapeDtypeStruct((clips * frames, 8, heads * HD), jnp.bfloat16)
    latents, query, key, value = pl.pallas_call(
        token_kernel,
        out_shape=(jax.ShapeDtypeStruct((1, 2, 2, 256), jnp.float32), tokens, tokens, tokens),
        in_specs=vmem(4),
        out_specs=tuple(vmem(4)),
        compiler_params=limit,
        cost_estimate=pl.CostEstimate(flops=10**8, bytes_accessed=10**6, transcendentals=0),
        name="tokens",
    )(
        partials,
        merged,
        base,
        table,
    )
    full = (clips, frames, 1, 8, heads * HD)
    return latents, query.reshape(full), key.reshape(full), value.reshape(full)


def pick(mesh, *arrays):
    if one_group_each(mesh, arrays[0], arrays[1], arrays[4], arrays[8]):
        return grouped(*arrays)
    return shards(*arrays)


def solution(mesh):
    placed = (
        P("dp", "tm", "height", None, None),
        P(("tm", "height"), "dp"),
        P("dp"),
        P("dp"),
        P(None, "dp", None),
        P(),
        P(),
        P(),
        P(("tm", "height"), "dp"),
        P("dp"),
        P(),
        P(),
        P("tm"),
        P("height"),
    )
    return jax.shard_map(
        functools.partial(pick, mesh),
        mesh=mesh,
        in_specs=placed,
        out_specs=(
            P("dp", "tm", "height", None),
            P(None, "tm", "height", None, "dp"),
            P(None, "tm", "height", None, "dp"),
            P(None, "tm", "height", None, "dp"),
        ),
        check_vma=False,
    )
```

```python
import functools

import jax
import jax.numpy as jnp
import numpy as np
from jax import lax
from jax.experimental import pallas as pl
from jax.experimental.pallas import tpu as pltpu
from jax.sharding import PartitionSpec as P

HD = 128
GROUPS = 32
TAPS = 27


norm_eps = 1e-06
latent_scale = 0.476986
rope_base = 256.0
time_dims = 16
row_dims = 56


def from_behind(value, axis, steps):
    count = lax.axis_size(axis)
    first, last = (max(0, -steps), min(count, count - steps))
    return lax.ppermute(value, axis, [(source, source + steps) for source in range(first, last)])


def padded_2(block, sides, width):
    for axis, dim in sides:
        count = lax.axis_size(axis)
        forward = [(i, i + 1) for i in range(count - 1)]
        backward = [(target, source) for source, target in forward]
        low = lax.ppermute(
            lax.slice_in_dim(block, block.shape[dim] - width, None, axis=dim), axis, forward
        )
        high = lax.ppermute(lax.slice_in_dim(block, 0, width, axis=dim), axis, backward)
        block = jnp.concatenate([low, block, high], axis=dim)
    return block


def repeat_first(block):
    return jnp.concatenate([block[:, :1], block[:, :1]], axis=1)


def time_join(block, earlier):
    start = jnp.where(lax.axis_index("tm") == 0, repeat_first(block), earlier)
    return jnp.concatenate([start, block], axis=1)


def rows_finish(grown):
    place = lax.axis_index("height")
    top = jnp.where(place == 0, grown[:, :, 1:2], grown[:, :, :1])
    bottom = jnp.where(place == lax.axis_size("height") - 1, grown[:, :, -2:-1], grown[:, :, -1:])
    inner = jnp.concatenate([top, grown[:, :, 1:-1], bottom], axis=2)
    return jnp.pad(inner, ((0, 0), (0, 0), (0, 0), (1, 1), (0, 0)), mode="edge")


def edges_before(block):
    earlier = from_behind(block, "tm", 1)
    longer = time_join(block, earlier)
    return rows_finish(padded_2(longer, (("height", 2),), 1))


def edges_norm(block):
    earlier = from_behind(block, "tm", 1)
    longer = time_join(block, earlier)
    return rows_finish(padded_2(longer, (("height", 2),), 1))


def convolve(padded, weight):
    clips = padded.shape[0]
    frames = padded.shape[1] - 2
    rows = padded.shape[2] - 2
    cols = padded.shape[3] - 2
    total = jnp.zeros((clips * frames * rows * cols, weight.shape[2]), jnp.float32)
    for shift_t in range(3):
        for shift_r in range(3):
            for shift_c in range(3):
                window = padded[
                    :,
                    shift_t : shift_t + frames,
                    shift_r : shift_r + rows,
                    shift_c : shift_c + cols,
                ]
                window = window.reshape(-1, padded.shape[4])
                total = total + jnp.dot(
                    window,
                    weight[9 * shift_t + 3 * shift_r + shift_c],
                    preferred_element_type=jnp.float32,
                )
    return total.reshape(clips, frames, rows, cols, weight.shape[2])


def section_freqs(dims):
    return jnp.power(rope_base, -jnp.arange(0, dims, 2, dtype=jnp.float32) / dims)


def rope_angles(tpos, hpos, width):
    frames = tpos.shape[0]
    rows = hpos.shape[0]
    cols = jnp.arange(width, dtype=jnp.float32)
    part_t = tpos[:, None, None, None] * section_freqs(time_dims)
    part_h = hpos[None, :, None, None] * section_freqs(row_dims)
    part_w = cols[None, None, :, None] * section_freqs(row_dims)
    shape = (frames, rows, width)
    return jnp.concatenate(
        [
            jnp.broadcast_to(part_t, shape + (time_dims // 2,)),
            jnp.broadcast_to(part_h, shape + (row_dims // 2,)),
            jnp.broadcast_to(part_w, shape + (row_dims // 2,)),
        ],
        axis=-1,
    )


def rotate(vectors, angles):
    pairs = vectors.reshape(vectors.shape[:-1] + (vectors.shape[-1] // 2, 2))
    first = pairs[..., 0]
    second = pairs[..., 1]
    cosine = jnp.cos(angles)[..., None, :]
    sine = jnp.sin(angles)[..., None, :]
    turned = jnp.stack([first * cosine - second * sine, first * sine + second * cosine], axis=-1)
    return turned.reshape(vectors.shape)


def rms_scale(vectors, gain):
    return (
        vectors
        * lax.rsqrt(jnp.mean(vectors * vectors, axis=-1, keepdims=True) + norm_eps)
        * gain.astype(jnp.float32)
    )


def shards(
    clip_inputs,
    conv_in_weight,
    group_gain,
    group_bias,
    conv_out_weight,
    out_bias,
    patch_weight,
    patch_bias,
    qkv_weight,
    qkv_bias,
    q_gain,
    k_gain,
    frame_pos,
    row_pos,
):
    channels = clip_inputs.shape[4]
    frames = clip_inputs.shape[1]
    rows = clip_inputs.shape[2]
    cols = clip_inputs.shape[3]
    padded = lax.all_gather(edges_before(clip_inputs), "dp", axis=0, tiled=True)
    clips = padded.shape[0]
    weight_in = lax.all_gather(conv_in_weight, ("tm", "height"), axis=0, tiled=True).reshape(
        TAPS, channels, -1
    )
    hidden = convolve(padded, weight_in)
    block_width = hidden.shape[4]
    group_width = channels // GROUPS
    local_groups = block_width // group_width
    grouped = hidden.reshape(clips, -1, local_groups, group_width)
    sums_local = jnp.sum(grouped, axis=(1, 3))
    squares_local = jnp.sum(grouped * grouped, axis=(1, 3))
    sums_all, squares_all = lax.psum((sums_local, squares_local), ("tm", "height"))
    count = float(
        frames * lax.axis_size("tm") * rows * lax.axis_size("height") * cols * group_width
    )
    mean = sums_all / count
    var = squares_all / count - mean * mean
    scaled = (grouped - mean[:, None, :, None]) * lax.rsqrt(var + norm_eps)[:, None, :, None]
    scaled = scaled.reshape(hidden.shape) * group_gain.astype(jnp.float32) + group_bias.astype(
        jnp.float32
    )
    normed = jax.nn.silu(scaled).astype(jnp.bfloat16)
    partial_latent = convolve(edges_norm(normed), conv_out_weight)
    own_sum = lax.psum_scatter(partial_latent, "dp", scatter_dimension=0, tiled=True)
    own_latent = (own_sum + out_bias) * latent_scale
    every_latent = lax.all_gather(own_latent.astype(jnp.bfloat16), "dp", axis=0, tiled=True)
    latent_dims = every_latent.shape[4]
    latents = own_latent.reshape(1, frames, rows, cols * latent_dims)
    tok_rows = rows // 2
    tok_cols = cols // 2
    patches = every_latent.reshape(clips, frames, tok_rows, 2, tok_cols, 2, latent_dims)
    patches = patches.transpose(0, 1, 2, 4, 3, 5, 6).reshape(-1, 4 * latent_dims)
    embedded = (
        jnp.dot(patches, patch_weight, preferred_element_type=jnp.float32)
        + patch_bias.astype(jnp.float32)
    ).astype(jnp.bfloat16)
    projected = jnp.dot(
        embedded,
        lax.all_gather(qkv_weight, ("tm", "height"), axis=0, tiled=True),
        preferred_element_type=jnp.float32,
    )
    projected = projected + qkv_bias.astype(jnp.float32)
    local_heads = qkv_weight.shape[1] // (3 * HD)
    projected = projected.reshape(clips, frames, tok_rows, tok_cols, local_heads, 3, HD)
    angles = rope_angles(frame_pos.astype(jnp.float32), row_pos.astype(jnp.float32), tok_cols)
    query = rotate(rms_scale(projected[..., 0, :], q_gain), angles)
    key = rotate(rms_scale(projected[..., 1, :], k_gain), angles)
    value = projected[..., 2, :]
    merged = (clips, frames, tok_rows, tok_cols, local_heads * HD)
    return (
        latents,
        query.reshape(merged).astype(jnp.bfloat16),
        key.reshape(merged).astype(jnp.bfloat16),
        value.reshape(merged).astype(jnp.bfloat16),
    )


LANES = 128
TILE = 16
GROUP = 16


def one_group_each(mesh, clip_inputs, conv_in_weight, conv_out_weight, qkv_weight):
    plane = mesh.shape["tm"] * mesh.shape["height"]
    return (
        clip_inputs.shape[:4] == (1, 2, 2, 16)
        and mesh.shape["height"] == 2
        and mesh.shape["tm"] == 4
        and mesh.shape["dp"] == 4
        and conv_in_weight.shape[1] == plane * GROUP
        and clip_inputs.shape[4] == GROUP * GROUPS
        and conv_out_weight.shape[2] == TILE
        and qkv_weight.shape[1] == 6 * HD
    )


def lane_shifts(lane):
    col = lane % 16
    row = lane // 16 % 2
    half = lane // 64

    def cols(left, mid, right):
        left = jnp.where(col == 0, left, pltpu.roll(left, 1, 1))
        right = jnp.where(col == 15, right, pltpu.roll(right, LANES - 1, 1))
        return mid + left + right

    def rows(up, mid, down):
        up = jnp.where(
            row == 1, pltpu.roll(up, 16, 1), jnp.where(half == 1, pltpu.roll(up, 48, 1), up)
        )
        down = jnp.where(
            row == 0,
            pltpu.roll(down, LANES - 16, 1),
            jnp.where(half == 0, pltpu.roll(down, LANES - 48, 1), down),
        )
        return mid + up + down

    return cols, rows


def tap_sums(source, tiles):
    lane = lax.broadcasted_iota(jnp.int32, (TILE, LANES), 1)
    second = lane // 32 % 2 == 1
    cols, rows = lane_shifts(lane)
    sums = []
    before = None
    for tile in range(tiles):

        def part(tap):
            return source(tap, slice(tile * LANES, (tile + 1) * LANES))

        oldest, older, now = (
            rows(*(cols(*(part(9 * i + 3 * j + l) for l in range(3))) for j in range(3)))
            for i in range(3)
        )
        turned = pltpu.roll(older, 32, 1)
        if before is None:
            start = jnp.where(second, pltpu.roll(oldest, 32, 1), oldest)
            total = now + jnp.where(second, turned, older) + start
        else:
            total = now + jnp.where(second, turned, pltpu.roll(before[1], 96, 1)) + before[0]
        before = (oldest, older)
        sums.append(total)
    return sums


def pack_kernel(
    w_hbm, qkv_hbm, patch_hbm, patch_bias_hbm, own_hbm, side_hbm, high_hbm, far_hbm,
    w_ref, qkv_ref, patch_ref, patch_bias_ref, rows_ref, turned_ref, merged_ref, out_ref, lines_ref, sems,
):
    _, channels, width = out_ref.shape
    depth = w_ref.shape[0]
    rows = qkv_ref.shape[0]
    side = lax.axis_index("height")
    high = lax.axis_index("tm") // 2
    place = lax.axis_index("tm") * 2 + side
    at = pl.ds(pl.multiple_of(place * rows, LANES), rows)
    loads = [
        pltpu.make_async_copy(w_hbm, w_ref, sems.at[0]),
        pltpu.make_async_copy(qkv_hbm, qkv_ref, sems.at[1]),
        pltpu.make_async_copy(patch_hbm.at[:, at], patch_ref, sems.at[2]),
        pltpu.make_async_copy(patch_bias_hbm, patch_bias_ref, sems.at[3]),
    ]
    for load in loads:
        load.start()
    whole = depth // LANES * LANES
    loads[0].wait()
    turned_ref[...] = w_ref[...].T
    for load in loads[1:]:
        load.wait()
    merged_ref[...] = jnp.dot(patch_ref[...], qkv_ref[...], preferred_element_type=jnp.float32)
    stores = []
    own_main = own_hbm.at[:, :width]
    for flip, out_hbm in ((1, side_hbm), (2, high_hbm), (3, far_hbm), (0, own_main)):
        first = pl.multiple_of((high ^ (flip // 2)) * channels, channels)
        out_ref[flip, :, :whole] = turned_ref[pl.ds(first, channels), :whole]
        lower = turned_ref[pl.ds(first, channels), whole:]
        chip = (2 * high + side) ^ flip
        tail, upper = [], []
        for half in range(2):
            mine = merged_ref[pl.ds(pl.multiple_of(chip * 16 + half * 8, 8), 8)]
            mine = [mine[:, q * LANES : (q + 1) * LANES] for q in range(6)]
            tail += mine[:4]
            upper += [pltpu.roll(mine[4], 64, 1), mine[4], pltpu.roll(mine[5], 64, 1), mine[5]]
        upper = jnp.concatenate(upper, axis=0)[:, 64:].astype(jnp.bfloat16)
        out_ref[flip, :, whole : whole + LANES] = jnp.concatenate([lower, upper], axis=1)
        out_ref[flip, :, whole + LANES :] = jnp.concatenate(tail, axis=0).astype(jnp.bfloat16)
        stores.append(pltpu.make_async_copy(out_ref.at[flip], out_hbm, sems.at[4 + flip]))
        stores[-1].start()
    rows_ref[...] = patch_bias_ref[...].astype(jnp.float32).reshape(rows_ref.shape)
    count = rows // LANES
    bias = [rows_ref[pl.ds(count * place + part, 1), :] for part in range(count)]
    bias = jnp.broadcast_to(jnp.concatenate(bias, axis=1), (8, rows)).astype(jnp.bfloat16)
    bias = jnp.dot(bias, qkv_ref[...], preferred_element_type=jnp.float32)
    line = lax.broadcasted_iota(jnp.int32, (8, LANES), 0)
    lines = jnp.zeros((8, LANES), jnp.float32)
    for part in range(bias.shape[1] // LANES):
        lines = jnp.where(line == part, bias[:, part * LANES : (part + 1) * LANES], lines)
    lines_ref[...] = jnp.concatenate([lines, jnp.zeros_like(lines)], axis=0).astype(jnp.bfloat16)
    stores.append(
        pltpu.make_async_copy(lines_ref, own_hbm.at[:16, width : width + LANES], sems.at[8])
    )
    stores[-1].start()
    for store in stores:
        store.wait()


def column(row_ref, first, size):
    length = row_ref.shape[0]
    row = row_ref[...].astype(jnp.float32).reshape(1, length)
    line = lax.broadcasted_iota(jnp.int32, (size, length), 0)
    lane = lax.broadcasted_iota(jnp.int32, (size, length), 1)
    picked = jnp.where(lane == line + first, jnp.broadcast_to(row, (size, length)), 0.0)
    return jnp.sum(picked, axis=1, keepdims=True)


def table_kernel(
    frame_ref, row_pos_ref, freq_ref, gain_hbm, bias_hbm, out_bias_hbm, qkv_hbm, q_hbm, k_hbm,
    scale_ref, table_ref, flag_ref,
    gain_v, bias_v, out_bias_v, qkv_v, q_v, k_v, sems,
):
    pairs = (
        (gain_hbm, gain_v), (bias_hbm, bias_v), (out_bias_hbm, out_bias_v),
        (qkv_hbm, qkv_v), (q_hbm, q_v), (k_hbm, k_v),
    )
    loads = [
        pltpu.make_async_copy(source, to, sems.at[index])
        for index, (source, to) in enumerate(pairs)
    ]
    for load in loads:
        load.start()
    flag_ref[0] = frame_ref[0]
    shape = (TILE, LANES)
    line = lax.broadcasted_iota(jnp.int32, shape, 0)
    lane = lax.broadcasted_iota(jnp.int32, shape, 1)
    frame = jnp.where(line // 8 == 0, frame_ref[0], frame_ref[1]).astype(jnp.float32)
    row = jnp.broadcast_to(row_pos_ref[0], shape).astype(jnp.float32)
    spot = jnp.where(lane < 72, row, (line % 8).astype(jnp.float32))
    angles = jnp.where(lane < 16, frame, spot) * freq_ref[...]
    table_ref[:16] = jnp.cos(angles)
    sine = jnp.sin(angles)
    table_ref[16:32] = jnp.where(lane % 2 == 0, -sine, sine)
    for load in loads:
        load.wait()
    first = lax.axis_index("tm") // 2 * (4 * GROUP)
    scale_ref[:, 0:1] = column(gain_v, first, 4 * GROUP)
    scale_ref[:, 1:2] = column(bias_v, first, 4 * GROUP)
    table_ref[32:48] = jnp.broadcast_to(column(out_bias_v, 0, TILE), shape)
    table_ref[48:49] = q_v[...].astype(jnp.float32).reshape(1, HD)
    table_ref[49:50] = k_v[...].astype(jnp.float32).reshape(1, HD)
    table_ref[50:56] = qkv_v[...].astype(jnp.float32).reshape(6, LANES)


def arrange_kernel(*refs):
    pieces, (_, keep_ref, send_ref, all_ref) = refs[:4], refs[4:]
    side = lax.axis_index("height")
    layer = lax.axis_index("dp")
    for step, piece in enumerate(pieces):
        all_ref[(layer + 4 - step) % 4] = piece[...]
    for core in range(2):
        keep_ref[core] = all_ref[2 * side + core]
        send_ref[core] = all_ref[2 - 2 * side + core]


def core_taps(core):
    quarter = TAPS / 4
    taps = []
    for tm in (core, core + 2):
        taps += range(int(quarter * tm), min(TAPS, -int(-quarter * (tm + 1) // 1)))
    return taps


def join_kernel(own_ref, side_ref, high_ref, far_ref, wt_ref, all_ref):
    channels, width = side_ref.shape
    inner = wt_ref.shape[1]
    depth = TAPS * inner // 8
    here = lax.axis_index("tm") // 2 * 2 + lax.axis_index("height")
    for flip, ref in enumerate((own_ref, side_ref, high_ref, far_ref)):
        all_ref[here ^ flip] = ref[:, :width]

    def assemble(core):
        for index, tap in enumerate(core_taps(core)):
            rows = slice(index * channels, (index + 1) * channels)
            start, end = tap * inner, (tap + 1) * inner
            while start < end:
                source = start // depth
                stop = min(end, (source + 1) * depth)
                to = slice(start - tap * inner, stop - tap * inner)
                if source // 2 % 2 == core:
                    chip = source // 4 * 2 + source % 2
                    first = start - source * depth
                    wt_ref[rows, to] = all_ref[chip, :, first : first + stop - start]
                else:
                    wt_ref[rows, to] = jnp.zeros((channels, stop - start), jnp.bfloat16)
                start = stop

    core = lax.axis_index("tm") % 2
    pl.when(core == 0)(functools.partial(assemble, 0))
    pl.when(core == 1)(functools.partial(assemble, 1))
    total = sum(all_ref[chip, :, width - 2 * LANES :].astype(jnp.float32) for chip in range(4))
    low = lax.broadcasted_iota(jnp.int32, (8, LANES), 1) < 64
    empty = jnp.zeros((8, LANES), jnp.float32)
    wide, narrow = [], []
    for half in range(2):
        top = 32 * half
        wide.append([total[top + 8 * q : top + 8 * q + 8, LANES:] for q in range(4)])
        some = []
        for q in range(2):
            one = total[top + 16 * q : top + 16 * q + 8, :LANES]
            two = total[top + 16 * q + 8 : top + 16 * q + 16, :LANES]
            some.append(jnp.where(low, pltpu.roll(one, 64, 1), two))
        lines = own_ref[:16, width:].astype(jnp.float32)[8 * half : 8 * half + 8]
        narrow.append(some + [lines, empty])
    share = jnp.concatenate([jnp.concatenate(row, axis=1) for row in wide + narrow], axis=0)
    wt_ref[wt_ref.shape[0] - 32 :] = share.astype(jnp.bfloat16)


def place_kernel(*refs):
    pieces, (turned_ref, x_ref) = refs[:4], refs[4:]
    place = lax.axis_index("tm") // 2 * 4 + lax.axis_index("height")
    for flip, piece in zip((0, 1, 4, 5), pieces):
        for core in range(2):
            x_ref[(place ^ flip) + 2 * core] = piece[core]
    turned_ref[...] = x_ref[...].reshape(turned_ref.shape[1], turned_ref.shape[0]).T


def tap_parts(y_ref, group, channels):
    held = [core_taps(core) for core in range(2)]

    def part(tap, lanes):
        found = []
        for core in range(2):
            if tap in held[core]:
                at = held[core].index(tap) * channels + group * GROUP
                found.append(y_ref[core, at : at + GROUP, lanes])
        return sum(found[1:], found[0])

    return part


def conv_kernel(
    x_ref, wt_ref, pair_ref, scale_ref, w2_ref, out_ref, y_ref
):
    channels = 4 * GROUP
    tiles = x_ref.shape[1] // LANES
    count = float(tiles * LANES * GROUP)
    core = lax.axis_index("tm") % 2
    height = y_ref.shape[1]
    for ref, at in ((wt_ref, core), (pair_ref, 1 - core)):
        y_ref[at] = jnp.dot(ref[:height], x_ref[...], preferred_element_type=jnp.float32)
    normed = []
    for group in range(4):
        hidden = tap_sums(tap_parts(y_ref, group, channels), tiles)
        at = slice(group * GROUP, (group + 1) * GROUP)
        mean = jnp.sum(sum(hidden), keepdims=True) / count
        square = jnp.sum(sum(part * part for part in hidden), keepdims=True) / count
        scale = lax.rsqrt(square - mean * mean + norm_eps)
        parts = []
        for part in hidden:
            scaled = (part - mean) * scale * scale_ref[at, 0:1] + scale_ref[at, 1:2]
            parts.append((scaled / (1.0 + jnp.exp(-scaled))).astype(jnp.bfloat16))
        normed.append(jnp.concatenate(parts, axis=1))
    y_ref[0, : TAPS * TILE] = jnp.dot(
        w2_ref[...], jnp.concatenate(normed, axis=0), preferred_element_type=jnp.float32
    )

    def part(tap, lanes):
        return y_ref[0, tap * TILE : (tap + 1) * TILE, lanes]

    low = lax.broadcasted_iota(jnp.int32, (8, LANES), 1) < 64
    layers = out_ref.shape[0] // (2 * tiles)
    for tile, latent in enumerate(tap_sums(part, tiles)):
        turned = pltpu.roll(latent, 64, 1)
        near = jnp.where(low, latent[:8], turned[8:])
        far = jnp.where(low, turned[:8], latent[8:])
        for layer in range(layers):
            out_ref[layer * 2 * tiles + 2 * tile] = near
            out_ref[layer * 2 * tiles + 2 * tile + 1] = far


def share_kernel(m0_ref, m1_ref, m2_ref, m3_ref, table_ref, merged_ref, base_ref, m_ref):
    here = lax.axis_index("tm") // 2 * 2 + lax.axis_index("height")
    lines = table_ref[48:56]
    for flip, ref in enumerate((m0_ref, m1_ref, m2_ref, m3_ref)):
        share = ref[...].astype(jnp.float32)
        m_ref[here ^ flip, :, : 4 * LANES] = share[:16]
        m_ref[here ^ flip, :, 4 * LANES :] = share[16:, : 2 * LANES]
        lines = lines + pltpu.roll(share[16:24, 2 * LANES : 3 * LANES], 2, 0)
    base_ref[...] = jnp.concatenate([lines[2 + part : 3 + part] for part in range(6)], axis=1)
    merged_ref[...] = m_ref[...].reshape(merged_ref.shape).astype(jnp.bfloat16)


def token_kernel(p_ref, m_ref, base_ref, table_ref, lat_ref, q_ref, k_ref, v_ref):
    low = lax.broadcasted_iota(jnp.int32, (8, LANES), 1) < 64
    pairs = []
    for side in range(2):
        one, two = (
            sum(p_ref[4 * index + 2 * core + side] for index in range(p_ref.shape[0] // 4))
            for core in range(2)
        )
        top = jnp.where(low, one, pltpu.roll(two, 64, 1))
        bottom = jnp.where(low, pltpu.roll(one, 64, 1), two)
        pairs.append(jnp.concatenate([top, bottom], axis=0))
    total = jnp.concatenate(pairs, axis=1)
    lat = (total + table_ref[32:48, :1]) * latent_scale
    clips = lat.shape[1] // 64
    tokens = clips * 16
    place = lax.axis_index("dp")
    own = lat[:, :LANES]
    for pair in range(1, clips // 2):
        own = jnp.where(place // 2 == pair, lat[:, pair * LANES : (pair + 1) * LANES], own)
    own = jnp.where(place % 2 == 1, pltpu.roll(own, 64, 1), own)
    turned = own.T[:64]
    wide = jnp.concatenate([turned] * 16, axis=1)
    spot = lax.broadcasted_iota(jnp.int32, wide.shape, 0) % 16
    spread = lax.broadcasted_iota(jnp.int32, wide.shape, 1) // 16
    merged = jnp.sum(jnp.where(spot == spread, wide, 0.0).reshape(4, 16, 256), axis=1)
    lat_ref[0, 0] = merged[:2]
    lat_ref[0, 1] = merged[2:]

    lat_bf = lat.astype(jnp.bfloat16)
    token = lax.broadcasted_iota(jnp.int32, (tokens, clips * 64), 0)
    lane = lax.broadcasted_iota(jnp.int32, (tokens, clips * 64), 1)
    first = token // 8 * 32 + token % 8 * 2
    heads = q_ref.shape[2] // HD
    projected = base_ref[...]
    for a in range(2):
        for e in range(2):
            chosen = jnp.where(lane == first + (16 * a + e), 1.0, 0.0).astype(jnp.bfloat16)
            patch = lax.dot_general(
                chosen, lat_bf, (((1,), (1,)), ((), ())), preferred_element_type=jnp.float32
            ).astype(jnp.bfloat16)
            weight = m_ref[(2 * a + e) * TILE : (2 * a + e + 1) * TILE]
            projected = projected + jnp.dot(patch, weight, preferred_element_type=jnp.float32)

    even = lax.broadcasted_iota(jnp.int32, (tokens, HD), 1) % 2 == 0
    cosine = jnp.concatenate([table_ref[:16]] * clips, axis=0)
    sine = jnp.concatenate([table_ref[16:32]] * clips, axis=0)

    def turn(vectors, gain):
        square = jnp.mean(vectors * vectors, axis=-1, keepdims=True)
        vectors = vectors * lax.rsqrt(square + norm_eps) * gain
        swapped = jnp.where(even, pltpu.roll(vectors, HD - 1, 1), pltpu.roll(vectors, 1, 1))
        return vectors * cosine + swapped * sine

    def keep(ref, head, value):
        value = value.reshape(tokens // 8, 8, HD).astype(jnp.bfloat16)
        ref[:, :, head * HD : (head + 1) * HD] = value

    for head in range(heads):
        at = 3 * HD * head
        keep(q_ref, head, turn(projected[:, at : at + HD], table_ref[48:49]))
        keep(k_ref, head, turn(projected[:, at + HD : at + 2 * HD], table_ref[49:50]))
        keep(v_ref, head, projected[:, at + 2 * HD : at + 3 * HD])


def rope_freqs():
    freqs = []
    for dims in (time_dims, row_dims, row_dims):
        freqs.append(rope_base ** (-np.arange(0, dims, 2, dtype=np.float64) / dims))
    return np.repeat(np.concatenate(freqs), 2)[None].astype(np.float32)


def vmem(count):
    return [pl.BlockSpec(memory_space=pltpu.VMEM)] * count


def grouped(
    clip_inputs,
    conv_in_weight,
    group_gain,
    group_bias,
    conv_out_weight,
    out_bias,
    patch_weight,
    patch_bias,
    qkv_weight,
    qkv_bias,
    q_gain,
    k_gain,
    frame_pos,
    row_pos,
):
    plane_axes = ("tm", "height")
    clips = lax.axis_size("dp")
    steps = lax.axis_size("tm")
    plane = steps * lax.axis_size("height")
    channels = clip_inputs.shape[4]
    depth = conv_in_weight.shape[0]

    width = -(-depth // LANES) * LANES + LANES
    hbm = pl.BlockSpec(memory_space=pltpu.HBM)
    wide = pltpu.CompilerParams(vmem_limit_bytes=60 * 1024 * 1024)
    limit = pltpu.CompilerParams(vmem_limit_bytes=32 * 1024 * 1024)
    small = pl.CostEstimate(flops=10**6, bytes_accessed=10**6, transcendentals=0)
    with jax.named_scope("weight_by_group"):
        weight_block = jax.ShapeDtypeStruct((4 * GROUP, width), jnp.bfloat16)
        own_block = jax.ShapeDtypeStruct((4 * GROUP, width + LANES), jnp.bfloat16)
        packed = pl.pallas_call(
            pack_kernel,
            out_shape=(own_block,) + (weight_block,) * 3,
            in_specs=[hbm] * 4,
            out_specs=(hbm,) * 4,
            scratch_shapes=[
                pltpu.VMEM(conv_in_weight.shape, jnp.bfloat16),
                pltpu.VMEM(qkv_weight.shape, jnp.bfloat16),
                pltpu.VMEM((patch_weight.shape[0], qkv_weight.shape[0]), jnp.bfloat16),
                pltpu.VMEM(patch_bias.shape, jnp.bfloat16),
                pltpu.VMEM((patch_bias.shape[0] // LANES, LANES), jnp.float32),
                pltpu.VMEM((8 * GROUP, depth), jnp.bfloat16),
                pltpu.VMEM((patch_weight.shape[0], qkv_weight.shape[1]), jnp.float32),
                pltpu.VMEM((4, 4 * GROUP, width), jnp.bfloat16),
                pltpu.VMEM((16, LANES), jnp.bfloat16),
                pltpu.SemaphoreType.DMA((9,)),
            ],
            compiler_params=wide,
            cost_estimate=pl.CostEstimate(flops=10**8, bytes_accessed=10**6, transcendentals=0),
            name="pack_weights",
        )(conv_in_weight, qkv_weight, patch_weight, patch_bias)
        blocks = [packed[0]]
        for flip, block in zip((1, 4, 5), packed[1:]):
            blocks.append(lax.ppermute(block, plane_axes, [(i, i ^ flip) for i in range(plane)]))
    with jax.named_scope("tables"):
        smem = pl.BlockSpec(memory_space=pltpu.SMEM)
        small_arrays = (group_gain, group_bias, out_bias, qkv_bias, q_gain, k_gain)
        scale, table, flag = pl.pallas_call(
            table_kernel,
            out_shape=(
                jax.ShapeDtypeStruct((4 * GROUP, 2), jnp.float32),
                jax.ShapeDtypeStruct((56, LANES), jnp.float32),
                jax.ShapeDtypeStruct((1,), jnp.int32),
            ),
            in_specs=[smem, smem, vmem(1)[0]] + [hbm] * 6,
            out_specs=tuple(vmem(2)) + (smem,),
            scratch_shapes=[pltpu.VMEM(array.shape, array.dtype) for array in small_arrays]
            + [pltpu.SemaphoreType.DMA((6,))],
            compiler_params=wide,
            cost_estimate=small,
            name="tables",
        )(frame_pos, row_pos, rope_freqs(), *small_arrays)
    with jax.named_scope("gather_clips"):
        own = clip_inputs.reshape(64, channels)
        layers = []
        for step in range(clips):
            pairs = []
            for layer in range(clips):
                for tm in range(steps):
                    to = (layer // 2 * 2 + tm % 2 + step) % clips
                    pairs.append((layer * steps + tm, to * steps + tm // 2 * 2 + layer % 2))
            layers.append(lax.ppermute(own, ("dp", "tm"), pairs))
    with jax.named_scope("spread_clips"):
        keep, send = pl.pallas_call(
            arrange_kernel,
            out_shape=(jax.ShapeDtypeStruct((2, 64, channels), jnp.bfloat16),) * 2,
            in_specs=vmem(4) + [smem],
            out_specs=tuple(vmem(2)),
            scratch_shapes=[pltpu.VMEM((4, 64, channels), jnp.bfloat16)],
            compiler_params=limit,
            cost_estimate=small,
            name="arrange_clips",
        )(*layers, flag)
        pieces = [keep]
        for flip in (1, 4, 5):
            pairs = [(i, i ^ flip) for i in range(plane)]
            pieces.append(lax.ppermute(send if flip % 2 else keep, plane_axes, pairs))
    with jax.named_scope("small_weights"):
        first = lax.axis_index("tm") // 2 * (4 * GROUP)
        weight_out = lax.dynamic_slice_in_dim(conv_out_weight, first, 4 * GROUP, axis=1)
        weight_out = weight_out.transpose(0, 2, 1).reshape(TAPS * TILE, 4 * GROUP)
    with jax.named_scope("join_weights"):
        height = len(core_taps(0)) * 4 * GROUP
        joined = pl.pallas_call(
            join_kernel,
            out_shape=jax.ShapeDtypeStruct((height + 32, channels), jnp.bfloat16),
            in_specs=vmem(4),
            out_specs=vmem(1)[0],
            scratch_shapes=[pltpu.VMEM((4, 4 * GROUP, width), jnp.bfloat16)],
            compiler_params=limit,
            cost_estimate=small,
            name="join_weights",
        )(*blocks)
        joined_pair = lax.ppermute(joined, "tm", [(i, i ^ 1) for i in range(steps)])
    with jax.named_scope("merged_projection"):
        share = joined[height:].astype(jnp.float32) + joined_pair[height:].astype(jnp.float32)
        share = share.astype(jnp.bfloat16)
        shares = [share]
        for flip in (1, 4, 5):
            pairs = [(i, i ^ flip) for i in range(plane)]
            shares.append(lax.ppermute(share, plane_axes, pairs))

        merged, base = pl.pallas_call(
            share_kernel,
            out_shape=(
                jax.ShapeDtypeStruct((64, 6 * HD), jnp.bfloat16),
                jax.ShapeDtypeStruct((1, 6 * HD), jnp.float32),
            ),
            in_specs=vmem(5),
            out_specs=tuple(vmem(2)),
            scratch_shapes=[pltpu.VMEM((4, 16, 6 * HD), jnp.float32)],
            compiler_params=limit,
            cost_estimate=small,
            name="share_rows",
        )(*shares, table)

    flops = 4 * height * steps * LANES * channels
    clip = pl.pallas_call(
        place_kernel,
        out_shape=jax.ShapeDtypeStruct((channels, plane * 64), jnp.bfloat16),
        in_specs=vmem(4),
        out_specs=vmem(1)[0],
        scratch_shapes=[pltpu.VMEM((plane, 64, channels), jnp.bfloat16)],
        compiler_params=limit,
        cost_estimate=pl.CostEstimate(flops=4 * 10**10, bytes_accessed=10**6, transcendentals=0),
        name="place_clip",
    )(*pieces)
    partial = pl.pallas_call(
        conv_kernel,
        out_shape=jax.ShapeDtypeStruct((clips * plane, 8, LANES), jnp.float32),
        in_specs=vmem(5),
        out_specs=vmem(1)[0],
        scratch_shapes=[
            pltpu.VMEM((2, height, steps * LANES), jnp.float32),
        ],
        compiler_params=limit,
        cost_estimate=pl.CostEstimate(flops=flops, bytes_accessed=10**6, transcendentals=0),
        name="convolutions",
    )(clip, joined, joined_pair, scale, weight_out)

    with jax.named_scope("sum_latents"):
        partials = lax.all_to_all(partial, ("dp",) + plane_axes, 0, 0, tiled=True)

    heads = qkv_weight.shape[1] // (3 * HD)
    frames = clip_inputs.shape[1]
    tokens = jax.ShapeDtypeStruct((clips * frames, 8, heads * HD), jnp.bfloat16)
    latents, query, key, value = pl.pallas_call(
        token_kernel,
        out_shape=(jax.ShapeDtypeStruct((1, 2, 2, 256), jnp.float32), tokens, tokens, tokens),
        in_specs=vmem(4),
        out_specs=tuple(vmem(4)),
        compiler_params=limit,
        cost_estimate=pl.CostEstimate(flops=10**8, bytes_accessed=10**6, transcendentals=0),
        name="tokens",
    )(
        partials,
        merged,
        base,
        table,
    )
    full = (clips, frames, 1, 8, heads * HD)
    return latents, query.reshape(full), key.reshape(full), value.reshape(full)


def pick(mesh, *arrays):
    if one_group_each(mesh, arrays[0], arrays[1], arrays[4], arrays[8]):
        return grouped(*arrays)
    return shards(*arrays)


def solution(mesh):
    placed = (
        P("dp", "tm", "height", None, None),
        P(("tm", "height"), "dp"),
        P("dp"),
        P("dp"),
        P(None, "dp", None),
        P(),
        P(),
        P(),
        P(("tm", "height"), "dp"),
        P("dp"),
        P(),
        P(),
        P("tm"),
        P("height"),
    )
    return jax.shard_map(
        functools.partial(pick, mesh),
        mesh=mesh,
        in_specs=placed,
        out_specs=(
            P("dp", "tm", "height", None),
            P(None, "tm", "height", None, "dp"),
            P(None, "tm", "height", None, "dp"),
            P(None, "tm", "height", None, "dp"),
        ),
        check_vma=False,
    )
```

```python
import functools

import jax
import jax.numpy as jnp
import numpy as np
from jax import lax
from jax.experimental import pallas as pl
from jax.experimental.pallas import tpu as pltpu
from jax.sharding import PartitionSpec as P

HD = 128
GROUPS = 32
TAPS = 27


norm_eps = 1e-06
latent_scale = 0.476986
rope_base = 256.0
time_dims = 16
row_dims = 56


def from_behind(value, axis, steps):
    count = lax.axis_size(axis)
    first, last = (max(0, -steps), min(count, count - steps))
    return lax.ppermute(value, axis, [(source, source + steps) for source in range(first, last)])


def padded_2(block, sides, width):
    for axis, dim in sides:
        count = lax.axis_size(axis)
        forward = [(i, i + 1) for i in range(count - 1)]
        backward = [(target, source) for source, target in forward]
        low = lax.ppermute(
            lax.slice_in_dim(block, block.shape[dim] - width, None, axis=dim), axis, forward
        )
        high = lax.ppermute(lax.slice_in_dim(block, 0, width, axis=dim), axis, backward)
        block = jnp.concatenate([low, block, high], axis=dim)
    return block


def repeat_first(block):
    return jnp.concatenate([block[:, :1], block[:, :1]], axis=1)


def time_join(block, earlier):
    start = jnp.where(lax.axis_index("tm") == 0, repeat_first(block), earlier)
    return jnp.concatenate([start, block], axis=1)


def rows_finish(grown):
    place = lax.axis_index("height")
    top = jnp.where(place == 0, grown[:, :, 1:2], grown[:, :, :1])
    bottom = jnp.where(place == lax.axis_size("height") - 1, grown[:, :, -2:-1], grown[:, :, -1:])
    inner = jnp.concatenate([top, grown[:, :, 1:-1], bottom], axis=2)
    return jnp.pad(inner, ((0, 0), (0, 0), (0, 0), (1, 1), (0, 0)), mode="edge")


def edges_before(block):
    earlier = from_behind(block, "tm", 1)
    longer = time_join(block, earlier)
    return rows_finish(padded_2(longer, (("height", 2),), 1))


def edges_norm(block):
    earlier = from_behind(block, "tm", 1)
    longer = time_join(block, earlier)
    return rows_finish(padded_2(longer, (("height", 2),), 1))


def convolve(padded, weight):
    clips = padded.shape[0]
    frames = padded.shape[1] - 2
    rows = padded.shape[2] - 2
    cols = padded.shape[3] - 2
    total = jnp.zeros((clips * frames * rows * cols, weight.shape[2]), jnp.float32)
    for shift_t in range(3):
        for shift_r in range(3):
            for shift_c in range(3):
                window = padded[
                    :,
                    shift_t : shift_t + frames,
                    shift_r : shift_r + rows,
                    shift_c : shift_c + cols,
                ]
                window = window.reshape(-1, padded.shape[4])
                total = total + jnp.dot(
                    window,
                    weight[9 * shift_t + 3 * shift_r + shift_c],
                    preferred_element_type=jnp.float32,
                )
    return total.reshape(clips, frames, rows, cols, weight.shape[2])


def section_freqs(dims):
    return jnp.power(rope_base, -jnp.arange(0, dims, 2, dtype=jnp.float32) / dims)


def rope_angles(tpos, hpos, width):
    frames = tpos.shape[0]
    rows = hpos.shape[0]
    cols = jnp.arange(width, dtype=jnp.float32)
    part_t = tpos[:, None, None, None] * section_freqs(time_dims)
    part_h = hpos[None, :, None, None] * section_freqs(row_dims)
    part_w = cols[None, None, :, None] * section_freqs(row_dims)
    shape = (frames, rows, width)
    return jnp.concatenate(
        [
            jnp.broadcast_to(part_t, shape + (time_dims // 2,)),
            jnp.broadcast_to(part_h, shape + (row_dims // 2,)),
            jnp.broadcast_to(part_w, shape + (row_dims // 2,)),
        ],
        axis=-1,
    )


def rotate(vectors, angles):
    pairs = vectors.reshape(vectors.shape[:-1] + (vectors.shape[-1] // 2, 2))
    first = pairs[..., 0]
    second = pairs[..., 1]
    cosine = jnp.cos(angles)[..., None, :]
    sine = jnp.sin(angles)[..., None, :]
    turned = jnp.stack([first * cosine - second * sine, first * sine + second * cosine], axis=-1)
    return turned.reshape(vectors.shape)


def rms_scale(vectors, gain):
    return (
        vectors
        * lax.rsqrt(jnp.mean(vectors * vectors, axis=-1, keepdims=True) + norm_eps)
        * gain.astype(jnp.float32)
    )


def shards(
    clip_inputs,
    conv_in_weight,
    group_gain,
    group_bias,
    conv_out_weight,
    out_bias,
    patch_weight,
    patch_bias,
    qkv_weight,
    qkv_bias,
    q_gain,
    k_gain,
    frame_pos,
    row_pos,
):
    channels = clip_inputs.shape[4]
    frames = clip_inputs.shape[1]
    rows = clip_inputs.shape[2]
    cols = clip_inputs.shape[3]
    padded = lax.all_gather(edges_before(clip_inputs), "dp", axis=0, tiled=True)
    clips = padded.shape[0]
    weight_in = lax.all_gather(conv_in_weight, ("tm", "height"), axis=0, tiled=True).reshape(
        TAPS, channels, -1
    )
    hidden = convolve(padded, weight_in)
    block_width = hidden.shape[4]
    group_width = channels // GROUPS
    local_groups = block_width // group_width
    grouped = hidden.reshape(clips, -1, local_groups, group_width)
    sums_local = jnp.sum(grouped, axis=(1, 3))
    squares_local = jnp.sum(grouped * grouped, axis=(1, 3))
    sums_all, squares_all = lax.psum((sums_local, squares_local), ("tm", "height"))
    count = float(
        frames * lax.axis_size("tm") * rows * lax.axis_size("height") * cols * group_width
    )
    mean = sums_all / count
    var = squares_all / count - mean * mean
    scaled = (grouped - mean[:, None, :, None]) * lax.rsqrt(var + norm_eps)[:, None, :, None]
    scaled = scaled.reshape(hidden.shape) * group_gain.astype(jnp.float32) + group_bias.astype(
        jnp.float32
    )
    normed = jax.nn.silu(scaled).astype(jnp.bfloat16)
    partial_latent = convolve(edges_norm(normed), conv_out_weight)
    own_sum = lax.psum_scatter(partial_latent, "dp", scatter_dimension=0, tiled=True)
    own_latent = (own_sum + out_bias) * latent_scale
    every_latent = lax.all_gather(own_latent.astype(jnp.bfloat16), "dp", axis=0, tiled=True)
    latent_dims = every_latent.shape[4]
    latents = own_latent.reshape(1, frames, rows, cols * latent_dims)
    tok_rows = rows // 2
    tok_cols = cols // 2
    patches = every_latent.reshape(clips, frames, tok_rows, 2, tok_cols, 2, latent_dims)
    patches = patches.transpose(0, 1, 2, 4, 3, 5, 6).reshape(-1, 4 * latent_dims)
    embedded = (
        jnp.dot(patches, patch_weight, preferred_element_type=jnp.float32)
        + patch_bias.astype(jnp.float32)
    ).astype(jnp.bfloat16)
    projected = jnp.dot(
        embedded,
        lax.all_gather(qkv_weight, ("tm", "height"), axis=0, tiled=True),
        preferred_element_type=jnp.float32,
    )
    projected = projected + qkv_bias.astype(jnp.float32)
    local_heads = qkv_weight.shape[1] // (3 * HD)
    projected = projected.reshape(clips, frames, tok_rows, tok_cols, local_heads, 3, HD)
    angles = rope_angles(frame_pos.astype(jnp.float32), row_pos.astype(jnp.float32), tok_cols)
    query = rotate(rms_scale(projected[..., 0, :], q_gain), angles)
    key = rotate(rms_scale(projected[..., 1, :], k_gain), angles)
    value = projected[..., 2, :]
    merged = (clips, frames, tok_rows, tok_cols, local_heads * HD)
    return (
        latents,
        query.reshape(merged).astype(jnp.bfloat16),
        key.reshape(merged).astype(jnp.bfloat16),
        value.reshape(merged).astype(jnp.bfloat16),
    )


LANES = 128
TILE = 16
GROUP = 16


def one_group_each(mesh, clip_inputs, conv_in_weight, conv_out_weight, qkv_weight):
    plane = mesh.shape["tm"] * mesh.shape["height"]
    return (
        clip_inputs.shape[:4] == (1, 2, 2, 16)
        and mesh.shape["height"] == 2
        and mesh.shape["tm"] == 4
        and mesh.shape["dp"] == 4
        and conv_in_weight.shape[1] == plane * GROUP
        and clip_inputs.shape[4] == GROUP * GROUPS
        and conv_out_weight.shape[2] == TILE
        and qkv_weight.shape[1] == 6 * HD
    )


def lane_shifts(lane):
    col = lane % 16
    row = lane // 16 % 2
    half = lane // 64

    def cols(left, mid, right):
        left = jnp.where(col == 0, left, pltpu.roll(left, 1, 1))
        right = jnp.where(col == 15, right, pltpu.roll(right, LANES - 1, 1))
        return mid + left + right

    def rows(up, mid, down):
        up = jnp.where(
            row == 1, pltpu.roll(up, 16, 1), jnp.where(half == 1, pltpu.roll(up, 48, 1), up)
        )
        down = jnp.where(
            row == 0,
            pltpu.roll(down, LANES - 16, 1),
            jnp.where(half == 0, pltpu.roll(down, LANES - 48, 1), down),
        )
        return mid + up + down

    return cols, rows


def tap_sums(source, tiles):
    lane = lax.broadcasted_iota(jnp.int32, (TILE, LANES), 1)
    second = lane // 32 % 2 == 1
    cols, rows = lane_shifts(lane)
    sums = []
    before = None
    for tile in range(tiles):

        def part(tap):
            return source(tap, slice(tile * LANES, (tile + 1) * LANES))

        oldest, older, now = (
            rows(*(cols(*(part(9 * i + 3 * j + l) for l in range(3))) for j in range(3)))
            for i in range(3)
        )
        turned = pltpu.roll(older, 32, 1)
        if before is None:
            start = jnp.where(second, pltpu.roll(oldest, 32, 1), oldest)
            total = now + jnp.where(second, turned, older) + start
        else:
            total = now + jnp.where(second, turned, pltpu.roll(before[1], 96, 1)) + before[0]
        before = (oldest, older)
        sums.append(total)
    return sums


def pack_kernel(
    w_hbm, qkv_hbm, patch_hbm, patch_bias_hbm, own_hbm, side_hbm, high_hbm, far_hbm,
    w_ref, qkv_ref, patch_ref, patch_bias_ref, rows_ref, turned_ref, merged_ref, out_ref, lines_ref, sems,
):
    _, channels, width = out_ref.shape
    depth = w_ref.shape[0]
    rows = qkv_ref.shape[0]
    side = lax.axis_index("height")
    high = lax.axis_index("tm") // 2
    place = lax.axis_index("tm") * 2 + side
    at = pl.ds(pl.multiple_of(place * rows, LANES), rows)
    loads = [
        pltpu.make_async_copy(w_hbm, w_ref, sems.at[0]),
        pltpu.make_async_copy(qkv_hbm, qkv_ref, sems.at[1]),
        pltpu.make_async_copy(patch_hbm.at[:, at], patch_ref, sems.at[2]),
        pltpu.make_async_copy(patch_bias_hbm, patch_bias_ref, sems.at[3]),
    ]
    for load in loads:
        load.start()
    whole = depth // LANES * LANES
    loads[0].wait()
    turned_ref[...] = w_ref[...].T
    for load in loads[1:]:
        load.wait()
    merged_ref[...] = jnp.dot(patch_ref[...], qkv_ref[...], preferred_element_type=jnp.float32)
    stores = []
    own_main = own_hbm.at[:, :width]
    for flip, out_hbm in ((1, side_hbm), (2, high_hbm), (3, far_hbm), (0, own_main)):
        first = pl.multiple_of((high ^ (flip // 2)) * channels, channels)
        out_ref[flip, :, :whole] = turned_ref[pl.ds(first, channels), :whole]
        lower = turned_ref[pl.ds(first, channels), whole:]
        chip = (2 * high + side) ^ flip
        tail, upper = [], []
        for half in range(2):
            mine = merged_ref[pl.ds(pl.multiple_of(chip * 16 + half * 8, 8), 8)]
            mine = [mine[:, q * LANES : (q + 1) * LANES] for q in range(6)]
            tail += mine[:4]
            upper += [pltpu.roll(mine[4], 64, 1), mine[4], pltpu.roll(mine[5], 64, 1), mine[5]]
        upper = jnp.concatenate(upper, axis=0)[:, 64:].astype(jnp.bfloat16)
        out_ref[flip, :, whole : whole + LANES] = jnp.concatenate([lower, upper], axis=1)
        out_ref[flip, :, whole + LANES :] = jnp.concatenate(tail, axis=0).astype(jnp.bfloat16)
        stores.append(pltpu.make_async_copy(out_ref.at[flip], out_hbm, sems.at[4 + flip]))
        stores[-1].start()
    rows_ref[...] = patch_bias_ref[...].astype(jnp.float32).reshape(rows_ref.shape)
    count = rows // LANES
    bias = [rows_ref[pl.ds(count * place + part, 1), :] for part in range(count)]
    bias = jnp.broadcast_to(jnp.concatenate(bias, axis=1), (8, rows)).astype(jnp.bfloat16)
    bias = jnp.dot(bias, qkv_ref[...], preferred_element_type=jnp.float32)
    line = lax.broadcasted_iota(jnp.int32, (8, LANES), 0)
    lines = jnp.zeros((8, LANES), jnp.float32)
    for part in range(bias.shape[1] // LANES):
        lines = jnp.where(line == part, bias[:, part * LANES : (part + 1) * LANES], lines)
    lines_ref[...] = jnp.concatenate([lines, jnp.zeros_like(lines)], axis=0).astype(jnp.bfloat16)
    stores.append(
        pltpu.make_async_copy(lines_ref, own_hbm.at[:16, width : width + LANES], sems.at[8])
    )
    stores[-1].start()
    for store in stores:
        store.wait()


def column(row_ref, first, size):
    length = row_ref.shape[0]
    row = row_ref[...].astype(jnp.float32).reshape(1, length)
    line = lax.broadcasted_iota(jnp.int32, (size, length), 0)
    lane = lax.broadcasted_iota(jnp.int32, (size, length), 1)
    picked = jnp.where(lane == line + first, jnp.broadcast_to(row, (size, length)), 0.0)
    return jnp.sum(picked, axis=1, keepdims=True)


def table_kernel(
    frame_ref, row_pos_ref, freq_ref, block_hbm, gain_hbm, bias_hbm, out_bias_hbm, qkv_hbm, q_hbm, k_hbm,
    scale_ref, table_ref, late_hbm,
    gain_v, bias_v, out_bias_v, qkv_v, q_v, k_v, sems,
):
    pairs = (
        (gain_hbm, gain_v), (bias_hbm, bias_v), (out_bias_hbm, out_bias_v),
        (qkv_hbm, qkv_v), (q_hbm, q_v), (k_hbm, k_v),
    )
    loads = [
        pltpu.make_async_copy(source, to, sems.at[index])
        for index, (source, to) in enumerate(pairs)
    ]
    for load in loads:
        load.start()
    handed = pltpu.make_async_copy(block_hbm, late_hbm, sems.at[6])
    handed.start()
    shape = (TILE, LANES)
    line = lax.broadcasted_iota(jnp.int32, shape, 0)
    lane = lax.broadcasted_iota(jnp.int32, shape, 1)
    frame = jnp.where(line // 8 == 0, frame_ref[0], frame_ref[1]).astype(jnp.float32)
    row = jnp.broadcast_to(row_pos_ref[0], shape).astype(jnp.float32)
    spot = jnp.where(lane < 72, row, (line % 8).astype(jnp.float32))
    angles = jnp.where(lane < 16, frame, spot) * freq_ref[...]
    table_ref[:16] = jnp.cos(angles)
    sine = jnp.sin(angles)
    table_ref[16:32] = jnp.where(lane % 2 == 0, -sine, sine)
    for load in loads:
        load.wait()
    first = lax.axis_index("tm") // 2 * (4 * GROUP)
    scale_ref[:, 0:1] = column(gain_v, first, 4 * GROUP)
    scale_ref[:, 1:2] = column(bias_v, first, 4 * GROUP)
    table_ref[32:48] = jnp.broadcast_to(column(out_bias_v, 0, TILE), shape)
    table_ref[48:49] = q_v[...].astype(jnp.float32).reshape(1, HD)
    table_ref[49:50] = k_v[...].astype(jnp.float32).reshape(1, HD)
    table_ref[50:56] = qkv_v[...].astype(jnp.float32).reshape(6, LANES)
    handed.wait()


def arrange_kernel(*refs):
    pieces, (keep_ref, send_ref, all_ref) = refs[:4], refs[4:]
    side = lax.axis_index("height")
    layer = lax.axis_index("dp")
    for step, piece in enumerate(pieces):
        all_ref[(layer + 4 - step) % 4] = piece[...]
    for core in range(2):
        keep_ref[core] = all_ref[2 * side + core]
        send_ref[core] = all_ref[2 - 2 * side + core]


def core_taps(core):
    quarter = TAPS / 4
    taps = []
    for tm in (core, core + 2):
        taps += range(int(quarter * tm), min(TAPS, -int(-quarter * (tm + 1) // 1)))
    return taps


def join_kernel(own_ref, side_ref, high_ref, far_ref, wt_ref, all_ref):
    channels, width = side_ref.shape
    inner = wt_ref.shape[1]
    depth = TAPS * inner // 8
    here = lax.axis_index("tm") // 2 * 2 + lax.axis_index("height")
    for flip, ref in enumerate((own_ref, side_ref, high_ref, far_ref)):
        all_ref[here ^ flip] = ref[:, :width]

    def assemble(core):
        for index, tap in enumerate(core_taps(core)):
            rows = slice(index * channels, (index + 1) * channels)
            start, end = tap * inner, (tap + 1) * inner
            while start < end:
                source = start // depth
                stop = min(end, (source + 1) * depth)
                to = slice(start - tap * inner, stop - tap * inner)
                if source // 2 % 2 == core:
                    chip = source // 4 * 2 + source % 2
                    first = start - source * depth
                    wt_ref[rows, to] = all_ref[chip, :, first : first + stop - start]
                else:
                    wt_ref[rows, to] = jnp.zeros((channels, stop - start), jnp.bfloat16)
                start = stop

    core = lax.axis_index("tm") % 2
    pl.when(core == 0)(functools.partial(assemble, 0))
    pl.when(core == 1)(functools.partial(assemble, 1))
    total = sum(all_ref[chip, :, width - 2 * LANES :].astype(jnp.float32) for chip in range(4))
    low = lax.broadcasted_iota(jnp.int32, (8, LANES), 1) < 64
    empty = jnp.zeros((8, LANES), jnp.float32)
    wide, narrow = [], []
    for half in range(2):
        top = 32 * half
        wide.append([total[top + 8 * q : top + 8 * q + 8, LANES:] for q in range(4)])
        some = []
        for q in range(2):
            one = total[top + 16 * q : top + 16 * q + 8, :LANES]
            two = total[top + 16 * q + 8 : top + 16 * q + 16, :LANES]
            some.append(jnp.where(low, pltpu.roll(one, 64, 1), two))
        lines = own_ref[:16, width:].astype(jnp.float32)[8 * half : 8 * half + 8]
        narrow.append(some + [lines, empty])
    share = jnp.concatenate([jnp.concatenate(row, axis=1) for row in wide + narrow], axis=0)
    wt_ref[wt_ref.shape[0] - 32 :] = share.astype(jnp.bfloat16)


def place_kernel(*refs):
    pieces, x_ref = refs[:4], refs[4]
    place = lax.axis_index("tm") // 2 * 4 + lax.axis_index("height")
    for flip, piece in zip((0, 1, 4, 5), pieces):
        for core in range(2):
            x_ref[(place ^ flip) + 2 * core] = piece[core]


def tap_parts(y_ref, group, channels):
    held = [core_taps(core) for core in range(2)]

    def part(tap, lanes):
        found = []
        for core in range(2):
            if tap in held[core]:
                at = held[core].index(tap) * channels + group * GROUP
                found.append(y_ref[core, at : at + GROUP, lanes])
        return sum(found[1:], found[0])

    return part


def conv_kernel(
    x_ref, wt_ref, pair_ref, scale_ref, w2_ref, out_ref, y_ref
):
    channels = 4 * GROUP
    tiles = x_ref.shape[0] // 2
    count = float(tiles * LANES * GROUP)
    core = lax.axis_index("tm") % 2
    height = y_ref.shape[1]
    x = x_ref[...].reshape(tiles * LANES, x_ref.shape[2])
    for ref, at in ((wt_ref, core), (pair_ref, 1 - core)):
        y_ref[at] = lax.dot_general(
            ref[:height], x, (((1,), (1,)), ((), ())), preferred_element_type=jnp.float32
        )
    normed = []
    for group in range(4):
        hidden = tap_sums(tap_parts(y_ref, group, channels), tiles)
        at = slice(group * GROUP, (group + 1) * GROUP)
        mean = jnp.sum(sum(hidden), keepdims=True) / count
        square = jnp.sum(sum(part * part for part in hidden), keepdims=True) / count
        scale = lax.rsqrt(square - mean * mean + norm_eps)
        parts = []
        for part in hidden:
            scaled = (part - mean) * scale * scale_ref[at, 0:1] + scale_ref[at, 1:2]
            parts.append((scaled / (1.0 + jnp.exp(-scaled))).astype(jnp.bfloat16))
        normed.append(jnp.concatenate(parts, axis=1))
    y_ref[0, : TAPS * TILE] = jnp.dot(
        w2_ref[...], jnp.concatenate(normed, axis=0), preferred_element_type=jnp.float32
    )

    def part(tap, lanes):
        return y_ref[0, tap * TILE : (tap + 1) * TILE, lanes]

    low = lax.broadcasted_iota(jnp.int32, (8, LANES), 1) < 64
    layers = out_ref.shape[0] // (2 * tiles)
    for tile, latent in enumerate(tap_sums(part, tiles)):
        turned = pltpu.roll(latent, 64, 1)
        near = jnp.where(low, latent[:8], turned[8:])
        far = jnp.where(low, turned[:8], latent[8:])
        for layer in range(layers):
            out_ref[layer * 2 * tiles + 2 * tile] = near
            out_ref[layer * 2 * tiles + 2 * tile + 1] = far


def share_kernel(m0_ref, m1_ref, m2_ref, m3_ref, table_ref, merged_ref, base_ref, m_ref):
    here = lax.axis_index("tm") // 2 * 2 + lax.axis_index("height")
    lines = table_ref[48:56]
    for flip, ref in enumerate((m0_ref, m1_ref, m2_ref, m3_ref)):
        share = ref[...].astype(jnp.float32)
        m_ref[here ^ flip, :, : 4 * LANES] = share[:16]
        m_ref[here ^ flip, :, 4 * LANES :] = share[16:, : 2 * LANES]
        lines = lines + pltpu.roll(share[16:24, 2 * LANES : 3 * LANES], 2, 0)
    base_ref[...] = jnp.concatenate([lines[2 + part : 3 + part] for part in range(6)], axis=1)
    merged_ref[...] = m_ref[...].reshape(merged_ref.shape).astype(jnp.bfloat16)


def token_kernel(p_ref, m_ref, base_ref, table_ref, lat_ref, q_ref, k_ref, v_ref):
    low = lax.broadcasted_iota(jnp.int32, (8, LANES), 1) < 64
    pairs = []
    for side in range(2):
        one, two = (
            sum(p_ref[4 * index + 2 * core + side] for index in range(p_ref.shape[0] // 4))
            for core in range(2)
        )
        top = jnp.where(low, one, pltpu.roll(two, 64, 1))
        bottom = jnp.where(low, pltpu.roll(one, 64, 1), two)
        pairs.append(jnp.concatenate([top, bottom], axis=0))
    total = jnp.concatenate(pairs, axis=1)
    lat = (total + table_ref[32:48, :1]) * latent_scale
    clips = lat.shape[1] // 64
    tokens = clips * 16
    place = lax.axis_index("dp")
    own = lat[:, :LANES]
    for pair in range(1, clips // 2):
        own = jnp.where(place // 2 == pair, lat[:, pair * LANES : (pair + 1) * LANES], own)
    own = jnp.where(place % 2 == 1, pltpu.roll(own, 64, 1), own)
    turned = own.T[:64]
    wide = jnp.concatenate([turned] * 16, axis=1)
    spot = lax.broadcasted_iota(jnp.int32, wide.shape, 0) % 16
    spread = lax.broadcasted_iota(jnp.int32, wide.shape, 1) // 16
    merged = jnp.sum(jnp.where(spot == spread, wide, 0.0).reshape(4, 16, 256), axis=1)
    lat_ref[0, 0] = merged[:2]
    lat_ref[0, 1] = merged[2:]

    lat_bf = lat.astype(jnp.bfloat16)
    token = lax.broadcasted_iota(jnp.int32, (tokens, clips * 64), 0)
    lane = lax.broadcasted_iota(jnp.int32, (tokens, clips * 64), 1)
    first = token // 8 * 32 + token % 8 * 2
    heads = q_ref.shape[2] // HD
    projected = base_ref[...]
    for a in range(2):
        for e in range(2):
            chosen = jnp.where(lane == first + (16 * a + e), 1.0, 0.0).astype(jnp.bfloat16)
            patch = lax.dot_general(
                chosen, lat_bf, (((1,), (1,)), ((), ())), preferred_element_type=jnp.float32
            ).astype(jnp.bfloat16)
            weight = m_ref[(2 * a + e) * TILE : (2 * a + e + 1) * TILE]
            projected = projected + jnp.dot(patch, weight, preferred_element_type=jnp.float32)

    even = lax.broadcasted_iota(jnp.int32, (tokens, HD), 1) % 2 == 0
    cosine = jnp.concatenate([table_ref[:16]] * clips, axis=0)
    sine = jnp.concatenate([table_ref[16:32]] * clips, axis=0)

    def turn(vectors, gain):
        square = jnp.mean(vectors * vectors, axis=-1, keepdims=True)
        vectors = vectors * lax.rsqrt(square + norm_eps) * gain
        swapped = jnp.where(even, pltpu.roll(vectors, HD - 1, 1), pltpu.roll(vectors, 1, 1))
        return vectors * cosine + swapped * sine

    def keep(ref, head, value):
        value = value.reshape(tokens // 8, 8, HD).astype(jnp.bfloat16)
        ref[:, :, head * HD : (head + 1) * HD] = value

    for head in range(heads):
        at = 3 * HD * head
        keep(q_ref, head, turn(projected[:, at : at + HD], table_ref[48:49]))
        keep(k_ref, head, turn(projected[:, at + HD : at + 2 * HD], table_ref[49:50]))
        keep(v_ref, head, projected[:, at + 2 * HD : at + 3 * HD])


def rope_freqs():
    freqs = []
    for dims in (time_dims, row_dims, row_dims):
        freqs.append(rope_base ** (-np.arange(0, dims, 2, dtype=np.float64) / dims))
    return np.repeat(np.concatenate(freqs), 2)[None].astype(np.float32)


def vmem(count):
    return [pl.BlockSpec(memory_space=pltpu.VMEM)] * count


def grouped(
    clip_inputs,
    conv_in_weight,
    group_gain,
    group_bias,
    conv_out_weight,
    out_bias,
    patch_weight,
    patch_bias,
    qkv_weight,
    qkv_bias,
    q_gain,
    k_gain,
    frame_pos,
    row_pos,
):
    plane_axes = ("tm", "height")
    clips = lax.axis_size("dp")
    steps = lax.axis_size("tm")
    plane = steps * lax.axis_size("height")
    channels = clip_inputs.shape[4]
    depth = conv_in_weight.shape[0]

    width = -(-depth // LANES) * LANES + LANES
    hbm = pl.BlockSpec(memory_space=pltpu.HBM)
    wide = pltpu.CompilerParams(vmem_limit_bytes=60 * 1024 * 1024)
    limit = pltpu.CompilerParams(vmem_limit_bytes=32 * 1024 * 1024)
    small = pl.CostEstimate(flops=10**6, bytes_accessed=10**6, transcendentals=0)
    with jax.named_scope("weight_by_group"):
        weight_block = jax.ShapeDtypeStruct((4 * GROUP, width), jnp.bfloat16)
        own_block = jax.ShapeDtypeStruct((4 * GROUP, width + LANES), jnp.bfloat16)
        packed = pl.pallas_call(
            pack_kernel,
            out_shape=(own_block,) + (weight_block,) * 3,
            in_specs=[hbm] * 4,
            out_specs=(hbm,) * 4,
            scratch_shapes=[
                pltpu.VMEM(conv_in_weight.shape, jnp.bfloat16),
                pltpu.VMEM(qkv_weight.shape, jnp.bfloat16),
                pltpu.VMEM((patch_weight.shape[0], qkv_weight.shape[0]), jnp.bfloat16),
                pltpu.VMEM(patch_bias.shape, jnp.bfloat16),
                pltpu.VMEM((patch_bias.shape[0] // LANES, LANES), jnp.float32),
                pltpu.VMEM((8 * GROUP, depth), jnp.bfloat16),
                pltpu.VMEM((patch_weight.shape[0], qkv_weight.shape[1]), jnp.float32),
                pltpu.VMEM((4, 4 * GROUP, width), jnp.bfloat16),
                pltpu.VMEM((16, LANES), jnp.bfloat16),
                pltpu.SemaphoreType.DMA((9,)),
            ],
            compiler_params=wide,
            cost_estimate=pl.CostEstimate(flops=10**8, bytes_accessed=10**6, transcendentals=0),
            name="pack_weights",
        )(conv_in_weight, qkv_weight, patch_weight, patch_bias)
        blocks = [packed[0]]
        for flip, block in zip((1, 4, 5), packed[1:]):
            blocks.append(lax.ppermute(block, plane_axes, [(i, i ^ flip) for i in range(plane)]))
    with jax.named_scope("tables"):
        smem = pl.BlockSpec(memory_space=pltpu.SMEM)
        small_arrays = (group_gain, group_bias, out_bias, qkv_bias, q_gain, k_gain)
        own = clip_inputs.reshape(64, channels)
        scale, table, late = pl.pallas_call(
            table_kernel,
            out_shape=(
                jax.ShapeDtypeStruct((4 * GROUP, 2), jnp.float32),
                jax.ShapeDtypeStruct((56, LANES), jnp.float32),
                jax.ShapeDtypeStruct((64, channels), jnp.bfloat16),
            ),
            in_specs=[smem, smem, vmem(1)[0]] + [hbm] * 7,
            out_specs=tuple(vmem(2)) + (hbm,),
            scratch_shapes=[pltpu.VMEM(array.shape, array.dtype) for array in small_arrays]
            + [pltpu.SemaphoreType.DMA((7,))],
            compiler_params=wide,
            cost_estimate=pl.CostEstimate(
                flops=4 * 10**9, bytes_accessed=10**6, transcendentals=0
            ),
            name="tables",
        )(frame_pos, row_pos, rope_freqs(), own, *small_arrays)
    with jax.named_scope("gather_clips"):
        layers = []
        for step in range(clips):
            pairs = []
            for layer in range(clips):
                for tm in range(steps):
                    to = (layer // 2 * 2 + tm % 2 + step) % clips
                    pairs.append((layer * steps + tm, to * steps + tm // 2 * 2 + layer % 2))
            layers.append(lax.ppermute(late if step < 2 else own, ("dp", "tm"), pairs))
    with jax.named_scope("spread_clips"):
        keep, send = pl.pallas_call(
            arrange_kernel,
            out_shape=(jax.ShapeDtypeStruct((2, 64, channels), jnp.bfloat16),) * 2,
            in_specs=vmem(4),
            out_specs=tuple(vmem(2)),
            scratch_shapes=[pltpu.VMEM((4, 64, channels), jnp.bfloat16)],
            compiler_params=limit,
            cost_estimate=small,
            name="arrange_clips",
        )(*layers)
        pieces = [keep]
        for flip in (1, 4, 5):
            pairs = [(i, i ^ flip) for i in range(plane)]
            pieces.append(lax.ppermute(send if flip % 2 else keep, plane_axes, pairs))
    with jax.named_scope("small_weights"):
        first = lax.axis_index("tm") // 2 * (4 * GROUP)
        weight_out = lax.dynamic_slice_in_dim(conv_out_weight, first, 4 * GROUP, axis=1)
        weight_out = weight_out.transpose(0, 2, 1).reshape(TAPS * TILE, 4 * GROUP)
    with jax.named_scope("join_weights"):
        height = len(core_taps(0)) * 4 * GROUP
        joined = pl.pallas_call(
            join_kernel,
            out_shape=jax.ShapeDtypeStruct((height + 32, channels), jnp.bfloat16),
            in_specs=vmem(4),
            out_specs=vmem(1)[0],
            scratch_shapes=[pltpu.VMEM((4, 4 * GROUP, width), jnp.bfloat16)],
            compiler_params=limit,
            cost_estimate=small,
            name="join_weights",
        )(*blocks)
        joined_pair = lax.ppermute(joined, "tm", [(i, i ^ 1) for i in range(steps)])
    with jax.named_scope("merged_projection"):
        share = joined[height:].astype(jnp.float32) + joined_pair[height:].astype(jnp.float32)
        share = share.astype(jnp.bfloat16)
        shares = [share]
        for flip in (1, 4, 5):
            pairs = [(i, i ^ flip) for i in range(plane)]
            shares.append(lax.ppermute(share, plane_axes, pairs))

        merged, base = pl.pallas_call(
            share_kernel,
            out_shape=(
                jax.ShapeDtypeStruct((64, 6 * HD), jnp.bfloat16),
                jax.ShapeDtypeStruct((1, 6 * HD), jnp.float32),
            ),
            in_specs=vmem(5),
            out_specs=tuple(vmem(2)),
            scratch_shapes=[pltpu.VMEM((4, 16, 6 * HD), jnp.float32)],
            compiler_params=limit,
            cost_estimate=small,
            name="share_rows",
        )(*shares, table)

    flops = 4 * height * steps * LANES * channels
    clip = pl.pallas_call(
        place_kernel,
        out_shape=jax.ShapeDtypeStruct((plane, 64, channels), jnp.bfloat16),
        in_specs=vmem(4),
        out_specs=vmem(1)[0],
        compiler_params=limit,
        cost_estimate=pl.CostEstimate(flops=4 * 10**10, bytes_accessed=10**6, transcendentals=0),
        name="place_clip",
    )(*pieces)
    partial = pl.pallas_call(
        conv_kernel,
        out_shape=jax.ShapeDtypeStruct((clips * plane, 8, LANES), jnp.float32),
        in_specs=vmem(5),
        out_specs=vmem(1)[0],
        scratch_shapes=[
            pltpu.VMEM((2, height, steps * LANES), jnp.float32),
        ],
        compiler_params=limit,
        cost_estimate=pl.CostEstimate(flops=flops, bytes_accessed=10**6, transcendentals=0),
        name="convolutions",
    )(clip, joined, joined_pair, scale, weight_out)

    with jax.named_scope("sum_latents"):
        partials = lax.all_to_all(partial, ("dp",) + plane_axes, 0, 0, tiled=True)

    heads = qkv_weight.shape[1] // (3 * HD)
    frames = clip_inputs.shape[1]
    tokens = jax.ShapeDtypeStruct((clips * frames, 8, heads * HD), jnp.bfloat16)
    latents, query, key, value = pl.pallas_call(
        token_kernel,
        out_shape=(jax.ShapeDtypeStruct((1, 2, 2, 256), jnp.float32), tokens, tokens, tokens),
        in_specs=vmem(4),
        out_specs=tuple(vmem(4)),
        compiler_params=limit,
        cost_estimate=pl.CostEstimate(flops=10**8, bytes_accessed=10**6, transcendentals=0),
        name="tokens",
    )(
        partials,
        merged,
        base,
        table,
    )
    full = (clips, frames, 1, 8, heads * HD)
    return latents, query.reshape(full), key.reshape(full), value.reshape(full)


def pick(mesh, *arrays):
    if one_group_each(mesh, arrays[0], arrays[1], arrays[4], arrays[8]):
        return grouped(*arrays)
    return shards(*arrays)


def solution(mesh):
    placed = (
        P("dp", "tm", "height", None, None),
        P(("tm", "height"), "dp"),
        P("dp"),
        P("dp"),
        P(None, "dp", None),
        P(),
        P(),
        P(),
        P(("tm", "height"), "dp"),
        P("dp"),
        P(),
        P(),
        P("tm"),
        P("height"),
    )
    return jax.shard_map(
        functools.partial(pick, mesh),
        mesh=mesh,
        in_specs=placed,
        out_specs=(
            P("dp", "tm", "height", None),
            P(None, "tm", "height", None, "dp"),
            P(None, "tm", "height", None, "dp"),
            P(None, "tm", "height", None, "dp"),
        ),
        check_vma=False,
    )
```

```python
import functools

import jax
import jax.numpy as jnp
import numpy as np
from jax import lax
from jax.experimental import pallas as pl
from jax.experimental.pallas import tpu as pltpu
from jax.sharding import PartitionSpec as P

HD = 128
GROUPS = 32
TAPS = 27


norm_eps = 1e-06
latent_scale = 0.476986
rope_base = 256.0
time_dims = 16
row_dims = 56


def from_behind(value, axis, steps):
    count = lax.axis_size(axis)
    first, last = (max(0, -steps), min(count, count - steps))
    return lax.ppermute(value, axis, [(source, source + steps) for source in range(first, last)])


def padded_2(block, sides, width):
    for axis, dim in sides:
        count = lax.axis_size(axis)
        forward = [(i, i + 1) for i in range(count - 1)]
        backward = [(target, source) for source, target in forward]
        low = lax.ppermute(
            lax.slice_in_dim(block, block.shape[dim] - width, None, axis=dim), axis, forward
        )
        high = lax.ppermute(lax.slice_in_dim(block, 0, width, axis=dim), axis, backward)
        block = jnp.concatenate([low, block, high], axis=dim)
    return block


def repeat_first(block):
    return jnp.concatenate([block[:, :1], block[:, :1]], axis=1)


def time_join(block, earlier):
    start = jnp.where(lax.axis_index("tm") == 0, repeat_first(block), earlier)
    return jnp.concatenate([start, block], axis=1)


def rows_finish(grown):
    place = lax.axis_index("height")
    top = jnp.where(place == 0, grown[:, :, 1:2], grown[:, :, :1])
    bottom = jnp.where(place == lax.axis_size("height") - 1, grown[:, :, -2:-1], grown[:, :, -1:])
    inner = jnp.concatenate([top, grown[:, :, 1:-1], bottom], axis=2)
    return jnp.pad(inner, ((0, 0), (0, 0), (0, 0), (1, 1), (0, 0)), mode="edge")


def edges_before(block):
    earlier = from_behind(block, "tm", 1)
    longer = time_join(block, earlier)
    return rows_finish(padded_2(longer, (("height", 2),), 1))


def edges_norm(block):
    earlier = from_behind(block, "tm", 1)
    longer = time_join(block, earlier)
    return rows_finish(padded_2(longer, (("height", 2),), 1))


def convolve(padded, weight):
    clips = padded.shape[0]
    frames = padded.shape[1] - 2
    rows = padded.shape[2] - 2
    cols = padded.shape[3] - 2
    total = jnp.zeros((clips * frames * rows * cols, weight.shape[2]), jnp.float32)
    for shift_t in range(3):
        for shift_r in range(3):
            for shift_c in range(3):
                window = padded[
                    :,
                    shift_t : shift_t + frames,
                    shift_r : shift_r + rows,
                    shift_c : shift_c + cols,
                ]
                window = window.reshape(-1, padded.shape[4])
                total = total + jnp.dot(
                    window,
                    weight[9 * shift_t + 3 * shift_r + shift_c],
                    preferred_element_type=jnp.float32,
                )
    return total.reshape(clips, frames, rows, cols, weight.shape[2])


def section_freqs(dims):
    return jnp.power(rope_base, -jnp.arange(0, dims, 2, dtype=jnp.float32) / dims)


def rope_angles(tpos, hpos, width):
    frames = tpos.shape[0]
    rows = hpos.shape[0]
    cols = jnp.arange(width, dtype=jnp.float32)
    part_t = tpos[:, None, None, None] * section_freqs(time_dims)
    part_h = hpos[None, :, None, None] * section_freqs(row_dims)
    part_w = cols[None, None, :, None] * section_freqs(row_dims)
    shape = (frames, rows, width)
    return jnp.concatenate(
        [
            jnp.broadcast_to(part_t, shape + (time_dims // 2,)),
            jnp.broadcast_to(part_h, shape + (row_dims // 2,)),
            jnp.broadcast_to(part_w, shape + (row_dims // 2,)),
        ],
        axis=-1,
    )


def rotate(vectors, angles):
    pairs = vectors.reshape(vectors.shape[:-1] + (vectors.shape[-1] // 2, 2))
    first = pairs[..., 0]
    second = pairs[..., 1]
    cosine = jnp.cos(angles)[..., None, :]
    sine = jnp.sin(angles)[..., None, :]
    turned = jnp.stack([first * cosine - second * sine, first * sine + second * cosine], axis=-1)
    return turned.reshape(vectors.shape)


def rms_scale(vectors, gain):
    return (
        vectors
        * lax.rsqrt(jnp.mean(vectors * vectors, axis=-1, keepdims=True) + norm_eps)
        * gain.astype(jnp.float32)
    )


def shards(
    clip_inputs,
    conv_in_weight,
    group_gain,
    group_bias,
    conv_out_weight,
    out_bias,
    patch_weight,
    patch_bias,
    qkv_weight,
    qkv_bias,
    q_gain,
    k_gain,
    frame_pos,
    row_pos,
):
    channels = clip_inputs.shape[4]
    frames = clip_inputs.shape[1]
    rows = clip_inputs.shape[2]
    cols = clip_inputs.shape[3]
    padded = lax.all_gather(edges_before(clip_inputs), "dp", axis=0, tiled=True)
    clips = padded.shape[0]
    weight_in = lax.all_gather(conv_in_weight, ("tm", "height"), axis=0, tiled=True).reshape(
        TAPS, channels, -1
    )
    hidden = convolve(padded, weight_in)
    block_width = hidden.shape[4]
    group_width = channels // GROUPS
    local_groups = block_width // group_width
    grouped = hidden.reshape(clips, -1, local_groups, group_width)
    sums_local = jnp.sum(grouped, axis=(1, 3))
    squares_local = jnp.sum(grouped * grouped, axis=(1, 3))
    sums_all, squares_all = lax.psum((sums_local, squares_local), ("tm", "height"))
    count = float(
        frames * lax.axis_size("tm") * rows * lax.axis_size("height") * cols * group_width
    )
    mean = sums_all / count
    var = squares_all / count - mean * mean
    scaled = (grouped - mean[:, None, :, None]) * lax.rsqrt(var + norm_eps)[:, None, :, None]
    scaled = scaled.reshape(hidden.shape) * group_gain.astype(jnp.float32) + group_bias.astype(
        jnp.float32
    )
    normed = jax.nn.silu(scaled).astype(jnp.bfloat16)
    partial_latent = convolve(edges_norm(normed), conv_out_weight)
    own_sum = lax.psum_scatter(partial_latent, "dp", scatter_dimension=0, tiled=True)
    own_latent = (own_sum + out_bias) * latent_scale
    every_latent = lax.all_gather(own_latent.astype(jnp.bfloat16), "dp", axis=0, tiled=True)
    latent_dims = every_latent.shape[4]
    latents = own_latent.reshape(1, frames, rows, cols * latent_dims)
    tok_rows = rows // 2
    tok_cols = cols // 2
    patches = every_latent.reshape(clips, frames, tok_rows, 2, tok_cols, 2, latent_dims)
    patches = patches.transpose(0, 1, 2, 4, 3, 5, 6).reshape(-1, 4 * latent_dims)
    embedded = (
        jnp.dot(patches, patch_weight, preferred_element_type=jnp.float32)
        + patch_bias.astype(jnp.float32)
    ).astype(jnp.bfloat16)
    projected = jnp.dot(
        embedded,
        lax.all_gather(qkv_weight, ("tm", "height"), axis=0, tiled=True),
        preferred_element_type=jnp.float32,
    )
    projected = projected + qkv_bias.astype(jnp.float32)
    local_heads = qkv_weight.shape[1] // (3 * HD)
    projected = projected.reshape(clips, frames, tok_rows, tok_cols, local_heads, 3, HD)
    angles = rope_angles(frame_pos.astype(jnp.float32), row_pos.astype(jnp.float32), tok_cols)
    query = rotate(rms_scale(projected[..., 0, :], q_gain), angles)
    key = rotate(rms_scale(projected[..., 1, :], k_gain), angles)
    value = projected[..., 2, :]
    merged = (clips, frames, tok_rows, tok_cols, local_heads * HD)
    return (
        latents,
        query.reshape(merged).astype(jnp.bfloat16),
        key.reshape(merged).astype(jnp.bfloat16),
        value.reshape(merged).astype(jnp.bfloat16),
    )


LANES = 128
TILE = 16
GROUP = 16


def one_group_each(mesh, clip_inputs, conv_in_weight, conv_out_weight, qkv_weight):
    plane = mesh.shape["tm"] * mesh.shape["height"]
    return (
        clip_inputs.shape[:4] == (1, 2, 2, 16)
        and mesh.shape["height"] == 2
        and mesh.shape["tm"] == 4
        and mesh.shape["dp"] == 4
        and conv_in_weight.shape[1] == plane * GROUP
        and clip_inputs.shape[4] == GROUP * GROUPS
        and conv_out_weight.shape[2] == TILE
        and qkv_weight.shape[1] == 6 * HD
    )


def lane_shifts(lane):
    col = lane % 16
    row = lane // 16 % 2
    half = lane // 64

    def cols(left, mid, right):
        left = jnp.where(col == 0, left, pltpu.roll(left, 1, 1))
        right = jnp.where(col == 15, right, pltpu.roll(right, LANES - 1, 1))
        return mid + left + right

    def rows(up, mid, down):
        up = jnp.where(
            row == 1, pltpu.roll(up, 16, 1), jnp.where(half == 1, pltpu.roll(up, 48, 1), up)
        )
        down = jnp.where(
            row == 0,
            pltpu.roll(down, LANES - 16, 1),
            jnp.where(half == 0, pltpu.roll(down, LANES - 48, 1), down),
        )
        return mid + up + down

    return cols, rows


def tap_sums(source, tiles):
    lane = lax.broadcasted_iota(jnp.int32, (TILE, LANES), 1)
    second = lane // 32 % 2 == 1
    cols, rows = lane_shifts(lane)
    sums = []
    before = None
    for tile in range(tiles):

        def part(tap):
            return source(tap, slice(tile * LANES, (tile + 1) * LANES))

        oldest, older, now = (
            rows(*(cols(*(part(9 * i + 3 * j + l) for l in range(3))) for j in range(3)))
            for i in range(3)
        )
        turned = pltpu.roll(older, 32, 1)
        if before is None:
            start = jnp.where(second, pltpu.roll(oldest, 32, 1), oldest)
            total = now + jnp.where(second, turned, older) + start
        else:
            total = now + jnp.where(second, turned, pltpu.roll(before[1], 96, 1)) + before[0]
        before = (oldest, older)
        sums.append(total)
    return sums


def pack_kernel(
    frame_ref, row_pos_ref, freq_ref, w_hbm, qkv_hbm, patch_hbm, patch_bias_hbm,
    gain_hbm, bias_hbm, out_bias_hbm, qkv_bias_hbm, q_hbm, k_hbm,
    own_hbm, side_hbm, high_hbm, far_hbm, scale_hbm, table_hbm,
    w_ref, qkv_ref, patch_ref, patch_bias_ref, gain_v, bias_v, out_bias_v, qkv_bias_v, q_v, k_v,
    rows_ref, turned_ref, merged_ref, out_ref, lines_ref, scale_ref, table_ref, sems,
):
    _, channels, width = out_ref.shape
    depth = w_ref.shape[0]
    rows = qkv_ref.shape[0]
    side = lax.axis_index("height")
    high = lax.axis_index("tm") // 2
    place = lax.axis_index("tm") * 2 + side
    at = pl.ds(pl.multiple_of(place * rows, LANES), rows)
    pairs = (
        (w_hbm, w_ref),
        (qkv_hbm, qkv_ref),
        (patch_hbm.at[:, at], patch_ref),
        (patch_bias_hbm, patch_bias_ref),
        (gain_hbm, gain_v),
        (bias_hbm, bias_v),
        (out_bias_hbm, out_bias_v),
        (qkv_bias_hbm, qkv_bias_v),
        (q_hbm, q_v),
        (k_hbm, k_v),
    )
    loads = [
        pltpu.make_async_copy(source, to, sems.at[index])
        for index, (source, to) in enumerate(pairs)
    ]
    for load in loads[4:] + loads[:4]:
        load.start()
    for load in loads[4:]:
        load.wait()
    fill_tables(
        frame_ref, row_pos_ref, freq_ref, gain_v, bias_v, out_bias_v, qkv_bias_v, q_v, k_v,
        scale_ref, table_ref,
    )
    stores = [
        pltpu.make_async_copy(scale_ref, scale_hbm, sems.at[15]),
        pltpu.make_async_copy(table_ref, table_hbm, sems.at[16]),
    ]
    for store in stores:
        store.start()
    whole = depth // LANES * LANES
    loads[0].wait()
    turned_ref[...] = w_ref[...].T
    for load in loads[1:4]:
        load.wait()
    merged_ref[...] = jnp.dot(patch_ref[...], qkv_ref[...], preferred_element_type=jnp.float32)
    own_main = own_hbm.at[:, :width]
    for flip, out_hbm in ((1, side_hbm), (2, high_hbm), (3, far_hbm), (0, own_main)):
        first = pl.multiple_of((high ^ (flip // 2)) * channels, channels)
        out_ref[flip, :, :whole] = turned_ref[pl.ds(first, channels), :whole]
        lower = turned_ref[pl.ds(first, channels), whole:]
        chip = (2 * high + side) ^ flip
        tail, upper = [], []
        for half in range(2):
            mine = merged_ref[pl.ds(pl.multiple_of(chip * 16 + half * 8, 8), 8)]
            mine = [mine[:, q * LANES : (q + 1) * LANES] for q in range(6)]
            tail += mine[:4]
            upper += [pltpu.roll(mine[4], 64, 1), mine[4], pltpu.roll(mine[5], 64, 1), mine[5]]
        upper = jnp.concatenate(upper, axis=0)[:, 64:].astype(jnp.bfloat16)
        out_ref[flip, :, whole : whole + LANES] = jnp.concatenate([lower, upper], axis=1)
        out_ref[flip, :, whole + LANES :] = jnp.concatenate(tail, axis=0).astype(jnp.bfloat16)
        stores.append(pltpu.make_async_copy(out_ref.at[flip], out_hbm, sems.at[10 + flip]))
        stores[-1].start()
    rows_ref[...] = patch_bias_ref[...].astype(jnp.float32).reshape(rows_ref.shape)
    count = rows // LANES
    bias = [rows_ref[pl.ds(count * place + part, 1), :] for part in range(count)]
    bias = jnp.broadcast_to(jnp.concatenate(bias, axis=1), (8, rows)).astype(jnp.bfloat16)
    bias = jnp.dot(bias, qkv_ref[...], preferred_element_type=jnp.float32)
    line = lax.broadcasted_iota(jnp.int32, (8, LANES), 0)
    lines = jnp.zeros((8, LANES), jnp.float32)
    for part in range(bias.shape[1] // LANES):
        lines = jnp.where(line == part, bias[:, part * LANES : (part + 1) * LANES], lines)
    lines_ref[...] = jnp.concatenate([lines, jnp.zeros_like(lines)], axis=0).astype(jnp.bfloat16)
    stores.append(
        pltpu.make_async_copy(lines_ref, own_hbm.at[:16, width : width + LANES], sems.at[14])
    )
    stores[-1].start()
    for store in stores:
        store.wait()


def column(row_ref, first, size):
    length = row_ref.shape[0]
    row = row_ref[...].astype(jnp.float32).reshape(1, length)
    line = lax.broadcasted_iota(jnp.int32, (size, length), 0)
    lane = lax.broadcasted_iota(jnp.int32, (size, length), 1)
    picked = jnp.where(lane == line + first, jnp.broadcast_to(row, (size, length)), 0.0)
    return jnp.sum(picked, axis=1, keepdims=True)


def fill_tables(
    frame_ref, row_pos_ref, freq_ref, gain_v, bias_v, out_bias_v, qkv_v, q_v, k_v,
    scale_ref, table_ref,
):
    shape = (TILE, LANES)
    line = lax.broadcasted_iota(jnp.int32, shape, 0)
    lane = lax.broadcasted_iota(jnp.int32, shape, 1)
    frame = jnp.where(line // 8 == 0, frame_ref[0], frame_ref[1]).astype(jnp.float32)
    row = jnp.broadcast_to(row_pos_ref[0], shape).astype(jnp.float32)
    spot = jnp.where(lane < 72, row, (line % 8).astype(jnp.float32))
    angles = jnp.where(lane < 16, frame, spot) * freq_ref[...]
    table_ref[:16] = jnp.cos(angles)
    sine = jnp.sin(angles)
    table_ref[16:32] = jnp.where(lane % 2 == 0, -sine, sine)
    first = lax.axis_index("tm") // 2 * (4 * GROUP)
    scale_ref[:, 0:1] = column(gain_v, first, 4 * GROUP)
    scale_ref[:, 1:2] = column(bias_v, first, 4 * GROUP)
    table_ref[32:48] = jnp.broadcast_to(column(out_bias_v, 0, TILE), shape)
    table_ref[48:49] = q_v[...].astype(jnp.float32).reshape(1, HD)
    table_ref[49:50] = k_v[...].astype(jnp.float32).reshape(1, HD)
    table_ref[50:56] = qkv_v[...].astype(jnp.float32).reshape(6, LANES)


def arrange_kernel(*refs):
    pieces, (own_ref, keep_ref, send_ref, all_ref) = refs[:4], refs[4:]
    side = lax.axis_index("height")
    layer = lax.axis_index("dp")
    for step, piece in enumerate(pieces):
        all_ref[(layer + 4 - step) % 4] = piece[...]

    @pl.when(layer % 2 == lax.axis_index("tm") % 2)
    def _():
        all_ref[layer] = own_ref[...]

    for core in range(2):
        keep_ref[core] = all_ref[2 * side + core]
        send_ref[core] = all_ref[2 - 2 * side + core]


def core_taps(core):
    quarter = TAPS / 4
    taps = []
    for tm in (core, core + 2):
        taps += range(int(quarter * tm), min(TAPS, -int(-quarter * (tm + 1) // 1)))
    return taps


def join_kernel(own_ref, side_ref, high_ref, far_ref, wt_ref, all_ref):
    channels, width = side_ref.shape
    inner = wt_ref.shape[1]
    depth = TAPS * inner // 8
    here = lax.axis_index("tm") // 2 * 2 + lax.axis_index("height")
    for flip, ref in enumerate((own_ref, side_ref, high_ref, far_ref)):
        all_ref[here ^ flip] = ref[:, :width]

    def assemble(core):
        for index, tap in enumerate(core_taps(core)):
            rows = slice(index * channels, (index + 1) * channels)
            start, end = tap * inner, (tap + 1) * inner
            while start < end:
                source = start // depth
                stop = min(end, (source + 1) * depth)
                to = slice(start - tap * inner, stop - tap * inner)
                if source // 2 % 2 == core:
                    chip = source // 4 * 2 + source % 2
                    first = start - source * depth
                    wt_ref[rows, to] = all_ref[chip, :, first : first + stop - start]
                else:
                    wt_ref[rows, to] = jnp.zeros((channels, stop - start), jnp.bfloat16)
                start = stop

    core = lax.axis_index("tm") % 2
    pl.when(core == 0)(functools.partial(assemble, 0))
    pl.when(core == 1)(functools.partial(assemble, 1))
    total = sum(all_ref[chip, :, width - 2 * LANES :].astype(jnp.float32) for chip in range(4))
    low = lax.broadcasted_iota(jnp.int32, (8, LANES), 1) < 64
    empty = jnp.zeros((8, LANES), jnp.float32)
    wide, narrow = [], []
    for half in range(2):
        top = 32 * half
        wide.append([total[top + 8 * q : top + 8 * q + 8, LANES:] for q in range(4)])
        some = []
        for q in range(2):
            one = total[top + 16 * q : top + 16 * q + 8, :LANES]
            two = total[top + 16 * q + 8 : top + 16 * q + 16, :LANES]
            some.append(jnp.where(low, pltpu.roll(one, 64, 1), two))
        lines = own_ref[:16, width:].astype(jnp.float32)[8 * half : 8 * half + 8]
        narrow.append(some + [lines, empty])
    share = jnp.concatenate([jnp.concatenate(row, axis=1) for row in wide + narrow], axis=0)
    wt_ref[wt_ref.shape[0] - 32 :] = share.astype(jnp.bfloat16)


def place_kernel(*refs):
    pieces, x_ref = refs[:4], refs[4]
    place = lax.axis_index("tm") // 2 * 4 + lax.axis_index("height")
    for flip, piece in zip((0, 1, 4, 5), pieces):
        for core in range(2):
            x_ref[(place ^ flip) + 2 * core] = piece[core]


def tap_parts(y_ref, group, channels):
    held = [core_taps(core) for core in range(2)]

    def part(tap, lanes):
        found = []
        for core in range(2):
            if tap in held[core]:
                at = held[core].index(tap) * channels + group * GROUP
                found.append(y_ref[core, at : at + GROUP, lanes])
        return sum(found[1:], found[0])

    return part


def conv_kernel(
    x_ref, wt_ref, pair_ref, scale_ref, w2_ref, out_ref, y_ref
):
    channels = 4 * GROUP
    tiles = x_ref.shape[0] // 2
    count = float(tiles * LANES * GROUP)
    core = lax.axis_index("tm") % 2
    height = y_ref.shape[1]
    x = x_ref[...].reshape(tiles * LANES, x_ref.shape[2])
    for ref, at in ((wt_ref, core), (pair_ref, 1 - core)):
        y_ref[at] = lax.dot_general(
            ref[:height], x, (((1,), (1,)), ((), ())), preferred_element_type=jnp.float32
        )
    normed = []
    for group in range(4):
        hidden = tap_sums(tap_parts(y_ref, group, channels), tiles)
        at = slice(group * GROUP, (group + 1) * GROUP)
        mean = jnp.sum(sum(hidden), keepdims=True) / count
        square = jnp.sum(sum(part * part for part in hidden), keepdims=True) / count
        scale = lax.rsqrt(square - mean * mean + norm_eps)
        parts = []
        for part in hidden:
            scaled = (part - mean) * scale * scale_ref[at, 0:1] + scale_ref[at, 1:2]
            parts.append((scaled / (1.0 + jnp.exp(-scaled))).astype(jnp.bfloat16))
        normed.append(jnp.concatenate(parts, axis=1))
    y_ref[0, : TAPS * TILE] = jnp.dot(
        w2_ref[...], jnp.concatenate(normed, axis=0), preferred_element_type=jnp.float32
    )

    def part(tap, lanes):
        return y_ref[0, tap * TILE : (tap + 1) * TILE, lanes]

    low = lax.broadcasted_iota(jnp.int32, (8, LANES), 1) < 64
    layers = out_ref.shape[0] // (2 * tiles)
    for tile, latent in enumerate(tap_sums(part, tiles)):
        turned = pltpu.roll(latent, 64, 1)
        near = jnp.where(low, latent[:8], turned[8:])
        far = jnp.where(low, turned[:8], latent[8:])
        for layer in range(layers):
            out_ref[layer * 2 * tiles + 2 * tile] = near
            out_ref[layer * 2 * tiles + 2 * tile + 1] = far


def share_kernel(m0_ref, m1_ref, m2_ref, m3_ref, table_ref, merged_ref, base_ref, m_ref):
    here = lax.axis_index("tm") // 2 * 2 + lax.axis_index("height")
    lines = table_ref[48:56]
    for flip, ref in enumerate((m0_ref, m1_ref, m2_ref, m3_ref)):
        share = ref[...].astype(jnp.float32)
        m_ref[here ^ flip, :, : 4 * LANES] = share[:16]
        m_ref[here ^ flip, :, 4 * LANES :] = share[16:, : 2 * LANES]
        lines = lines + pltpu.roll(share[16:24, 2 * LANES : 3 * LANES], 2, 0)
    base_ref[...] = jnp.concatenate([lines[2 + part : 3 + part] for part in range(6)], axis=1)
    merged_ref[...] = m_ref[...].reshape(merged_ref.shape).astype(jnp.bfloat16)


def token_kernel(p_ref, m_ref, base_ref, table_ref, lat_ref, q_ref, k_ref, v_ref):
    low = lax.broadcasted_iota(jnp.int32, (8, LANES), 1) < 64
    pairs = []
    for side in range(2):
        one, two = (
            sum(p_ref[4 * index + 2 * core + side] for index in range(p_ref.shape[0] // 4))
            for core in range(2)
        )
        top = jnp.where(low, one, pltpu.roll(two, 64, 1))
        bottom = jnp.where(low, pltpu.roll(one, 64, 1), two)
        pairs.append(jnp.concatenate([top, bottom], axis=0))
    total = jnp.concatenate(pairs, axis=1)
    lat = (total + table_ref[32:48, :1]) * latent_scale
    clips = lat.shape[1] // 64
    tokens = clips * 16
    place = lax.axis_index("dp")
    own = lat[:, :LANES]
    for pair in range(1, clips // 2):
        own = jnp.where(place // 2 == pair, lat[:, pair * LANES : (pair + 1) * LANES], own)
    own = jnp.where(place % 2 == 1, pltpu.roll(own, 64, 1), own)
    turned = own.T[:64]
    wide = jnp.concatenate([turned] * 16, axis=1)
    spot = lax.broadcasted_iota(jnp.int32, wide.shape, 0) % 16
    spread = lax.broadcasted_iota(jnp.int32, wide.shape, 1) // 16
    merged = jnp.sum(jnp.where(spot == spread, wide, 0.0).reshape(4, 16, 256), axis=1)
    lat_ref[0, 0] = merged[:2]
    lat_ref[0, 1] = merged[2:]

    lat_bf = lat.astype(jnp.bfloat16)
    token = lax.broadcasted_iota(jnp.int32, (tokens, clips * 64), 0)
    lane = lax.broadcasted_iota(jnp.int32, (tokens, clips * 64), 1)
    first = token // 8 * 32 + token % 8 * 2
    heads = q_ref.shape[2] // HD
    projected = base_ref[...]
    for a in range(2):
        for e in range(2):
            chosen = jnp.where(lane == first + (16 * a + e), 1.0, 0.0).astype(jnp.bfloat16)
            patch = lax.dot_general(
                chosen, lat_bf, (((1,), (1,)), ((), ())), preferred_element_type=jnp.float32
            ).astype(jnp.bfloat16)
            weight = m_ref[(2 * a + e) * TILE : (2 * a + e + 1) * TILE]
            projected = projected + jnp.dot(patch, weight, preferred_element_type=jnp.float32)

    even = lax.broadcasted_iota(jnp.int32, (tokens, HD), 1) % 2 == 0
    cosine = jnp.concatenate([table_ref[:16]] * clips, axis=0)
    sine = jnp.concatenate([table_ref[16:32]] * clips, axis=0)

    def turn(vectors, gain):
        square = jnp.mean(vectors * vectors, axis=-1, keepdims=True)
        vectors = vectors * lax.rsqrt(square + norm_eps) * gain
        swapped = jnp.where(even, pltpu.roll(vectors, HD - 1, 1), pltpu.roll(vectors, 1, 1))
        return vectors * cosine + swapped * sine

    def keep(ref, head, value):
        value = value.reshape(tokens // 8, 8, HD).astype(jnp.bfloat16)
        ref[:, :, head * HD : (head + 1) * HD] = value

    for head in range(heads):
        at = 3 * HD * head
        keep(q_ref, head, turn(projected[:, at : at + HD], table_ref[48:49]))
        keep(k_ref, head, turn(projected[:, at + HD : at + 2 * HD], table_ref[49:50]))
        keep(v_ref, head, projected[:, at + 2 * HD : at + 3 * HD])


def rope_freqs():
    freqs = []
    for dims in (time_dims, row_dims, row_dims):
        freqs.append(rope_base ** (-np.arange(0, dims, 2, dtype=np.float64) / dims))
    return np.repeat(np.concatenate(freqs), 2)[None].astype(np.float32)


def vmem(count):
    return [pl.BlockSpec(memory_space=pltpu.VMEM)] * count


def grouped(
    clip_inputs,
    conv_in_weight,
    group_gain,
    group_bias,
    conv_out_weight,
    out_bias,
    patch_weight,
    patch_bias,
    qkv_weight,
    qkv_bias,
    q_gain,
    k_gain,
    frame_pos,
    row_pos,
):
    plane_axes = ("tm", "height")
    clips = lax.axis_size("dp")
    steps = lax.axis_size("tm")
    plane = steps * lax.axis_size("height")
    channels = clip_inputs.shape[4]
    depth = conv_in_weight.shape[0]

    width = -(-depth // LANES) * LANES + LANES
    hbm = pl.BlockSpec(memory_space=pltpu.HBM)
    wide = pltpu.CompilerParams(vmem_limit_bytes=60 * 1024 * 1024)
    limit = pltpu.CompilerParams(vmem_limit_bytes=32 * 1024 * 1024)
    small = pl.CostEstimate(flops=10**6, bytes_accessed=10**6, transcendentals=0)
    with jax.named_scope("weight_by_group"):
        weight_block = jax.ShapeDtypeStruct((4 * GROUP, width), jnp.bfloat16)
        own_block = jax.ShapeDtypeStruct((4 * GROUP, width + LANES), jnp.bfloat16)
        smem = pl.BlockSpec(memory_space=pltpu.SMEM)
        small_arrays = (group_gain, group_bias, out_bias, qkv_bias, q_gain, k_gain)
        *packed, scale, table = pl.pallas_call(
            pack_kernel,
            out_shape=(own_block,)
            + (weight_block,) * 3
            + (
                jax.ShapeDtypeStruct((4 * GROUP, 2), jnp.float32),
                jax.ShapeDtypeStruct((56, LANES), jnp.float32),
            ),
            in_specs=[smem, smem, vmem(1)[0]] + [hbm] * 10,
            out_specs=(hbm,) * 6,
            scratch_shapes=[
                pltpu.VMEM(conv_in_weight.shape, jnp.bfloat16),
                pltpu.VMEM(qkv_weight.shape, jnp.bfloat16),
                pltpu.VMEM((patch_weight.shape[0], qkv_weight.shape[0]), jnp.bfloat16),
                pltpu.VMEM(patch_bias.shape, jnp.bfloat16),
                *[pltpu.VMEM(array.shape, array.dtype) for array in small_arrays],
                pltpu.VMEM((patch_bias.shape[0] // LANES, LANES), jnp.float32),
                pltpu.VMEM((8 * GROUP, depth), jnp.bfloat16),
                pltpu.VMEM((patch_weight.shape[0], qkv_weight.shape[1]), jnp.float32),
                pltpu.VMEM((4, 4 * GROUP, width), jnp.bfloat16),
                pltpu.VMEM((16, LANES), jnp.bfloat16),
                pltpu.VMEM((4 * GROUP, 2), jnp.float32),
                pltpu.VMEM((56, LANES), jnp.float32),
                pltpu.SemaphoreType.DMA((17,)),
            ],
            compiler_params=wide,
            cost_estimate=pl.CostEstimate(flops=10**8, bytes_accessed=10**6, transcendentals=0),
            name="pack_weights",
        )(
            frame_pos,
            row_pos,
            rope_freqs(),
            conv_in_weight,
            qkv_weight,
            patch_weight,
            patch_bias,
            *small_arrays,
        )
        blocks = [packed[0]]
        for flip, block in zip((1, 4, 5), packed[1:]):
            blocks.append(lax.ppermute(block, plane_axes, [(i, i ^ flip) for i in range(plane)]))
    with jax.named_scope("gather_clips"):
        own = clip_inputs.reshape(64, channels)
        layers = []
        for step in range(clips):
            pairs = []
            for layer in range(clips):
                for tm in range(steps):
                    to = (layer // 2 * 2 + tm % 2 + step) % clips
                    pair = (layer * steps + tm, to * steps + tm // 2 * 2 + layer % 2)
                    if pair[0] != pair[1]:
                        pairs.append(pair)
            layers.append(lax.ppermute(own, ("dp", "tm"), pairs))
    with jax.named_scope("spread_clips"):
        keep, send = pl.pallas_call(
            arrange_kernel,
            out_shape=(jax.ShapeDtypeStruct((2, 64, channels), jnp.bfloat16),) * 2,
            in_specs=vmem(5),
            out_specs=tuple(vmem(2)),
            scratch_shapes=[pltpu.VMEM((4, 64, channels), jnp.bfloat16)],
            compiler_params=limit,
            cost_estimate=small,
            name="arrange_clips",
        )(*layers, own)
        pieces = [keep]
        for flip in (1, 4, 5):
            pairs = [(i, i ^ flip) for i in range(plane)]
            pieces.append(lax.ppermute(send if flip % 2 else keep, plane_axes, pairs))
    with jax.named_scope("small_weights"):
        first = lax.axis_index("tm") // 2 * (4 * GROUP)
        weight_out = lax.dynamic_slice_in_dim(conv_out_weight, first, 4 * GROUP, axis=1)
        weight_out = weight_out.transpose(0, 2, 1).reshape(TAPS * TILE, 4 * GROUP)
    with jax.named_scope("join_weights"):
        height = len(core_taps(0)) * 4 * GROUP
        joined = pl.pallas_call(
            join_kernel,
            out_shape=jax.ShapeDtypeStruct((height + 32, channels), jnp.bfloat16),
            in_specs=vmem(4),
            out_specs=vmem(1)[0],
            scratch_shapes=[pltpu.VMEM((4, 4 * GROUP, width), jnp.bfloat16)],
            compiler_params=limit,
            cost_estimate=small,
            name="join_weights",
        )(*blocks)
        joined_pair = lax.ppermute(joined, "tm", [(i, i ^ 1) for i in range(steps)])
    with jax.named_scope("merged_projection"):
        share = joined[height:].astype(jnp.float32) + joined_pair[height:].astype(jnp.float32)
        share = share.astype(jnp.bfloat16)
        shares = [share]
        for flip in (1, 4, 5):
            pairs = [(i, i ^ flip) for i in range(plane)]
            shares.append(lax.ppermute(share, plane_axes, pairs))

        merged, base = pl.pallas_call(
            share_kernel,
            out_shape=(
                jax.ShapeDtypeStruct((64, 6 * HD), jnp.bfloat16),
                jax.ShapeDtypeStruct((1, 6 * HD), jnp.float32),
            ),
            in_specs=vmem(5),
            out_specs=tuple(vmem(2)),
            scratch_shapes=[pltpu.VMEM((4, 16, 6 * HD), jnp.float32)],
            compiler_params=limit,
            cost_estimate=small,
            name="share_rows",
        )(*shares, table)

    flops = 4 * height * steps * LANES * channels
    clip = pl.pallas_call(
        place_kernel,
        out_shape=jax.ShapeDtypeStruct((plane, 64, channels), jnp.bfloat16),
        in_specs=vmem(4),
        out_specs=vmem(1)[0],
        compiler_params=limit,
        cost_estimate=pl.CostEstimate(flops=4 * 10**10, bytes_accessed=10**6, transcendentals=0),
        name="place_clip",
    )(*pieces)
    partial = pl.pallas_call(
        conv_kernel,
        out_shape=jax.ShapeDtypeStruct((clips * plane, 8, LANES), jnp.float32),
        in_specs=vmem(5),
        out_specs=vmem(1)[0],
        scratch_shapes=[
            pltpu.VMEM((2, height, steps * LANES), jnp.float32),
        ],
        compiler_params=limit,
        cost_estimate=pl.CostEstimate(flops=flops, bytes_accessed=10**6, transcendentals=0),
        name="convolutions",
    )(clip, joined, joined_pair, scale, weight_out)

    with jax.named_scope("sum_latents"):
        partials = lax.all_to_all(partial, ("dp",) + plane_axes, 0, 0, tiled=True)

    heads = qkv_weight.shape[1] // (3 * HD)
    frames = clip_inputs.shape[1]
    tokens = jax.ShapeDtypeStruct((clips * frames, 8, heads * HD), jnp.bfloat16)
    latents, query, key, value = pl.pallas_call(
        token_kernel,
        out_shape=(jax.ShapeDtypeStruct((1, 2, 2, 256), jnp.float32), tokens, tokens, tokens),
        in_specs=vmem(4),
        out_specs=tuple(vmem(4)),
        compiler_params=limit,
        cost_estimate=pl.CostEstimate(flops=10**8, bytes_accessed=10**6, transcendentals=0),
        name="tokens",
    )(
        partials,
        merged,
        base,
        table,
    )
    full = (clips, frames, 1, 8, heads * HD)
    return latents, query.reshape(full), key.reshape(full), value.reshape(full)


def pick(mesh, *arrays):
    if one_group_each(mesh, arrays[0], arrays[1], arrays[4], arrays[8]):
        return grouped(*arrays)
    return shards(*arrays)


def solution(mesh):
    placed = (
        P("dp", "tm", "height", None, None),
        P(("tm", "height"), "dp"),
        P("dp"),
        P("dp"),
        P(None, "dp", None),
        P(),
        P(),
        P(),
        P(("tm", "height"), "dp"),
        P("dp"),
        P(),
        P(),
        P("tm"),
        P("height"),
    )
    return jax.shard_map(
        functools.partial(pick, mesh),
        mesh=mesh,
        in_specs=placed,
        out_specs=(
            P("dp", "tm", "height", None),
            P(None, "tm", "height", None, "dp"),
            P(None, "tm", "height", None, "dp"),
            P(None, "tm", "height", None, "dp"),
        ),
        check_vma=False,
    )
```

```python
import functools

import jax
import jax.numpy as jnp
import numpy as np
from jax import lax
from jax.experimental import pallas as pl
from jax.experimental.pallas import tpu as pltpu
from jax.sharding import PartitionSpec as P

HD = 128
GROUPS = 32
TAPS = 27


norm_eps = 1e-06
latent_scale = 0.476986
rope_base = 256.0
time_dims = 16
row_dims = 56


def from_behind(value, axis, steps):
    count = lax.axis_size(axis)
    first, last = (max(0, -steps), min(count, count - steps))
    return lax.ppermute(value, axis, [(source, source + steps) for source in range(first, last)])


def padded_2(block, sides, width):
    for axis, dim in sides:
        count = lax.axis_size(axis)
        forward = [(i, i + 1) for i in range(count - 1)]
        backward = [(target, source) for source, target in forward]
        low = lax.ppermute(
            lax.slice_in_dim(block, block.shape[dim] - width, None, axis=dim), axis, forward
        )
        high = lax.ppermute(lax.slice_in_dim(block, 0, width, axis=dim), axis, backward)
        block = jnp.concatenate([low, block, high], axis=dim)
    return block


def repeat_first(block):
    return jnp.concatenate([block[:, :1], block[:, :1]], axis=1)


def time_join(block, earlier):
    start = jnp.where(lax.axis_index("tm") == 0, repeat_first(block), earlier)
    return jnp.concatenate([start, block], axis=1)


def rows_finish(grown):
    place = lax.axis_index("height")
    top = jnp.where(place == 0, grown[:, :, 1:2], grown[:, :, :1])
    bottom = jnp.where(place == lax.axis_size("height") - 1, grown[:, :, -2:-1], grown[:, :, -1:])
    inner = jnp.concatenate([top, grown[:, :, 1:-1], bottom], axis=2)
    return jnp.pad(inner, ((0, 0), (0, 0), (0, 0), (1, 1), (0, 0)), mode="edge")


def edges_before(block):
    earlier = from_behind(block, "tm", 1)
    longer = time_join(block, earlier)
    return rows_finish(padded_2(longer, (("height", 2),), 1))


def edges_norm(block):
    earlier = from_behind(block, "tm", 1)
    longer = time_join(block, earlier)
    return rows_finish(padded_2(longer, (("height", 2),), 1))


def convolve(padded, weight):
    clips = padded.shape[0]
    frames = padded.shape[1] - 2
    rows = padded.shape[2] - 2
    cols = padded.shape[3] - 2
    total = jnp.zeros((clips * frames * rows * cols, weight.shape[2]), jnp.float32)
    for shift_t in range(3):
        for shift_r in range(3):
            for shift_c in range(3):
                window = padded[
                    :,
                    shift_t : shift_t + frames,
                    shift_r : shift_r + rows,
                    shift_c : shift_c + cols,
                ]
                window = window.reshape(-1, padded.shape[4])
                total = total + jnp.dot(
                    window,
                    weight[9 * shift_t + 3 * shift_r + shift_c],
                    preferred_element_type=jnp.float32,
                )
    return total.reshape(clips, frames, rows, cols, weight.shape[2])


def section_freqs(dims):
    return jnp.power(rope_base, -jnp.arange(0, dims, 2, dtype=jnp.float32) / dims)


def rope_angles(tpos, hpos, width):
    frames = tpos.shape[0]
    rows = hpos.shape[0]
    cols = jnp.arange(width, dtype=jnp.float32)
    part_t = tpos[:, None, None, None] * section_freqs(time_dims)
    part_h = hpos[None, :, None, None] * section_freqs(row_dims)
    part_w = cols[None, None, :, None] * section_freqs(row_dims)
    shape = (frames, rows, width)
    return jnp.concatenate(
        [
            jnp.broadcast_to(part_t, shape + (time_dims // 2,)),
            jnp.broadcast_to(part_h, shape + (row_dims // 2,)),
            jnp.broadcast_to(part_w, shape + (row_dims // 2,)),
        ],
        axis=-1,
    )


def rotate(vectors, angles):
    pairs = vectors.reshape(vectors.shape[:-1] + (vectors.shape[-1] // 2, 2))
    first = pairs[..., 0]
    second = pairs[..., 1]
    cosine = jnp.cos(angles)[..., None, :]
    sine = jnp.sin(angles)[..., None, :]
    turned = jnp.stack([first * cosine - second * sine, first * sine + second * cosine], axis=-1)
    return turned.reshape(vectors.shape)


def rms_scale(vectors, gain):
    return (
        vectors
        * lax.rsqrt(jnp.mean(vectors * vectors, axis=-1, keepdims=True) + norm_eps)
        * gain.astype(jnp.float32)
    )


def shards(
    clip_inputs,
    conv_in_weight,
    group_gain,
    group_bias,
    conv_out_weight,
    out_bias,
    patch_weight,
    patch_bias,
    qkv_weight,
    qkv_bias,
    q_gain,
    k_gain,
    frame_pos,
    row_pos,
):
    channels = clip_inputs.shape[4]
    frames = clip_inputs.shape[1]
    rows = clip_inputs.shape[2]
    cols = clip_inputs.shape[3]
    padded = lax.all_gather(edges_before(clip_inputs), "dp", axis=0, tiled=True)
    clips = padded.shape[0]
    weight_in = lax.all_gather(conv_in_weight, ("tm", "height"), axis=0, tiled=True).reshape(
        TAPS, channels, -1
    )
    hidden = convolve(padded, weight_in)
    block_width = hidden.shape[4]
    group_width = channels // GROUPS
    local_groups = block_width // group_width
    grouped = hidden.reshape(clips, -1, local_groups, group_width)
    sums_local = jnp.sum(grouped, axis=(1, 3))
    squares_local = jnp.sum(grouped * grouped, axis=(1, 3))
    sums_all, squares_all = lax.psum((sums_local, squares_local), ("tm", "height"))
    count = float(
        frames * lax.axis_size("tm") * rows * lax.axis_size("height") * cols * group_width
    )
    mean = sums_all / count
    var = squares_all / count - mean * mean
    scaled = (grouped - mean[:, None, :, None]) * lax.rsqrt(var + norm_eps)[:, None, :, None]
    scaled = scaled.reshape(hidden.shape) * group_gain.astype(jnp.float32) + group_bias.astype(
        jnp.float32
    )
    normed = jax.nn.silu(scaled).astype(jnp.bfloat16)
    partial_latent = convolve(edges_norm(normed), conv_out_weight)
    own_sum = lax.psum_scatter(partial_latent, "dp", scatter_dimension=0, tiled=True)
    own_latent = (own_sum + out_bias) * latent_scale
    every_latent = lax.all_gather(own_latent.astype(jnp.bfloat16), "dp", axis=0, tiled=True)
    latent_dims = every_latent.shape[4]
    latents = own_latent.reshape(1, frames, rows, cols * latent_dims)
    tok_rows = rows // 2
    tok_cols = cols // 2
    patches = every_latent.reshape(clips, frames, tok_rows, 2, tok_cols, 2, latent_dims)
    patches = patches.transpose(0, 1, 2, 4, 3, 5, 6).reshape(-1, 4 * latent_dims)
    embedded = (
        jnp.dot(patches, patch_weight, preferred_element_type=jnp.float32)
        + patch_bias.astype(jnp.float32)
    ).astype(jnp.bfloat16)
    projected = jnp.dot(
        embedded,
        lax.all_gather(qkv_weight, ("tm", "height"), axis=0, tiled=True),
        preferred_element_type=jnp.float32,
    )
    projected = projected + qkv_bias.astype(jnp.float32)
    local_heads = qkv_weight.shape[1] // (3 * HD)
    projected = projected.reshape(clips, frames, tok_rows, tok_cols, local_heads, 3, HD)
    angles = rope_angles(frame_pos.astype(jnp.float32), row_pos.astype(jnp.float32), tok_cols)
    query = rotate(rms_scale(projected[..., 0, :], q_gain), angles)
    key = rotate(rms_scale(projected[..., 1, :], k_gain), angles)
    value = projected[..., 2, :]
    merged = (clips, frames, tok_rows, tok_cols, local_heads * HD)
    return (
        latents,
        query.reshape(merged).astype(jnp.bfloat16),
        key.reshape(merged).astype(jnp.bfloat16),
        value.reshape(merged).astype(jnp.bfloat16),
    )


LANES = 128
TILE = 16
GROUP = 16


def one_group_each(mesh, clip_inputs, conv_in_weight, conv_out_weight, qkv_weight):
    plane = mesh.shape["tm"] * mesh.shape["height"]
    return (
        clip_inputs.shape[:4] == (1, 2, 2, 16)
        and mesh.shape["height"] == 2
        and mesh.shape["tm"] == 4
        and mesh.shape["dp"] == 4
        and conv_in_weight.shape[1] == plane * GROUP
        and clip_inputs.shape[4] == GROUP * GROUPS
        and conv_out_weight.shape[2] == TILE
        and qkv_weight.shape[1] == 6 * HD
    )


def lane_shifts(lane):
    col = lane % 16
    row = lane // 16 % 2
    half = lane // 64

    def cols(left, mid, right):
        left = jnp.where(col == 0, left, pltpu.roll(left, 1, 1))
        right = jnp.where(col == 15, right, pltpu.roll(right, LANES - 1, 1))
        return mid + left + right

    def rows(up, mid, down):
        up = jnp.where(
            row == 1, pltpu.roll(up, 16, 1), jnp.where(half == 1, pltpu.roll(up, 48, 1), up)
        )
        down = jnp.where(
            row == 0,
            pltpu.roll(down, LANES - 16, 1),
            jnp.where(half == 0, pltpu.roll(down, LANES - 48, 1), down),
        )
        return mid + up + down

    return cols, rows


def tap_sums(source, tiles):
    lane = lax.broadcasted_iota(jnp.int32, (TILE, LANES), 1)
    second = lane // 32 % 2 == 1
    cols, rows = lane_shifts(lane)
    sums = []
    before = None
    for tile in range(tiles):

        def part(tap):
            return source(tap, slice(tile * LANES, (tile + 1) * LANES))

        oldest, older, now = (
            rows(*(cols(*(part(9 * i + 3 * j + l) for l in range(3))) for j in range(3)))
            for i in range(3)
        )
        turned = pltpu.roll(older, 32, 1)
        if before is None:
            start = jnp.where(second, pltpu.roll(oldest, 32, 1), oldest)
            total = now + jnp.where(second, turned, older) + start
        else:
            total = now + jnp.where(second, turned, pltpu.roll(before[1], 96, 1)) + before[0]
        before = (oldest, older)
        sums.append(total)
    return sums


def pack_kernel(
    freq_hbm, w_hbm, qkv_hbm, patch_hbm, patch_bias_hbm, gain_hbm, bias_hbm, out_bias_hbm,
    qkv_bias_hbm, q_hbm, k_hbm, frame_hbm,
    own_hbm, side_hbm, high_hbm, far_hbm, scale_hbm, table_hbm,
    w_ref, qkv_ref, patch_ref, patch_bias_ref, gain_v, bias_v, out_bias_v, qkv_bias_v, q_v, k_v,
    frame_v, freq_ref, rows_ref, turned_ref, merged_ref, out_ref, lines_ref, scale_ref, table_ref, sems,
):
    _, channels, width = out_ref.shape
    depth = w_ref.shape[0]
    rows = qkv_ref.shape[0]
    side = lax.axis_index("height")
    high = lax.axis_index("tm") // 2
    place = lax.axis_index("tm") * 2 + side
    at = pl.ds(pl.multiple_of(place * rows, LANES), rows)
    pairs = (
        (w_hbm, w_ref),
        (qkv_hbm, qkv_ref),
        (patch_hbm.at[:, at], patch_ref),
        (patch_bias_hbm, patch_bias_ref),
        (gain_hbm, gain_v),
        (bias_hbm, bias_v),
        (out_bias_hbm, out_bias_v),
        (qkv_bias_hbm, qkv_bias_v),
        (q_hbm, q_v),
        (k_hbm, k_v),
        (frame_hbm, frame_v),
        (freq_hbm, freq_ref),
    )
    loads = [
        pltpu.make_async_copy(source, to, sems.at[index])
        for index, (source, to) in enumerate(pairs)
    ]
    for load in loads:
        load.start()
    whole = depth // LANES * LANES
    loads[0].wait()
    turned_ref[...] = w_ref[...].T
    for load in loads[1:4]:
        load.wait()
    merged_ref[...] = jnp.dot(patch_ref[...], qkv_ref[...], preferred_element_type=jnp.float32)
    stores = []
    own_main = own_hbm.at[:, :width]
    for flip, out_hbm in ((1, side_hbm), (2, high_hbm), (3, far_hbm), (0, own_main)):
        first = pl.multiple_of((high ^ (flip // 2)) * channels, channels)
        out_ref[flip, :, :whole] = turned_ref[pl.ds(first, channels), :whole]
        lower = turned_ref[pl.ds(first, channels), whole:]
        chip = (2 * high + side) ^ flip
        tail, upper = [], []
        for half in range(2):
            mine = merged_ref[pl.ds(pl.multiple_of(chip * 16 + half * 8, 8), 8)]
            mine = [mine[:, q * LANES : (q + 1) * LANES] for q in range(6)]
            tail += mine[:4]
            upper += [pltpu.roll(mine[4], 64, 1), mine[4], pltpu.roll(mine[5], 64, 1), mine[5]]
        upper = jnp.concatenate(upper, axis=0)[:, 64:].astype(jnp.bfloat16)
        out_ref[flip, :, whole : whole + LANES] = jnp.concatenate([lower, upper], axis=1)
        out_ref[flip, :, whole + LANES :] = jnp.concatenate(tail, axis=0).astype(jnp.bfloat16)
        stores.append(pltpu.make_async_copy(out_ref.at[flip], out_hbm, sems.at[13 + flip]))
        stores[-1].start()
    rows_ref[...] = patch_bias_ref[...].astype(jnp.float32).reshape(rows_ref.shape)
    count = rows // LANES
    bias = [rows_ref[pl.ds(count * place + part, 1), :] for part in range(count)]
    bias = jnp.broadcast_to(jnp.concatenate(bias, axis=1), (8, rows)).astype(jnp.bfloat16)
    bias = jnp.dot(bias, qkv_ref[...], preferred_element_type=jnp.float32)
    line = lax.broadcasted_iota(jnp.int32, (8, LANES), 0)
    lines = jnp.zeros((8, LANES), jnp.float32)
    for part in range(bias.shape[1] // LANES):
        lines = jnp.where(line == part, bias[:, part * LANES : (part + 1) * LANES], lines)
    lines_ref[...] = jnp.concatenate([lines, jnp.zeros_like(lines)], axis=0).astype(jnp.bfloat16)
    stores.append(
        pltpu.make_async_copy(lines_ref, own_hbm.at[:16, width : width + LANES], sems.at[17])
    )
    stores[-1].start()
    for load in loads[4:]:
        load.wait()
    fill_tables(
        frame_v, freq_ref, gain_v, bias_v, out_bias_v, qkv_bias_v, q_v, k_v,
        scale_ref, table_ref,
    )
    for index, (source, to) in enumerate(((scale_ref, scale_hbm), (table_ref, table_hbm))):
        stores.append(pltpu.make_async_copy(source, to, sems.at[18 + index]))
        stores[-1].start()
    for store in stores:
        store.wait()


def column(row_ref, first, size):
    length = row_ref.shape[0]
    row = row_ref[...].astype(jnp.float32).reshape(1, length)
    line = lax.broadcasted_iota(jnp.int32, (size, length), 0)
    lane = lax.broadcasted_iota(jnp.int32, (size, length), 1)
    picked = jnp.where(lane == line + first, jnp.broadcast_to(row, (size, length)), 0.0)
    return jnp.sum(picked, axis=1, keepdims=True)


def fill_tables(
    frame_ref, freq_ref, gain_v, bias_v, out_bias_v, qkv_v, q_v, k_v,
    scale_ref, table_ref,
):
    shape = (TILE, LANES)
    line = lax.broadcasted_iota(jnp.int32, shape, 0)
    lane = lax.broadcasted_iota(jnp.int32, shape, 1)
    frames = frame_ref[...].astype(jnp.float32).reshape(1, 2)
    one, two = (jnp.broadcast_to(frames[:, part : part + 1], shape) for part in range(2))
    frame = jnp.where(line // 8 == 0, one, two)
    spot = jnp.where(lane < 72, 1.0, (line % 8).astype(jnp.float32))
    table_ref[:16] = jnp.where(lane < 16, frame, spot) * freq_ref[...]
    table_ref[16:32] = jnp.zeros(shape, jnp.float32)
    first = lax.axis_index("tm") // 2 * (4 * GROUP)
    scale_ref[:, 0:1] = column(gain_v, first, 4 * GROUP)
    scale_ref[:, 1:2] = column(bias_v, first, 4 * GROUP)
    table_ref[32:48] = jnp.broadcast_to(column(out_bias_v, 0, TILE), shape)
    table_ref[48:49] = q_v[...].astype(jnp.float32).reshape(1, HD)
    table_ref[49:50] = k_v[...].astype(jnp.float32).reshape(1, HD)
    table_ref[50:56] = qkv_v[...].astype(jnp.float32).reshape(6, LANES)


def arrange_kernel(*refs):
    pieces, (own_ref, keep_ref, send_ref, all_ref) = refs[:4], refs[4:]
    side = lax.axis_index("height")
    layer = lax.axis_index("dp")
    for step, piece in enumerate(pieces):
        all_ref[(layer + 4 - step) % 4] = piece[...]

    @pl.when(layer % 2 == lax.axis_index("tm") % 2)
    def _():
        all_ref[layer] = own_ref[...]

    for core in range(2):
        keep_ref[core] = all_ref[2 * side + core]
        send_ref[core] = all_ref[2 - 2 * side + core]


def core_taps(core):
    quarter = TAPS / 4
    taps = []
    for tm in (core, core + 2):
        taps += range(int(quarter * tm), min(TAPS, -int(-quarter * (tm + 1) // 1)))
    return taps


def join_kernel(own_ref, side_ref, high_ref, far_ref, wt_ref, all_ref):
    channels, width = side_ref.shape
    inner = wt_ref.shape[1]
    depth = TAPS * inner // 8
    here = lax.axis_index("tm") // 2 * 2 + lax.axis_index("height")
    for flip, ref in enumerate((own_ref, side_ref, high_ref, far_ref)):
        all_ref[here ^ flip] = ref[:, :width]

    def assemble(core):
        for index, tap in enumerate(core_taps(core)):
            rows = slice(index * channels, (index + 1) * channels)
            start, end = tap * inner, (tap + 1) * inner
            while start < end:
                source = start // depth
                stop = min(end, (source + 1) * depth)
                to = slice(start - tap * inner, stop - tap * inner)
                if source // 2 % 2 == core:
                    chip = source // 4 * 2 + source % 2
                    first = start - source * depth
                    wt_ref[rows, to] = all_ref[chip, :, first : first + stop - start]
                else:
                    wt_ref[rows, to] = jnp.zeros((channels, stop - start), jnp.bfloat16)
                start = stop

    core = lax.axis_index("tm") % 2
    pl.when(core == 0)(functools.partial(assemble, 0))
    pl.when(core == 1)(functools.partial(assemble, 1))
    total = sum(all_ref[chip, :, width - 2 * LANES :].astype(jnp.float32) for chip in range(4))
    low = lax.broadcasted_iota(jnp.int32, (8, LANES), 1) < 64
    empty = jnp.zeros((8, LANES), jnp.float32)
    wide, narrow = [], []
    for half in range(2):
        top = 32 * half
        wide.append([total[top + 8 * q : top + 8 * q + 8, LANES:] for q in range(4)])
        some = []
        for q in range(2):
            one = total[top + 16 * q : top + 16 * q + 8, :LANES]
            two = total[top + 16 * q + 8 : top + 16 * q + 16, :LANES]
            some.append(jnp.where(low, pltpu.roll(one, 64, 1), two))
        lines = own_ref[:16, width:].astype(jnp.float32)[8 * half : 8 * half + 8]
        narrow.append(some + [lines, empty])
    share = jnp.concatenate([jnp.concatenate(row, axis=1) for row in wide + narrow], axis=0)
    wt_ref[wt_ref.shape[0] - 32 :] = share.astype(jnp.bfloat16)


def place_kernel(*refs):
    pieces, x_ref = refs[:4], refs[4]
    place = lax.axis_index("tm") // 2 * 4 + lax.axis_index("height")
    for flip, piece in zip((0, 1, 4, 5), pieces):
        for core in range(2):
            x_ref[(place ^ flip) + 2 * core] = piece[core]


def tap_parts(y_ref, group, channels):
    held = [core_taps(core) for core in range(2)]

    def part(tap, lanes):
        found = []
        for core in range(2):
            if tap in held[core]:
                at = held[core].index(tap) * channels + group * GROUP
                found.append(y_ref[core, at : at + GROUP, lanes])
        return sum(found[1:], found[0])

    return part


def conv_kernel(
    x_ref, wt_ref, pair_ref, scale_ref, w2_ref, out_ref, y_ref
):
    channels = 4 * GROUP
    tiles = x_ref.shape[0] // 2
    count = float(tiles * LANES * GROUP)
    core = lax.axis_index("tm") % 2
    height = y_ref.shape[1]
    x = x_ref[...].reshape(tiles * LANES, x_ref.shape[2])
    for ref, at in ((wt_ref, core), (pair_ref, 1 - core)):
        y_ref[at] = lax.dot_general(
            ref[:height], x, (((1,), (1,)), ((), ())), preferred_element_type=jnp.float32
        )
    normed = []
    for group in range(4):
        hidden = tap_sums(tap_parts(y_ref, group, channels), tiles)
        at = slice(group * GROUP, (group + 1) * GROUP)
        mean = jnp.sum(sum(hidden), keepdims=True) / count
        square = jnp.sum(sum(part * part for part in hidden), keepdims=True) / count
        scale = lax.rsqrt(square - mean * mean + norm_eps)
        parts = []
        for part in hidden:
            scaled = (part - mean) * scale * scale_ref[at, 0:1] + scale_ref[at, 1:2]
            parts.append((scaled / (1.0 + jnp.exp(-scaled))).astype(jnp.bfloat16))
        normed.append(jnp.concatenate(parts, axis=1))
    y_ref[0, : TAPS * TILE] = jnp.dot(
        w2_ref[...], jnp.concatenate(normed, axis=0), preferred_element_type=jnp.float32
    )

    def part(tap, lanes):
        return y_ref[0, tap * TILE : (tap + 1) * TILE, lanes]

    low = lax.broadcasted_iota(jnp.int32, (8, LANES), 1) < 64
    layers = out_ref.shape[0] // (2 * tiles)
    for tile, latent in enumerate(tap_sums(part, tiles)):
        turned = pltpu.roll(latent, 64, 1)
        near = jnp.where(low, latent[:8], turned[8:])
        far = jnp.where(low, turned[:8], latent[8:])
        for layer in range(layers):
            out_ref[layer * 2 * tiles + 2 * tile] = near
            out_ref[layer * 2 * tiles + 2 * tile + 1] = far


def share_kernel(
    m0_ref, m1_ref, m2_ref, m3_ref, table_ref, row_ref, merged_ref, base_ref, rope_ref, m_ref
):
    lane = lax.broadcasted_iota(jnp.int32, (16, LANES), 1)
    row = jnp.broadcast_to(row_ref[0], lane.shape).astype(jnp.float32)
    angles = table_ref[:16] * jnp.where((lane < 16) | (lane >= 72), 1.0, row)
    rope_ref[:16] = jnp.cos(angles)
    sine = jnp.sin(angles)
    rope_ref[16:] = jnp.where(lane % 2 == 0, -sine, sine)
    here = lax.axis_index("tm") // 2 * 2 + lax.axis_index("height")
    lines = table_ref[48:56]
    for flip, ref in enumerate((m0_ref, m1_ref, m2_ref, m3_ref)):
        share = ref[...].astype(jnp.float32)
        m_ref[here ^ flip, :, : 4 * LANES] = share[:16]
        m_ref[here ^ flip, :, 4 * LANES :] = share[16:, : 2 * LANES]
        lines = lines + pltpu.roll(share[16:24, 2 * LANES : 3 * LANES], 2, 0)
    base_ref[...] = jnp.concatenate([lines[2 + part : 3 + part] for part in range(6)], axis=1)
    merged_ref[...] = m_ref[...].reshape(merged_ref.shape).astype(jnp.bfloat16)


def token_kernel(p_ref, m_ref, base_ref, rope_ref, table_ref, lat_ref, q_ref, k_ref, v_ref):
    low = lax.broadcasted_iota(jnp.int32, (8, LANES), 1) < 64
    pairs = []
    for side in range(2):
        one, two = (
            sum(p_ref[4 * index + 2 * core + side] for index in range(p_ref.shape[0] // 4))
            for core in range(2)
        )
        top = jnp.where(low, one, pltpu.roll(two, 64, 1))
        bottom = jnp.where(low, pltpu.roll(one, 64, 1), two)
        pairs.append(jnp.concatenate([top, bottom], axis=0))
    total = jnp.concatenate(pairs, axis=1)
    lat = (total + table_ref[32:48, :1]) * latent_scale
    clips = lat.shape[1] // 64
    tokens = clips * 16
    place = lax.axis_index("dp")
    own = lat[:, :LANES]
    for pair in range(1, clips // 2):
        own = jnp.where(place // 2 == pair, lat[:, pair * LANES : (pair + 1) * LANES], own)
    own = jnp.where(place % 2 == 1, pltpu.roll(own, 64, 1), own)
    turned = own.T[:64]
    wide = jnp.concatenate([turned] * 16, axis=1)
    spot = lax.broadcasted_iota(jnp.int32, wide.shape, 0) % 16
    spread = lax.broadcasted_iota(jnp.int32, wide.shape, 1) // 16
    merged = jnp.sum(jnp.where(spot == spread, wide, 0.0).reshape(4, 16, 256), axis=1)
    lat_ref[0, 0] = merged[:2]
    lat_ref[0, 1] = merged[2:]

    lat_bf = lat.astype(jnp.bfloat16)
    token = lax.broadcasted_iota(jnp.int32, (tokens, clips * 64), 0)
    lane = lax.broadcasted_iota(jnp.int32, (tokens, clips * 64), 1)
    first = token // 8 * 32 + token % 8 * 2
    heads = q_ref.shape[2] // HD
    projected = base_ref[...]
    for a in range(2):
        for e in range(2):
            chosen = jnp.where(lane == first + (16 * a + e), 1.0, 0.0).astype(jnp.bfloat16)
            patch = lax.dot_general(
                chosen, lat_bf, (((1,), (1,)), ((), ())), preferred_element_type=jnp.float32
            ).astype(jnp.bfloat16)
            weight = m_ref[(2 * a + e) * TILE : (2 * a + e + 1) * TILE]
            projected = projected + jnp.dot(patch, weight, preferred_element_type=jnp.float32)

    even = lax.broadcasted_iota(jnp.int32, (tokens, HD), 1) % 2 == 0
    cosine = jnp.concatenate([rope_ref[:16]] * clips, axis=0)
    sine = jnp.concatenate([rope_ref[16:]] * clips, axis=0)

    def turn(vectors, gain):
        square = jnp.mean(vectors * vectors, axis=-1, keepdims=True)
        vectors = vectors * lax.rsqrt(square + norm_eps) * gain
        swapped = jnp.where(even, pltpu.roll(vectors, HD - 1, 1), pltpu.roll(vectors, 1, 1))
        return vectors * cosine + swapped * sine

    def keep(ref, head, value):
        value = value.reshape(tokens // 8, 8, HD).astype(jnp.bfloat16)
        ref[:, :, head * HD : (head + 1) * HD] = value

    for head in range(heads):
        at = 3 * HD * head
        keep(q_ref, head, turn(projected[:, at : at + HD], table_ref[48:49]))
        keep(k_ref, head, turn(projected[:, at + HD : at + 2 * HD], table_ref[49:50]))
        keep(v_ref, head, projected[:, at + 2 * HD : at + 3 * HD])


def rope_freqs():
    freqs = []
    for dims in (time_dims, row_dims, row_dims):
        freqs.append(rope_base ** (-np.arange(0, dims, 2, dtype=np.float64) / dims))
    return np.repeat(np.concatenate(freqs), 2)[None].astype(np.float32)


def vmem(count):
    return [pl.BlockSpec(memory_space=pltpu.VMEM)] * count


def grouped(
    clip_inputs,
    conv_in_weight,
    group_gain,
    group_bias,
    conv_out_weight,
    out_bias,
    patch_weight,
    patch_bias,
    qkv_weight,
    qkv_bias,
    q_gain,
    k_gain,
    frame_pos,
    row_pos,
):
    plane_axes = ("tm", "height")
    clips = lax.axis_size("dp")
    steps = lax.axis_size("tm")
    plane = steps * lax.axis_size("height")
    channels = clip_inputs.shape[4]
    depth = conv_in_weight.shape[0]

    width = -(-depth // LANES) * LANES + LANES
    hbm = pl.BlockSpec(memory_space=pltpu.HBM)
    wide = pltpu.CompilerParams(vmem_limit_bytes=60 * 1024 * 1024)
    limit = pltpu.CompilerParams(vmem_limit_bytes=32 * 1024 * 1024)
    small = pl.CostEstimate(flops=10**6, bytes_accessed=10**6, transcendentals=0)
    with jax.named_scope("weight_by_group"):
        weight_block = jax.ShapeDtypeStruct((4 * GROUP, width), jnp.bfloat16)
        own_block = jax.ShapeDtypeStruct((4 * GROUP, width + LANES), jnp.bfloat16)
        small_arrays = (group_gain, group_bias, out_bias, qkv_bias, q_gain, k_gain)
        small_arrays += (frame_pos,)
        *packed, scale, table = pl.pallas_call(
            pack_kernel,
            out_shape=(own_block,)
            + (weight_block,) * 3
            + (
                jax.ShapeDtypeStruct((4 * GROUP, 2), jnp.float32),
                jax.ShapeDtypeStruct((56, LANES), jnp.float32),
            ),
            in_specs=[hbm] * 12,
            out_specs=(hbm,) * 6,
            scratch_shapes=[
                pltpu.VMEM(conv_in_weight.shape, jnp.bfloat16),
                pltpu.VMEM(qkv_weight.shape, jnp.bfloat16),
                pltpu.VMEM((patch_weight.shape[0], qkv_weight.shape[0]), jnp.bfloat16),
                pltpu.VMEM(patch_bias.shape, jnp.bfloat16),
                *[pltpu.VMEM(array.shape, array.dtype) for array in small_arrays],
                pltpu.VMEM((1, HD), jnp.float32),
                pltpu.VMEM((patch_bias.shape[0] // LANES, LANES), jnp.float32),
                pltpu.VMEM((8 * GROUP, depth), jnp.bfloat16),
                pltpu.VMEM((patch_weight.shape[0], qkv_weight.shape[1]), jnp.float32),
                pltpu.VMEM((4, 4 * GROUP, width), jnp.bfloat16),
                pltpu.VMEM((16, LANES), jnp.bfloat16),
                pltpu.VMEM((4 * GROUP, 2), jnp.float32),
                pltpu.VMEM((56, LANES), jnp.float32),
                pltpu.SemaphoreType.DMA((20,)),
            ],
            compiler_params=wide,
            cost_estimate=pl.CostEstimate(flops=10**8, bytes_accessed=10**6, transcendentals=0),
            name="pack_weights",
        )(
            rope_freqs(),
            conv_in_weight,
            qkv_weight,
            patch_weight,
            patch_bias,
            *small_arrays,
        )
        blocks = [packed[0]]
        for flip, block in zip((1, 4, 5), packed[1:]):
            blocks.append(lax.ppermute(block, plane_axes, [(i, i ^ flip) for i in range(plane)]))
    with jax.named_scope("gather_clips"):
        own = clip_inputs.reshape(64, channels)
        layers = []
        for step in range(clips):
            pairs = []
            for layer in range(clips):
                for tm in range(steps):
                    to = (layer // 2 * 2 + tm % 2 + step) % clips
                    pair = (layer * steps + tm, to * steps + tm // 2 * 2 + layer % 2)
                    if pair[0] != pair[1]:
                        pairs.append(pair)
            layers.append(lax.ppermute(own, ("dp", "tm"), pairs))
    with jax.named_scope("spread_clips"):
        keep, send = pl.pallas_call(
            arrange_kernel,
            out_shape=(jax.ShapeDtypeStruct((2, 64, channels), jnp.bfloat16),) * 2,
            in_specs=vmem(5),
            out_specs=tuple(vmem(2)),
            scratch_shapes=[pltpu.VMEM((4, 64, channels), jnp.bfloat16)],
            compiler_params=limit,
            cost_estimate=small,
            name="arrange_clips",
        )(*layers, own)
        pieces = [keep]
        for flip in (1, 4, 5):
            pairs = [(i, i ^ flip) for i in range(plane)]
            pieces.append(lax.ppermute(send if flip % 2 else keep, plane_axes, pairs))
    with jax.named_scope("small_weights"):
        first = lax.axis_index("tm") // 2 * (4 * GROUP)
        weight_out = lax.dynamic_slice_in_dim(conv_out_weight, first, 4 * GROUP, axis=1)
        weight_out = weight_out.transpose(0, 2, 1).reshape(TAPS * TILE, 4 * GROUP)
    with jax.named_scope("join_weights"):
        height = len(core_taps(0)) * 4 * GROUP
        joined = pl.pallas_call(
            join_kernel,
            out_shape=jax.ShapeDtypeStruct((height + 32, channels), jnp.bfloat16),
            in_specs=vmem(4),
            out_specs=vmem(1)[0],
            scratch_shapes=[pltpu.VMEM((4, 4 * GROUP, width), jnp.bfloat16)],
            compiler_params=limit,
            cost_estimate=small,
            name="join_weights",
        )(*blocks)
        joined_pair = lax.ppermute(joined, "tm", [(i, i ^ 1) for i in range(steps)])
    with jax.named_scope("merged_projection"):
        share = joined[height:].astype(jnp.float32) + joined_pair[height:].astype(jnp.float32)
        share = share.astype(jnp.bfloat16)
        shares = [share]
        for flip in (1, 4, 5):
            pairs = [(i, i ^ flip) for i in range(plane)]
            shares.append(lax.ppermute(share, plane_axes, pairs))

        merged, base, rope = pl.pallas_call(
            share_kernel,
            out_shape=(
                jax.ShapeDtypeStruct((64, 6 * HD), jnp.bfloat16),
                jax.ShapeDtypeStruct((1, 6 * HD), jnp.float32),
                jax.ShapeDtypeStruct((32, LANES), jnp.float32),
            ),
            in_specs=vmem(5) + [pl.BlockSpec(memory_space=pltpu.SMEM)],
            out_specs=tuple(vmem(3)),
            scratch_shapes=[pltpu.VMEM((4, 16, 6 * HD), jnp.float32)],
            compiler_params=limit,
            cost_estimate=small,
            name="share_rows",
        )(*shares, table, row_pos)

    flops = 4 * height * steps * LANES * channels
    clip = pl.pallas_call(
        place_kernel,
        out_shape=jax.ShapeDtypeStruct((plane, 64, channels), jnp.bfloat16),
        in_specs=vmem(4),
        out_specs=vmem(1)[0],
        compiler_params=limit,
        cost_estimate=pl.CostEstimate(flops=4 * 10**10, bytes_accessed=10**6, transcendentals=0),
        name="place_clip",
    )(*pieces)
    partial = pl.pallas_call(
        conv_kernel,
        out_shape=jax.ShapeDtypeStruct((clips * plane, 8, LANES), jnp.float32),
        in_specs=vmem(5),
        out_specs=vmem(1)[0],
        scratch_shapes=[
            pltpu.VMEM((2, height, steps * LANES), jnp.float32),
        ],
        compiler_params=limit,
        cost_estimate=pl.CostEstimate(flops=flops, bytes_accessed=10**6, transcendentals=0),
        name="convolutions",
    )(clip, joined, joined_pair, scale, weight_out)

    with jax.named_scope("sum_latents"):
        partials = lax.all_to_all(partial, ("dp",) + plane_axes, 0, 0, tiled=True)

    heads = qkv_weight.shape[1] // (3 * HD)
    frames = clip_inputs.shape[1]
    tokens = jax.ShapeDtypeStruct((clips * frames, 8, heads * HD), jnp.bfloat16)
    latents, query, key, value = pl.pallas_call(
        token_kernel,
        out_shape=(jax.ShapeDtypeStruct((1, 2, 2, 256), jnp.float32), tokens, tokens, tokens),
        in_specs=vmem(5),
        out_specs=tuple(vmem(4)),
        compiler_params=limit,
        cost_estimate=pl.CostEstimate(flops=10**8, bytes_accessed=10**6, transcendentals=0),
        name="tokens",
    )(
        partials,
        merged,
        base,
        rope,
        table,
    )
    full = (clips, frames, 1, 8, heads * HD)
    return latents, query.reshape(full), key.reshape(full), value.reshape(full)


def pick(mesh, *arrays):
    if one_group_each(mesh, arrays[0], arrays[1], arrays[4], arrays[8]):
        return grouped(*arrays)
    return shards(*arrays)


def solution(mesh):
    placed = (
        P("dp", "tm", "height", None, None),
        P(("tm", "height"), "dp"),
        P("dp"),
        P("dp"),
        P(None, "dp", None),
        P(),
        P(),
        P(),
        P(("tm", "height"), "dp"),
        P("dp"),
        P(),
        P(),
        P("tm"),
        P("height"),
    )
    return jax.shard_map(
        functools.partial(pick, mesh),
        mesh=mesh,
        in_specs=placed,
        out_specs=(
            P("dp", "tm", "height", None),
            P(None, "tm", "height", None, "dp"),
            P(None, "tm", "height", None, "dp"),
            P(None, "tm", "height", None, "dp"),
        ),
        check_vma=False,
    )
```

```python
import functools

import jax
import jax.numpy as jnp
import numpy as np
from jax import lax
from jax.experimental import pallas as pl
from jax.experimental.pallas import tpu as pltpu
from jax.sharding import PartitionSpec as P

HD = 128
GROUPS = 32
TAPS = 27


norm_eps = 1e-06
latent_scale = 0.476986
rope_base = 256.0
time_dims = 16
row_dims = 56


def from_behind(value, axis, steps):
    count = lax.axis_size(axis)
    first, last = (max(0, -steps), min(count, count - steps))
    return lax.ppermute(value, axis, [(source, source + steps) for source in range(first, last)])


def padded_2(block, sides, width):
    for axis, dim in sides:
        count = lax.axis_size(axis)
        forward = [(i, i + 1) for i in range(count - 1)]
        backward = [(target, source) for source, target in forward]
        low = lax.ppermute(
            lax.slice_in_dim(block, block.shape[dim] - width, None, axis=dim), axis, forward
        )
        high = lax.ppermute(lax.slice_in_dim(block, 0, width, axis=dim), axis, backward)
        block = jnp.concatenate([low, block, high], axis=dim)
    return block


def repeat_first(block):
    return jnp.concatenate([block[:, :1], block[:, :1]], axis=1)


def time_join(block, earlier):
    start = jnp.where(lax.axis_index("tm") == 0, repeat_first(block), earlier)
    return jnp.concatenate([start, block], axis=1)


def rows_finish(grown):
    place = lax.axis_index("height")
    top = jnp.where(place == 0, grown[:, :, 1:2], grown[:, :, :1])
    bottom = jnp.where(place == lax.axis_size("height") - 1, grown[:, :, -2:-1], grown[:, :, -1:])
    inner = jnp.concatenate([top, grown[:, :, 1:-1], bottom], axis=2)
    return jnp.pad(inner, ((0, 0), (0, 0), (0, 0), (1, 1), (0, 0)), mode="edge")


def edges_before(block):
    earlier = from_behind(block, "tm", 1)
    longer = time_join(block, earlier)
    return rows_finish(padded_2(longer, (("height", 2),), 1))


def edges_norm(block):
    earlier = from_behind(block, "tm", 1)
    longer = time_join(block, earlier)
    return rows_finish(padded_2(longer, (("height", 2),), 1))


def convolve(padded, weight):
    clips = padded.shape[0]
    frames = padded.shape[1] - 2
    rows = padded.shape[2] - 2
    cols = padded.shape[3] - 2
    total = jnp.zeros((clips * frames * rows * cols, weight.shape[2]), jnp.float32)
    for shift_t in range(3):
        for shift_r in range(3):
            for shift_c in range(3):
                window = padded[
                    :,
                    shift_t : shift_t + frames,
                    shift_r : shift_r + rows,
                    shift_c : shift_c + cols,
                ]
                window = window.reshape(-1, padded.shape[4])
                total = total + jnp.dot(
                    window,
                    weight[9 * shift_t + 3 * shift_r + shift_c],
                    preferred_element_type=jnp.float32,
                )
    return total.reshape(clips, frames, rows, cols, weight.shape[2])


def section_freqs(dims):
    return jnp.power(rope_base, -jnp.arange(0, dims, 2, dtype=jnp.float32) / dims)


def rope_angles(tpos, hpos, width):
    frames = tpos.shape[0]
    rows = hpos.shape[0]
    cols = jnp.arange(width, dtype=jnp.float32)
    part_t = tpos[:, None, None, None] * section_freqs(time_dims)
    part_h = hpos[None, :, None, None] * section_freqs(row_dims)
    part_w = cols[None, None, :, None] * section_freqs(row_dims)
    shape = (frames, rows, width)
    return jnp.concatenate(
        [
            jnp.broadcast_to(part_t, shape + (time_dims // 2,)),
            jnp.broadcast_to(part_h, shape + (row_dims // 2,)),
            jnp.broadcast_to(part_w, shape + (row_dims // 2,)),
        ],
        axis=-1,
    )


def rotate(vectors, angles):
    pairs = vectors.reshape(vectors.shape[:-1] + (vectors.shape[-1] // 2, 2))
    first = pairs[..., 0]
    second = pairs[..., 1]
    cosine = jnp.cos(angles)[..., None, :]
    sine = jnp.sin(angles)[..., None, :]
    turned = jnp.stack([first * cosine - second * sine, first * sine + second * cosine], axis=-1)
    return turned.reshape(vectors.shape)


def rms_scale(vectors, gain):
    return (
        vectors
        * lax.rsqrt(jnp.mean(vectors * vectors, axis=-1, keepdims=True) + norm_eps)
        * gain.astype(jnp.float32)
    )


def shards(
    clip_inputs,
    conv_in_weight,
    group_gain,
    group_bias,
    conv_out_weight,
    out_bias,
    patch_weight,
    patch_bias,
    qkv_weight,
    qkv_bias,
    q_gain,
    k_gain,
    frame_pos,
    row_pos,
):
    channels = clip_inputs.shape[4]
    frames = clip_inputs.shape[1]
    rows = clip_inputs.shape[2]
    cols = clip_inputs.shape[3]
    padded = lax.all_gather(edges_before(clip_inputs), "dp", axis=0, tiled=True)
    clips = padded.shape[0]
    weight_in = lax.all_gather(conv_in_weight, ("tm", "height"), axis=0, tiled=True).reshape(
        TAPS, channels, -1
    )
    hidden = convolve(padded, weight_in)
    block_width = hidden.shape[4]
    group_width = channels // GROUPS
    local_groups = block_width // group_width
    grouped = hidden.reshape(clips, -1, local_groups, group_width)
    sums_local = jnp.sum(grouped, axis=(1, 3))
    squares_local = jnp.sum(grouped * grouped, axis=(1, 3))
    sums_all, squares_all = lax.psum((sums_local, squares_local), ("tm", "height"))
    count = float(
        frames * lax.axis_size("tm") * rows * lax.axis_size("height") * cols * group_width
    )
    mean = sums_all / count
    var = squares_all / count - mean * mean
    scaled = (grouped - mean[:, None, :, None]) * lax.rsqrt(var + norm_eps)[:, None, :, None]
    scaled = scaled.reshape(hidden.shape) * group_gain.astype(jnp.float32) + group_bias.astype(
        jnp.float32
    )
    normed = jax.nn.silu(scaled).astype(jnp.bfloat16)
    partial_latent = convolve(edges_norm(normed), conv_out_weight)
    own_sum = lax.psum_scatter(partial_latent, "dp", scatter_dimension=0, tiled=True)
    own_latent = (own_sum + out_bias) * latent_scale
    every_latent = lax.all_gather(own_latent.astype(jnp.bfloat16), "dp", axis=0, tiled=True)
    latent_dims = every_latent.shape[4]
    latents = own_latent.reshape(1, frames, rows, cols * latent_dims)
    tok_rows = rows // 2
    tok_cols = cols // 2
    patches = every_latent.reshape(clips, frames, tok_rows, 2, tok_cols, 2, latent_dims)
    patches = patches.transpose(0, 1, 2, 4, 3, 5, 6).reshape(-1, 4 * latent_dims)
    embedded = (
        jnp.dot(patches, patch_weight, preferred_element_type=jnp.float32)
        + patch_bias.astype(jnp.float32)
    ).astype(jnp.bfloat16)
    projected = jnp.dot(
        embedded,
        lax.all_gather(qkv_weight, ("tm", "height"), axis=0, tiled=True),
        preferred_element_type=jnp.float32,
    )
    projected = projected + qkv_bias.astype(jnp.float32)
    local_heads = qkv_weight.shape[1] // (3 * HD)
    projected = projected.reshape(clips, frames, tok_rows, tok_cols, local_heads, 3, HD)
    angles = rope_angles(frame_pos.astype(jnp.float32), row_pos.astype(jnp.float32), tok_cols)
    query = rotate(rms_scale(projected[..., 0, :], q_gain), angles)
    key = rotate(rms_scale(projected[..., 1, :], k_gain), angles)
    value = projected[..., 2, :]
    merged = (clips, frames, tok_rows, tok_cols, local_heads * HD)
    return (
        latents,
        query.reshape(merged).astype(jnp.bfloat16),
        key.reshape(merged).astype(jnp.bfloat16),
        value.reshape(merged).astype(jnp.bfloat16),
    )


LANES = 128
TILE = 16
GROUP = 16


def one_group_each(mesh, clip_inputs, conv_in_weight, conv_out_weight, qkv_weight):
    plane = mesh.shape["tm"] * mesh.shape["height"]
    return (
        clip_inputs.shape[:4] == (1, 2, 2, 16)
        and mesh.shape["height"] == 2
        and mesh.shape["tm"] == 4
        and mesh.shape["dp"] == 4
        and conv_in_weight.shape[1] == plane * GROUP
        and clip_inputs.shape[4] == GROUP * GROUPS
        and conv_out_weight.shape[2] == TILE
        and qkv_weight.shape[1] == 6 * HD
    )


def lane_shifts(lane):
    col = lane % 16
    row = lane // 16 % 2
    half = lane // 64

    def cols(left, mid, right):
        left = jnp.where(col == 0, left, pltpu.roll(left, 1, 1))
        right = jnp.where(col == 15, right, pltpu.roll(right, LANES - 1, 1))
        return mid + left + right

    def rows(up, mid, down):
        up = jnp.where(
            row == 1, pltpu.roll(up, 16, 1), jnp.where(half == 1, pltpu.roll(up, 48, 1), up)
        )
        down = jnp.where(
            row == 0,
            pltpu.roll(down, LANES - 16, 1),
            jnp.where(half == 0, pltpu.roll(down, LANES - 48, 1), down),
        )
        return mid + up + down

    return cols, rows


def tap_sums(source, tiles):
    lane = lax.broadcasted_iota(jnp.int32, (TILE, LANES), 1)
    second = lane // 32 % 2 == 1
    cols, rows = lane_shifts(lane)
    sums = []
    before = None
    for tile in range(tiles):

        def part(tap):
            return source(tap, slice(tile * LANES, (tile + 1) * LANES))

        oldest, older, now = (
            rows(*(cols(*(part(9 * i + 3 * j + l) for l in range(3))) for j in range(3)))
            for i in range(3)
        )
        turned = pltpu.roll(older, 32, 1)
        if before is None:
            start = jnp.where(second, pltpu.roll(oldest, 32, 1), oldest)
            total = now + jnp.where(second, turned, older) + start
        else:
            total = now + jnp.where(second, turned, pltpu.roll(before[1], 96, 1)) + before[0]
        before = (oldest, older)
        sums.append(total)
    return sums


def pack_kernel(
    freq_hbm, w_hbm, qkv_hbm, patch_hbm, patch_bias_hbm, gain_hbm, bias_hbm, out_bias_hbm,
    qkv_bias_hbm, q_hbm, k_hbm, frame_hbm,
    own_hbm, side_hbm, high_hbm, far_hbm, scale_hbm, table_hbm,
    w_ref, qkv_ref, patch_ref, patch_bias_ref, gain_v, bias_v, out_bias_v, qkv_bias_v, q_v, k_v,
    frame_v, freq_ref, rows_ref, turned_ref, merged_ref, out_ref, lines_ref, scale_ref, table_ref, sems,
):
    _, channels, width = out_ref.shape
    depth = w_ref.shape[0]
    rows = qkv_ref.shape[0]
    side = lax.axis_index("height")
    high = lax.axis_index("tm") // 2
    place = lax.axis_index("tm") * 2 + side
    at = pl.ds(pl.multiple_of(place * rows, LANES), rows)
    pairs = (
        (w_hbm, w_ref),
        (qkv_hbm, qkv_ref),
        (patch_hbm.at[:, at], patch_ref),
        (patch_bias_hbm, patch_bias_ref),
        (gain_hbm, gain_v),
        (bias_hbm, bias_v),
        (out_bias_hbm, out_bias_v),
        (qkv_bias_hbm, qkv_bias_v),
        (q_hbm, q_v),
        (k_hbm, k_v),
        (frame_hbm, frame_v),
        (freq_hbm, freq_ref),
    )
    loads = [
        pltpu.make_async_copy(source, to, sems.at[index])
        for index, (source, to) in enumerate(pairs)
    ]
    for load in loads:
        load.start()
    whole = depth // LANES * LANES
    loads[0].wait()
    turned_ref[...] = w_ref[...].T
    for load in loads[1:4]:
        load.wait()
    merged_ref[...] = jnp.dot(patch_ref[...], qkv_ref[...], preferred_element_type=jnp.float32)
    stores = []
    own_main = own_hbm.at[:, :width]
    for flip, out_hbm in ((1, side_hbm), (2, high_hbm), (3, far_hbm), (0, own_main)):
        first = pl.multiple_of((high ^ (flip // 2)) * channels, channels)
        out_ref[flip, :, :whole] = turned_ref[pl.ds(first, channels), :whole]
        lower = turned_ref[pl.ds(first, channels), whole:]
        chip = (2 * high + side) ^ flip
        tail, upper = [], []
        for half in range(2):
            mine = merged_ref[pl.ds(pl.multiple_of(chip * 16 + half * 8, 8), 8)]
            mine = [mine[:, q * LANES : (q + 1) * LANES] for q in range(6)]
            tail += mine[:4]
            upper += [pltpu.roll(mine[4], 64, 1), mine[4], pltpu.roll(mine[5], 64, 1), mine[5]]
        upper = jnp.concatenate(upper, axis=0)[:, 64:].astype(jnp.bfloat16)
        out_ref[flip, :, whole : whole + LANES] = jnp.concatenate([lower, upper], axis=1)
        out_ref[flip, :, whole + LANES :] = jnp.concatenate(tail, axis=0).astype(jnp.bfloat16)
        stores.append(pltpu.make_async_copy(out_ref.at[flip], out_hbm, sems.at[13 + flip]))
        stores[-1].start()
    rows_ref[...] = patch_bias_ref[...].astype(jnp.float32).reshape(rows_ref.shape)
    count = rows // LANES
    bias = [rows_ref[pl.ds(count * place + part, 1), :] for part in range(count)]
    bias = jnp.broadcast_to(jnp.concatenate(bias, axis=1), (8, rows)).astype(jnp.bfloat16)
    bias = jnp.dot(bias, qkv_ref[...], preferred_element_type=jnp.float32)
    line = lax.broadcasted_iota(jnp.int32, (8, LANES), 0)
    lines = jnp.zeros((8, LANES), jnp.float32)
    for part in range(bias.shape[1] // LANES):
        lines = jnp.where(line == part, bias[:, part * LANES : (part + 1) * LANES], lines)
    lines_ref[...] = jnp.concatenate([lines, jnp.zeros_like(lines)], axis=0).astype(jnp.bfloat16)
    stores.append(
        pltpu.make_async_copy(lines_ref, own_hbm.at[:16, width : width + LANES], sems.at[17])
    )
    stores[-1].start()
    for load in loads[4:]:
        load.wait()
    fill_tables(
        frame_v, freq_ref, gain_v, bias_v, out_bias_v, qkv_bias_v, q_v, k_v,
        scale_ref, table_ref,
    )
    for index, (source, to) in enumerate(((scale_ref, scale_hbm), (table_ref, table_hbm))):
        stores.append(pltpu.make_async_copy(source, to, sems.at[18 + index]))
        stores[-1].start()
    for store in stores:
        store.wait()


def column(row_ref, first, size):
    length = row_ref.shape[0]
    row = row_ref[...].astype(jnp.float32).reshape(1, length)
    line = lax.broadcasted_iota(jnp.int32, (size, length), 0)
    lane = lax.broadcasted_iota(jnp.int32, (size, length), 1)
    picked = jnp.where(lane == line + first, jnp.broadcast_to(row, (size, length)), 0.0)
    return jnp.sum(picked, axis=1, keepdims=True)


def fill_tables(
    frame_ref, freq_ref, gain_v, bias_v, out_bias_v, qkv_v, q_v, k_v,
    scale_ref, table_ref,
):
    shape = (TILE, LANES)
    line = lax.broadcasted_iota(jnp.int32, shape, 0)
    lane = lax.broadcasted_iota(jnp.int32, shape, 1)
    frames = frame_ref[...].astype(jnp.float32).reshape(1, 2)
    one, two = (jnp.broadcast_to(frames[:, part : part + 1], shape) for part in range(2))
    frame = jnp.where(line // 8 == 0, one, two)
    spot = jnp.where(lane < 72, 1.0, (line % 8).astype(jnp.float32))
    table_ref[:16] = jnp.where(lane < 16, frame, spot) * freq_ref[...]
    table_ref[16:32] = jnp.zeros(shape, jnp.float32)
    first = lax.axis_index("tm") // 2 * (4 * GROUP)
    scale_ref[:, 0:1] = column(gain_v, first, 4 * GROUP)
    scale_ref[:, 1:2] = column(bias_v, first, 4 * GROUP)
    table_ref[32:48] = jnp.broadcast_to(column(out_bias_v, 0, TILE), shape)
    table_ref[48:49] = q_v[...].astype(jnp.float32).reshape(1, HD)
    table_ref[49:50] = k_v[...].astype(jnp.float32).reshape(1, HD)
    table_ref[50:56] = qkv_v[...].astype(jnp.float32).reshape(6, LANES)


def arrange_kernel(*refs):
    pieces, (own_ref, keep_ref, send_ref, all_ref) = refs[:4], refs[4:]
    side = lax.axis_index("height")
    layer = lax.axis_index("dp")
    for step, piece in enumerate(pieces):
        all_ref[(layer + 4 - step) % 4] = piece[...]

    @pl.when(layer % 2 == lax.axis_index("tm") % 2)
    def _():
        all_ref[layer] = own_ref[...]

    for core in range(2):
        keep_ref[core] = all_ref[2 * side + core]
        send_ref[core] = all_ref[2 - 2 * side + core]


def core_taps(core):
    quarter = TAPS / 4
    taps = []
    for tm in (core, core + 2):
        taps += range(int(quarter * tm), min(TAPS, -int(-quarter * (tm + 1) // 1)))
    return taps


def join_kernel(own_ref, side_ref, high_ref, far_ref, wt_ref, all_ref):
    channels, width = side_ref.shape
    inner = wt_ref.shape[1]
    depth = TAPS * inner // 8
    here = lax.axis_index("tm") // 2 * 2 + lax.axis_index("height")
    for flip, ref in enumerate((own_ref, side_ref, high_ref, far_ref)):
        all_ref[here ^ flip] = ref[:, :width]

    def assemble(core):
        for index, tap in enumerate(core_taps(core)):
            rows = slice(index * channels, (index + 1) * channels)
            start, end = tap * inner, (tap + 1) * inner
            while start < end:
                source = start // depth
                stop = min(end, (source + 1) * depth)
                to = slice(start - tap * inner, stop - tap * inner)
                if source // 2 % 2 == core:
                    chip = source // 4 * 2 + source % 2
                    first = start - source * depth
                    wt_ref[rows, to] = all_ref[chip, :, first : first + stop - start]
                else:
                    wt_ref[rows, to] = jnp.zeros((channels, stop - start), jnp.bfloat16)
                start = stop

    core = lax.axis_index("tm") % 2
    pl.when(core == 0)(functools.partial(assemble, 0))
    pl.when(core == 1)(functools.partial(assemble, 1))
    total = sum(all_ref[chip, :, width - 2 * LANES :].astype(jnp.float32) for chip in range(4))
    low = lax.broadcasted_iota(jnp.int32, (8, LANES), 1) < 64
    empty = jnp.zeros((8, LANES), jnp.float32)
    wide, narrow = [], []
    for half in range(2):
        top = 32 * half
        wide.append([total[top + 8 * q : top + 8 * q + 8, LANES:] for q in range(4)])
        some = []
        for q in range(2):
            one = total[top + 16 * q : top + 16 * q + 8, :LANES]
            two = total[top + 16 * q + 8 : top + 16 * q + 16, :LANES]
            some.append(jnp.where(low, pltpu.roll(one, 64, 1), two))
        lines = own_ref[:16, width:].astype(jnp.float32)[8 * half : 8 * half + 8]
        narrow.append(some + [lines, empty])
    share = jnp.concatenate([jnp.concatenate(row, axis=1) for row in wide + narrow], axis=0)
    wt_ref[wt_ref.shape[0] - 32 :] = share.astype(jnp.bfloat16)


def place_kernel(*refs):
    pieces, x_ref = refs[:4], refs[4]
    place = lax.axis_index("tm") // 2 * 4 + lax.axis_index("height")
    for flip, piece in zip((0, 1, 4, 5), pieces):
        for core in range(2):
            x_ref[(place ^ flip) + 2 * core] = piece[core]


def tap_parts(y_ref, group, channels):
    held = [core_taps(core) for core in range(2)]

    def part(tap, lanes):
        found = []
        for core in range(2):
            if tap in held[core]:
                at = held[core].index(tap) * channels + group * GROUP
                found.append(y_ref[core, at : at + GROUP, lanes])
        return sum(found[1:], found[0])

    return part


def conv_kernel(
    x_ref, wt_ref, pair_ref, scale_ref, w2_ref, out_ref, y_ref
):
    channels = 4 * GROUP
    tiles = x_ref.shape[0] // 2
    count = float(tiles * LANES * GROUP)
    core = lax.axis_index("tm") % 2
    height = y_ref.shape[1]
    x = x_ref[...].reshape(tiles * LANES, x_ref.shape[2])
    for ref, at in ((wt_ref, core), (pair_ref, 1 - core)):
        y_ref[at] = lax.dot_general(
            ref[:height], x, (((1,), (1,)), ((), ())), preferred_element_type=jnp.float32
        )
    normed = []
    for group in range(4):
        hidden = tap_sums(tap_parts(y_ref, group, channels), tiles)
        at = slice(group * GROUP, (group + 1) * GROUP)
        mean = jnp.sum(sum(hidden), keepdims=True) / count
        square = jnp.sum(sum(part * part for part in hidden), keepdims=True) / count
        scale = lax.rsqrt(square - mean * mean + norm_eps)
        parts = []
        for part in hidden:
            scaled = (part - mean) * scale * scale_ref[at, 0:1] + scale_ref[at, 1:2]
            parts.append((scaled / (1.0 + jnp.exp(-scaled))).astype(jnp.bfloat16))
        normed.append(jnp.concatenate(parts, axis=1))
    y_ref[0, : TAPS * TILE] = jnp.dot(
        w2_ref[...], jnp.concatenate(normed, axis=0), preferred_element_type=jnp.float32
    )

    def part(tap, lanes):
        return y_ref[0, tap * TILE : (tap + 1) * TILE, lanes]

    low = lax.broadcasted_iota(jnp.int32, (8, LANES), 1) < 64
    layers = out_ref.shape[0] // (2 * tiles)
    for tile, latent in enumerate(tap_sums(part, tiles)):
        turned = pltpu.roll(latent, 64, 1)
        near = jnp.where(low, latent[:8], turned[8:])
        far = jnp.where(low, turned[:8], latent[8:])
        for layer in range(layers):
            out_ref[layer * 2 * tiles + 2 * tile] = near
            out_ref[layer * 2 * tiles + 2 * tile + 1] = far


def share_kernel(
    m0_ref, m1_ref, m2_ref, m3_ref, table_ref, row_ref, merged_ref, base_ref, rope_ref, m_ref
):
    lane = lax.broadcasted_iota(jnp.int32, (16, LANES), 1)
    row = jnp.broadcast_to(row_ref[0], lane.shape).astype(jnp.float32)
    angles = table_ref[:16] * jnp.where((lane < 16) | (lane >= 72), 1.0, row)
    rope_ref[:16] = jnp.cos(angles)
    sine = jnp.sin(angles)
    rope_ref[16:] = jnp.where(lane % 2 == 0, -sine, sine)
    here = lax.axis_index("tm") // 2 * 2 + lax.axis_index("height")
    lines = table_ref[48:56]
    for flip, ref in enumerate((m0_ref, m1_ref, m2_ref, m3_ref)):
        share = ref[...].astype(jnp.float32)
        m_ref[here ^ flip, :, : 4 * LANES] = share[:16]
        m_ref[here ^ flip, :, 4 * LANES :] = share[16:, : 2 * LANES]
        lines = lines + pltpu.roll(share[16:24, 2 * LANES : 3 * LANES], 2, 0)
    base_ref[...] = jnp.concatenate([lines[2 + part : 3 + part] for part in range(6)], axis=1)
    merged_ref[...] = m_ref[...].reshape(merged_ref.shape).astype(jnp.bfloat16)


def token_kernel(p_ref, m_ref, base_ref, rope_ref, table_ref, lat_ref, q_ref, k_ref, v_ref):
    low = lax.broadcasted_iota(jnp.int32, (8, LANES), 1) < 64
    pairs = []
    for side in range(2):
        one, two = (
            sum(p_ref[4 * index + 2 * core + side] for index in range(p_ref.shape[0] // 4))
            for core in range(2)
        )
        top = jnp.where(low, one, pltpu.roll(two, 64, 1))
        bottom = jnp.where(low, pltpu.roll(one, 64, 1), two)
        pairs.append(jnp.concatenate([top, bottom], axis=0))
    total = jnp.concatenate(pairs, axis=1)
    lat = (total + table_ref[32:48, :1]) * latent_scale
    clips = lat.shape[1] // 64
    tokens = clips * 16
    place = lax.axis_index("dp")
    own = lat[:, :LANES]
    for pair in range(1, clips // 2):
        own = jnp.where(place // 2 == pair, lat[:, pair * LANES : (pair + 1) * LANES], own)
    own = jnp.where(place % 2 == 1, pltpu.roll(own, 64, 1), own)
    turned = own.T[:64]
    wide = jnp.concatenate([turned] * 16, axis=1)
    spot = lax.broadcasted_iota(jnp.int32, wide.shape, 0) % 16
    spread = lax.broadcasted_iota(jnp.int32, wide.shape, 1) // 16
    merged = jnp.sum(jnp.where(spot == spread, wide, 0.0).reshape(4, 16, 256), axis=1)
    lat_ref[0, 0] = merged[:2]
    lat_ref[0, 1] = merged[2:]

    lat_bf = lat.astype(jnp.bfloat16)
    token = lax.broadcasted_iota(jnp.int32, (tokens, clips * 64), 0)
    lane = lax.broadcasted_iota(jnp.int32, (tokens, clips * 64), 1)
    first = token // 8 * 32 + token % 8 * 2
    heads = q_ref.shape[2] // HD
    projected = base_ref[...]
    for a in range(2):
        for e in range(2):
            chosen = jnp.where(lane == first + (16 * a + e), 1.0, 0.0).astype(jnp.bfloat16)
            patch = lax.dot_general(
                chosen, lat_bf, (((1,), (1,)), ((), ())), preferred_element_type=jnp.float32
            ).astype(jnp.bfloat16)
            weight = m_ref[(2 * a + e) * TILE : (2 * a + e + 1) * TILE]
            projected = projected + jnp.dot(patch, weight, preferred_element_type=jnp.float32)

    even = lax.broadcasted_iota(jnp.int32, (tokens, HD), 1) % 2 == 0
    cosine = jnp.concatenate([rope_ref[:16]] * clips, axis=0)
    sine = jnp.concatenate([rope_ref[16:]] * clips, axis=0)

    def turn(vectors, gain):
        square = jnp.mean(vectors * vectors, axis=-1, keepdims=True)
        vectors = vectors * lax.rsqrt(square + norm_eps) * gain
        swapped = jnp.where(even, pltpu.roll(vectors, HD - 1, 1), pltpu.roll(vectors, 1, 1))
        return vectors * cosine + swapped * sine

    def keep(ref, head, value):
        value = value.reshape(tokens // 8, 8, HD).astype(jnp.bfloat16)
        ref[:, :, head * HD : (head + 1) * HD] = value

    for head in range(heads):
        at = 3 * HD * head
        keep(q_ref, head, turn(projected[:, at : at + HD], table_ref[48:49]))
        keep(k_ref, head, turn(projected[:, at + HD : at + 2 * HD], table_ref[49:50]))
        keep(v_ref, head, projected[:, at + 2 * HD : at + 3 * HD])


def rope_freqs():
    freqs = []
    for dims in (time_dims, row_dims, row_dims):
        freqs.append(rope_base ** (-np.arange(0, dims, 2, dtype=np.float64) / dims))
    return np.repeat(np.concatenate(freqs), 2)[None].astype(np.float32)


def vmem(count):
    return [pl.BlockSpec(memory_space=pltpu.VMEM)] * count


def grouped(
    clip_inputs,
    conv_in_weight,
    group_gain,
    group_bias,
    conv_out_weight,
    out_bias,
    patch_weight,
    patch_bias,
    qkv_weight,
    qkv_bias,
    q_gain,
    k_gain,
    frame_pos,
    row_pos,
):
    plane_axes = ("tm", "height")
    clips = lax.axis_size("dp")
    steps = lax.axis_size("tm")
    plane = steps * lax.axis_size("height")
    channels = clip_inputs.shape[4]
    depth = conv_in_weight.shape[0]

    width = -(-depth // LANES) * LANES + LANES
    hbm = pl.BlockSpec(memory_space=pltpu.HBM)
    wide = pltpu.CompilerParams(vmem_limit_bytes=60 * 1024 * 1024)
    limit = pltpu.CompilerParams(vmem_limit_bytes=32 * 1024 * 1024)
    small = pl.CostEstimate(flops=10**6, bytes_accessed=10**6, transcendentals=0)
    with jax.named_scope("weight_by_group"):
        weight_block = jax.ShapeDtypeStruct((4 * GROUP, width), jnp.bfloat16)
        own_block = jax.ShapeDtypeStruct((4 * GROUP, width + LANES), jnp.bfloat16)
        small_arrays = (group_gain, group_bias, out_bias, qkv_bias, q_gain, k_gain)
        small_arrays += (frame_pos,)
        *packed, scale, table = pl.pallas_call(
            pack_kernel,
            out_shape=(own_block,)
            + (weight_block,) * 3
            + (
                jax.ShapeDtypeStruct((4 * GROUP, 2), jnp.float32),
                jax.ShapeDtypeStruct((56, LANES), jnp.float32),
            ),
            in_specs=[hbm] * 12,
            out_specs=(hbm,) * 6,
            scratch_shapes=[
                pltpu.VMEM(conv_in_weight.shape, jnp.bfloat16),
                pltpu.VMEM(qkv_weight.shape, jnp.bfloat16),
                pltpu.VMEM((patch_weight.shape[0], qkv_weight.shape[0]), jnp.bfloat16),
                pltpu.VMEM(patch_bias.shape, jnp.bfloat16),
                *[pltpu.VMEM(array.shape, array.dtype) for array in small_arrays],
                pltpu.VMEM((1, HD), jnp.float32),
                pltpu.VMEM((patch_bias.shape[0] // LANES, LANES), jnp.float32),
                pltpu.VMEM((8 * GROUP, depth), jnp.bfloat16),
                pltpu.VMEM((patch_weight.shape[0], qkv_weight.shape[1]), jnp.float32),
                pltpu.VMEM((4, 4 * GROUP, width), jnp.bfloat16),
                pltpu.VMEM((16, LANES), jnp.bfloat16),
                pltpu.VMEM((4 * GROUP, 2), jnp.float32),
                pltpu.VMEM((56, LANES), jnp.float32),
                pltpu.SemaphoreType.DMA((20,)),
            ],
            compiler_params=wide,
            cost_estimate=pl.CostEstimate(flops=10**8, bytes_accessed=10**6, transcendentals=0),
            name="pack_weights",
        )(
            rope_freqs(),
            conv_in_weight,
            qkv_weight,
            patch_weight,
            patch_bias,
            *small_arrays,
        )
        blocks = [packed[0]]
        for flip, block in zip((1, 4, 5), packed[1:]):
            blocks.append(lax.ppermute(block, plane_axes, [(i, i ^ flip) for i in range(plane)]))
    with jax.named_scope("gather_clips"):
        own = clip_inputs.reshape(64, channels)
        layers = []
        for step in range(clips):
            pairs = []
            for layer in range(clips):
                for tm in range(steps):
                    to = (layer // 2 * 2 + tm % 2 + step) % clips
                    pair = (layer * steps + tm, to * steps + tm // 2 * 2 + layer % 2)
                    if pair[0] != pair[1]:
                        pairs.append(pair)
            layers.append(lax.ppermute(own, ("dp", "tm"), pairs))
    with jax.named_scope("spread_clips"):
        keep, send = pl.pallas_call(
            arrange_kernel,
            out_shape=(jax.ShapeDtypeStruct((2, 64, channels), jnp.bfloat16),) * 2,
            in_specs=vmem(5),
            out_specs=tuple(vmem(2)),
            scratch_shapes=[pltpu.VMEM((4, 64, channels), jnp.bfloat16)],
            compiler_params=limit,
            cost_estimate=small,
            name="arrange_clips",
        )(*layers, own)
        pieces = [keep]
        for flip in (1, 4, 5):
            pairs = [(i, i ^ flip) for i in range(plane)]
            pieces.append(lax.ppermute(send if flip % 2 else keep, plane_axes, pairs))
    with jax.named_scope("small_weights"):
        first = lax.axis_index("tm") // 2 * (4 * GROUP)
        weight_out = lax.dynamic_slice_in_dim(conv_out_weight, first, 4 * GROUP, axis=1)
        weight_out = weight_out.transpose(0, 2, 1).reshape(TAPS * TILE, 4 * GROUP)
    with jax.named_scope("join_weights"):
        height = len(core_taps(0)) * 4 * GROUP
        joined = pl.pallas_call(
            join_kernel,
            out_shape=jax.ShapeDtypeStruct((height + 32, channels), jnp.bfloat16),
            in_specs=vmem(4),
            out_specs=vmem(1)[0],
            scratch_shapes=[pltpu.VMEM((4, 4 * GROUP, width), jnp.bfloat16)],
            compiler_params=limit,
            cost_estimate=pl.CostEstimate(
                flops=3 * 10**9, bytes_accessed=10**6, transcendentals=0
            ),
            name="join_weights",
        )(*blocks)
        joined_pair = lax.ppermute(joined, "tm", [(i, i ^ 1) for i in range(steps)])
    with jax.named_scope("merged_projection"):
        share = joined[height:].astype(jnp.float32) + joined_pair[height:].astype(jnp.float32)
        share = share.astype(jnp.bfloat16)
        shares = [share]
        for flip in (1, 4, 5):
            pairs = [(i, i ^ flip) for i in range(plane)]
            shares.append(lax.ppermute(share, plane_axes, pairs))

        merged, base, rope = pl.pallas_call(
            share_kernel,
            out_shape=(
                jax.ShapeDtypeStruct((64, 6 * HD), jnp.bfloat16),
                jax.ShapeDtypeStruct((1, 6 * HD), jnp.float32),
                jax.ShapeDtypeStruct((32, LANES), jnp.float32),
            ),
            in_specs=vmem(5) + [pl.BlockSpec(memory_space=pltpu.SMEM)],
            out_specs=tuple(vmem(3)),
            scratch_shapes=[pltpu.VMEM((4, 16, 6 * HD), jnp.float32)],
            compiler_params=limit,
            cost_estimate=small,
            name="share_rows",
        )(*shares, table, row_pos)

    flops = 4 * height * steps * LANES * channels
    clip = pl.pallas_call(
        place_kernel,
        out_shape=jax.ShapeDtypeStruct((plane, 64, channels), jnp.bfloat16),
        in_specs=vmem(4),
        out_specs=vmem(1)[0],
        compiler_params=limit,
        cost_estimate=pl.CostEstimate(flops=4 * 10**10, bytes_accessed=10**6, transcendentals=0),
        name="place_clip",
    )(*pieces)
    partial = pl.pallas_call(
        conv_kernel,
        out_shape=jax.ShapeDtypeStruct((clips * plane, 8, LANES), jnp.float32),
        in_specs=vmem(5),
        out_specs=vmem(1)[0],
        scratch_shapes=[
            pltpu.VMEM((2, height, steps * LANES), jnp.float32),
        ],
        compiler_params=limit,
        cost_estimate=pl.CostEstimate(flops=flops, bytes_accessed=10**6, transcendentals=0),
        name="convolutions",
    )(clip, joined, joined_pair, scale, weight_out)

    with jax.named_scope("sum_latents"):
        partials = lax.all_to_all(partial, ("dp",) + plane_axes, 0, 0, tiled=True)

    heads = qkv_weight.shape[1] // (3 * HD)
    frames = clip_inputs.shape[1]
    tokens = jax.ShapeDtypeStruct((clips * frames, 8, heads * HD), jnp.bfloat16)
    latents, query, key, value = pl.pallas_call(
        token_kernel,
        out_shape=(jax.ShapeDtypeStruct((1, 2, 2, 256), jnp.float32), tokens, tokens, tokens),
        in_specs=vmem(5),
        out_specs=tuple(vmem(4)),
        compiler_params=limit,
        cost_estimate=pl.CostEstimate(flops=10**8, bytes_accessed=10**6, transcendentals=0),
        name="tokens",
    )(
        partials,
        merged,
        base,
        rope,
        table,
    )
    full = (clips, frames, 1, 8, heads * HD)
    return latents, query.reshape(full), key.reshape(full), value.reshape(full)


def pick(mesh, *arrays):
    if one_group_each(mesh, arrays[0], arrays[1], arrays[4], arrays[8]):
        return grouped(*arrays)
    return shards(*arrays)


def solution(mesh):
    placed = (
        P("dp", "tm", "height", None, None),
        P(("tm", "height"), "dp"),
        P("dp"),
        P("dp"),
        P(None, "dp", None),
        P(),
        P(),
        P(),
        P(("tm", "height"), "dp"),
        P("dp"),
        P(),
        P(),
        P("tm"),
        P("height"),
    )
    return jax.shard_map(
        functools.partial(pick, mesh),
        mesh=mesh,
        in_specs=placed,
        out_specs=(
            P("dp", "tm", "height", None),
            P(None, "tm", "height", None, "dp"),
            P(None, "tm", "height", None, "dp"),
            P(None, "tm", "height", None, "dp"),
        ),
        check_vma=False,
    )
```

```python
import functools

import jax
import jax.numpy as jnp
import numpy as np
from jax import lax
from jax.experimental import pallas as pl
from jax.experimental.pallas import tpu as pltpu
from jax.sharding import PartitionSpec as P

HD = 128
GROUPS = 32
TAPS = 27


norm_eps = 1e-06
latent_scale = 0.476986
rope_base = 256.0
time_dims = 16
row_dims = 56


def from_behind(value, axis, steps):
    count = lax.axis_size(axis)
    first, last = (max(0, -steps), min(count, count - steps))
    return lax.ppermute(value, axis, [(source, source + steps) for source in range(first, last)])


def padded_2(block, sides, width):
    for axis, dim in sides:
        count = lax.axis_size(axis)
        forward = [(i, i + 1) for i in range(count - 1)]
        backward = [(target, source) for source, target in forward]
        low = lax.ppermute(
            lax.slice_in_dim(block, block.shape[dim] - width, None, axis=dim), axis, forward
        )
        high = lax.ppermute(lax.slice_in_dim(block, 0, width, axis=dim), axis, backward)
        block = jnp.concatenate([low, block, high], axis=dim)
    return block


def repeat_first(block):
    return jnp.concatenate([block[:, :1], block[:, :1]], axis=1)


def time_join(block, earlier):
    start = jnp.where(lax.axis_index("tm") == 0, repeat_first(block), earlier)
    return jnp.concatenate([start, block], axis=1)


def rows_finish(grown):
    place = lax.axis_index("height")
    top = jnp.where(place == 0, grown[:, :, 1:2], grown[:, :, :1])
    bottom = jnp.where(place == lax.axis_size("height") - 1, grown[:, :, -2:-1], grown[:, :, -1:])
    inner = jnp.concatenate([top, grown[:, :, 1:-1], bottom], axis=2)
    return jnp.pad(inner, ((0, 0), (0, 0), (0, 0), (1, 1), (0, 0)), mode="edge")


def edges_before(block):
    earlier = from_behind(block, "tm", 1)
    longer = time_join(block, earlier)
    return rows_finish(padded_2(longer, (("height", 2),), 1))


def edges_norm(block):
    earlier = from_behind(block, "tm", 1)
    longer = time_join(block, earlier)
    return rows_finish(padded_2(longer, (("height", 2),), 1))


def convolve(padded, weight):
    clips = padded.shape[0]
    frames = padded.shape[1] - 2
    rows = padded.shape[2] - 2
    cols = padded.shape[3] - 2
    total = jnp.zeros((clips * frames * rows * cols, weight.shape[2]), jnp.float32)
    for shift_t in range(3):
        for shift_r in range(3):
            for shift_c in range(3):
                window = padded[
                    :,
                    shift_t : shift_t + frames,
                    shift_r : shift_r + rows,
                    shift_c : shift_c + cols,
                ]
                window = window.reshape(-1, padded.shape[4])
                total = total + jnp.dot(
                    window,
                    weight[9 * shift_t + 3 * shift_r + shift_c],
                    preferred_element_type=jnp.float32,
                )
    return total.reshape(clips, frames, rows, cols, weight.shape[2])


def section_freqs(dims):
    return jnp.power(rope_base, -jnp.arange(0, dims, 2, dtype=jnp.float32) / dims)


def rope_angles(tpos, hpos, width):
    frames = tpos.shape[0]
    rows = hpos.shape[0]
    cols = jnp.arange(width, dtype=jnp.float32)
    part_t = tpos[:, None, None, None] * section_freqs(time_dims)
    part_h = hpos[None, :, None, None] * section_freqs(row_dims)
    part_w = cols[None, None, :, None] * section_freqs(row_dims)
    shape = (frames, rows, width)
    return jnp.concatenate(
        [
            jnp.broadcast_to(part_t, shape + (time_dims // 2,)),
            jnp.broadcast_to(part_h, shape + (row_dims // 2,)),
            jnp.broadcast_to(part_w, shape + (row_dims // 2,)),
        ],
        axis=-1,
    )


def rotate(vectors, angles):
    pairs = vectors.reshape(vectors.shape[:-1] + (vectors.shape[-1] // 2, 2))
    first = pairs[..., 0]
    second = pairs[..., 1]
    cosine = jnp.cos(angles)[..., None, :]
    sine = jnp.sin(angles)[..., None, :]
    turned = jnp.stack([first * cosine - second * sine, first * sine + second * cosine], axis=-1)
    return turned.reshape(vectors.shape)


def rms_scale(vectors, gain):
    return (
        vectors
        * lax.rsqrt(jnp.mean(vectors * vectors, axis=-1, keepdims=True) + norm_eps)
        * gain.astype(jnp.float32)
    )


def shards(
    clip_inputs,
    conv_in_weight,
    group_gain,
    group_bias,
    conv_out_weight,
    out_bias,
    patch_weight,
    patch_bias,
    qkv_weight,
    qkv_bias,
    q_gain,
    k_gain,
    frame_pos,
    row_pos,
):
    channels = clip_inputs.shape[4]
    frames = clip_inputs.shape[1]
    rows = clip_inputs.shape[2]
    cols = clip_inputs.shape[3]
    padded = lax.all_gather(edges_before(clip_inputs), "dp", axis=0, tiled=True)
    clips = padded.shape[0]
    weight_in = lax.all_gather(conv_in_weight, ("tm", "height"), axis=0, tiled=True).reshape(
        TAPS, channels, -1
    )
    hidden = convolve(padded, weight_in)
    block_width = hidden.shape[4]
    group_width = channels // GROUPS
    local_groups = block_width // group_width
    grouped = hidden.reshape(clips, -1, local_groups, group_width)
    sums_local = jnp.sum(grouped, axis=(1, 3))
    squares_local = jnp.sum(grouped * grouped, axis=(1, 3))
    sums_all, squares_all = lax.psum((sums_local, squares_local), ("tm", "height"))
    count = float(
        frames * lax.axis_size("tm") * rows * lax.axis_size("height") * cols * group_width
    )
    mean = sums_all / count
    var = squares_all / count - mean * mean
    scaled = (grouped - mean[:, None, :, None]) * lax.rsqrt(var + norm_eps)[:, None, :, None]
    scaled = scaled.reshape(hidden.shape) * group_gain.astype(jnp.float32) + group_bias.astype(
        jnp.float32
    )
    normed = jax.nn.silu(scaled).astype(jnp.bfloat16)
    partial_latent = convolve(edges_norm(normed), conv_out_weight)
    own_sum = lax.psum_scatter(partial_latent, "dp", scatter_dimension=0, tiled=True)
    own_latent = (own_sum + out_bias) * latent_scale
    every_latent = lax.all_gather(own_latent.astype(jnp.bfloat16), "dp", axis=0, tiled=True)
    latent_dims = every_latent.shape[4]
    latents = own_latent.reshape(1, frames, rows, cols * latent_dims)
    tok_rows = rows // 2
    tok_cols = cols // 2
    patches = every_latent.reshape(clips, frames, tok_rows, 2, tok_cols, 2, latent_dims)
    patches = patches.transpose(0, 1, 2, 4, 3, 5, 6).reshape(-1, 4 * latent_dims)
    embedded = (
        jnp.dot(patches, patch_weight, preferred_element_type=jnp.float32)
        + patch_bias.astype(jnp.float32)
    ).astype(jnp.bfloat16)
    projected = jnp.dot(
        embedded,
        lax.all_gather(qkv_weight, ("tm", "height"), axis=0, tiled=True),
        preferred_element_type=jnp.float32,
    )
    projected = projected + qkv_bias.astype(jnp.float32)
    local_heads = qkv_weight.shape[1] // (3 * HD)
    projected = projected.reshape(clips, frames, tok_rows, tok_cols, local_heads, 3, HD)
    angles = rope_angles(frame_pos.astype(jnp.float32), row_pos.astype(jnp.float32), tok_cols)
    query = rotate(rms_scale(projected[..., 0, :], q_gain), angles)
    key = rotate(rms_scale(projected[..., 1, :], k_gain), angles)
    value = projected[..., 2, :]
    merged = (clips, frames, tok_rows, tok_cols, local_heads * HD)
    return (
        latents,
        query.reshape(merged).astype(jnp.bfloat16),
        key.reshape(merged).astype(jnp.bfloat16),
        value.reshape(merged).astype(jnp.bfloat16),
    )


LANES = 128
TILE = 16
GROUP = 16


def one_group_each(mesh, clip_inputs, conv_in_weight, conv_out_weight, qkv_weight):
    plane = mesh.shape["tm"] * mesh.shape["height"]
    return (
        clip_inputs.shape[:4] == (1, 2, 2, 16)
        and mesh.shape["height"] == 2
        and mesh.shape["tm"] == 4
        and mesh.shape["dp"] == 4
        and conv_in_weight.shape[1] == plane * GROUP
        and clip_inputs.shape[4] == GROUP * GROUPS
        and conv_out_weight.shape[2] == TILE
        and qkv_weight.shape[1] == 6 * HD
    )


def lane_shifts(lane):
    col = lane % 16
    row = lane // 16 % 2
    half = lane // 64

    def cols(left, mid, right):
        left = jnp.where(col == 0, left, pltpu.roll(left, 1, 1))
        right = jnp.where(col == 15, right, pltpu.roll(right, LANES - 1, 1))
        return mid + left + right

    def rows(up, mid, down):
        up = jnp.where(
            row == 1, pltpu.roll(up, 16, 1), jnp.where(half == 1, pltpu.roll(up, 48, 1), up)
        )
        down = jnp.where(
            row == 0,
            pltpu.roll(down, LANES - 16, 1),
            jnp.where(half == 0, pltpu.roll(down, LANES - 48, 1), down),
        )
        return mid + up + down

    return cols, rows


def tap_sums(source, tiles):
    lane = lax.broadcasted_iota(jnp.int32, (TILE, LANES), 1)
    second = lane // 32 % 2 == 1
    cols, rows = lane_shifts(lane)
    sums = []
    before = None
    for tile in range(tiles):

        def part(tap):
            return source(tap, slice(tile * LANES, (tile + 1) * LANES))

        oldest, older, now = (
            rows(*(cols(*(part(9 * i + 3 * j + l) for l in range(3))) for j in range(3)))
            for i in range(3)
        )
        turned = pltpu.roll(older, 32, 1)
        if before is None:
            start = jnp.where(second, pltpu.roll(oldest, 32, 1), oldest)
            total = now + jnp.where(second, turned, older) + start
        else:
            total = now + jnp.where(second, turned, pltpu.roll(before[1], 96, 1)) + before[0]
        before = (oldest, older)
        sums.append(total)
    return sums


def pack_kernel(
    freq_hbm, w_hbm, qkv_hbm, patch_hbm, patch_bias_hbm, gain_hbm, bias_hbm, out_bias_hbm,
    qkv_bias_hbm, q_hbm, k_hbm, frame_hbm,
    own_hbm, side_hbm, high_hbm, far_hbm, scale_hbm, table_hbm,
    w_ref, qkv_ref, patch_ref, patch_bias_ref, gain_v, bias_v, out_bias_v, qkv_bias_v, q_v, k_v,
    frame_v, freq_ref, rows_ref, turned_ref, merged_ref, out_ref, lines_ref, scale_ref, table_ref, sems,
):
    _, channels, width = out_ref.shape
    depth = w_ref.shape[0]
    rows = qkv_ref.shape[0]
    side = lax.axis_index("height")
    high = lax.axis_index("tm") // 2
    place = lax.axis_index("tm") * 2 + side
    at = pl.ds(pl.multiple_of(place * rows, LANES), rows)
    pairs = (
        (w_hbm, w_ref),
        (qkv_hbm, qkv_ref),
        (patch_hbm.at[:, at], patch_ref),
        (patch_bias_hbm, patch_bias_ref),
        (gain_hbm, gain_v),
        (bias_hbm, bias_v),
        (out_bias_hbm, out_bias_v),
        (qkv_bias_hbm, qkv_bias_v),
        (q_hbm, q_v),
        (k_hbm, k_v),
        (frame_hbm, frame_v),
        (freq_hbm, freq_ref),
    )
    loads = [
        pltpu.make_async_copy(source, to, sems.at[index])
        for index, (source, to) in enumerate(pairs)
    ]
    for load in loads:
        load.start()
    whole = depth // LANES * LANES
    loads[0].wait()
    turned_ref[...] = w_ref[...].T
    for load in loads[1:4]:
        load.wait()
    merged_ref[...] = jnp.dot(patch_ref[...], qkv_ref[...], preferred_element_type=jnp.float32)
    stores = []
    own_main = own_hbm.at[:, :width]
    for flip, out_hbm in ((1, side_hbm), (2, high_hbm), (3, far_hbm), (0, own_main)):
        first = pl.multiple_of((high ^ (flip // 2)) * channels, channels)
        out_ref[flip, :, :whole] = turned_ref[pl.ds(first, channels), :whole]
        lower = turned_ref[pl.ds(first, channels), whole:]
        chip = (2 * high + side) ^ flip
        tail, upper = [], []
        for half in range(2):
            mine = merged_ref[pl.ds(pl.multiple_of(chip * 16 + half * 8, 8), 8)]
            mine = [mine[:, q * LANES : (q + 1) * LANES] for q in range(6)]
            tail += mine[:4]
            upper += [pltpu.roll(mine[4], 64, 1), mine[4], pltpu.roll(mine[5], 64, 1), mine[5]]
        upper = jnp.concatenate(upper, axis=0)[:, 64:].astype(jnp.bfloat16)
        out_ref[flip, :, whole : whole + LANES] = jnp.concatenate([lower, upper], axis=1)
        out_ref[flip, :, whole + LANES :] = jnp.concatenate(tail, axis=0).astype(jnp.bfloat16)
        stores.append(pltpu.make_async_copy(out_ref.at[flip], out_hbm, sems.at[13 + flip]))
        stores[-1].start()
    rows_ref[...] = patch_bias_ref[...].astype(jnp.float32).reshape(rows_ref.shape)
    count = rows // LANES
    bias = [rows_ref[pl.ds(count * place + part, 1), :] for part in range(count)]
    bias = jnp.broadcast_to(jnp.concatenate(bias, axis=1), (8, rows)).astype(jnp.bfloat16)
    bias = jnp.dot(bias, qkv_ref[...], preferred_element_type=jnp.float32)
    line = lax.broadcasted_iota(jnp.int32, (8, LANES), 0)
    lines = jnp.zeros((8, LANES), jnp.float32)
    for part in range(bias.shape[1] // LANES):
        lines = jnp.where(line == part, bias[:, part * LANES : (part + 1) * LANES], lines)
    lines_ref[...] = jnp.concatenate([lines, jnp.zeros_like(lines)], axis=0).astype(jnp.bfloat16)
    stores.append(
        pltpu.make_async_copy(lines_ref, own_hbm.at[:16, width : width + LANES], sems.at[17])
    )
    stores[-1].start()
    for load in loads[4:]:
        load.wait()
    fill_tables(
        frame_v, freq_ref, gain_v, bias_v, out_bias_v, qkv_bias_v, q_v, k_v,
        scale_ref, table_ref,
    )
    for index, (source, to) in enumerate(((scale_ref, scale_hbm), (table_ref, table_hbm))):
        stores.append(pltpu.make_async_copy(source, to, sems.at[18 + index]))
        stores[-1].start()
    for store in stores:
        store.wait()


def column(row_ref, first, size):
    length = row_ref.shape[0]
    row = row_ref[...].astype(jnp.float32).reshape(1, length)
    line = lax.broadcasted_iota(jnp.int32, (size, length), 0)
    lane = lax.broadcasted_iota(jnp.int32, (size, length), 1)
    picked = jnp.where(lane == line + first, jnp.broadcast_to(row, (size, length)), 0.0)
    return jnp.sum(picked, axis=1, keepdims=True)


def fill_tables(
    frame_ref, freq_ref, gain_v, bias_v, out_bias_v, qkv_v, q_v, k_v,
    scale_ref, table_ref,
):
    shape = (TILE, LANES)
    line = lax.broadcasted_iota(jnp.int32, shape, 0)
    lane = lax.broadcasted_iota(jnp.int32, shape, 1)
    frames = frame_ref[...].astype(jnp.float32).reshape(1, 2)
    one, two = (jnp.broadcast_to(frames[:, part : part + 1], shape) for part in range(2))
    frame = jnp.where(line // 8 == 0, one, two)
    spot = jnp.where(lane < 72, 1.0, (line % 8).astype(jnp.float32))
    table_ref[:16] = jnp.where(lane < 16, frame, spot) * freq_ref[...]
    table_ref[16:32] = jnp.zeros(shape, jnp.float32)
    first = lax.axis_index("tm") // 2 * (4 * GROUP)
    scale_ref[:, 0:1] = column(gain_v, first, 4 * GROUP)
    scale_ref[:, 1:2] = column(bias_v, first, 4 * GROUP)
    table_ref[32:48] = jnp.broadcast_to(column(out_bias_v, 0, TILE), shape)
    table_ref[48:49] = q_v[...].astype(jnp.float32).reshape(1, HD)
    table_ref[49:50] = k_v[...].astype(jnp.float32).reshape(1, HD)
    table_ref[50:56] = qkv_v[...].astype(jnp.float32).reshape(6, LANES)


def arrange_kernel(*refs):
    pieces, (own_ref, keep_ref, send_ref, all_ref) = refs[:4], refs[4:]
    side = lax.axis_index("height")
    layer = lax.axis_index("dp")
    for step, piece in zip(reversed(range(4)), pieces):
        all_ref[(layer + 4 - step) % 4] = piece[...]

    @pl.when(layer % 2 == lax.axis_index("tm") % 2)
    def _():
        all_ref[layer] = own_ref[...]

    for core in range(2):
        keep_ref[core] = all_ref[2 * side + core]
        send_ref[core] = all_ref[2 - 2 * side + core]


def core_taps(core):
    quarter = TAPS / 4
    taps = []
    for tm in (core, core + 2):
        taps += range(int(quarter * tm), min(TAPS, -int(-quarter * (tm + 1) // 1)))
    return taps


def join_kernel(own_ref, side_ref, high_ref, far_ref, wt_ref, all_ref):
    channels, width = side_ref.shape
    inner = wt_ref.shape[1]
    depth = TAPS * inner // 8
    here = lax.axis_index("tm") // 2 * 2 + lax.axis_index("height")
    for flip, ref in enumerate((own_ref, side_ref, high_ref, far_ref)):
        all_ref[here ^ flip] = ref[:, :width]

    def assemble(core):
        for index, tap in enumerate(core_taps(core)):
            rows = slice(index * channels, (index + 1) * channels)
            start, end = tap * inner, (tap + 1) * inner
            while start < end:
                source = start // depth
                stop = min(end, (source + 1) * depth)
                to = slice(start - tap * inner, stop - tap * inner)
                if source // 2 % 2 == core:
                    chip = source // 4 * 2 + source % 2
                    first = start - source * depth
                    wt_ref[rows, to] = all_ref[chip, :, first : first + stop - start]
                else:
                    wt_ref[rows, to] = jnp.zeros((channels, stop - start), jnp.bfloat16)
                start = stop

    core = lax.axis_index("tm") % 2
    pl.when(core == 0)(functools.partial(assemble, 0))
    pl.when(core == 1)(functools.partial(assemble, 1))
    total = sum(all_ref[chip, :, width - 2 * LANES :].astype(jnp.float32) for chip in range(4))
    low = lax.broadcasted_iota(jnp.int32, (8, LANES), 1) < 64
    empty = jnp.zeros((8, LANES), jnp.float32)
    wide, narrow = [], []
    for half in range(2):
        top = 32 * half
        wide.append([total[top + 8 * q : top + 8 * q + 8, LANES:] for q in range(4)])
        some = []
        for q in range(2):
            one = total[top + 16 * q : top + 16 * q + 8, :LANES]
            two = total[top + 16 * q + 8 : top + 16 * q + 16, :LANES]
            some.append(jnp.where(low, pltpu.roll(one, 64, 1), two))
        lines = own_ref[:16, width:].astype(jnp.float32)[8 * half : 8 * half + 8]
        narrow.append(some + [lines, empty])
    share = jnp.concatenate([jnp.concatenate(row, axis=1) for row in wide + narrow], axis=0)
    wt_ref[wt_ref.shape[0] - 32 :] = share.astype(jnp.bfloat16)


def place_kernel(*refs):
    pieces, x_ref = refs[:4], refs[4]
    place = lax.axis_index("tm") // 2 * 4 + lax.axis_index("height")
    for flip, piece in zip((0, 1, 4, 5), pieces):
        for core in range(2):
            x_ref[(place ^ flip) + 2 * core] = piece[core]


def tap_parts(y_ref, group, channels):
    held = [core_taps(core) for core in range(2)]

    def part(tap, lanes):
        found = []
        for core in range(2):
            if tap in held[core]:
                at = held[core].index(tap) * channels + group * GROUP
                found.append(y_ref[core, at : at + GROUP, lanes])
        return sum(found[1:], found[0])

    return part


def conv_kernel(
    x_ref, wt_ref, pair_ref, scale_ref, w2_ref, out_ref, y_ref
):
    channels = 4 * GROUP
    tiles = x_ref.shape[0] // 2
    count = float(tiles * LANES * GROUP)
    core = lax.axis_index("tm") % 2
    height = y_ref.shape[1]
    x = x_ref[...].reshape(tiles * LANES, x_ref.shape[2])
    for ref, at in ((wt_ref, core), (pair_ref, 1 - core)):
        y_ref[at] = lax.dot_general(
            ref[:height], x, (((1,), (1,)), ((), ())), preferred_element_type=jnp.float32
        )
    normed = []
    for group in range(4):
        hidden = tap_sums(tap_parts(y_ref, group, channels), tiles)
        at = slice(group * GROUP, (group + 1) * GROUP)
        mean = jnp.sum(sum(hidden), keepdims=True) / count
        square = jnp.sum(sum(part * part for part in hidden), keepdims=True) / count
        scale = lax.rsqrt(square - mean * mean + norm_eps)
        parts = []
        for part in hidden:
            scaled = (part - mean) * scale * scale_ref[at, 0:1] + scale_ref[at, 1:2]
            parts.append((scaled / (1.0 + jnp.exp(-scaled))).astype(jnp.bfloat16))
        normed.append(jnp.concatenate(parts, axis=1))
    y_ref[0, : TAPS * TILE] = jnp.dot(
        w2_ref[...], jnp.concatenate(normed, axis=0), preferred_element_type=jnp.float32
    )

    def part(tap, lanes):
        return y_ref[0, tap * TILE : (tap + 1) * TILE, lanes]

    low = lax.broadcasted_iota(jnp.int32, (8, LANES), 1) < 64
    layers = out_ref.shape[0] // (2 * tiles)
    for tile, latent in enumerate(tap_sums(part, tiles)):
        turned = pltpu.roll(latent, 64, 1)
        near = jnp.where(low, latent[:8], turned[8:])
        far = jnp.where(low, turned[:8], latent[8:])
        for layer in range(layers):
            out_ref[layer * 2 * tiles + 2 * tile] = near
            out_ref[layer * 2 * tiles + 2 * tile + 1] = far


def share_kernel(
    m0_ref, m1_ref, m2_ref, m3_ref, table_ref, row_ref, merged_ref, base_ref, rope_ref, m_ref
):
    lane = lax.broadcasted_iota(jnp.int32, (16, LANES), 1)
    row = jnp.broadcast_to(row_ref[0], lane.shape).astype(jnp.float32)
    angles = table_ref[:16] * jnp.where((lane < 16) | (lane >= 72), 1.0, row)
    rope_ref[:16] = jnp.cos(angles)
    sine = jnp.sin(angles)
    rope_ref[16:] = jnp.where(lane % 2 == 0, -sine, sine)
    here = lax.axis_index("tm") // 2 * 2 + lax.axis_index("height")
    lines = table_ref[48:56]
    for flip, ref in enumerate((m0_ref, m1_ref, m2_ref, m3_ref)):
        share = ref[...].astype(jnp.float32)
        m_ref[here ^ flip, :, : 4 * LANES] = share[:16]
        m_ref[here ^ flip, :, 4 * LANES :] = share[16:, : 2 * LANES]
        lines = lines + pltpu.roll(share[16:24, 2 * LANES : 3 * LANES], 2, 0)
    base_ref[...] = jnp.concatenate([lines[2 + part : 3 + part] for part in range(6)], axis=1)
    merged_ref[...] = m_ref[...].reshape(merged_ref.shape).astype(jnp.bfloat16)


def token_kernel(p_ref, m_ref, base_ref, rope_ref, table_ref, lat_ref, q_ref, k_ref, v_ref):
    low = lax.broadcasted_iota(jnp.int32, (8, LANES), 1) < 64
    pairs = []
    for side in range(2):
        one, two = (
            sum(p_ref[4 * index + 2 * core + side] for index in range(p_ref.shape[0] // 4))
            for core in range(2)
        )
        top = jnp.where(low, one, pltpu.roll(two, 64, 1))
        bottom = jnp.where(low, pltpu.roll(one, 64, 1), two)
        pairs.append(jnp.concatenate([top, bottom], axis=0))
    total = jnp.concatenate(pairs, axis=1)
    lat = (total + table_ref[32:48, :1]) * latent_scale
    clips = lat.shape[1] // 64
    tokens = clips * 16
    place = lax.axis_index("dp")
    own = lat[:, :LANES]
    for pair in range(1, clips // 2):
        own = jnp.where(place // 2 == pair, lat[:, pair * LANES : (pair + 1) * LANES], own)
    own = jnp.where(place % 2 == 1, pltpu.roll(own, 64, 1), own)
    turned = own.T[:64]
    wide = jnp.concatenate([turned] * 16, axis=1)
    spot = lax.broadcasted_iota(jnp.int32, wide.shape, 0) % 16
    spread = lax.broadcasted_iota(jnp.int32, wide.shape, 1) // 16
    merged = jnp.sum(jnp.where(spot == spread, wide, 0.0).reshape(4, 16, 256), axis=1)
    lat_ref[0, 0] = merged[:2]
    lat_ref[0, 1] = merged[2:]

    lat_bf = lat.astype(jnp.bfloat16)
    token = lax.broadcasted_iota(jnp.int32, (tokens, clips * 64), 0)
    lane = lax.broadcasted_iota(jnp.int32, (tokens, clips * 64), 1)
    first = token // 8 * 32 + token % 8 * 2
    heads = q_ref.shape[2] // HD
    projected = base_ref[...]
    for a in range(2):
        for e in range(2):
            chosen = jnp.where(lane == first + (16 * a + e), 1.0, 0.0).astype(jnp.bfloat16)
            patch = lax.dot_general(
                chosen, lat_bf, (((1,), (1,)), ((), ())), preferred_element_type=jnp.float32
            ).astype(jnp.bfloat16)
            weight = m_ref[(2 * a + e) * TILE : (2 * a + e + 1) * TILE]
            projected = projected + jnp.dot(patch, weight, preferred_element_type=jnp.float32)

    even = lax.broadcasted_iota(jnp.int32, (tokens, HD), 1) % 2 == 0
    cosine = jnp.concatenate([rope_ref[:16]] * clips, axis=0)
    sine = jnp.concatenate([rope_ref[16:]] * clips, axis=0)

    def turn(vectors, gain):
        square = jnp.mean(vectors * vectors, axis=-1, keepdims=True)
        vectors = vectors * lax.rsqrt(square + norm_eps) * gain
        swapped = jnp.where(even, pltpu.roll(vectors, HD - 1, 1), pltpu.roll(vectors, 1, 1))
        return vectors * cosine + swapped * sine

    def keep(ref, head, value):
        value = value.reshape(tokens // 8, 8, HD).astype(jnp.bfloat16)
        ref[:, :, head * HD : (head + 1) * HD] = value

    for head in range(heads):
        at = 3 * HD * head
        keep(q_ref, head, turn(projected[:, at : at + HD], table_ref[48:49]))
        keep(k_ref, head, turn(projected[:, at + HD : at + 2 * HD], table_ref[49:50]))
        keep(v_ref, head, projected[:, at + 2 * HD : at + 3 * HD])


def rope_freqs():
    freqs = []
    for dims in (time_dims, row_dims, row_dims):
        freqs.append(rope_base ** (-np.arange(0, dims, 2, dtype=np.float64) / dims))
    return np.repeat(np.concatenate(freqs), 2)[None].astype(np.float32)


def vmem(count):
    return [pl.BlockSpec(memory_space=pltpu.VMEM)] * count


def grouped(
    clip_inputs,
    conv_in_weight,
    group_gain,
    group_bias,
    conv_out_weight,
    out_bias,
    patch_weight,
    patch_bias,
    qkv_weight,
    qkv_bias,
    q_gain,
    k_gain,
    frame_pos,
    row_pos,
):
    plane_axes = ("tm", "height")
    clips = lax.axis_size("dp")
    steps = lax.axis_size("tm")
    plane = steps * lax.axis_size("height")
    channels = clip_inputs.shape[4]
    depth = conv_in_weight.shape[0]

    width = -(-depth // LANES) * LANES + LANES
    hbm = pl.BlockSpec(memory_space=pltpu.HBM)
    wide = pltpu.CompilerParams(vmem_limit_bytes=60 * 1024 * 1024)
    limit = pltpu.CompilerParams(vmem_limit_bytes=32 * 1024 * 1024)
    small = pl.CostEstimate(flops=10**6, bytes_accessed=10**6, transcendentals=0)
    with jax.named_scope("weight_by_group"):
        weight_block = jax.ShapeDtypeStruct((4 * GROUP, width), jnp.bfloat16)
        own_block = jax.ShapeDtypeStruct((4 * GROUP, width + LANES), jnp.bfloat16)
        small_arrays = (group_gain, group_bias, out_bias, qkv_bias, q_gain, k_gain)
        small_arrays += (frame_pos,)
        *packed, scale, table = pl.pallas_call(
            pack_kernel,
            out_shape=(own_block,)
            + (weight_block,) * 3
            + (
                jax.ShapeDtypeStruct((4 * GROUP, 2), jnp.float32),
                jax.ShapeDtypeStruct((56, LANES), jnp.float32),
            ),
            in_specs=[hbm] * 12,
            out_specs=(hbm,) * 6,
            scratch_shapes=[
                pltpu.VMEM(conv_in_weight.shape, jnp.bfloat16),
                pltpu.VMEM(qkv_weight.shape, jnp.bfloat16),
                pltpu.VMEM((patch_weight.shape[0], qkv_weight.shape[0]), jnp.bfloat16),
                pltpu.VMEM(patch_bias.shape, jnp.bfloat16),
                *[pltpu.VMEM(array.shape, array.dtype) for array in small_arrays],
                pltpu.VMEM((1, HD), jnp.float32),
                pltpu.VMEM((patch_bias.shape[0] // LANES, LANES), jnp.float32),
                pltpu.VMEM((8 * GROUP, depth), jnp.bfloat16),
                pltpu.VMEM((patch_weight.shape[0], qkv_weight.shape[1]), jnp.float32),
                pltpu.VMEM((4, 4 * GROUP, width), jnp.bfloat16),
                pltpu.VMEM((16, LANES), jnp.bfloat16),
                pltpu.VMEM((4 * GROUP, 2), jnp.float32),
                pltpu.VMEM((56, LANES), jnp.float32),
                pltpu.SemaphoreType.DMA((20,)),
            ],
            compiler_params=wide,
            cost_estimate=pl.CostEstimate(flops=10**8, bytes_accessed=10**6, transcendentals=0),
            name="pack_weights",
        )(
            rope_freqs(),
            conv_in_weight,
            qkv_weight,
            patch_weight,
            patch_bias,
            *small_arrays,
        )
        blocks = [packed[0]]
        for flip, block in zip((1, 4, 5), packed[1:]):
            blocks.append(lax.ppermute(block, plane_axes, [(i, i ^ flip) for i in range(plane)]))
    with jax.named_scope("gather_clips"):
        own = clip_inputs.reshape(64, channels)
        layers = []
        for step in reversed(range(clips)):
            pairs = []
            for layer in range(clips):
                for tm in range(steps):
                    to = (layer // 2 * 2 + tm % 2 + step) % clips
                    pair = (layer * steps + tm, to * steps + tm // 2 * 2 + layer % 2)
                    if pair[0] != pair[1]:
                        pairs.append(pair)
            layers.append(lax.ppermute(own, ("dp", "tm"), pairs))
    with jax.named_scope("spread_clips"):
        keep, send = pl.pallas_call(
            arrange_kernel,
            out_shape=(jax.ShapeDtypeStruct((2, 64, channels), jnp.bfloat16),) * 2,
            in_specs=vmem(5),
            out_specs=tuple(vmem(2)),
            scratch_shapes=[pltpu.VMEM((4, 64, channels), jnp.bfloat16)],
            compiler_params=limit,
            cost_estimate=small,
            name="arrange_clips",
        )(*layers, own)
        pieces = [keep]
        for flip in (1, 4, 5):
            pairs = [(i, i ^ flip) for i in range(plane)]
            pieces.append(lax.ppermute(send if flip % 2 else keep, plane_axes, pairs))
    with jax.named_scope("small_weights"):
        first = lax.axis_index("tm") // 2 * (4 * GROUP)
        weight_out = lax.dynamic_slice_in_dim(conv_out_weight, first, 4 * GROUP, axis=1)
        weight_out = weight_out.transpose(0, 2, 1).reshape(TAPS * TILE, 4 * GROUP)
    with jax.named_scope("join_weights"):
        height = len(core_taps(0)) * 4 * GROUP
        joined = pl.pallas_call(
            join_kernel,
            out_shape=jax.ShapeDtypeStruct((height + 32, channels), jnp.bfloat16),
            in_specs=vmem(4),
            out_specs=vmem(1)[0],
            scratch_shapes=[pltpu.VMEM((4, 4 * GROUP, width), jnp.bfloat16)],
            compiler_params=limit,
            cost_estimate=small,
            name="join_weights",
        )(*blocks)
        joined_pair = lax.ppermute(joined, "tm", [(i, i ^ 1) for i in range(steps)])
    with jax.named_scope("merged_projection"):
        share = joined[height:].astype(jnp.float32) + joined_pair[height:].astype(jnp.float32)
        share = share.astype(jnp.bfloat16)
        shares = [share]
        for flip in (1, 4, 5):
            pairs = [(i, i ^ flip) for i in range(plane)]
            shares.append(lax.ppermute(share, plane_axes, pairs))

        merged, base, rope = pl.pallas_call(
            share_kernel,
            out_shape=(
                jax.ShapeDtypeStruct((64, 6 * HD), jnp.bfloat16),
                jax.ShapeDtypeStruct((1, 6 * HD), jnp.float32),
                jax.ShapeDtypeStruct((32, LANES), jnp.float32),
            ),
            in_specs=vmem(5) + [pl.BlockSpec(memory_space=pltpu.SMEM)],
            out_specs=tuple(vmem(3)),
            scratch_shapes=[pltpu.VMEM((4, 16, 6 * HD), jnp.float32)],
            compiler_params=limit,
            cost_estimate=small,
            name="share_rows",
        )(*shares, table, row_pos)

    flops = 4 * height * steps * LANES * channels
    clip = pl.pallas_call(
        place_kernel,
        out_shape=jax.ShapeDtypeStruct((plane, 64, channels), jnp.bfloat16),
        in_specs=vmem(4),
        out_specs=vmem(1)[0],
        compiler_params=limit,
        cost_estimate=pl.CostEstimate(flops=4 * 10**10, bytes_accessed=10**6, transcendentals=0),
        name="place_clip",
    )(*pieces)
    partial = pl.pallas_call(
        conv_kernel,
        out_shape=jax.ShapeDtypeStruct((clips * plane, 8, LANES), jnp.float32),
        in_specs=vmem(5),
        out_specs=vmem(1)[0],
        scratch_shapes=[
            pltpu.VMEM((2, height, steps * LANES), jnp.float32),
        ],
        compiler_params=limit,
        cost_estimate=pl.CostEstimate(flops=flops, bytes_accessed=10**6, transcendentals=0),
        name="convolutions",
    )(clip, joined, joined_pair, scale, weight_out)

    with jax.named_scope("sum_latents"):
        partials = lax.all_to_all(partial, ("dp",) + plane_axes, 0, 0, tiled=True)

    heads = qkv_weight.shape[1] // (3 * HD)
    frames = clip_inputs.shape[1]
    tokens = jax.ShapeDtypeStruct((clips * frames, 8, heads * HD), jnp.bfloat16)
    latents, query, key, value = pl.pallas_call(
        token_kernel,
        out_shape=(jax.ShapeDtypeStruct((1, 2, 2, 256), jnp.float32), tokens, tokens, tokens),
        in_specs=vmem(5),
        out_specs=tuple(vmem(4)),
        compiler_params=limit,
        cost_estimate=pl.CostEstimate(flops=10**8, bytes_accessed=10**6, transcendentals=0),
        name="tokens",
    )(
        partials,
        merged,
        base,
        rope,
        table,
    )
    full = (clips, frames, 1, 8, heads * HD)
    return latents, query.reshape(full), key.reshape(full), value.reshape(full)


def pick(mesh, *arrays):
    if one_group_each(mesh, arrays[0], arrays[1], arrays[4], arrays[8]):
        return grouped(*arrays)
    return shards(*arrays)


def solution(mesh):
    placed = (
        P("dp", "tm", "height", None, None),
        P(("tm", "height"), "dp"),
        P("dp"),
        P("dp"),
        P(None, "dp", None),
        P(),
        P(),
        P(),
        P(("tm", "height"), "dp"),
        P("dp"),
        P(),
        P(),
        P("tm"),
        P("height"),
    )
    return jax.shard_map(
        functools.partial(pick, mesh),
        mesh=mesh,
        in_specs=placed,
        out_specs=(
            P("dp", "tm", "height", None),
            P(None, "tm", "height", None, "dp"),
            P(None, "tm", "height", None, "dp"),
            P(None, "tm", "height", None, "dp"),
        ),
        check_vma=False,
    )
```

```python
import functools

import jax
import jax.numpy as jnp
import numpy as np
from jax import lax
from jax.experimental import pallas as pl
from jax.experimental.pallas import tpu as pltpu
from jax.sharding import PartitionSpec as P

HD = 128
GROUPS = 32
TAPS = 27


norm_eps = 1e-06
latent_scale = 0.476986
rope_base = 256.0
time_dims = 16
row_dims = 56


def from_behind(value, axis, steps):
    count = lax.axis_size(axis)
    first, last = (max(0, -steps), min(count, count - steps))
    return lax.ppermute(value, axis, [(source, source + steps) for source in range(first, last)])


def padded_2(block, sides, width):
    for axis, dim in sides:
        count = lax.axis_size(axis)
        forward = [(i, i + 1) for i in range(count - 1)]
        backward = [(target, source) for source, target in forward]
        low = lax.ppermute(
            lax.slice_in_dim(block, block.shape[dim] - width, None, axis=dim), axis, forward
        )
        high = lax.ppermute(lax.slice_in_dim(block, 0, width, axis=dim), axis, backward)
        block = jnp.concatenate([low, block, high], axis=dim)
    return block


def repeat_first(block):
    return jnp.concatenate([block[:, :1], block[:, :1]], axis=1)


def time_join(block, earlier):
    start = jnp.where(lax.axis_index("tm") == 0, repeat_first(block), earlier)
    return jnp.concatenate([start, block], axis=1)


def rows_finish(grown):
    place = lax.axis_index("height")
    top = jnp.where(place == 0, grown[:, :, 1:2], grown[:, :, :1])
    bottom = jnp.where(place == lax.axis_size("height") - 1, grown[:, :, -2:-1], grown[:, :, -1:])
    inner = jnp.concatenate([top, grown[:, :, 1:-1], bottom], axis=2)
    return jnp.pad(inner, ((0, 0), (0, 0), (0, 0), (1, 1), (0, 0)), mode="edge")


def edges_before(block):
    earlier = from_behind(block, "tm", 1)
    longer = time_join(block, earlier)
    return rows_finish(padded_2(longer, (("height", 2),), 1))


def edges_norm(block):
    earlier = from_behind(block, "tm", 1)
    longer = time_join(block, earlier)
    return rows_finish(padded_2(longer, (("height", 2),), 1))


def convolve(padded, weight):
    clips = padded.shape[0]
    frames = padded.shape[1] - 2
    rows = padded.shape[2] - 2
    cols = padded.shape[3] - 2
    total = jnp.zeros((clips * frames * rows * cols, weight.shape[2]), jnp.float32)
    for shift_t in range(3):
        for shift_r in range(3):
            for shift_c in range(3):
                window = padded[
                    :,
                    shift_t : shift_t + frames,
                    shift_r : shift_r + rows,
                    shift_c : shift_c + cols,
                ]
                window = window.reshape(-1, padded.shape[4])
                total = total + jnp.dot(
                    window,
                    weight[9 * shift_t + 3 * shift_r + shift_c],
                    preferred_element_type=jnp.float32,
                )
    return total.reshape(clips, frames, rows, cols, weight.shape[2])


def section_freqs(dims):
    return jnp.power(rope_base, -jnp.arange(0, dims, 2, dtype=jnp.float32) / dims)


def rope_angles(tpos, hpos, width):
    frames = tpos.shape[0]
    rows = hpos.shape[0]
    cols = jnp.arange(width, dtype=jnp.float32)
    part_t = tpos[:, None, None, None] * section_freqs(time_dims)
    part_h = hpos[None, :, None, None] * section_freqs(row_dims)
    part_w = cols[None, None, :, None] * section_freqs(row_dims)
    shape = (frames, rows, width)
    return jnp.concatenate(
        [
            jnp.broadcast_to(part_t, shape + (time_dims // 2,)),
            jnp.broadcast_to(part_h, shape + (row_dims // 2,)),
            jnp.broadcast_to(part_w, shape + (row_dims // 2,)),
        ],
        axis=-1,
    )


def rotate(vectors, angles):
    pairs = vectors.reshape(vectors.shape[:-1] + (vectors.shape[-1] // 2, 2))
    first = pairs[..., 0]
    second = pairs[..., 1]
    cosine = jnp.cos(angles)[..., None, :]
    sine = jnp.sin(angles)[..., None, :]
    turned = jnp.stack([first * cosine - second * sine, first * sine + second * cosine], axis=-1)
    return turned.reshape(vectors.shape)


def rms_scale(vectors, gain):
    return (
        vectors
        * lax.rsqrt(jnp.mean(vectors * vectors, axis=-1, keepdims=True) + norm_eps)
        * gain.astype(jnp.float32)
    )


def shards(
    clip_inputs,
    conv_in_weight,
    group_gain,
    group_bias,
    conv_out_weight,
    out_bias,
    patch_weight,
    patch_bias,
    qkv_weight,
    qkv_bias,
    q_gain,
    k_gain,
    frame_pos,
    row_pos,
):
    channels = clip_inputs.shape[4]
    frames = clip_inputs.shape[1]
    rows = clip_inputs.shape[2]
    cols = clip_inputs.shape[3]
    padded = lax.all_gather(edges_before(clip_inputs), "dp", axis=0, tiled=True)
    clips = padded.shape[0]
    weight_in = lax.all_gather(conv_in_weight, ("tm", "height"), axis=0, tiled=True).reshape(
        TAPS, channels, -1
    )
    hidden = convolve(padded, weight_in)
    block_width = hidden.shape[4]
    group_width = channels // GROUPS
    local_groups = block_width // group_width
    grouped = hidden.reshape(clips, -1, local_groups, group_width)
    sums_local = jnp.sum(grouped, axis=(1, 3))
    squares_local = jnp.sum(grouped * grouped, axis=(1, 3))
    sums_all, squares_all = lax.psum((sums_local, squares_local), ("tm", "height"))
    count = float(
        frames * lax.axis_size("tm") * rows * lax.axis_size("height") * cols * group_width
    )
    mean = sums_all / count
    var = squares_all / count - mean * mean
    scaled = (grouped - mean[:, None, :, None]) * lax.rsqrt(var + norm_eps)[:, None, :, None]
    scaled = scaled.reshape(hidden.shape) * group_gain.astype(jnp.float32) + group_bias.astype(
        jnp.float32
    )
    normed = jax.nn.silu(scaled).astype(jnp.bfloat16)
    partial_latent = convolve(edges_norm(normed), conv_out_weight)
    own_sum = lax.psum_scatter(partial_latent, "dp", scatter_dimension=0, tiled=True)
    own_latent = (own_sum + out_bias) * latent_scale
    every_latent = lax.all_gather(own_latent.astype(jnp.bfloat16), "dp", axis=0, tiled=True)
    latent_dims = every_latent.shape[4]
    latents = own_latent.reshape(1, frames, rows, cols * latent_dims)
    tok_rows = rows // 2
    tok_cols = cols // 2
    patches = every_latent.reshape(clips, frames, tok_rows, 2, tok_cols, 2, latent_dims)
    patches = patches.transpose(0, 1, 2, 4, 3, 5, 6).reshape(-1, 4 * latent_dims)
    embedded = (
        jnp.dot(patches, patch_weight, preferred_element_type=jnp.float32)
        + patch_bias.astype(jnp.float32)
    ).astype(jnp.bfloat16)
    projected = jnp.dot(
        embedded,
        lax.all_gather(qkv_weight, ("tm", "height"), axis=0, tiled=True),
        preferred_element_type=jnp.float32,
    )
    projected = projected + qkv_bias.astype(jnp.float32)
    local_heads = qkv_weight.shape[1] // (3 * HD)
    projected = projected.reshape(clips, frames, tok_rows, tok_cols, local_heads, 3, HD)
    angles = rope_angles(frame_pos.astype(jnp.float32), row_pos.astype(jnp.float32), tok_cols)
    query = rotate(rms_scale(projected[..., 0, :], q_gain), angles)
    key = rotate(rms_scale(projected[..., 1, :], k_gain), angles)
    value = projected[..., 2, :]
    merged = (clips, frames, tok_rows, tok_cols, local_heads * HD)
    return (
        latents,
        query.reshape(merged).astype(jnp.bfloat16),
        key.reshape(merged).astype(jnp.bfloat16),
        value.reshape(merged).astype(jnp.bfloat16),
    )


LANES = 128
TILE = 16
GROUP = 16


def one_group_each(mesh, clip_inputs, conv_in_weight, conv_out_weight, qkv_weight):
    plane = mesh.shape["tm"] * mesh.shape["height"]
    return (
        clip_inputs.shape[:4] == (1, 2, 2, 16)
        and mesh.shape["height"] == 2
        and mesh.shape["tm"] == 4
        and mesh.shape["dp"] == 4
        and conv_in_weight.shape[1] == plane * GROUP
        and clip_inputs.shape[4] == GROUP * GROUPS
        and conv_out_weight.shape[2] == TILE
        and qkv_weight.shape[1] == 6 * HD
    )


def lane_shifts(lane):
    col = lane % 16
    row = lane // 16 % 2
    half = lane // 64

    def cols(left, mid, right):
        left = jnp.where(col == 0, left, pltpu.roll(left, 1, 1))
        right = jnp.where(col == 15, right, pltpu.roll(right, LANES - 1, 1))
        return mid + left + right

    def rows(up, mid, down):
        up = jnp.where(
            row == 1, pltpu.roll(up, 16, 1), jnp.where(half == 1, pltpu.roll(up, 48, 1), up)
        )
        down = jnp.where(
            row == 0,
            pltpu.roll(down, LANES - 16, 1),
            jnp.where(half == 0, pltpu.roll(down, LANES - 48, 1), down),
        )
        return mid + up + down

    return cols, rows


def tap_sums(source, tiles):
    lane = lax.broadcasted_iota(jnp.int32, (TILE, LANES), 1)
    second = lane // 32 % 2 == 1
    cols, rows = lane_shifts(lane)
    sums = []
    before = None
    for tile in range(tiles):

        def part(tap):
            return source(tap, slice(tile * LANES, (tile + 1) * LANES))

        oldest, older, now = (
            rows(*(cols(*(part(9 * i + 3 * j + l) for l in range(3))) for j in range(3)))
            for i in range(3)
        )
        turned = pltpu.roll(older, 32, 1)
        if before is None:
            start = jnp.where(second, pltpu.roll(oldest, 32, 1), oldest)
            total = now + jnp.where(second, turned, older) + start
        else:
            total = now + jnp.where(second, turned, pltpu.roll(before[1], 96, 1)) + before[0]
        before = (oldest, older)
        sums.append(total)
    return sums


def pack_kernel(
    freq_hbm, w_hbm, qkv_hbm, patch_hbm, patch_bias_hbm, gain_hbm, bias_hbm, out_bias_hbm,
    qkv_bias_hbm, q_hbm, k_hbm, frame_hbm,
    own_hbm, side_hbm, high_hbm, far_hbm, scale_hbm, table_hbm,
    w_ref, qkv_ref, patch_ref, patch_bias_ref, gain_v, bias_v, out_bias_v, qkv_bias_v, q_v, k_v,
    frame_v, freq_ref, rows_ref, turned_ref, merged_ref, out_ref, lines_ref, scale_ref, table_ref, sems,
):
    _, channels, width = out_ref.shape
    depth = w_ref.shape[0]
    rows = qkv_ref.shape[0]
    side = lax.axis_index("height")
    high = lax.axis_index("tm") // 2
    place = lax.axis_index("tm") * 2 + side
    at = pl.ds(pl.multiple_of(place * rows, LANES), rows)
    pairs = (
        (w_hbm, w_ref),
        (qkv_hbm, qkv_ref),
        (patch_hbm.at[:, at], patch_ref),
        (patch_bias_hbm, patch_bias_ref),
        (gain_hbm, gain_v),
        (bias_hbm, bias_v),
        (out_bias_hbm, out_bias_v),
        (qkv_bias_hbm, qkv_bias_v),
        (q_hbm, q_v),
        (k_hbm, k_v),
        (frame_hbm, frame_v),
        (freq_hbm, freq_ref),
    )
    loads = [
        pltpu.make_async_copy(source, to, sems.at[index])
        for index, (source, to) in enumerate(pairs)
    ]
    for load in loads:
        load.start()
    whole = depth // LANES * LANES
    loads[0].wait()
    turned_ref[...] = w_ref[...].T
    for load in loads[1:4]:
        load.wait()
    merged_ref[...] = jnp.dot(patch_ref[...], qkv_ref[...], preferred_element_type=jnp.float32)
    stores = []
    own_main = own_hbm.at[:, :width]
    for flip, out_hbm in ((1, side_hbm), (2, high_hbm), (3, far_hbm), (0, own_main)):
        first = pl.multiple_of((high ^ (flip // 2)) * channels, channels)
        out_ref[flip, :, :whole] = turned_ref[pl.ds(first, channels), :whole]
        lower = turned_ref[pl.ds(first, channels), whole:]
        chip = (2 * high + side) ^ flip
        tail, upper = [], []
        for half in range(2):
            mine = merged_ref[pl.ds(pl.multiple_of(chip * 16 + half * 8, 8), 8)]
            mine = [mine[:, q * LANES : (q + 1) * LANES] for q in range(6)]
            tail += mine[:4]
            upper += [pltpu.roll(mine[4], 64, 1), mine[4], pltpu.roll(mine[5], 64, 1), mine[5]]
        upper = jnp.concatenate(upper, axis=0)[:, 64:].astype(jnp.bfloat16)
        out_ref[flip, :, whole : whole + LANES] = jnp.concatenate([lower, upper], axis=1)
        out_ref[flip, :, whole + LANES :] = jnp.concatenate(tail, axis=0).astype(jnp.bfloat16)
        stores.append(pltpu.make_async_copy(out_ref.at[flip], out_hbm, sems.at[13 + flip]))
        stores[-1].start()
    rows_ref[...] = patch_bias_ref[...].astype(jnp.float32).reshape(rows_ref.shape)
    count = rows // LANES
    bias = [rows_ref[pl.ds(count * place + part, 1), :] for part in range(count)]
    bias = jnp.broadcast_to(jnp.concatenate(bias, axis=1), (8, rows)).astype(jnp.bfloat16)
    bias = jnp.dot(bias, qkv_ref[...], preferred_element_type=jnp.float32)
    line = lax.broadcasted_iota(jnp.int32, (8, LANES), 0)
    lines = jnp.zeros((8, LANES), jnp.float32)
    for part in range(bias.shape[1] // LANES):
        lines = jnp.where(line == part, bias[:, part * LANES : (part + 1) * LANES], lines)
    lines_ref[...] = jnp.concatenate([lines, jnp.zeros_like(lines)], axis=0).astype(jnp.bfloat16)
    stores.append(
        pltpu.make_async_copy(lines_ref, own_hbm.at[:16, width : width + LANES], sems.at[17])
    )
    stores[-1].start()
    for load in loads[4:]:
        load.wait()
    fill_tables(
        frame_v, freq_ref, gain_v, bias_v, out_bias_v, qkv_bias_v, q_v, k_v,
        scale_ref, table_ref,
    )
    for index, (source, to) in enumerate(((scale_ref, scale_hbm), (table_ref, table_hbm))):
        stores.append(pltpu.make_async_copy(source, to, sems.at[18 + index]))
        stores[-1].start()
    for store in stores:
        store.wait()


def column(row_ref, first, size):
    length = row_ref.shape[0]
    row = row_ref[...].astype(jnp.float32).reshape(1, length)
    line = lax.broadcasted_iota(jnp.int32, (size, length), 0)
    lane = lax.broadcasted_iota(jnp.int32, (size, length), 1)
    picked = jnp.where(lane == line + first, jnp.broadcast_to(row, (size, length)), 0.0)
    return jnp.sum(picked, axis=1, keepdims=True)


def fill_tables(
    frame_ref, freq_ref, gain_v, bias_v, out_bias_v, qkv_v, q_v, k_v,
    scale_ref, table_ref,
):
    shape = (TILE, LANES)
    line = lax.broadcasted_iota(jnp.int32, shape, 0)
    lane = lax.broadcasted_iota(jnp.int32, shape, 1)
    frames = frame_ref[...].astype(jnp.float32).reshape(1, 2)
    one, two = (jnp.broadcast_to(frames[:, part : part + 1], shape) for part in range(2))
    frame = jnp.where(line // 8 == 0, one, two)
    spot = jnp.where(lane < 72, 1.0, (line % 8).astype(jnp.float32))
    table_ref[:16] = jnp.where(lane < 16, frame, spot) * freq_ref[...]
    table_ref[16:32] = jnp.zeros(shape, jnp.float32)
    first = lax.axis_index("tm") // 2 * (4 * GROUP)
    scale_ref[:, 0:1] = column(gain_v, first, 4 * GROUP)
    scale_ref[:, 1:2] = column(bias_v, first, 4 * GROUP)
    table_ref[32:48] = jnp.broadcast_to(column(out_bias_v, 0, TILE), shape)
    table_ref[48:49] = q_v[...].astype(jnp.float32).reshape(1, HD)
    table_ref[49:50] = k_v[...].astype(jnp.float32).reshape(1, HD)
    table_ref[50:56] = qkv_v[...].astype(jnp.float32).reshape(6, LANES)


def arrange_kernel(*refs):
    pieces, (own_ref, keep_ref, send_ref, all_ref) = refs[:4], refs[4:]
    side = lax.axis_index("height")
    layer = lax.axis_index("dp")
    for step, piece in zip(reversed(range(4)), pieces):
        all_ref[(layer + 4 - step) % 4] = piece[...]

    @pl.when(layer % 2 == lax.axis_index("tm") % 2)
    def _():
        all_ref[layer] = own_ref[...]

    for core in range(2):
        keep_ref[core] = all_ref[2 * side + core]
        send_ref[core] = all_ref[2 - 2 * side + core]


def core_taps(core):
    quarter = TAPS / 4
    taps = []
    for tm in (core, core + 2):
        taps += range(int(quarter * tm), min(TAPS, -int(-quarter * (tm + 1) // 1)))
    return taps


def join_kernel(own_ref, side_ref, high_ref, far_ref, wt_ref, all_ref):
    channels, width = side_ref.shape
    inner = wt_ref.shape[1]
    depth = TAPS * inner // 8
    here = lax.axis_index("tm") // 2 * 2 + lax.axis_index("height")
    for flip, ref in enumerate((own_ref, side_ref, high_ref, far_ref)):
        all_ref[here ^ flip] = ref[:, :width]

    def assemble(core):
        for index, tap in enumerate(core_taps(core)):
            rows = slice(index * channels, (index + 1) * channels)
            start, end = tap * inner, (tap + 1) * inner
            while start < end:
                source = start // depth
                stop = min(end, (source + 1) * depth)
                to = slice(start - tap * inner, stop - tap * inner)
                if source // 2 % 2 == core:
                    chip = source // 4 * 2 + source % 2
                    first = start - source * depth
                    wt_ref[rows, to] = all_ref[chip, :, first : first + stop - start]
                else:
                    wt_ref[rows, to] = jnp.zeros((channels, stop - start), jnp.bfloat16)
                start = stop

    core = lax.axis_index("tm") % 2
    pl.when(core == 0)(functools.partial(assemble, 0))
    pl.when(core == 1)(functools.partial(assemble, 1))
    total = sum(all_ref[chip, :, width - 2 * LANES :].astype(jnp.float32) for chip in range(4))
    low = lax.broadcasted_iota(jnp.int32, (8, LANES), 1) < 64
    empty = jnp.zeros((8, LANES), jnp.float32)
    wide, narrow = [], []
    for half in range(2):
        top = 32 * half
        wide.append([total[top + 8 * q : top + 8 * q + 8, LANES:] for q in range(4)])
        some = []
        for q in range(2):
            one = total[top + 16 * q : top + 16 * q + 8, :LANES]
            two = total[top + 16 * q + 8 : top + 16 * q + 16, :LANES]
            some.append(jnp.where(low, pltpu.roll(one, 64, 1), two))
        lines = own_ref[:16, width:].astype(jnp.float32)[8 * half : 8 * half + 8]
        narrow.append(some + [lines, empty])
    share = jnp.concatenate([jnp.concatenate(row, axis=1) for row in wide + narrow], axis=0)
    wt_ref[wt_ref.shape[0] - 32 :] = share.astype(jnp.bfloat16)


def place_kernel(*refs):
    pieces, x_ref = refs[:4], refs[4]
    place = lax.axis_index("tm") // 2 * 4 + lax.axis_index("height")
    for flip, piece in zip((0, 1, 4, 5), pieces):
        for core in range(2):
            x_ref[(place ^ flip) + 2 * core] = piece[core]


def tap_parts(y_ref, group, channels):
    held = [core_taps(core) for core in range(2)]

    def part(tap, lanes):
        found = []
        for core in range(2):
            if tap in held[core]:
                at = held[core].index(tap) * channels + group * GROUP
                found.append(y_ref[core, at : at + GROUP, lanes])
        return sum(found[1:], found[0])

    return part


def conv_kernel(
    x_ref, wt_ref, pair_ref, scale_ref, w2_ref, out_ref, y_ref
):
    channels = 4 * GROUP
    tiles = x_ref.shape[0] // 2
    count = float(tiles * LANES * GROUP)
    core = lax.axis_index("tm") % 2
    height = y_ref.shape[1]
    x = x_ref[...].reshape(tiles * LANES, x_ref.shape[2])
    for ref, at in ((wt_ref, core), (pair_ref, 1 - core)):
        y_ref[at] = lax.dot_general(
            ref[:height], x, (((1,), (1,)), ((), ())), preferred_element_type=jnp.float32
        )
    normed = []
    for group in range(4):
        hidden = tap_sums(tap_parts(y_ref, group, channels), tiles)
        at = slice(group * GROUP, (group + 1) * GROUP)
        mean = jnp.sum(sum(hidden), keepdims=True) / count
        square = jnp.sum(sum(part * part for part in hidden), keepdims=True) / count
        scale = lax.rsqrt(square - mean * mean + norm_eps)
        parts = []
        for part in hidden:
            scaled = (part - mean) * scale * scale_ref[at, 0:1] + scale_ref[at, 1:2]
            parts.append((scaled / (1.0 + jnp.exp(-scaled))).astype(jnp.bfloat16))
        normed.append(jnp.concatenate(parts, axis=1))
    y_ref[0, : TAPS * TILE] = jnp.dot(
        w2_ref[...], jnp.concatenate(normed, axis=0), preferred_element_type=jnp.float32
    )

    def part(tap, lanes):
        return y_ref[0, tap * TILE : (tap + 1) * TILE, lanes]

    low = lax.broadcasted_iota(jnp.int32, (8, LANES), 1) < 64
    layers = out_ref.shape[0] // (2 * tiles)
    for tile, latent in enumerate(tap_sums(part, tiles)):
        turned = pltpu.roll(latent, 64, 1)
        near = jnp.where(low, latent[:8], turned[8:])
        far = jnp.where(low, turned[:8], latent[8:])
        for layer in range(layers):
            out_ref[layer * 2 * tiles + 2 * tile] = near
            out_ref[layer * 2 * tiles + 2 * tile + 1] = far


def share_kernel(
    m0_ref, m1_ref, m2_ref, m3_ref, table_ref, row_ref, merged_ref, base_ref, rope_ref, m_ref
):
    lane = lax.broadcasted_iota(jnp.int32, (16, LANES), 1)
    row = jnp.broadcast_to(row_ref[0], lane.shape).astype(jnp.float32)
    angles = table_ref[:16] * jnp.where((lane < 16) | (lane >= 72), 1.0, row)
    rope_ref[:16] = jnp.cos(angles)
    sine = jnp.sin(angles)
    rope_ref[16:] = jnp.where(lane % 2 == 0, -sine, sine)
    here = lax.axis_index("tm") // 2 * 2 + lax.axis_index("height")
    lines = table_ref[48:56]
    for flip, ref in enumerate((m0_ref, m1_ref, m2_ref, m3_ref)):
        share = ref[...].astype(jnp.float32)
        m_ref[here ^ flip, :, : 4 * LANES] = share[:16]
        m_ref[here ^ flip, :, 4 * LANES :] = share[16:, : 2 * LANES]
        lines = lines + pltpu.roll(share[16:24, 2 * LANES : 3 * LANES], 2, 0)
    base_ref[...] = jnp.concatenate([lines[2 + part : 3 + part] for part in range(6)], axis=1)
    merged_ref[...] = m_ref[...].reshape(merged_ref.shape).astype(jnp.bfloat16)


def token_kernel(p_ref, m_ref, base_ref, rope_ref, table_ref, lat_ref, q_ref, k_ref, v_ref):
    low = lax.broadcasted_iota(jnp.int32, (8, LANES), 1) < 64
    pairs = []
    for side in range(2):
        one, two = (
            sum(p_ref[4 * index + 2 * core + side] for index in range(p_ref.shape[0] // 4))
            for core in range(2)
        )
        top = jnp.where(low, one, pltpu.roll(two, 64, 1))
        bottom = jnp.where(low, pltpu.roll(one, 64, 1), two)
        pairs.append(jnp.concatenate([top, bottom], axis=0))
    total = jnp.concatenate(pairs, axis=1)
    lat = (total + table_ref[32:48, :1]) * latent_scale
    clips = lat.shape[1] // 64
    tokens = clips * 16
    place = lax.axis_index("dp")
    own = lat[:, :LANES]
    for pair in range(1, clips // 2):
        own = jnp.where(place // 2 == pair, lat[:, pair * LANES : (pair + 1) * LANES], own)
    own = jnp.where(place % 2 == 1, pltpu.roll(own, 64, 1), own)
    turned = own.T[:64]
    wide = jnp.concatenate([turned] * 16, axis=1)
    spot = lax.broadcasted_iota(jnp.int32, wide.shape, 0) % 16
    spread = lax.broadcasted_iota(jnp.int32, wide.shape, 1) // 16
    merged = jnp.sum(jnp.where(spot == spread, wide, 0.0).reshape(4, 16, 256), axis=1)
    lat_ref[0, 0] = merged[:2]
    lat_ref[0, 1] = merged[2:]

    lat_bf = lat.astype(jnp.bfloat16)
    token = lax.broadcasted_iota(jnp.int32, (tokens, clips * 64), 0)
    lane = lax.broadcasted_iota(jnp.int32, (tokens, clips * 64), 1)
    first = token // 8 * 32 + token % 8 * 2
    heads = q_ref.shape[2] // HD
    projected = base_ref[...]
    for a in range(2):
        for e in range(2):
            chosen = jnp.where(lane == first + (16 * a + e), 1.0, 0.0).astype(jnp.bfloat16)
            patch = lax.dot_general(
                chosen, lat_bf, (((1,), (1,)), ((), ())), preferred_element_type=jnp.float32
            ).astype(jnp.bfloat16)
            weight = m_ref[(2 * a + e) * TILE : (2 * a + e + 1) * TILE]
            projected = projected + jnp.dot(patch, weight, preferred_element_type=jnp.float32)

    even = lax.broadcasted_iota(jnp.int32, (tokens, HD), 1) % 2 == 0
    cosine = jnp.concatenate([rope_ref[:16]] * clips, axis=0)
    sine = jnp.concatenate([rope_ref[16:]] * clips, axis=0)

    def turn(vectors, gain):
        square = jnp.mean(vectors * vectors, axis=-1, keepdims=True)
        vectors = vectors * lax.rsqrt(square + norm_eps) * gain
        swapped = jnp.where(even, pltpu.roll(vectors, HD - 1, 1), pltpu.roll(vectors, 1, 1))
        return vectors * cosine + swapped * sine

    def keep(ref, head, value):
        value = value.reshape(tokens // 8, 8, HD).astype(jnp.bfloat16)
        ref[:, :, head * HD : (head + 1) * HD] = value

    for head in range(heads):
        at = 3 * HD * head
        keep(q_ref, head, turn(projected[:, at : at + HD], table_ref[48:49]))
        keep(k_ref, head, turn(projected[:, at + HD : at + 2 * HD], table_ref[49:50]))
        keep(v_ref, head, projected[:, at + 2 * HD : at + 3 * HD])


def rope_freqs():
    freqs = []
    for dims in (time_dims, row_dims, row_dims):
        freqs.append(rope_base ** (-np.arange(0, dims, 2, dtype=np.float64) / dims))
    return np.repeat(np.concatenate(freqs), 2)[None].astype(np.float32)


def vmem(count):
    return [pl.BlockSpec(memory_space=pltpu.VMEM)] * count


def grouped(
    clip_inputs,
    conv_in_weight,
    group_gain,
    group_bias,
    conv_out_weight,
    out_bias,
    patch_weight,
    patch_bias,
    qkv_weight,
    qkv_bias,
    q_gain,
    k_gain,
    frame_pos,
    row_pos,
):
    plane_axes = ("tm", "height")
    clips = lax.axis_size("dp")
    steps = lax.axis_size("tm")
    plane = steps * lax.axis_size("height")
    channels = clip_inputs.shape[4]
    depth = conv_in_weight.shape[0]

    width = -(-depth // LANES) * LANES + LANES
    hbm = pl.BlockSpec(memory_space=pltpu.HBM)
    wide = pltpu.CompilerParams(vmem_limit_bytes=60 * 1024 * 1024)
    limit = pltpu.CompilerParams(vmem_limit_bytes=32 * 1024 * 1024)
    small = pl.CostEstimate(flops=10**6, bytes_accessed=10**6, transcendentals=0)
    with jax.named_scope("weight_by_group"):
        weight_block = jax.ShapeDtypeStruct((4 * GROUP, width), jnp.bfloat16)
        own_block = jax.ShapeDtypeStruct((4 * GROUP, width + LANES), jnp.bfloat16)
        small_arrays = (group_gain, group_bias, out_bias, qkv_bias, q_gain, k_gain)
        small_arrays += (frame_pos,)
        *packed, scale, table = pl.pallas_call(
            pack_kernel,
            out_shape=(own_block,)
            + (weight_block,) * 3
            + (
                jax.ShapeDtypeStruct((4 * GROUP, 2), jnp.float32),
                jax.ShapeDtypeStruct((56, LANES), jnp.float32),
            ),
            in_specs=[hbm] * 12,
            out_specs=(hbm,) * 6,
            scratch_shapes=[
                pltpu.VMEM(conv_in_weight.shape, jnp.bfloat16),
                pltpu.VMEM(qkv_weight.shape, jnp.bfloat16),
                pltpu.VMEM((patch_weight.shape[0], qkv_weight.shape[0]), jnp.bfloat16),
                pltpu.VMEM(patch_bias.shape, jnp.bfloat16),
                *[pltpu.VMEM(array.shape, array.dtype) for array in small_arrays],
                pltpu.VMEM((1, HD), jnp.float32),
                pltpu.VMEM((patch_bias.shape[0] // LANES, LANES), jnp.float32),
                pltpu.VMEM((8 * GROUP, depth), jnp.bfloat16),
                pltpu.VMEM((patch_weight.shape[0], qkv_weight.shape[1]), jnp.float32),
                pltpu.VMEM((4, 4 * GROUP, width), jnp.bfloat16),
                pltpu.VMEM((16, LANES), jnp.bfloat16),
                pltpu.VMEM((4 * GROUP, 2), jnp.float32),
                pltpu.VMEM((56, LANES), jnp.float32),
                pltpu.SemaphoreType.DMA((20,)),
            ],
            compiler_params=wide,
            cost_estimate=pl.CostEstimate(flops=10**8, bytes_accessed=10**6, transcendentals=0),
            name="pack_weights",
        )(
            rope_freqs(),
            conv_in_weight,
            qkv_weight,
            patch_weight,
            patch_bias,
            *small_arrays,
        )
        blocks = [packed[0]]
        for flip, block in zip((1, 4, 5), packed[1:]):
            blocks.append(lax.ppermute(block, plane_axes, [(i, i ^ flip) for i in range(plane)]))
    with jax.named_scope("gather_clips"):
        own = clip_inputs.reshape(64, channels)
        layers = []
        for step in reversed(range(clips)):
            pairs = []
            for layer in range(clips):
                for tm in range(steps):
                    to = (layer // 2 * 2 + tm % 2 + step) % clips
                    pair = (layer * steps + tm, to * steps + tm // 2 * 2 + layer % 2)
                    if pair[0] == pair[1]:
                        pair = (pair[0], (layer ^ 1) * steps + (tm ^ 1))
                    pairs.append(pair)
            layers.append(lax.ppermute(own, ("dp", "tm"), pairs))
    with jax.named_scope("spread_clips"):
        keep, send = pl.pallas_call(
            arrange_kernel,
            out_shape=(jax.ShapeDtypeStruct((2, 64, channels), jnp.bfloat16),) * 2,
            in_specs=vmem(5),
            out_specs=tuple(vmem(2)),
            scratch_shapes=[pltpu.VMEM((4, 64, channels), jnp.bfloat16)],
            compiler_params=limit,
            cost_estimate=small,
            name="arrange_clips",
        )(*layers, own)
        pieces = [keep]
        for flip in (1, 4, 5):
            pairs = [(i, i ^ flip) for i in range(plane)]
            pieces.append(lax.ppermute(send if flip % 2 else keep, plane_axes, pairs))
    with jax.named_scope("small_weights"):
        first = lax.axis_index("tm") // 2 * (4 * GROUP)
        weight_out = lax.dynamic_slice_in_dim(conv_out_weight, first, 4 * GROUP, axis=1)
        weight_out = weight_out.transpose(0, 2, 1).reshape(TAPS * TILE, 4 * GROUP)
    with jax.named_scope("join_weights"):
        height = len(core_taps(0)) * 4 * GROUP
        joined = pl.pallas_call(
            join_kernel,
            out_shape=jax.ShapeDtypeStruct((height + 32, channels), jnp.bfloat16),
            in_specs=vmem(4),
            out_specs=vmem(1)[0],
            scratch_shapes=[pltpu.VMEM((4, 4 * GROUP, width), jnp.bfloat16)],
            compiler_params=limit,
            cost_estimate=small,
            name="join_weights",
        )(*blocks)
        joined_pair = lax.ppermute(joined, "tm", [(i, i ^ 1) for i in range(steps)])
    with jax.named_scope("merged_projection"):
        share = joined[height:].astype(jnp.float32) + joined_pair[height:].astype(jnp.float32)
        share = share.astype(jnp.bfloat16)
        shares = [share]
        for flip in (1, 4, 5):
            pairs = [(i, i ^ flip) for i in range(plane)]
            shares.append(lax.ppermute(share, plane_axes, pairs))

        merged, base, rope = pl.pallas_call(
            share_kernel,
            out_shape=(
                jax.ShapeDtypeStruct((64, 6 * HD), jnp.bfloat16),
                jax.ShapeDtypeStruct((1, 6 * HD), jnp.float32),
                jax.ShapeDtypeStruct((32, LANES), jnp.float32),
            ),
            in_specs=vmem(5) + [pl.BlockSpec(memory_space=pltpu.SMEM)],
            out_specs=tuple(vmem(3)),
            scratch_shapes=[pltpu.VMEM((4, 16, 6 * HD), jnp.float32)],
            compiler_params=limit,
            cost_estimate=small,
            name="share_rows",
        )(*shares, table, row_pos)

    flops = 4 * height * steps * LANES * channels
    clip = pl.pallas_call(
        place_kernel,
        out_shape=jax.ShapeDtypeStruct((plane, 64, channels), jnp.bfloat16),
        in_specs=vmem(4),
        out_specs=vmem(1)[0],
        compiler_params=limit,
        cost_estimate=pl.CostEstimate(flops=4 * 10**10, bytes_accessed=10**6, transcendentals=0),
        name="place_clip",
    )(*pieces)
    partial = pl.pallas_call(
        conv_kernel,
        out_shape=jax.ShapeDtypeStruct((clips * plane, 8, LANES), jnp.float32),
        in_specs=vmem(5),
        out_specs=vmem(1)[0],
        scratch_shapes=[
            pltpu.VMEM((2, height, steps * LANES), jnp.float32),
        ],
        compiler_params=limit,
        cost_estimate=pl.CostEstimate(flops=flops, bytes_accessed=10**6, transcendentals=0),
        name="convolutions",
    )(clip, joined, joined_pair, scale, weight_out)

    with jax.named_scope("sum_latents"):
        partials = lax.all_to_all(partial, ("dp",) + plane_axes, 0, 0, tiled=True)

    heads = qkv_weight.shape[1] // (3 * HD)
    frames = clip_inputs.shape[1]
    tokens = jax.ShapeDtypeStruct((clips * frames, 8, heads * HD), jnp.bfloat16)
    latents, query, key, value = pl.pallas_call(
        token_kernel,
        out_shape=(jax.ShapeDtypeStruct((1, 2, 2, 256), jnp.float32), tokens, tokens, tokens),
        in_specs=vmem(5),
        out_specs=tuple(vmem(4)),
        compiler_params=limit,
        cost_estimate=pl.CostEstimate(flops=10**8, bytes_accessed=10**6, transcendentals=0),
        name="tokens",
    )(
        partials,
        merged,
        base,
        rope,
        table,
    )
    full = (clips, frames, 1, 8, heads * HD)
    return latents, query.reshape(full), key.reshape(full), value.reshape(full)


def pick(mesh, *arrays):
    if one_group_each(mesh, arrays[0], arrays[1], arrays[4], arrays[8]):
        return grouped(*arrays)
    return shards(*arrays)


def solution(mesh):
    placed = (
        P("dp", "tm", "height", None, None),
        P(("tm", "height"), "dp"),
        P("dp"),
        P("dp"),
        P(None, "dp", None),
        P(),
        P(),
        P(),
        P(("tm", "height"), "dp"),
        P("dp"),
        P(),
        P(),
        P("tm"),
        P("height"),
    )
    return jax.shard_map(
        functools.partial(pick, mesh),
        mesh=mesh,
        in_specs=placed,
        out_specs=(
            P("dp", "tm", "height", None),
            P(None, "tm", "height", None, "dp"),
            P(None, "tm", "height", None, "dp"),
            P(None, "tm", "height", None, "dp"),
        ),
        check_vma=False,
    )
```

```python
import functools

import jax
import jax.numpy as jnp
import numpy as np
from jax import lax
from jax.experimental import pallas as pl
from jax.experimental.pallas import tpu as pltpu
from jax.sharding import PartitionSpec as P

HD = 128
GROUPS = 32
TAPS = 27


norm_eps = 1e-06
latent_scale = 0.476986
rope_base = 256.0
time_dims = 16
row_dims = 56


def from_behind(value, axis, steps):
    count = lax.axis_size(axis)
    first, last = (max(0, -steps), min(count, count - steps))
    return lax.ppermute(value, axis, [(source, source + steps) for source in range(first, last)])


def padded_2(block, sides, width):
    for axis, dim in sides:
        count = lax.axis_size(axis)
        forward = [(i, i + 1) for i in range(count - 1)]
        backward = [(target, source) for source, target in forward]
        low = lax.ppermute(
            lax.slice_in_dim(block, block.shape[dim] - width, None, axis=dim), axis, forward
        )
        high = lax.ppermute(lax.slice_in_dim(block, 0, width, axis=dim), axis, backward)
        block = jnp.concatenate([low, block, high], axis=dim)
    return block


def repeat_first(block):
    return jnp.concatenate([block[:, :1], block[:, :1]], axis=1)


def time_join(block, earlier):
    start = jnp.where(lax.axis_index("tm") == 0, repeat_first(block), earlier)
    return jnp.concatenate([start, block], axis=1)


def rows_finish(grown):
    place = lax.axis_index("height")
    top = jnp.where(place == 0, grown[:, :, 1:2], grown[:, :, :1])
    bottom = jnp.where(place == lax.axis_size("height") - 1, grown[:, :, -2:-1], grown[:, :, -1:])
    inner = jnp.concatenate([top, grown[:, :, 1:-1], bottom], axis=2)
    return jnp.pad(inner, ((0, 0), (0, 0), (0, 0), (1, 1), (0, 0)), mode="edge")


def edges_before(block):
    earlier = from_behind(block, "tm", 1)
    longer = time_join(block, earlier)
    return rows_finish(padded_2(longer, (("height", 2),), 1))


def edges_norm(block):
    earlier = from_behind(block, "tm", 1)
    longer = time_join(block, earlier)
    return rows_finish(padded_2(longer, (("height", 2),), 1))


def convolve(padded, weight):
    clips = padded.shape[0]
    frames = padded.shape[1] - 2
    rows = padded.shape[2] - 2
    cols = padded.shape[3] - 2
    total = jnp.zeros((clips * frames * rows * cols, weight.shape[2]), jnp.float32)
    for shift_t in range(3):
        for shift_r in range(3):
            for shift_c in range(3):
                window = padded[
                    :,
                    shift_t : shift_t + frames,
                    shift_r : shift_r + rows,
                    shift_c : shift_c + cols,
                ]
                window = window.reshape(-1, padded.shape[4])
                total = total + jnp.dot(
                    window,
                    weight[9 * shift_t + 3 * shift_r + shift_c],
                    preferred_element_type=jnp.float32,
                )
    return total.reshape(clips, frames, rows, cols, weight.shape[2])


def section_freqs(dims):
    return jnp.power(rope_base, -jnp.arange(0, dims, 2, dtype=jnp.float32) / dims)


def rope_angles(tpos, hpos, width):
    frames = tpos.shape[0]
    rows = hpos.shape[0]
    cols = jnp.arange(width, dtype=jnp.float32)
    part_t = tpos[:, None, None, None] * section_freqs(time_dims)
    part_h = hpos[None, :, None, None] * section_freqs(row_dims)
    part_w = cols[None, None, :, None] * section_freqs(row_dims)
    shape = (frames, rows, width)
    return jnp.concatenate(
        [
            jnp.broadcast_to(part_t, shape + (time_dims // 2,)),
            jnp.broadcast_to(part_h, shape + (row_dims // 2,)),
            jnp.broadcast_to(part_w, shape + (row_dims // 2,)),
        ],
        axis=-1,
    )


def rotate(vectors, angles):
    pairs = vectors.reshape(vectors.shape[:-1] + (vectors.shape[-1] // 2, 2))
    first = pairs[..., 0]
    second = pairs[..., 1]
    cosine = jnp.cos(angles)[..., None, :]
    sine = jnp.sin(angles)[..., None, :]
    turned = jnp.stack([first * cosine - second * sine, first * sine + second * cosine], axis=-1)
    return turned.reshape(vectors.shape)


def rms_scale(vectors, gain):
    return (
        vectors
        * lax.rsqrt(jnp.mean(vectors * vectors, axis=-1, keepdims=True) + norm_eps)
        * gain.astype(jnp.float32)
    )


def shards(
    clip_inputs,
    conv_in_weight,
    group_gain,
    group_bias,
    conv_out_weight,
    out_bias,
    patch_weight,
    patch_bias,
    qkv_weight,
    qkv_bias,
    q_gain,
    k_gain,
    frame_pos,
    row_pos,
):
    channels = clip_inputs.shape[4]
    frames = clip_inputs.shape[1]
    rows = clip_inputs.shape[2]
    cols = clip_inputs.shape[3]
    padded = lax.all_gather(edges_before(clip_inputs), "dp", axis=0, tiled=True)
    clips = padded.shape[0]
    weight_in = lax.all_gather(conv_in_weight, ("tm", "height"), axis=0, tiled=True).reshape(
        TAPS, channels, -1
    )
    hidden = convolve(padded, weight_in)
    block_width = hidden.shape[4]
    group_width = channels // GROUPS
    local_groups = block_width // group_width
    grouped = hidden.reshape(clips, -1, local_groups, group_width)
    sums_local = jnp.sum(grouped, axis=(1, 3))
    squares_local = jnp.sum(grouped * grouped, axis=(1, 3))
    sums_all, squares_all = lax.psum((sums_local, squares_local), ("tm", "height"))
    count = float(
        frames * lax.axis_size("tm") * rows * lax.axis_size("height") * cols * group_width
    )
    mean = sums_all / count
    var = squares_all / count - mean * mean
    scaled = (grouped - mean[:, None, :, None]) * lax.rsqrt(var + norm_eps)[:, None, :, None]
    scaled = scaled.reshape(hidden.shape) * group_gain.astype(jnp.float32) + group_bias.astype(
        jnp.float32
    )
    normed = jax.nn.silu(scaled).astype(jnp.bfloat16)
    partial_latent = convolve(edges_norm(normed), conv_out_weight)
    own_sum = lax.psum_scatter(partial_latent, "dp", scatter_dimension=0, tiled=True)
    own_latent = (own_sum + out_bias) * latent_scale
    every_latent = lax.all_gather(own_latent.astype(jnp.bfloat16), "dp", axis=0, tiled=True)
    latent_dims = every_latent.shape[4]
    latents = own_latent.reshape(1, frames, rows, cols * latent_dims)
    tok_rows = rows // 2
    tok_cols = cols // 2
    patches = every_latent.reshape(clips, frames, tok_rows, 2, tok_cols, 2, latent_dims)
    patches = patches.transpose(0, 1, 2, 4, 3, 5, 6).reshape(-1, 4 * latent_dims)
    embedded = (
        jnp.dot(patches, patch_weight, preferred_element_type=jnp.float32)
        + patch_bias.astype(jnp.float32)
    ).astype(jnp.bfloat16)
    projected = jnp.dot(
        embedded,
        lax.all_gather(qkv_weight, ("tm", "height"), axis=0, tiled=True),
        preferred_element_type=jnp.float32,
    )
    projected = projected + qkv_bias.astype(jnp.float32)
    local_heads = qkv_weight.shape[1] // (3 * HD)
    projected = projected.reshape(clips, frames, tok_rows, tok_cols, local_heads, 3, HD)
    angles = rope_angles(frame_pos.astype(jnp.float32), row_pos.astype(jnp.float32), tok_cols)
    query = rotate(rms_scale(projected[..., 0, :], q_gain), angles)
    key = rotate(rms_scale(projected[..., 1, :], k_gain), angles)
    value = projected[..., 2, :]
    merged = (clips, frames, tok_rows, tok_cols, local_heads * HD)
    return (
        latents,
        query.reshape(merged).astype(jnp.bfloat16),
        key.reshape(merged).astype(jnp.bfloat16),
        value.reshape(merged).astype(jnp.bfloat16),
    )


LANES = 128
TILE = 16
GROUP = 16


def one_group_each(mesh, clip_inputs, conv_in_weight, conv_out_weight, qkv_weight):
    plane = mesh.shape["tm"] * mesh.shape["height"]
    return (
        clip_inputs.shape[:4] == (1, 2, 2, 16)
        and mesh.shape["height"] == 2
        and mesh.shape["tm"] == 4
        and mesh.shape["dp"] == 4
        and conv_in_weight.shape[1] == plane * GROUP
        and clip_inputs.shape[4] == GROUP * GROUPS
        and conv_out_weight.shape[2] == TILE
        and qkv_weight.shape[1] == 6 * HD
    )


def lane_shifts(lane):
    col = lane % 16
    row = lane // 16 % 2
    half = lane // 64

    def cols(left, mid, right):
        left = jnp.where(col == 0, left, pltpu.roll(left, 1, 1))
        right = jnp.where(col == 15, right, pltpu.roll(right, LANES - 1, 1))
        return mid + left + right

    def rows(up, mid, down):
        up = jnp.where(
            row == 1, pltpu.roll(up, 16, 1), jnp.where(half == 1, pltpu.roll(up, 48, 1), up)
        )
        down = jnp.where(
            row == 0,
            pltpu.roll(down, LANES - 16, 1),
            jnp.where(half == 0, pltpu.roll(down, LANES - 48, 1), down),
        )
        return mid + up + down

    return cols, rows


def tap_sums(source, tiles):
    lane = lax.broadcasted_iota(jnp.int32, (TILE, LANES), 1)
    second = lane // 32 % 2 == 1
    cols, rows = lane_shifts(lane)
    sums = []
    before = None
    for tile in range(tiles):

        def part(tap):
            return source(tap, slice(tile * LANES, (tile + 1) * LANES))

        oldest, older, now = (
            rows(*(cols(*(part(9 * i + 3 * j + l) for l in range(3))) for j in range(3)))
            for i in range(3)
        )
        turned = pltpu.roll(older, 32, 1)
        if before is None:
            start = jnp.where(second, pltpu.roll(oldest, 32, 1), oldest)
            total = now + jnp.where(second, turned, older) + start
        else:
            total = now + jnp.where(second, turned, pltpu.roll(before[1], 96, 1)) + before[0]
        before = (oldest, older)
        sums.append(total)
    return sums


def pack_kernel(
    freq_hbm, w_hbm, qkv_hbm, patch_hbm, patch_bias_hbm, gain_hbm, bias_hbm, out_bias_hbm,
    qkv_bias_hbm, q_hbm, k_hbm, frame_hbm,
    own_hbm, side_hbm, high_hbm, far_hbm, scale_hbm, table_hbm,
    w_ref, qkv_ref, patch_ref, patch_bias_ref, gain_v, bias_v, out_bias_v, qkv_bias_v, q_v, k_v,
    frame_v, freq_ref, rows_ref, turned_ref, merged_ref, out_ref, lines_ref, scale_ref, table_ref, sems,
):
    _, channels, width = out_ref.shape
    depth = w_ref.shape[0]
    rows = qkv_ref.shape[0]
    side = lax.axis_index("height")
    high = lax.axis_index("tm") // 2
    place = lax.axis_index("tm") * 2 + side
    at = pl.ds(pl.multiple_of(place * rows, LANES), rows)
    pairs = (
        (w_hbm, w_ref),
        (qkv_hbm, qkv_ref),
        (patch_hbm.at[:, at], patch_ref),
        (patch_bias_hbm, patch_bias_ref),
        (gain_hbm, gain_v),
        (bias_hbm, bias_v),
        (out_bias_hbm, out_bias_v),
        (qkv_bias_hbm, qkv_bias_v),
        (q_hbm, q_v),
        (k_hbm, k_v),
        (frame_hbm, frame_v),
        (freq_hbm, freq_ref),
    )
    loads = [
        pltpu.make_async_copy(source, to, sems.at[index])
        for index, (source, to) in enumerate(pairs)
    ]
    for load in loads:
        load.start()
    whole = depth // LANES * LANES
    loads[0].wait()
    turned_ref[...] = w_ref[...].T
    for load in loads[1:4]:
        load.wait()
    merged_ref[...] = jnp.dot(patch_ref[...], qkv_ref[...], preferred_element_type=jnp.float32)
    stores = []
    own_main = own_hbm.at[:, :width]
    for flip, out_hbm in ((1, side_hbm), (2, high_hbm), (3, far_hbm), (0, own_main)):
        first = pl.multiple_of((high ^ (flip // 2)) * channels, channels)
        out_ref[flip, :, :whole] = turned_ref[pl.ds(first, channels), :whole]
        lower = turned_ref[pl.ds(first, channels), whole:]
        chip = (2 * high + side) ^ flip
        tail, upper = [], []
        for half in range(2):
            mine = merged_ref[pl.ds(pl.multiple_of(chip * 16 + half * 8, 8), 8)]
            mine = [mine[:, q * LANES : (q + 1) * LANES] for q in range(6)]
            tail += mine[:4]
            upper += [pltpu.roll(mine[4], 64, 1), mine[4], pltpu.roll(mine[5], 64, 1), mine[5]]
        upper = jnp.concatenate(upper, axis=0)[:, 64:].astype(jnp.bfloat16)
        out_ref[flip, :, whole : whole + LANES] = jnp.concatenate([lower, upper], axis=1)
        out_ref[flip, :, whole + LANES :] = jnp.concatenate(tail, axis=0).astype(jnp.bfloat16)
        stores.append(pltpu.make_async_copy(out_ref.at[flip], out_hbm, sems.at[13 + flip]))
        stores[-1].start()
    rows_ref[...] = patch_bias_ref[...].astype(jnp.float32).reshape(rows_ref.shape)
    count = rows // LANES
    bias = [rows_ref[pl.ds(count * place + part, 1), :] for part in range(count)]
    bias = jnp.broadcast_to(jnp.concatenate(bias, axis=1), (8, rows)).astype(jnp.bfloat16)
    bias = jnp.dot(bias, qkv_ref[...], preferred_element_type=jnp.float32)
    line = lax.broadcasted_iota(jnp.int32, (8, LANES), 0)
    lines = jnp.zeros((8, LANES), jnp.float32)
    for part in range(bias.shape[1] // LANES):
        lines = jnp.where(line == part, bias[:, part * LANES : (part + 1) * LANES], lines)
    lines_ref[...] = jnp.concatenate([lines, jnp.zeros_like(lines)], axis=0).astype(jnp.bfloat16)
    stores.append(
        pltpu.make_async_copy(lines_ref, own_hbm.at[:16, width : width + LANES], sems.at[17])
    )
    stores[-1].start()
    for load in loads[4:]:
        load.wait()
    fill_tables(
        frame_v, freq_ref, gain_v, bias_v, out_bias_v, qkv_bias_v, q_v, k_v,
        scale_ref, table_ref,
    )
    for index, (source, to) in enumerate(((scale_ref, scale_hbm), (table_ref, table_hbm))):
        stores.append(pltpu.make_async_copy(source, to, sems.at[18 + index]))
        stores[-1].start()
    for store in stores:
        store.wait()


def column(row_ref, first, size):
    length = row_ref.shape[0]
    row = row_ref[...].astype(jnp.float32).reshape(1, length)
    line = lax.broadcasted_iota(jnp.int32, (size, length), 0)
    lane = lax.broadcasted_iota(jnp.int32, (size, length), 1)
    picked = jnp.where(lane == line + first, jnp.broadcast_to(row, (size, length)), 0.0)
    return jnp.sum(picked, axis=1, keepdims=True)


def fill_tables(
    frame_ref, freq_ref, gain_v, bias_v, out_bias_v, qkv_v, q_v, k_v,
    scale_ref, table_ref,
):
    shape = (TILE, LANES)
    line = lax.broadcasted_iota(jnp.int32, shape, 0)
    lane = lax.broadcasted_iota(jnp.int32, shape, 1)
    frames = frame_ref[...].astype(jnp.float32).reshape(1, 2)
    one, two = (jnp.broadcast_to(frames[:, part : part + 1], shape) for part in range(2))
    frame = jnp.where(line // 8 == 0, one, two)
    spot = jnp.where(lane < 72, 1.0, (line % 8).astype(jnp.float32))
    table_ref[:16] = jnp.where(lane < 16, frame, spot) * freq_ref[...]
    table_ref[16:32] = jnp.zeros(shape, jnp.float32)
    first = lax.axis_index("tm") // 2 * (4 * GROUP)
    scale_ref[:, 0:1] = column(gain_v, first, 4 * GROUP)
    scale_ref[:, 1:2] = column(bias_v, first, 4 * GROUP)
    table_ref[32:48] = jnp.broadcast_to(column(out_bias_v, 0, TILE), shape)
    table_ref[48:49] = q_v[...].astype(jnp.float32).reshape(1, HD)
    table_ref[49:50] = k_v[...].astype(jnp.float32).reshape(1, HD)
    table_ref[50:56] = qkv_v[...].astype(jnp.float32).reshape(6, LANES)


def arrange_kernel(*refs):
    pieces, (own_ref, keep_ref, send_ref, all_ref) = refs[:4], refs[4:]
    side = lax.axis_index("height")
    layer = lax.axis_index("dp")
    for step, piece in zip(reversed(range(4)), pieces):
        all_ref[(layer + 4 - step) % 4] = piece[...]

    @pl.when(layer % 2 == lax.axis_index("tm") % 2)
    def _():
        all_ref[layer] = own_ref[...]

    for core in range(2):
        keep_ref[core] = all_ref[2 * side + core]
        send_ref[core] = all_ref[2 - 2 * side + core]


def core_taps(core):
    quarter = TAPS / 4
    taps = []
    for tm in (core, core + 2):
        taps += range(int(quarter * tm), min(TAPS, -int(-quarter * (tm + 1) // 1)))
    return taps


def join_kernel(own_ref, side_ref, high_ref, far_ref, wt_ref, all_ref):
    channels, width = side_ref.shape
    inner = wt_ref.shape[1]
    depth = TAPS * inner // 8
    here = lax.axis_index("tm") // 2 * 2 + lax.axis_index("height")
    for flip, ref in enumerate((own_ref, side_ref, high_ref, far_ref)):
        all_ref[here ^ flip] = ref[:, :width]

    def assemble(core):
        for index, tap in enumerate(core_taps(core)):
            rows = slice(index * channels, (index + 1) * channels)
            start, end = tap * inner, (tap + 1) * inner
            while start < end:
                source = start // depth
                stop = min(end, (source + 1) * depth)
                to = slice(start - tap * inner, stop - tap * inner)
                if source // 2 % 2 == core:
                    chip = source // 4 * 2 + source % 2
                    first = start - source * depth
                    wt_ref[rows, to] = all_ref[chip, :, first : first + stop - start]
                else:
                    wt_ref[rows, to] = jnp.zeros((channels, stop - start), jnp.bfloat16)
                start = stop

    core = lax.axis_index("tm") % 2
    pl.when(core == 0)(functools.partial(assemble, 0))
    pl.when(core == 1)(functools.partial(assemble, 1))
    total = sum(all_ref[chip, :, width - 2 * LANES :].astype(jnp.float32) for chip in range(4))
    low = lax.broadcasted_iota(jnp.int32, (8, LANES), 1) < 64
    empty = jnp.zeros((8, LANES), jnp.float32)
    wide, narrow = [], []
    for half in range(2):
        top = 32 * half
        wide.append([total[top + 8 * q : top + 8 * q + 8, LANES:] for q in range(4)])
        some = []
        for q in range(2):
            one = total[top + 16 * q : top + 16 * q + 8, :LANES]
            two = total[top + 16 * q + 8 : top + 16 * q + 16, :LANES]
            some.append(jnp.where(low, pltpu.roll(one, 64, 1), two))
        lines = own_ref[:16, width:].astype(jnp.float32)[8 * half : 8 * half + 8]
        narrow.append(some + [lines, empty])
    share = jnp.concatenate([jnp.concatenate(row, axis=1) for row in wide + narrow], axis=0)
    wt_ref[wt_ref.shape[0] - 32 :] = share.astype(jnp.bfloat16)


def place_kernel(*refs):
    pieces, x_ref = refs[:4], refs[4]
    place = lax.axis_index("tm") // 2 * 4 + lax.axis_index("height")
    for flip, piece in zip((0, 5, 4, 1), pieces):
        for core in range(2):
            x_ref[(place ^ flip) + 2 * core] = piece[core]


def tap_parts(y_ref, group, channels):
    held = [core_taps(core) for core in range(2)]

    def part(tap, lanes):
        found = []
        for core in range(2):
            if tap in held[core]:
                at = held[core].index(tap) * channels + group * GROUP
                found.append(y_ref[core, at : at + GROUP, lanes])
        return sum(found[1:], found[0])

    return part


def conv_kernel(
    x_ref, wt_ref, pair_ref, scale_ref, w2_ref, out_ref, y_ref
):
    channels = 4 * GROUP
    tiles = x_ref.shape[0] // 2
    count = float(tiles * LANES * GROUP)
    core = lax.axis_index("tm") % 2
    height = y_ref.shape[1]
    x = x_ref[...].reshape(tiles * LANES, x_ref.shape[2])
    for ref, at in ((wt_ref, core), (pair_ref, 1 - core)):
        y_ref[at] = lax.dot_general(
            ref[:height], x, (((1,), (1,)), ((), ())), preferred_element_type=jnp.float32
        )
    normed = []
    for group in range(4):
        hidden = tap_sums(tap_parts(y_ref, group, channels), tiles)
        at = slice(group * GROUP, (group + 1) * GROUP)
        mean = jnp.sum(sum(hidden), keepdims=True) / count
        square = jnp.sum(sum(part * part for part in hidden), keepdims=True) / count
        scale = lax.rsqrt(square - mean * mean + norm_eps)
        parts = []
        for part in hidden:
            scaled = (part - mean) * scale * scale_ref[at, 0:1] + scale_ref[at, 1:2]
            parts.append((scaled / (1.0 + jnp.exp(-scaled))).astype(jnp.bfloat16))
        normed.append(jnp.concatenate(parts, axis=1))
    y_ref[0, : TAPS * TILE] = jnp.dot(
        w2_ref[...], jnp.concatenate(normed, axis=0), preferred_element_type=jnp.float32
    )

    def part(tap, lanes):
        return y_ref[0, tap * TILE : (tap + 1) * TILE, lanes]

    low = lax.broadcasted_iota(jnp.int32, (8, LANES), 1) < 64
    layers = out_ref.shape[0] // (2 * tiles)
    for tile, latent in enumerate(tap_sums(part, tiles)):
        turned = pltpu.roll(latent, 64, 1)
        near = jnp.where(low, latent[:8], turned[8:])
        far = jnp.where(low, turned[:8], latent[8:])
        for layer in range(layers):
            out_ref[layer * 2 * tiles + 2 * tile] = near
            out_ref[layer * 2 * tiles + 2 * tile + 1] = far


def share_kernel(
    m0_ref, m1_ref, m2_ref, m3_ref, table_ref, row_ref, merged_ref, base_ref, rope_ref, m_ref
):
    lane = lax.broadcasted_iota(jnp.int32, (16, LANES), 1)
    row = jnp.broadcast_to(row_ref[0], lane.shape).astype(jnp.float32)
    angles = table_ref[:16] * jnp.where((lane < 16) | (lane >= 72), 1.0, row)
    rope_ref[:16] = jnp.cos(angles)
    sine = jnp.sin(angles)
    rope_ref[16:] = jnp.where(lane % 2 == 0, -sine, sine)
    here = lax.axis_index("tm") // 2 * 2 + lax.axis_index("height")
    lines = table_ref[48:56]
    for flip, ref in enumerate((m0_ref, m1_ref, m2_ref, m3_ref)):
        share = ref[...].astype(jnp.float32)
        m_ref[here ^ flip, :, : 4 * LANES] = share[:16]
        m_ref[here ^ flip, :, 4 * LANES :] = share[16:, : 2 * LANES]
        lines = lines + pltpu.roll(share[16:24, 2 * LANES : 3 * LANES], 2, 0)
    base_ref[...] = jnp.concatenate([lines[2 + part : 3 + part] for part in range(6)], axis=1)
    merged_ref[...] = m_ref[...].reshape(merged_ref.shape).astype(jnp.bfloat16)


def token_kernel(p_ref, m_ref, base_ref, rope_ref, table_ref, lat_ref, q_ref, k_ref, v_ref):
    low = lax.broadcasted_iota(jnp.int32, (8, LANES), 1) < 64
    pairs = []
    for side in range(2):
        one, two = (
            sum(p_ref[4 * index + 2 * core + side] for index in range(p_ref.shape[0] // 4))
            for core in range(2)
        )
        top = jnp.where(low, one, pltpu.roll(two, 64, 1))
        bottom = jnp.where(low, pltpu.roll(one, 64, 1), two)
        pairs.append(jnp.concatenate([top, bottom], axis=0))
    total = jnp.concatenate(pairs, axis=1)
    lat = (total + table_ref[32:48, :1]) * latent_scale
    clips = lat.shape[1] // 64
    tokens = clips * 16
    place = lax.axis_index("dp")
    own = lat[:, :LANES]
    for pair in range(1, clips // 2):
        own = jnp.where(place // 2 == pair, lat[:, pair * LANES : (pair + 1) * LANES], own)
    own = jnp.where(place % 2 == 1, pltpu.roll(own, 64, 1), own)
    turned = own.T[:64]
    wide = jnp.concatenate([turned] * 16, axis=1)
    spot = lax.broadcasted_iota(jnp.int32, wide.shape, 0) % 16
    spread = lax.broadcasted_iota(jnp.int32, wide.shape, 1) // 16
    merged = jnp.sum(jnp.where(spot == spread, wide, 0.0).reshape(4, 16, 256), axis=1)
    lat_ref[0, 0] = merged[:2]
    lat_ref[0, 1] = merged[2:]

    lat_bf = lat.astype(jnp.bfloat16)
    token = lax.broadcasted_iota(jnp.int32, (tokens, clips * 64), 0)
    lane = lax.broadcasted_iota(jnp.int32, (tokens, clips * 64), 1)
    first = token // 8 * 32 + token % 8 * 2
    heads = q_ref.shape[2] // HD
    projected = base_ref[...]
    for a in range(2):
        for e in range(2):
            chosen = jnp.where(lane == first + (16 * a + e), 1.0, 0.0).astype(jnp.bfloat16)
            patch = lax.dot_general(
                chosen, lat_bf, (((1,), (1,)), ((), ())), preferred_element_type=jnp.float32
            ).astype(jnp.bfloat16)
            weight = m_ref[(2 * a + e) * TILE : (2 * a + e + 1) * TILE]
            projected = projected + jnp.dot(patch, weight, preferred_element_type=jnp.float32)

    even = lax.broadcasted_iota(jnp.int32, (tokens, HD), 1) % 2 == 0
    cosine = jnp.concatenate([rope_ref[:16]] * clips, axis=0)
    sine = jnp.concatenate([rope_ref[16:]] * clips, axis=0)

    def turn(vectors, gain):
        square = jnp.mean(vectors * vectors, axis=-1, keepdims=True)
        vectors = vectors * lax.rsqrt(square + norm_eps) * gain
        swapped = jnp.where(even, pltpu.roll(vectors, HD - 1, 1), pltpu.roll(vectors, 1, 1))
        return vectors * cosine + swapped * sine

    def keep(ref, head, value):
        value = value.reshape(tokens // 8, 8, HD).astype(jnp.bfloat16)
        ref[:, :, head * HD : (head + 1) * HD] = value

    for head in range(heads):
        at = 3 * HD * head
        keep(q_ref, head, turn(projected[:, at : at + HD], table_ref[48:49]))
        keep(k_ref, head, turn(projected[:, at + HD : at + 2 * HD], table_ref[49:50]))
        keep(v_ref, head, projected[:, at + 2 * HD : at + 3 * HD])


def rope_freqs():
    freqs = []
    for dims in (time_dims, row_dims, row_dims):
        freqs.append(rope_base ** (-np.arange(0, dims, 2, dtype=np.float64) / dims))
    return np.repeat(np.concatenate(freqs), 2)[None].astype(np.float32)


def vmem(count):
    return [pl.BlockSpec(memory_space=pltpu.VMEM)] * count


def grouped(
    clip_inputs,
    conv_in_weight,
    group_gain,
    group_bias,
    conv_out_weight,
    out_bias,
    patch_weight,
    patch_bias,
    qkv_weight,
    qkv_bias,
    q_gain,
    k_gain,
    frame_pos,
    row_pos,
):
    plane_axes = ("tm", "height")
    clips = lax.axis_size("dp")
    steps = lax.axis_size("tm")
    plane = steps * lax.axis_size("height")
    channels = clip_inputs.shape[4]
    depth = conv_in_weight.shape[0]

    width = -(-depth // LANES) * LANES + LANES
    hbm = pl.BlockSpec(memory_space=pltpu.HBM)
    wide = pltpu.CompilerParams(vmem_limit_bytes=60 * 1024 * 1024)
    limit = pltpu.CompilerParams(vmem_limit_bytes=32 * 1024 * 1024)
    small = pl.CostEstimate(flops=10**6, bytes_accessed=10**6, transcendentals=0)
    with jax.named_scope("weight_by_group"):
        weight_block = jax.ShapeDtypeStruct((4 * GROUP, width), jnp.bfloat16)
        own_block = jax.ShapeDtypeStruct((4 * GROUP, width + LANES), jnp.bfloat16)
        small_arrays = (group_gain, group_bias, out_bias, qkv_bias, q_gain, k_gain)
        small_arrays += (frame_pos,)
        *packed, scale, table = pl.pallas_call(
            pack_kernel,
            out_shape=(own_block,)
            + (weight_block,) * 3
            + (
                jax.ShapeDtypeStruct((4 * GROUP, 2), jnp.float32),
                jax.ShapeDtypeStruct((56, LANES), jnp.float32),
            ),
            in_specs=[hbm] * 12,
            out_specs=(hbm,) * 6,
            scratch_shapes=[
                pltpu.VMEM(conv_in_weight.shape, jnp.bfloat16),
                pltpu.VMEM(qkv_weight.shape, jnp.bfloat16),
                pltpu.VMEM((patch_weight.shape[0], qkv_weight.shape[0]), jnp.bfloat16),
                pltpu.VMEM(patch_bias.shape, jnp.bfloat16),
                *[pltpu.VMEM(array.shape, array.dtype) for array in small_arrays],
                pltpu.VMEM((1, HD), jnp.float32),
                pltpu.VMEM((patch_bias.shape[0] // LANES, LANES), jnp.float32),
                pltpu.VMEM((8 * GROUP, depth), jnp.bfloat16),
                pltpu.VMEM((patch_weight.shape[0], qkv_weight.shape[1]), jnp.float32),
                pltpu.VMEM((4, 4 * GROUP, width), jnp.bfloat16),
                pltpu.VMEM((16, LANES), jnp.bfloat16),
                pltpu.VMEM((4 * GROUP, 2), jnp.float32),
                pltpu.VMEM((56, LANES), jnp.float32),
                pltpu.SemaphoreType.DMA((20,)),
            ],
            compiler_params=wide,
            cost_estimate=pl.CostEstimate(flops=10**8, bytes_accessed=10**6, transcendentals=0),
            name="pack_weights",
        )(
            rope_freqs(),
            conv_in_weight,
            qkv_weight,
            patch_weight,
            patch_bias,
            *small_arrays,
        )
        blocks = [packed[0]]
        for flip, block in zip((1, 4, 5), packed[1:]):
            blocks.append(lax.ppermute(block, plane_axes, [(i, i ^ flip) for i in range(plane)]))
    with jax.named_scope("gather_clips"):
        own = clip_inputs.reshape(64, channels)
        layers = []
        for step in reversed(range(clips)):
            pairs = []
            for layer in range(clips):
                for tm in range(steps):
                    to = (layer // 2 * 2 + tm % 2 + step) % clips
                    pair = (layer * steps + tm, to * steps + tm // 2 * 2 + layer % 2)
                    if pair[0] != pair[1]:
                        pairs.append(pair)
            layers.append(lax.ppermute(own, ("dp", "tm"), pairs))
    with jax.named_scope("spread_clips"):
        keep, send = pl.pallas_call(
            arrange_kernel,
            out_shape=(jax.ShapeDtypeStruct((2, 64, channels), jnp.bfloat16),) * 2,
            in_specs=vmem(5),
            out_specs=tuple(vmem(2)),
            scratch_shapes=[pltpu.VMEM((4, 64, channels), jnp.bfloat16)],
            compiler_params=limit,
            cost_estimate=small,
            name="arrange_clips",
        )(*layers, own)
        pieces = [keep]
        for flip in (5, 4, 1):
            pairs = [(i, i ^ flip) for i in range(plane)]
            pieces.append(lax.ppermute(send if flip % 2 else keep, plane_axes, pairs))
    with jax.named_scope("small_weights"):
        first = lax.axis_index("tm") // 2 * (4 * GROUP)
        weight_out = lax.dynamic_slice_in_dim(conv_out_weight, first, 4 * GROUP, axis=1)
        weight_out = weight_out.transpose(0, 2, 1).reshape(TAPS * TILE, 4 * GROUP)
    with jax.named_scope("join_weights"):
        height = len(core_taps(0)) * 4 * GROUP
        joined = pl.pallas_call(
            join_kernel,
            out_shape=jax.ShapeDtypeStruct((height + 32, channels), jnp.bfloat16),
            in_specs=vmem(4),
            out_specs=vmem(1)[0],
            scratch_shapes=[pltpu.VMEM((4, 4 * GROUP, width), jnp.bfloat16)],
            compiler_params=limit,
            cost_estimate=small,
            name="join_weights",
        )(*blocks)
        joined_pair = lax.ppermute(joined, "tm", [(i, i ^ 1) for i in range(steps)])
    with jax.named_scope("merged_projection"):
        share = joined[height:].astype(jnp.float32) + joined_pair[height:].astype(jnp.float32)
        share = share.astype(jnp.bfloat16)
        shares = [share]
        for flip in (1, 4, 5):
            pairs = [(i, i ^ flip) for i in range(plane)]
            shares.append(lax.ppermute(share, plane_axes, pairs))

        merged, base, rope = pl.pallas_call(
            share_kernel,
            out_shape=(
                jax.ShapeDtypeStruct((64, 6 * HD), jnp.bfloat16),
                jax.ShapeDtypeStruct((1, 6 * HD), jnp.float32),
                jax.ShapeDtypeStruct((32, LANES), jnp.float32),
            ),
            in_specs=vmem(5) + [pl.BlockSpec(memory_space=pltpu.SMEM)],
            out_specs=tuple(vmem(3)),
            scratch_shapes=[pltpu.VMEM((4, 16, 6 * HD), jnp.float32)],
            compiler_params=limit,
            cost_estimate=small,
            name="share_rows",
        )(*shares, table, row_pos)

    flops = 4 * height * steps * LANES * channels
    clip = pl.pallas_call(
        place_kernel,
        out_shape=jax.ShapeDtypeStruct((plane, 64, channels), jnp.bfloat16),
        in_specs=vmem(4),
        out_specs=vmem(1)[0],
        compiler_params=limit,
        cost_estimate=pl.CostEstimate(flops=4 * 10**10, bytes_accessed=10**6, transcendentals=0),
        name="place_clip",
    )(*pieces)
    partial = pl.pallas_call(
        conv_kernel,
        out_shape=jax.ShapeDtypeStruct((clips * plane, 8, LANES), jnp.float32),
        in_specs=vmem(5),
        out_specs=vmem(1)[0],
        scratch_shapes=[
            pltpu.VMEM((2, height, steps * LANES), jnp.float32),
        ],
        compiler_params=limit,
        cost_estimate=pl.CostEstimate(flops=flops, bytes_accessed=10**6, transcendentals=0),
        name="convolutions",
    )(clip, joined, joined_pair, scale, weight_out)

    with jax.named_scope("sum_latents"):
        partials = lax.all_to_all(partial, ("dp",) + plane_axes, 0, 0, tiled=True)

    heads = qkv_weight.shape[1] // (3 * HD)
    frames = clip_inputs.shape[1]
    tokens = jax.ShapeDtypeStruct((clips * frames, 8, heads * HD), jnp.bfloat16)
    latents, query, key, value = pl.pallas_call(
        token_kernel,
        out_shape=(jax.ShapeDtypeStruct((1, 2, 2, 256), jnp.float32), tokens, tokens, tokens),
        in_specs=vmem(5),
        out_specs=tuple(vmem(4)),
        compiler_params=limit,
        cost_estimate=pl.CostEstimate(flops=10**8, bytes_accessed=10**6, transcendentals=0),
        name="tokens",
    )(
        partials,
        merged,
        base,
        rope,
        table,
    )
    full = (clips, frames, 1, 8, heads * HD)
    return latents, query.reshape(full), key.reshape(full), value.reshape(full)


def pick(mesh, *arrays):
    if one_group_each(mesh, arrays[0], arrays[1], arrays[4], arrays[8]):
        return grouped(*arrays)
    return shards(*arrays)


def solution(mesh):
    placed = (
        P("dp", "tm", "height", None, None),
        P(("tm", "height"), "dp"),
        P("dp"),
        P("dp"),
        P(None, "dp", None),
        P(),
        P(),
        P(),
        P(("tm", "height"), "dp"),
        P("dp"),
        P(),
        P(),
        P("tm"),
        P("height"),
    )
    return jax.shard_map(
        functools.partial(pick, mesh),
        mesh=mesh,
        in_specs=placed,
        out_specs=(
            P("dp", "tm", "height", None),
            P(None, "tm", "height", None, "dp"),
            P(None, "tm", "height", None, "dp"),
            P(None, "tm", "height", None, "dp"),
        ),
        check_vma=False,
    )
```

```python
import functools

import jax
import jax.numpy as jnp
import numpy as np
from jax import lax
from jax.experimental import pallas as pl
from jax.experimental.pallas import tpu as pltpu
from jax.sharding import PartitionSpec as P

HD = 128
GROUPS = 32
TAPS = 27


norm_eps = 1e-06
latent_scale = 0.476986
rope_base = 256.0
time_dims = 16
row_dims = 56


def from_behind(value, axis, steps):
    count = lax.axis_size(axis)
    first, last = (max(0, -steps), min(count, count - steps))
    return lax.ppermute(value, axis, [(source, source + steps) for source in range(first, last)])


def padded_2(block, sides, width):
    for axis, dim in sides:
        count = lax.axis_size(axis)
        forward = [(i, i + 1) for i in range(count - 1)]
        backward = [(target, source) for source, target in forward]
        low = lax.ppermute(
            lax.slice_in_dim(block, block.shape[dim] - width, None, axis=dim), axis, forward
        )
        high = lax.ppermute(lax.slice_in_dim(block, 0, width, axis=dim), axis, backward)
        block = jnp.concatenate([low, block, high], axis=dim)
    return block


def repeat_first(block):
    return jnp.concatenate([block[:, :1], block[:, :1]], axis=1)


def time_join(block, earlier):
    start = jnp.where(lax.axis_index("tm") == 0, repeat_first(block), earlier)
    return jnp.concatenate([start, block], axis=1)


def rows_finish(grown):
    place = lax.axis_index("height")
    top = jnp.where(place == 0, grown[:, :, 1:2], grown[:, :, :1])
    bottom = jnp.where(place == lax.axis_size("height") - 1, grown[:, :, -2:-1], grown[:, :, -1:])
    inner = jnp.concatenate([top, grown[:, :, 1:-1], bottom], axis=2)
    return jnp.pad(inner, ((0, 0), (0, 0), (0, 0), (1, 1), (0, 0)), mode="edge")


def edges_before(block):
    earlier = from_behind(block, "tm", 1)
    longer = time_join(block, earlier)
    return rows_finish(padded_2(longer, (("height", 2),), 1))


def edges_norm(block):
    earlier = from_behind(block, "tm", 1)
    longer = time_join(block, earlier)
    return rows_finish(padded_2(longer, (("height", 2),), 1))


def convolve(padded, weight):
    clips = padded.shape[0]
    frames = padded.shape[1] - 2
    rows = padded.shape[2] - 2
    cols = padded.shape[3] - 2
    total = jnp.zeros((clips * frames * rows * cols, weight.shape[2]), jnp.float32)
    for shift_t in range(3):
        for shift_r in range(3):
            for shift_c in range(3):
                window = padded[
                    :,
                    shift_t : shift_t + frames,
                    shift_r : shift_r + rows,
                    shift_c : shift_c + cols,
                ]
                window = window.reshape(-1, padded.shape[4])
                total = total + jnp.dot(
                    window,
                    weight[9 * shift_t + 3 * shift_r + shift_c],
                    preferred_element_type=jnp.float32,
                )
    return total.reshape(clips, frames, rows, cols, weight.shape[2])


def section_freqs(dims):
    return jnp.power(rope_base, -jnp.arange(0, dims, 2, dtype=jnp.float32) / dims)


def rope_angles(tpos, hpos, width):
    frames = tpos.shape[0]
    rows = hpos.shape[0]
    cols = jnp.arange(width, dtype=jnp.float32)
    part_t = tpos[:, None, None, None] * section_freqs(time_dims)
    part_h = hpos[None, :, None, None] * section_freqs(row_dims)
    part_w = cols[None, None, :, None] * section_freqs(row_dims)
    shape = (frames, rows, width)
    return jnp.concatenate(
        [
            jnp.broadcast_to(part_t, shape + (time_dims // 2,)),
            jnp.broadcast_to(part_h, shape + (row_dims // 2,)),
            jnp.broadcast_to(part_w, shape + (row_dims // 2,)),
        ],
        axis=-1,
    )


def rotate(vectors, angles):
    pairs = vectors.reshape(vectors.shape[:-1] + (vectors.shape[-1] // 2, 2))
    first = pairs[..., 0]
    second = pairs[..., 1]
    cosine = jnp.cos(angles)[..., None, :]
    sine = jnp.sin(angles)[..., None, :]
    turned = jnp.stack([first * cosine - second * sine, first * sine + second * cosine], axis=-1)
    return turned.reshape(vectors.shape)


def rms_scale(vectors, gain):
    return (
        vectors
        * lax.rsqrt(jnp.mean(vectors * vectors, axis=-1, keepdims=True) + norm_eps)
        * gain.astype(jnp.float32)
    )


def shards(
    clip_inputs,
    conv_in_weight,
    group_gain,
    group_bias,
    conv_out_weight,
    out_bias,
    patch_weight,
    patch_bias,
    qkv_weight,
    qkv_bias,
    q_gain,
    k_gain,
    frame_pos,
    row_pos,
):
    channels = clip_inputs.shape[4]
    frames = clip_inputs.shape[1]
    rows = clip_inputs.shape[2]
    cols = clip_inputs.shape[3]
    padded = lax.all_gather(edges_before(clip_inputs), "dp", axis=0, tiled=True)
    clips = padded.shape[0]
    weight_in = lax.all_gather(conv_in_weight, ("tm", "height"), axis=0, tiled=True).reshape(
        TAPS, channels, -1
    )
    hidden = convolve(padded, weight_in)
    block_width = hidden.shape[4]
    group_width = channels // GROUPS
    local_groups = block_width // group_width
    grouped = hidden.reshape(clips, -1, local_groups, group_width)
    sums_local = jnp.sum(grouped, axis=(1, 3))
    squares_local = jnp.sum(grouped * grouped, axis=(1, 3))
    sums_all, squares_all = lax.psum((sums_local, squares_local), ("tm", "height"))
    count = float(
        frames * lax.axis_size("tm") * rows * lax.axis_size("height") * cols * group_width
    )
    mean = sums_all / count
    var = squares_all / count - mean * mean
    scaled = (grouped - mean[:, None, :, None]) * lax.rsqrt(var + norm_eps)[:, None, :, None]
    scaled = scaled.reshape(hidden.shape) * group_gain.astype(jnp.float32) + group_bias.astype(
        jnp.float32
    )
    normed = jax.nn.silu(scaled).astype(jnp.bfloat16)
    partial_latent = convolve(edges_norm(normed), conv_out_weight)
    own_sum = lax.psum_scatter(partial_latent, "dp", scatter_dimension=0, tiled=True)
    own_latent = (own_sum + out_bias) * latent_scale
    every_latent = lax.all_gather(own_latent.astype(jnp.bfloat16), "dp", axis=0, tiled=True)
    latent_dims = every_latent.shape[4]
    latents = own_latent.reshape(1, frames, rows, cols * latent_dims)
    tok_rows = rows // 2
    tok_cols = cols // 2
    patches = every_latent.reshape(clips, frames, tok_rows, 2, tok_cols, 2, latent_dims)
    patches = patches.transpose(0, 1, 2, 4, 3, 5, 6).reshape(-1, 4 * latent_dims)
    embedded = (
        jnp.dot(patches, patch_weight, preferred_element_type=jnp.float32)
        + patch_bias.astype(jnp.float32)
    ).astype(jnp.bfloat16)
    projected = jnp.dot(
        embedded,
        lax.all_gather(qkv_weight, ("tm", "height"), axis=0, tiled=True),
        preferred_element_type=jnp.float32,
    )
    projected = projected + qkv_bias.astype(jnp.float32)
    local_heads = qkv_weight.shape[1] // (3 * HD)
    projected = projected.reshape(clips, frames, tok_rows, tok_cols, local_heads, 3, HD)
    angles = rope_angles(frame_pos.astype(jnp.float32), row_pos.astype(jnp.float32), tok_cols)
    query = rotate(rms_scale(projected[..., 0, :], q_gain), angles)
    key = rotate(rms_scale(projected[..., 1, :], k_gain), angles)
    value = projected[..., 2, :]
    merged = (clips, frames, tok_rows, tok_cols, local_heads * HD)
    return (
        latents,
        query.reshape(merged).astype(jnp.bfloat16),
        key.reshape(merged).astype(jnp.bfloat16),
        value.reshape(merged).astype(jnp.bfloat16),
    )


LANES = 128
TILE = 16
GROUP = 16


def one_group_each(mesh, clip_inputs, conv_in_weight, conv_out_weight, qkv_weight):
    plane = mesh.shape["tm"] * mesh.shape["height"]
    return (
        clip_inputs.shape[:4] == (1, 2, 2, 16)
        and mesh.shape["height"] == 2
        and mesh.shape["tm"] == 4
        and mesh.shape["dp"] == 4
        and conv_in_weight.shape[1] == plane * GROUP
        and clip_inputs.shape[4] == GROUP * GROUPS
        and conv_out_weight.shape[2] == TILE
        and qkv_weight.shape[1] == 6 * HD
    )


def lane_shifts(lane):
    col = lane % 16
    row = lane // 16 % 2
    half = lane // 64

    def cols(left, mid, right):
        left = jnp.where(col == 0, left, pltpu.roll(left, 1, 1))
        right = jnp.where(col == 15, right, pltpu.roll(right, LANES - 1, 1))
        return mid + left + right

    def rows(up, mid, down):
        up = jnp.where(
            row == 1, pltpu.roll(up, 16, 1), jnp.where(half == 1, pltpu.roll(up, 48, 1), up)
        )
        down = jnp.where(
            row == 0,
            pltpu.roll(down, LANES - 16, 1),
            jnp.where(half == 0, pltpu.roll(down, LANES - 48, 1), down),
        )
        return mid + up + down

    return cols, rows


def tap_sums(source, tiles):
    lane = lax.broadcasted_iota(jnp.int32, (TILE, LANES), 1)
    second = lane // 32 % 2 == 1
    cols, rows = lane_shifts(lane)
    sums = []
    before = None
    for tile in range(tiles):

        def part(tap):
            return source(tap, slice(tile * LANES, (tile + 1) * LANES))

        oldest, older, now = (
            rows(*(cols(*(part(9 * i + 3 * j + l) for l in range(3))) for j in range(3)))
            for i in range(3)
        )
        turned = pltpu.roll(older, 32, 1)
        if before is None:
            start = jnp.where(second, pltpu.roll(oldest, 32, 1), oldest)
            total = now + jnp.where(second, turned, older) + start
        else:
            total = now + jnp.where(second, turned, pltpu.roll(before[1], 96, 1)) + before[0]
        before = (oldest, older)
        sums.append(total)
    return sums


def pack_kernel(
    freq_hbm, w_hbm, qkv_hbm, patch_hbm, patch_bias_hbm, gain_hbm, bias_hbm, out_bias_hbm,
    qkv_bias_hbm, q_hbm, k_hbm, frame_hbm,
    own_hbm, side_hbm, high_hbm, far_hbm, scale_hbm, table_hbm,
    w_ref, qkv_ref, patch_ref, patch_bias_ref, gain_v, bias_v, out_bias_v, qkv_bias_v, q_v, k_v,
    frame_v, freq_ref, rows_ref, turned_ref, merged_ref, out_ref, lines_ref, scale_ref, table_ref, sems,
):
    _, channels, width = out_ref.shape
    depth = w_ref.shape[0]
    rows = qkv_ref.shape[0]
    side = lax.axis_index("height")
    high = lax.axis_index("tm") // 2
    place = lax.axis_index("tm") * 2 + side
    at = pl.ds(pl.multiple_of(place * rows, LANES), rows)
    pairs = (
        (w_hbm, w_ref),
        (qkv_hbm, qkv_ref),
        (patch_hbm.at[:, at], patch_ref),
        (patch_bias_hbm, patch_bias_ref),
        (gain_hbm, gain_v),
        (bias_hbm, bias_v),
        (out_bias_hbm, out_bias_v),
        (qkv_bias_hbm, qkv_bias_v),
        (q_hbm, q_v),
        (k_hbm, k_v),
        (frame_hbm, frame_v),
        (freq_hbm, freq_ref),
    )
    loads = [
        pltpu.make_async_copy(source, to, sems.at[index])
        for index, (source, to) in enumerate(pairs)
    ]
    for load in loads:
        load.start()
    whole = depth // LANES * LANES
    loads[0].wait()
    turned_ref[...] = w_ref[...].T
    for load in loads[1:4]:
        load.wait()
    merged_ref[...] = jnp.dot(patch_ref[...], qkv_ref[...], preferred_element_type=jnp.float32)
    stores = []
    own_main = own_hbm.at[:, :width]
    for flip, out_hbm in ((1, side_hbm), (2, high_hbm), (3, far_hbm), (0, own_main)):
        first = pl.multiple_of((high ^ (flip // 2)) * channels, channels)
        out_ref[flip, :, :whole] = turned_ref[pl.ds(first, channels), :whole]
        lower = turned_ref[pl.ds(first, channels), whole:]
        chip = (2 * high + side) ^ flip
        tail, upper = [], []
        for half in range(2):
            mine = merged_ref[pl.ds(pl.multiple_of(chip * 16 + half * 8, 8), 8)]
            mine = [mine[:, q * LANES : (q + 1) * LANES] for q in range(6)]
            tail += mine[:4]
            upper += [pltpu.roll(mine[4], 64, 1), mine[4], pltpu.roll(mine[5], 64, 1), mine[5]]
        upper = jnp.concatenate(upper, axis=0)[:, 64:].astype(jnp.bfloat16)
        out_ref[flip, :, whole : whole + LANES] = jnp.concatenate([lower, upper], axis=1)
        out_ref[flip, :, whole + LANES :] = jnp.concatenate(tail, axis=0).astype(jnp.bfloat16)
        stores.append(pltpu.make_async_copy(out_ref.at[flip], out_hbm, sems.at[13 + flip]))
        stores[-1].start()
    rows_ref[...] = patch_bias_ref[...].astype(jnp.float32).reshape(rows_ref.shape)
    count = rows // LANES
    bias = [rows_ref[pl.ds(count * place + part, 1), :] for part in range(count)]
    bias = jnp.broadcast_to(jnp.concatenate(bias, axis=1), (8, rows)).astype(jnp.bfloat16)
    bias = jnp.dot(bias, qkv_ref[...], preferred_element_type=jnp.float32)
    line = lax.broadcasted_iota(jnp.int32, (8, LANES), 0)
    lines = jnp.zeros((8, LANES), jnp.float32)
    for part in range(bias.shape[1] // LANES):
        lines = jnp.where(line == part, bias[:, part * LANES : (part + 1) * LANES], lines)
    lines_ref[...] = jnp.concatenate([lines, jnp.zeros_like(lines)], axis=0).astype(jnp.bfloat16)
    stores.append(
        pltpu.make_async_copy(lines_ref, own_hbm.at[:16, width : width + LANES], sems.at[17])
    )
    stores[-1].start()
    for load in loads[4:]:
        load.wait()
    fill_tables(
        frame_v, freq_ref, gain_v, bias_v, out_bias_v, qkv_bias_v, q_v, k_v,
        scale_ref, table_ref,
    )
    for index, (source, to) in enumerate(((scale_ref, scale_hbm), (table_ref, table_hbm))):
        stores.append(pltpu.make_async_copy(source, to, sems.at[18 + index]))
        stores[-1].start()
    for store in stores:
        store.wait()


def column(row_ref, first, size):
    length = row_ref.shape[0]
    row = row_ref[...].astype(jnp.float32).reshape(1, length)
    line = lax.broadcasted_iota(jnp.int32, (size, length), 0)
    lane = lax.broadcasted_iota(jnp.int32, (size, length), 1)
    picked = jnp.where(lane == line + first, jnp.broadcast_to(row, (size, length)), 0.0)
    return jnp.sum(picked, axis=1, keepdims=True)


def fill_tables(
    frame_ref, freq_ref, gain_v, bias_v, out_bias_v, qkv_v, q_v, k_v,
    scale_ref, table_ref,
):
    shape = (TILE, LANES)
    line = lax.broadcasted_iota(jnp.int32, shape, 0)
    lane = lax.broadcasted_iota(jnp.int32, shape, 1)
    frames = frame_ref[...].astype(jnp.float32).reshape(1, 2)
    one, two = (jnp.broadcast_to(frames[:, part : part + 1], shape) for part in range(2))
    frame = jnp.where(line // 8 == 0, one, two)
    spot = jnp.where(lane < 72, 1.0, (line % 8).astype(jnp.float32))
    table_ref[:16] = jnp.where(lane < 16, frame, spot) * freq_ref[...]
    table_ref[16:32] = jnp.zeros(shape, jnp.float32)
    first = lax.axis_index("tm") // 2 * (4 * GROUP)
    scale_ref[:, 0:1] = column(gain_v, first, 4 * GROUP)
    scale_ref[:, 1:2] = column(bias_v, first, 4 * GROUP)
    table_ref[32:48] = jnp.broadcast_to(column(out_bias_v, 0, TILE), shape)
    table_ref[48:49] = q_v[...].astype(jnp.float32).reshape(1, HD)
    table_ref[49:50] = k_v[...].astype(jnp.float32).reshape(1, HD)
    table_ref[50:56] = qkv_v[...].astype(jnp.float32).reshape(6, LANES)


def arrange_kernel(*refs):
    pieces, (own_ref, keep_ref, send_ref, all_ref) = refs[:4], refs[4:]
    side = lax.axis_index("height")
    layer = lax.axis_index("dp")
    for step, piece in zip(reversed(range(4)), pieces):
        all_ref[(layer + 4 - step) % 4] = piece[...]

    @pl.when(layer % 2 == lax.axis_index("tm") % 2)
    def _():
        all_ref[layer] = own_ref[...]

    for core in range(2):
        keep_ref[core] = all_ref[2 * side + core]
        send_ref[core] = all_ref[2 - 2 * side + core]


def core_taps(core):
    quarter = TAPS / 4
    taps = []
    for tm in (core, core + 2):
        taps += range(int(quarter * tm), min(TAPS, -int(-quarter * (tm + 1) // 1)))
    return taps


def join_kernel(own_ref, far_ref, high_ref, side_ref, wt_ref, all_ref):
    channels, width = side_ref.shape
    inner = wt_ref.shape[1]
    depth = TAPS * inner // 8
    here = lax.axis_index("tm") // 2 * 2 + lax.axis_index("height")
    for flip, ref in enumerate((own_ref, side_ref, high_ref, far_ref)):
        all_ref[here ^ flip] = ref[:, :width]

    def assemble(core):
        for index, tap in enumerate(core_taps(core)):
            rows = slice(index * channels, (index + 1) * channels)
            start, end = tap * inner, (tap + 1) * inner
            while start < end:
                source = start // depth
                stop = min(end, (source + 1) * depth)
                to = slice(start - tap * inner, stop - tap * inner)
                if source // 2 % 2 == core:
                    chip = source // 4 * 2 + source % 2
                    first = start - source * depth
                    wt_ref[rows, to] = all_ref[chip, :, first : first + stop - start]
                else:
                    wt_ref[rows, to] = jnp.zeros((channels, stop - start), jnp.bfloat16)
                start = stop

    core = lax.axis_index("tm") % 2
    pl.when(core == 0)(functools.partial(assemble, 0))
    pl.when(core == 1)(functools.partial(assemble, 1))
    total = sum(all_ref[chip, :, width - 2 * LANES :].astype(jnp.float32) for chip in range(4))
    low = lax.broadcasted_iota(jnp.int32, (8, LANES), 1) < 64
    empty = jnp.zeros((8, LANES), jnp.float32)
    wide, narrow = [], []
    for half in range(2):
        top = 32 * half
        wide.append([total[top + 8 * q : top + 8 * q + 8, LANES:] for q in range(4)])
        some = []
        for q in range(2):
            one = total[top + 16 * q : top + 16 * q + 8, :LANES]
            two = total[top + 16 * q + 8 : top + 16 * q + 16, :LANES]
            some.append(jnp.where(low, pltpu.roll(one, 64, 1), two))
        lines = own_ref[:16, width:].astype(jnp.float32)[8 * half : 8 * half + 8]
        narrow.append(some + [lines, empty])
    share = jnp.concatenate([jnp.concatenate(row, axis=1) for row in wide + narrow], axis=0)
    wt_ref[wt_ref.shape[0] - 32 :] = share.astype(jnp.bfloat16)


def place_kernel(*refs):
    pieces, x_ref = refs[:4], refs[4]
    place = lax.axis_index("tm") // 2 * 4 + lax.axis_index("height")
    for flip, piece in zip((0, 1, 4, 5), pieces):
        for core in range(2):
            x_ref[(place ^ flip) + 2 * core] = piece[core]


def tap_parts(y_ref, group, channels):
    held = [core_taps(core) for core in range(2)]

    def part(tap, lanes):
        found = []
        for core in range(2):
            if tap in held[core]:
                at = held[core].index(tap) * channels + group * GROUP
                found.append(y_ref[core, at : at + GROUP, lanes])
        return sum(found[1:], found[0])

    return part


def conv_kernel(
    x_ref, wt_ref, pair_ref, scale_ref, w2_ref, out_ref, y_ref
):
    channels = 4 * GROUP
    tiles = x_ref.shape[0] // 2
    count = float(tiles * LANES * GROUP)
    core = lax.axis_index("tm") % 2
    height = y_ref.shape[1]
    x = x_ref[...].reshape(tiles * LANES, x_ref.shape[2])
    for ref, at in ((wt_ref, core), (pair_ref, 1 - core)):
        y_ref[at] = lax.dot_general(
            ref[:height], x, (((1,), (1,)), ((), ())), preferred_element_type=jnp.float32
        )
    normed = []
    for group in range(4):
        hidden = tap_sums(tap_parts(y_ref, group, channels), tiles)
        at = slice(group * GROUP, (group + 1) * GROUP)
        mean = jnp.sum(sum(hidden), keepdims=True) / count
        square = jnp.sum(sum(part * part for part in hidden), keepdims=True) / count
        scale = lax.rsqrt(square - mean * mean + norm_eps)
        parts = []
        for part in hidden:
            scaled = (part - mean) * scale * scale_ref[at, 0:1] + scale_ref[at, 1:2]
            parts.append((scaled / (1.0 + jnp.exp(-scaled))).astype(jnp.bfloat16))
        normed.append(jnp.concatenate(parts, axis=1))
    y_ref[0, : TAPS * TILE] = jnp.dot(
        w2_ref[...], jnp.concatenate(normed, axis=0), preferred_element_type=jnp.float32
    )

    def part(tap, lanes):
        return y_ref[0, tap * TILE : (tap + 1) * TILE, lanes]

    low = lax.broadcasted_iota(jnp.int32, (8, LANES), 1) < 64
    layers = out_ref.shape[0] // (2 * tiles)
    for tile, latent in enumerate(tap_sums(part, tiles)):
        turned = pltpu.roll(latent, 64, 1)
        near = jnp.where(low, latent[:8], turned[8:])
        far = jnp.where(low, turned[:8], latent[8:])
        for layer in range(layers):
            out_ref[layer * 2 * tiles + 2 * tile] = near
            out_ref[layer * 2 * tiles + 2 * tile + 1] = far


def share_kernel(
    m0_ref, m1_ref, m2_ref, m3_ref, table_ref, row_ref, merged_ref, base_ref, rope_ref, m_ref
):
    lane = lax.broadcasted_iota(jnp.int32, (16, LANES), 1)
    row = jnp.broadcast_to(row_ref[0], lane.shape).astype(jnp.float32)
    angles = table_ref[:16] * jnp.where((lane < 16) | (lane >= 72), 1.0, row)
    rope_ref[:16] = jnp.cos(angles)
    sine = jnp.sin(angles)
    rope_ref[16:] = jnp.where(lane % 2 == 0, -sine, sine)
    here = lax.axis_index("tm") // 2 * 2 + lax.axis_index("height")
    lines = table_ref[48:56]
    for flip, ref in enumerate((m0_ref, m1_ref, m2_ref, m3_ref)):
        share = ref[...].astype(jnp.float32)
        m_ref[here ^ flip, :, : 4 * LANES] = share[:16]
        m_ref[here ^ flip, :, 4 * LANES :] = share[16:, : 2 * LANES]
        lines = lines + pltpu.roll(share[16:24, 2 * LANES : 3 * LANES], 2, 0)
    base_ref[...] = jnp.concatenate([lines[2 + part : 3 + part] for part in range(6)], axis=1)
    merged_ref[...] = m_ref[...].reshape(merged_ref.shape).astype(jnp.bfloat16)


def token_kernel(p_ref, m_ref, base_ref, rope_ref, table_ref, lat_ref, q_ref, k_ref, v_ref):
    low = lax.broadcasted_iota(jnp.int32, (8, LANES), 1) < 64
    pairs = []
    for side in range(2):
        one, two = (
            sum(p_ref[4 * index + 2 * core + side] for index in range(p_ref.shape[0] // 4))
            for core in range(2)
        )
        top = jnp.where(low, one, pltpu.roll(two, 64, 1))
        bottom = jnp.where(low, pltpu.roll(one, 64, 1), two)
        pairs.append(jnp.concatenate([top, bottom], axis=0))
    total = jnp.concatenate(pairs, axis=1)
    lat = (total + table_ref[32:48, :1]) * latent_scale
    clips = lat.shape[1] // 64
    tokens = clips * 16
    place = lax.axis_index("dp")
    own = lat[:, :LANES]
    for pair in range(1, clips // 2):
        own = jnp.where(place // 2 == pair, lat[:, pair * LANES : (pair + 1) * LANES], own)
    own = jnp.where(place % 2 == 1, pltpu.roll(own, 64, 1), own)
    turned = own.T[:64]
    wide = jnp.concatenate([turned] * 16, axis=1)
    spot = lax.broadcasted_iota(jnp.int32, wide.shape, 0) % 16
    spread = lax.broadcasted_iota(jnp.int32, wide.shape, 1) // 16
    merged = jnp.sum(jnp.where(spot == spread, wide, 0.0).reshape(4, 16, 256), axis=1)
    lat_ref[0, 0] = merged[:2]
    lat_ref[0, 1] = merged[2:]

    lat_bf = lat.astype(jnp.bfloat16)
    token = lax.broadcasted_iota(jnp.int32, (tokens, clips * 64), 0)
    lane = lax.broadcasted_iota(jnp.int32, (tokens, clips * 64), 1)
    first = token // 8 * 32 + token % 8 * 2
    heads = q_ref.shape[2] // HD
    projected = base_ref[...]
    for a in range(2):
        for e in range(2):
            chosen = jnp.where(lane == first + (16 * a + e), 1.0, 0.0).astype(jnp.bfloat16)
            patch = lax.dot_general(
                chosen, lat_bf, (((1,), (1,)), ((), ())), preferred_element_type=jnp.float32
            ).astype(jnp.bfloat16)
            weight = m_ref[(2 * a + e) * TILE : (2 * a + e + 1) * TILE]
            projected = projected + jnp.dot(patch, weight, preferred_element_type=jnp.float32)

    even = lax.broadcasted_iota(jnp.int32, (tokens, HD), 1) % 2 == 0
    cosine = jnp.concatenate([rope_ref[:16]] * clips, axis=0)
    sine = jnp.concatenate([rope_ref[16:]] * clips, axis=0)

    def turn(vectors, gain):
        square = jnp.mean(vectors * vectors, axis=-1, keepdims=True)
        vectors = vectors * lax.rsqrt(square + norm_eps) * gain
        swapped = jnp.where(even, pltpu.roll(vectors, HD - 1, 1), pltpu.roll(vectors, 1, 1))
        return vectors * cosine + swapped * sine

    def keep(ref, head, value):
        value = value.reshape(tokens // 8, 8, HD).astype(jnp.bfloat16)
        ref[:, :, head * HD : (head + 1) * HD] = value

    for head in range(heads):
        at = 3 * HD * head
        keep(q_ref, head, turn(projected[:, at : at + HD], table_ref[48:49]))
        keep(k_ref, head, turn(projected[:, at + HD : at + 2 * HD], table_ref[49:50]))
        keep(v_ref, head, projected[:, at + 2 * HD : at + 3 * HD])


def rope_freqs():
    freqs = []
    for dims in (time_dims, row_dims, row_dims):
        freqs.append(rope_base ** (-np.arange(0, dims, 2, dtype=np.float64) / dims))
    return np.repeat(np.concatenate(freqs), 2)[None].astype(np.float32)


def vmem(count):
    return [pl.BlockSpec(memory_space=pltpu.VMEM)] * count


def grouped(
    clip_inputs,
    conv_in_weight,
    group_gain,
    group_bias,
    conv_out_weight,
    out_bias,
    patch_weight,
    patch_bias,
    qkv_weight,
    qkv_bias,
    q_gain,
    k_gain,
    frame_pos,
    row_pos,
):
    plane_axes = ("tm", "height")
    clips = lax.axis_size("dp")
    steps = lax.axis_size("tm")
    plane = steps * lax.axis_size("height")
    channels = clip_inputs.shape[4]
    depth = conv_in_weight.shape[0]

    width = -(-depth // LANES) * LANES + LANES
    hbm = pl.BlockSpec(memory_space=pltpu.HBM)
    wide = pltpu.CompilerParams(vmem_limit_bytes=60 * 1024 * 1024)
    limit = pltpu.CompilerParams(vmem_limit_bytes=32 * 1024 * 1024)
    small = pl.CostEstimate(flops=10**6, bytes_accessed=10**6, transcendentals=0)
    with jax.named_scope("weight_by_group"):
        weight_block = jax.ShapeDtypeStruct((4 * GROUP, width), jnp.bfloat16)
        own_block = jax.ShapeDtypeStruct((4 * GROUP, width + LANES), jnp.bfloat16)
        small_arrays = (group_gain, group_bias, out_bias, qkv_bias, q_gain, k_gain)
        small_arrays += (frame_pos,)
        *packed, scale, table = pl.pallas_call(
            pack_kernel,
            out_shape=(own_block,)
            + (weight_block,) * 3
            + (
                jax.ShapeDtypeStruct((4 * GROUP, 2), jnp.float32),
                jax.ShapeDtypeStruct((56, LANES), jnp.float32),
            ),
            in_specs=[hbm] * 12,
            out_specs=(hbm,) * 6,
            scratch_shapes=[
                pltpu.VMEM(conv_in_weight.shape, jnp.bfloat16),
                pltpu.VMEM(qkv_weight.shape, jnp.bfloat16),
                pltpu.VMEM((patch_weight.shape[0], qkv_weight.shape[0]), jnp.bfloat16),
                pltpu.VMEM(patch_bias.shape, jnp.bfloat16),
                *[pltpu.VMEM(array.shape, array.dtype) for array in small_arrays],
                pltpu.VMEM((1, HD), jnp.float32),
                pltpu.VMEM((patch_bias.shape[0] // LANES, LANES), jnp.float32),
                pltpu.VMEM((8 * GROUP, depth), jnp.bfloat16),
                pltpu.VMEM((patch_weight.shape[0], qkv_weight.shape[1]), jnp.float32),
                pltpu.VMEM((4, 4 * GROUP, width), jnp.bfloat16),
                pltpu.VMEM((16, LANES), jnp.bfloat16),
                pltpu.VMEM((4 * GROUP, 2), jnp.float32),
                pltpu.VMEM((56, LANES), jnp.float32),
                pltpu.SemaphoreType.DMA((20,)),
            ],
            compiler_params=wide,
            cost_estimate=pl.CostEstimate(flops=10**8, bytes_accessed=10**6, transcendentals=0),
            name="pack_weights",
        )(
            rope_freqs(),
            conv_in_weight,
            qkv_weight,
            patch_weight,
            patch_bias,
            *small_arrays,
        )
        blocks = [packed[0]]
        for flip, block in zip((5, 4, 1), packed[:0:-1]):
            blocks.append(lax.ppermute(block, plane_axes, [(i, i ^ flip) for i in range(plane)]))
    with jax.named_scope("gather_clips"):
        own = clip_inputs.reshape(64, channels)
        layers = []
        for step in reversed(range(clips)):
            pairs = []
            for layer in range(clips):
                for tm in range(steps):
                    to = (layer // 2 * 2 + tm % 2 + step) % clips
                    pair = (layer * steps + tm, to * steps + tm // 2 * 2 + layer % 2)
                    if pair[0] != pair[1]:
                        pairs.append(pair)
            layers.append(lax.ppermute(own, ("dp", "tm"), pairs))
    with jax.named_scope("spread_clips"):
        keep, send = pl.pallas_call(
            arrange_kernel,
            out_shape=(jax.ShapeDtypeStruct((2, 64, channels), jnp.bfloat16),) * 2,
            in_specs=vmem(5),
            out_specs=tuple(vmem(2)),
            scratch_shapes=[pltpu.VMEM((4, 64, channels), jnp.bfloat16)],
            compiler_params=limit,
            cost_estimate=small,
            name="arrange_clips",
        )(*layers, own)
        pieces = [keep]
        for flip in (1, 4, 5):
            pairs = [(i, i ^ flip) for i in range(plane)]
            pieces.append(lax.ppermute(send if flip % 2 else keep, plane_axes, pairs))
    with jax.named_scope("small_weights"):
        first = lax.axis_index("tm") // 2 * (4 * GROUP)
        weight_out = lax.dynamic_slice_in_dim(conv_out_weight, first, 4 * GROUP, axis=1)
        weight_out = weight_out.transpose(0, 2, 1).reshape(TAPS * TILE, 4 * GROUP)
    with jax.named_scope("join_weights"):
        height = len(core_taps(0)) * 4 * GROUP
        joined = pl.pallas_call(
            join_kernel,
            out_shape=jax.ShapeDtypeStruct((height + 32, channels), jnp.bfloat16),
            in_specs=vmem(4),
            out_specs=vmem(1)[0],
            scratch_shapes=[pltpu.VMEM((4, 4 * GROUP, width), jnp.bfloat16)],
            compiler_params=limit,
            cost_estimate=small,
            name="join_weights",
        )(*blocks)
        joined_pair = lax.ppermute(joined, "tm", [(i, i ^ 1) for i in range(steps)])
    with jax.named_scope("merged_projection"):
        share = joined[height:].astype(jnp.float32) + joined_pair[height:].astype(jnp.float32)
        share = share.astype(jnp.bfloat16)
        shares = [share]
        for flip in (1, 4, 5):
            pairs = [(i, i ^ flip) for i in range(plane)]
            shares.append(lax.ppermute(share, plane_axes, pairs))

        merged, base, rope = pl.pallas_call(
            share_kernel,
            out_shape=(
                jax.ShapeDtypeStruct((64, 6 * HD), jnp.bfloat16),
                jax.ShapeDtypeStruct((1, 6 * HD), jnp.float32),
                jax.ShapeDtypeStruct((32, LANES), jnp.float32),
            ),
            in_specs=vmem(5) + [pl.BlockSpec(memory_space=pltpu.SMEM)],
            out_specs=tuple(vmem(3)),
            scratch_shapes=[pltpu.VMEM((4, 16, 6 * HD), jnp.float32)],
            compiler_params=limit,
            cost_estimate=small,
            name="share_rows",
        )(*shares, table, row_pos)

    flops = 4 * height * steps * LANES * channels
    clip = pl.pallas_call(
        place_kernel,
        out_shape=jax.ShapeDtypeStruct((plane, 64, channels), jnp.bfloat16),
        in_specs=vmem(4),
        out_specs=vmem(1)[0],
        compiler_params=limit,
        cost_estimate=pl.CostEstimate(flops=4 * 10**10, bytes_accessed=10**6, transcendentals=0),
        name="place_clip",
    )(*pieces)
    partial = pl.pallas_call(
        conv_kernel,
        out_shape=jax.ShapeDtypeStruct((clips * plane, 8, LANES), jnp.float32),
        in_specs=vmem(5),
        out_specs=vmem(1)[0],
        scratch_shapes=[
            pltpu.VMEM((2, height, steps * LANES), jnp.float32),
        ],
        compiler_params=limit,
        cost_estimate=pl.CostEstimate(flops=flops, bytes_accessed=10**6, transcendentals=0),
        name="convolutions",
    )(clip, joined, joined_pair, scale, weight_out)

    with jax.named_scope("sum_latents"):
        partials = lax.all_to_all(partial, ("dp",) + plane_axes, 0, 0, tiled=True)

    heads = qkv_weight.shape[1] // (3 * HD)
    frames = clip_inputs.shape[1]
    tokens = jax.ShapeDtypeStruct((clips * frames, 8, heads * HD), jnp.bfloat16)
    latents, query, key, value = pl.pallas_call(
        token_kernel,
        out_shape=(jax.ShapeDtypeStruct((1, 2, 2, 256), jnp.float32), tokens, tokens, tokens),
        in_specs=vmem(5),
        out_specs=tuple(vmem(4)),
        compiler_params=limit,
        cost_estimate=pl.CostEstimate(flops=10**8, bytes_accessed=10**6, transcendentals=0),
        name="tokens",
    )(
        partials,
        merged,
        base,
        rope,
        table,
    )
    full = (clips, frames, 1, 8, heads * HD)
    return latents, query.reshape(full), key.reshape(full), value.reshape(full)


def pick(mesh, *arrays):
    if one_group_each(mesh, arrays[0], arrays[1], arrays[4], arrays[8]):
        return grouped(*arrays)
    return shards(*arrays)


def solution(mesh):
    placed = (
        P("dp", "tm", "height", None, None),
        P(("tm", "height"), "dp"),
        P("dp"),
        P("dp"),
        P(None, "dp", None),
        P(),
        P(),
        P(),
        P(("tm", "height"), "dp"),
        P("dp"),
        P(),
        P(),
        P("tm"),
        P("height"),
    )
    return jax.shard_map(
        functools.partial(pick, mesh),
        mesh=mesh,
        in_specs=placed,
        out_specs=(
            P("dp", "tm", "height", None),
            P(None, "tm", "height", None, "dp"),
            P(None, "tm", "height", None, "dp"),
            P(None, "tm", "height", None, "dp"),
        ),
        check_vma=False,
    )
```

```python
import functools

import jax
import jax.numpy as jnp
import numpy as np
from jax import lax
from jax.experimental import pallas as pl
from jax.experimental.pallas import tpu as pltpu
from jax.sharding import PartitionSpec as P

HD = 128
GROUPS = 32
TAPS = 27


norm_eps = 1e-06
latent_scale = 0.476986
rope_base = 256.0
time_dims = 16
row_dims = 56


def from_behind(value, axis, steps):
    count = lax.axis_size(axis)
    first, last = (max(0, -steps), min(count, count - steps))
    return lax.ppermute(value, axis, [(source, source + steps) for source in range(first, last)])


def padded_2(block, sides, width):
    for axis, dim in sides:
        count = lax.axis_size(axis)
        forward = [(i, i + 1) for i in range(count - 1)]
        backward = [(target, source) for source, target in forward]
        low = lax.ppermute(
            lax.slice_in_dim(block, block.shape[dim] - width, None, axis=dim), axis, forward
        )
        high = lax.ppermute(lax.slice_in_dim(block, 0, width, axis=dim), axis, backward)
        block = jnp.concatenate([low, block, high], axis=dim)
    return block


def repeat_first(block):
    return jnp.concatenate([block[:, :1], block[:, :1]], axis=1)


def time_join(block, earlier):
    start = jnp.where(lax.axis_index("tm") == 0, repeat_first(block), earlier)
    return jnp.concatenate([start, block], axis=1)


def rows_finish(grown):
    place = lax.axis_index("height")
    top = jnp.where(place == 0, grown[:, :, 1:2], grown[:, :, :1])
    bottom = jnp.where(place == lax.axis_size("height") - 1, grown[:, :, -2:-1], grown[:, :, -1:])
    inner = jnp.concatenate([top, grown[:, :, 1:-1], bottom], axis=2)
    return jnp.pad(inner, ((0, 0), (0, 0), (0, 0), (1, 1), (0, 0)), mode="edge")


def edges_before(block):
    earlier = from_behind(block, "tm", 1)
    longer = time_join(block, earlier)
    return rows_finish(padded_2(longer, (("height", 2),), 1))


def edges_norm(block):
    earlier = from_behind(block, "tm", 1)
    longer = time_join(block, earlier)
    return rows_finish(padded_2(longer, (("height", 2),), 1))


def convolve(padded, weight):
    clips = padded.shape[0]
    frames = padded.shape[1] - 2
    rows = padded.shape[2] - 2
    cols = padded.shape[3] - 2
    total = jnp.zeros((clips * frames * rows * cols, weight.shape[2]), jnp.float32)
    for shift_t in range(3):
        for shift_r in range(3):
            for shift_c in range(3):
                window = padded[
                    :,
                    shift_t : shift_t + frames,
                    shift_r : shift_r + rows,
                    shift_c : shift_c + cols,
                ]
                window = window.reshape(-1, padded.shape[4])
                total = total + jnp.dot(
                    window,
                    weight[9 * shift_t + 3 * shift_r + shift_c],
                    preferred_element_type=jnp.float32,
                )
    return total.reshape(clips, frames, rows, cols, weight.shape[2])


def section_freqs(dims):
    return jnp.power(rope_base, -jnp.arange(0, dims, 2, dtype=jnp.float32) / dims)


def rope_angles(tpos, hpos, width):
    frames = tpos.shape[0]
    rows = hpos.shape[0]
    cols = jnp.arange(width, dtype=jnp.float32)
    part_t = tpos[:, None, None, None] * section_freqs(time_dims)
    part_h = hpos[None, :, None, None] * section_freqs(row_dims)
    part_w = cols[None, None, :, None] * section_freqs(row_dims)
    shape = (frames, rows, width)
    return jnp.concatenate(
        [
            jnp.broadcast_to(part_t, shape + (time_dims // 2,)),
            jnp.broadcast_to(part_h, shape + (row_dims // 2,)),
            jnp.broadcast_to(part_w, shape + (row_dims // 2,)),
        ],
        axis=-1,
    )


def rotate(vectors, angles):
    pairs = vectors.reshape(vectors.shape[:-1] + (vectors.shape[-1] // 2, 2))
    first = pairs[..., 0]
    second = pairs[..., 1]
    cosine = jnp.cos(angles)[..., None, :]
    sine = jnp.sin(angles)[..., None, :]
    turned = jnp.stack([first * cosine - second * sine, first * sine + second * cosine], axis=-1)
    return turned.reshape(vectors.shape)


def rms_scale(vectors, gain):
    return (
        vectors
        * lax.rsqrt(jnp.mean(vectors * vectors, axis=-1, keepdims=True) + norm_eps)
        * gain.astype(jnp.float32)
    )


def shards(
    clip_inputs,
    conv_in_weight,
    group_gain,
    group_bias,
    conv_out_weight,
    out_bias,
    patch_weight,
    patch_bias,
    qkv_weight,
    qkv_bias,
    q_gain,
    k_gain,
    frame_pos,
    row_pos,
):
    channels = clip_inputs.shape[4]
    frames = clip_inputs.shape[1]
    rows = clip_inputs.shape[2]
    cols = clip_inputs.shape[3]
    padded = lax.all_gather(edges_before(clip_inputs), "dp", axis=0, tiled=True)
    clips = padded.shape[0]
    weight_in = lax.all_gather(conv_in_weight, ("tm", "height"), axis=0, tiled=True).reshape(
        TAPS, channels, -1
    )
    hidden = convolve(padded, weight_in)
    block_width = hidden.shape[4]
    group_width = channels // GROUPS
    local_groups = block_width // group_width
    grouped = hidden.reshape(clips, -1, local_groups, group_width)
    sums_local = jnp.sum(grouped, axis=(1, 3))
    squares_local = jnp.sum(grouped * grouped, axis=(1, 3))
    sums_all, squares_all = lax.psum((sums_local, squares_local), ("tm", "height"))
    count = float(
        frames * lax.axis_size("tm") * rows * lax.axis_size("height") * cols * group_width
    )
    mean = sums_all / count
    var = squares_all / count - mean * mean
    scaled = (grouped - mean[:, None, :, None]) * lax.rsqrt(var + norm_eps)[:, None, :, None]
    scaled = scaled.reshape(hidden.shape) * group_gain.astype(jnp.float32) + group_bias.astype(
        jnp.float32
    )
    normed = jax.nn.silu(scaled).astype(jnp.bfloat16)
    partial_latent = convolve(edges_norm(normed), conv_out_weight)
    own_sum = lax.psum_scatter(partial_latent, "dp", scatter_dimension=0, tiled=True)
    own_latent = (own_sum + out_bias) * latent_scale
    every_latent = lax.all_gather(own_latent.astype(jnp.bfloat16), "dp", axis=0, tiled=True)
    latent_dims = every_latent.shape[4]
    latents = own_latent.reshape(1, frames, rows, cols * latent_dims)
    tok_rows = rows // 2
    tok_cols = cols // 2
    patches = every_latent.reshape(clips, frames, tok_rows, 2, tok_cols, 2, latent_dims)
    patches = patches.transpose(0, 1, 2, 4, 3, 5, 6).reshape(-1, 4 * latent_dims)
    embedded = (
        jnp.dot(patches, patch_weight, preferred_element_type=jnp.float32)
        + patch_bias.astype(jnp.float32)
    ).astype(jnp.bfloat16)
    projected = jnp.dot(
        embedded,
        lax.all_gather(qkv_weight, ("tm", "height"), axis=0, tiled=True),
        preferred_element_type=jnp.float32,
    )
    projected = projected + qkv_bias.astype(jnp.float32)
    local_heads = qkv_weight.shape[1] // (3 * HD)
    projected = projected.reshape(clips, frames, tok_rows, tok_cols, local_heads, 3, HD)
    angles = rope_angles(frame_pos.astype(jnp.float32), row_pos.astype(jnp.float32), tok_cols)
    query = rotate(rms_scale(projected[..., 0, :], q_gain), angles)
    key = rotate(rms_scale(projected[..., 1, :], k_gain), angles)
    value = projected[..., 2, :]
    merged = (clips, frames, tok_rows, tok_cols, local_heads * HD)
    return (
        latents,
        query.reshape(merged).astype(jnp.bfloat16),
        key.reshape(merged).astype(jnp.bfloat16),
        value.reshape(merged).astype(jnp.bfloat16),
    )


LANES = 128
TILE = 16
GROUP = 16


def one_group_each(mesh, clip_inputs, conv_in_weight, conv_out_weight, qkv_weight):
    plane = mesh.shape["tm"] * mesh.shape["height"]
    return (
        clip_inputs.shape[:4] == (1, 2, 2, 16)
        and mesh.shape["height"] == 2
        and mesh.shape["tm"] == 4
        and mesh.shape["dp"] == 4
        and conv_in_weight.shape[1] == plane * GROUP
        and clip_inputs.shape[4] == GROUP * GROUPS
        and conv_out_weight.shape[2] == TILE
        and qkv_weight.shape[1] == 6 * HD
    )


def lane_shifts(lane):
    col = lane % 16
    row = lane // 16 % 2
    half = lane // 64

    def cols(left, mid, right):
        left = jnp.where(col == 0, left, pltpu.roll(left, 1, 1))
        right = jnp.where(col == 15, right, pltpu.roll(right, LANES - 1, 1))
        return mid + left + right

    def rows(up, mid, down):
        up = jnp.where(
            row == 1, pltpu.roll(up, 16, 1), jnp.where(half == 1, pltpu.roll(up, 48, 1), up)
        )
        down = jnp.where(
            row == 0,
            pltpu.roll(down, LANES - 16, 1),
            jnp.where(half == 0, pltpu.roll(down, LANES - 48, 1), down),
        )
        return mid + up + down

    return cols, rows


def tap_sums(source, tiles):
    lane = lax.broadcasted_iota(jnp.int32, (TILE, LANES), 1)
    second = lane // 32 % 2 == 1
    cols, rows = lane_shifts(lane)
    sums = []
    before = None
    for tile in range(tiles):

        def part(tap):
            return source(tap, slice(tile * LANES, (tile + 1) * LANES))

        oldest, older, now = (
            rows(*(cols(*(part(9 * i + 3 * j + l) for l in range(3))) for j in range(3)))
            for i in range(3)
        )
        turned = pltpu.roll(older, 32, 1)
        if before is None:
            start = jnp.where(second, pltpu.roll(oldest, 32, 1), oldest)
            total = now + jnp.where(second, turned, older) + start
        else:
            total = now + jnp.where(second, turned, pltpu.roll(before[1], 96, 1)) + before[0]
        before = (oldest, older)
        sums.append(total)
    return sums


def pack_kernel(
    freq_hbm, w_hbm, qkv_hbm, patch_hbm, patch_bias_hbm, gain_hbm, bias_hbm, out_bias_hbm,
    qkv_bias_hbm, q_hbm, k_hbm, frame_hbm,
    own_hbm, side_hbm, high_hbm, far_hbm, scale_hbm, table_hbm,
    w_ref, qkv_ref, patch_ref, patch_bias_ref, gain_v, bias_v, out_bias_v, qkv_bias_v, q_v, k_v,
    frame_v, freq_ref, rows_ref, turned_ref, merged_ref, out_ref, lines_ref, scale_ref, table_ref, sems,
):
    _, channels, width = out_ref.shape
    depth = w_ref.shape[0]
    rows = qkv_ref.shape[0]
    side = lax.axis_index("height")
    high = lax.axis_index("tm") // 2
    place = lax.axis_index("tm") * 2 + side
    at = pl.ds(pl.multiple_of(place * rows, LANES), rows)
    pairs = (
        (w_hbm, w_ref),
        (qkv_hbm, qkv_ref),
        (patch_hbm.at[:, at], patch_ref),
        (patch_bias_hbm, patch_bias_ref),
        (gain_hbm, gain_v),
        (bias_hbm, bias_v),
        (out_bias_hbm, out_bias_v),
        (qkv_bias_hbm, qkv_bias_v),
        (q_hbm, q_v),
        (k_hbm, k_v),
        (frame_hbm, frame_v),
        (freq_hbm, freq_ref),
    )
    loads = [
        pltpu.make_async_copy(source, to, sems.at[index])
        for index, (source, to) in enumerate(pairs)
    ]
    for load in loads:
        load.start()
    whole = depth // LANES * LANES
    loads[0].wait()
    turned_ref[...] = w_ref[...].T
    for load in loads[1:4]:
        load.wait()
    merged_ref[...] = jnp.dot(patch_ref[...], qkv_ref[...], preferred_element_type=jnp.float32)
    stores = []
    own_main = own_hbm.at[:, :width]
    for flip, out_hbm in ((1, side_hbm), (2, high_hbm), (3, far_hbm), (0, own_main)):
        first = pl.multiple_of((high ^ (flip // 2)) * channels, channels)
        out_ref[flip, :, :whole] = turned_ref[pl.ds(first, channels), :whole]
        lower = turned_ref[pl.ds(first, channels), whole:]
        chip = (2 * high + side) ^ flip
        tail, upper = [], []
        for half in range(2):
            mine = merged_ref[pl.ds(pl.multiple_of(chip * 16 + half * 8, 8), 8)]
            mine = [mine[:, q * LANES : (q + 1) * LANES] for q in range(6)]
            tail += mine[:4]
            upper += [pltpu.roll(mine[4], 64, 1), mine[4], pltpu.roll(mine[5], 64, 1), mine[5]]
        upper = jnp.concatenate(upper, axis=0)[:, 64:].astype(jnp.bfloat16)
        out_ref[flip, :, whole : whole + LANES] = jnp.concatenate([lower, upper], axis=1)
        out_ref[flip, :, whole + LANES :] = jnp.concatenate(tail, axis=0).astype(jnp.bfloat16)
        stores.append(pltpu.make_async_copy(out_ref.at[flip], out_hbm, sems.at[13 + flip]))
        stores[-1].start()
    rows_ref[...] = patch_bias_ref[...].astype(jnp.float32).reshape(rows_ref.shape)
    count = rows // LANES
    bias = [rows_ref[pl.ds(count * place + part, 1), :] for part in range(count)]
    bias = jnp.broadcast_to(jnp.concatenate(bias, axis=1), (8, rows)).astype(jnp.bfloat16)
    bias = jnp.dot(bias, qkv_ref[...], preferred_element_type=jnp.float32)
    line = lax.broadcasted_iota(jnp.int32, (8, LANES), 0)
    lines = jnp.zeros((8, LANES), jnp.float32)
    for part in range(bias.shape[1] // LANES):
        lines = jnp.where(line == part, bias[:, part * LANES : (part + 1) * LANES], lines)
    lines_ref[...] = jnp.concatenate([lines, jnp.zeros_like(lines)], axis=0).astype(jnp.bfloat16)
    stores.append(
        pltpu.make_async_copy(lines_ref, own_hbm.at[:16, width : width + LANES], sems.at[17])
    )
    stores[-1].start()
    for load in loads[4:]:
        load.wait()
    fill_tables(
        frame_v, freq_ref, gain_v, bias_v, out_bias_v, qkv_bias_v, q_v, k_v,
        scale_ref, table_ref,
    )
    for index, (source, to) in enumerate(((scale_ref, scale_hbm), (table_ref, table_hbm))):
        stores.append(pltpu.make_async_copy(source, to, sems.at[18 + index]))
        stores[-1].start()
    for store in stores:
        store.wait()


def column(row_ref, first, size):
    length = row_ref.shape[0]
    row = row_ref[...].astype(jnp.float32).reshape(1, length)
    line = lax.broadcasted_iota(jnp.int32, (size, length), 0)
    lane = lax.broadcasted_iota(jnp.int32, (size, length), 1)
    picked = jnp.where(lane == line + first, jnp.broadcast_to(row, (size, length)), 0.0)
    return jnp.sum(picked, axis=1, keepdims=True)


def fill_tables(
    frame_ref, freq_ref, gain_v, bias_v, out_bias_v, qkv_v, q_v, k_v,
    scale_ref, table_ref,
):
    shape = (TILE, LANES)
    line = lax.broadcasted_iota(jnp.int32, shape, 0)
    lane = lax.broadcasted_iota(jnp.int32, shape, 1)
    frames = frame_ref[...].astype(jnp.float32).reshape(1, 2)
    one, two = (jnp.broadcast_to(frames[:, part : part + 1], shape) for part in range(2))
    frame = jnp.where(line // 8 == 0, one, two)
    spot = jnp.where(lane < 72, 1.0, (line % 8).astype(jnp.float32))
    table_ref[:16] = jnp.where(lane < 16, frame, spot) * freq_ref[...]
    table_ref[16:32] = jnp.zeros(shape, jnp.float32)
    first = lax.axis_index("tm") // 2 * (4 * GROUP)
    scale_ref[:, 0:1] = column(gain_v, first, 4 * GROUP)
    scale_ref[:, 1:2] = column(bias_v, first, 4 * GROUP)
    table_ref[32:48] = jnp.broadcast_to(column(out_bias_v, 0, TILE), shape)
    table_ref[48:49] = q_v[...].astype(jnp.float32).reshape(1, HD)
    table_ref[49:50] = k_v[...].astype(jnp.float32).reshape(1, HD)
    table_ref[50:56] = qkv_v[...].astype(jnp.float32).reshape(6, LANES)


def arrange_kernel(*refs):
    pieces, (own_ref, keep_ref, send_ref, all_ref) = refs[:4], refs[4:]
    side = lax.axis_index("height")
    layer = lax.axis_index("dp")
    for step, piece in zip((3, 0, 2, 1), pieces):
        all_ref[(layer + 4 - step) % 4] = piece[...]

    @pl.when(layer % 2 == lax.axis_index("tm") % 2)
    def _():
        all_ref[layer] = own_ref[...]

    for core in range(2):
        keep_ref[core] = all_ref[2 * side + core]
        send_ref[core] = all_ref[2 - 2 * side + core]


def core_taps(core):
    quarter = TAPS / 4
    taps = []
    for tm in (core, core + 2):
        taps += range(int(quarter * tm), min(TAPS, -int(-quarter * (tm + 1) // 1)))
    return taps


def join_kernel(own_ref, side_ref, high_ref, far_ref, wt_ref, all_ref):
    channels, width = side_ref.shape
    inner = wt_ref.shape[1]
    depth = TAPS * inner // 8
    here = lax.axis_index("tm") // 2 * 2 + lax.axis_index("height")
    for flip, ref in enumerate((own_ref, side_ref, high_ref, far_ref)):
        all_ref[here ^ flip] = ref[:, :width]

    def assemble(core):
        for index, tap in enumerate(core_taps(core)):
            rows = slice(index * channels, (index + 1) * channels)
            start, end = tap * inner, (tap + 1) * inner
            while start < end:
                source = start // depth
                stop = min(end, (source + 1) * depth)
                to = slice(start - tap * inner, stop - tap * inner)
                if source // 2 % 2 == core:
                    chip = source // 4 * 2 + source % 2
                    first = start - source * depth
                    wt_ref[rows, to] = all_ref[chip, :, first : first + stop - start]
                else:
                    wt_ref[rows, to] = jnp.zeros((channels, stop - start), jnp.bfloat16)
                start = stop

    core = lax.axis_index("tm") % 2
    pl.when(core == 0)(functools.partial(assemble, 0))
    pl.when(core == 1)(functools.partial(assemble, 1))
    total = sum(all_ref[chip, :, width - 2 * LANES :].astype(jnp.float32) for chip in range(4))
    low = lax.broadcasted_iota(jnp.int32, (8, LANES), 1) < 64
    empty = jnp.zeros((8, LANES), jnp.float32)
    wide, narrow = [], []
    for half in range(2):
        top = 32 * half
        wide.append([total[top + 8 * q : top + 8 * q + 8, LANES:] for q in range(4)])
        some = []
        for q in range(2):
            one = total[top + 16 * q : top + 16 * q + 8, :LANES]
            two = total[top + 16 * q + 8 : top + 16 * q + 16, :LANES]
            some.append(jnp.where(low, pltpu.roll(one, 64, 1), two))
        lines = own_ref[:16, width:].astype(jnp.float32)[8 * half : 8 * half + 8]
        narrow.append(some + [lines, empty])
    share = jnp.concatenate([jnp.concatenate(row, axis=1) for row in wide + narrow], axis=0)
    wt_ref[wt_ref.shape[0] - 32 :] = share.astype(jnp.bfloat16)


def place_kernel(*refs):
    pieces, x_ref = refs[:4], refs[4]
    place = lax.axis_index("tm") // 2 * 4 + lax.axis_index("height")
    for flip, piece in zip((0, 1, 4, 5), pieces):
        for core in range(2):
            x_ref[(place ^ flip) + 2 * core] = piece[core]


def tap_parts(y_ref, group, channels):
    held = [core_taps(core) for core in range(2)]

    def part(tap, lanes):
        found = []
        for core in range(2):
            if tap in held[core]:
                at = held[core].index(tap) * channels + group * GROUP
                found.append(y_ref[core, at : at + GROUP, lanes])
        return sum(found[1:], found[0])

    return part


def conv_kernel(
    x_ref, wt_ref, pair_ref, scale_ref, w2_ref, out_ref, y_ref
):
    channels = 4 * GROUP
    tiles = x_ref.shape[0] // 2
    count = float(tiles * LANES * GROUP)
    core = lax.axis_index("tm") % 2
    height = y_ref.shape[1]
    x = x_ref[...].reshape(tiles * LANES, x_ref.shape[2])
    for ref, at in ((wt_ref, core), (pair_ref, 1 - core)):
        y_ref[at] = lax.dot_general(
            ref[:height], x, (((1,), (1,)), ((), ())), preferred_element_type=jnp.float32
        )
    normed = []
    for group in range(4):
        hidden = tap_sums(tap_parts(y_ref, group, channels), tiles)
        at = slice(group * GROUP, (group + 1) * GROUP)
        mean = jnp.sum(sum(hidden), keepdims=True) / count
        square = jnp.sum(sum(part * part for part in hidden), keepdims=True) / count
        scale = lax.rsqrt(square - mean * mean + norm_eps)
        parts = []
        for part in hidden:
            scaled = (part - mean) * scale * scale_ref[at, 0:1] + scale_ref[at, 1:2]
            parts.append((scaled / (1.0 + jnp.exp(-scaled))).astype(jnp.bfloat16))
        normed.append(jnp.concatenate(parts, axis=1))
    y_ref[0, : TAPS * TILE] = jnp.dot(
        w2_ref[...], jnp.concatenate(normed, axis=0), preferred_element_type=jnp.float32
    )

    def part(tap, lanes):
        return y_ref[0, tap * TILE : (tap + 1) * TILE, lanes]

    low = lax.broadcasted_iota(jnp.int32, (8, LANES), 1) < 64
    layers = out_ref.shape[0] // (2 * tiles)
    for tile, latent in enumerate(tap_sums(part, tiles)):
        turned = pltpu.roll(latent, 64, 1)
        near = jnp.where(low, latent[:8], turned[8:])
        far = jnp.where(low, turned[:8], latent[8:])
        for layer in range(layers):
            out_ref[layer * 2 * tiles + 2 * tile] = near
            out_ref[layer * 2 * tiles + 2 * tile + 1] = far


def share_kernel(
    m0_ref, m1_ref, m2_ref, m3_ref, table_ref, row_ref, merged_ref, base_ref, rope_ref, m_ref
):
    lane = lax.broadcasted_iota(jnp.int32, (16, LANES), 1)
    row = jnp.broadcast_to(row_ref[0], lane.shape).astype(jnp.float32)
    angles = table_ref[:16] * jnp.where((lane < 16) | (lane >= 72), 1.0, row)
    rope_ref[:16] = jnp.cos(angles)
    sine = jnp.sin(angles)
    rope_ref[16:] = jnp.where(lane % 2 == 0, -sine, sine)
    here = lax.axis_index("tm") // 2 * 2 + lax.axis_index("height")
    lines = table_ref[48:56]
    for flip, ref in enumerate((m0_ref, m1_ref, m2_ref, m3_ref)):
        share = ref[...].astype(jnp.float32)
        m_ref[here ^ flip, :, : 4 * LANES] = share[:16]
        m_ref[here ^ flip, :, 4 * LANES :] = share[16:, : 2 * LANES]
        lines = lines + pltpu.roll(share[16:24, 2 * LANES : 3 * LANES], 2, 0)
    base_ref[...] = jnp.concatenate([lines[2 + part : 3 + part] for part in range(6)], axis=1)
    merged_ref[...] = m_ref[...].reshape(merged_ref.shape).astype(jnp.bfloat16)


def token_kernel(p_ref, m_ref, base_ref, rope_ref, table_ref, lat_ref, q_ref, k_ref, v_ref):
    low = lax.broadcasted_iota(jnp.int32, (8, LANES), 1) < 64
    pairs = []
    for side in range(2):
        one, two = (
            sum(p_ref[4 * index + 2 * core + side] for index in range(p_ref.shape[0] // 4))
            for core in range(2)
        )
        top = jnp.where(low, one, pltpu.roll(two, 64, 1))
        bottom = jnp.where(low, pltpu.roll(one, 64, 1), two)
        pairs.append(jnp.concatenate([top, bottom], axis=0))
    total = jnp.concatenate(pairs, axis=1)
    lat = (total + table_ref[32:48, :1]) * latent_scale
    clips = lat.shape[1] // 64
    tokens = clips * 16
    place = lax.axis_index("dp")
    own = lat[:, :LANES]
    for pair in range(1, clips // 2):
        own = jnp.where(place // 2 == pair, lat[:, pair * LANES : (pair + 1) * LANES], own)
    own = jnp.where(place % 2 == 1, pltpu.roll(own, 64, 1), own)
    turned = own.T[:64]
    wide = jnp.concatenate([turned] * 16, axis=1)
    spot = lax.broadcasted_iota(jnp.int32, wide.shape, 0) % 16
    spread = lax.broadcasted_iota(jnp.int32, wide.shape, 1) // 16
    merged = jnp.sum(jnp.where(spot == spread, wide, 0.0).reshape(4, 16, 256), axis=1)
    lat_ref[0, 0] = merged[:2]
    lat_ref[0, 1] = merged[2:]

    lat_bf = lat.astype(jnp.bfloat16)
    token = lax.broadcasted_iota(jnp.int32, (tokens, clips * 64), 0)
    lane = lax.broadcasted_iota(jnp.int32, (tokens, clips * 64), 1)
    first = token // 8 * 32 + token % 8 * 2
    heads = q_ref.shape[2] // HD
    projected = base_ref[...]
    for a in range(2):
        for e in range(2):
            chosen = jnp.where(lane == first + (16 * a + e), 1.0, 0.0).astype(jnp.bfloat16)
            patch = lax.dot_general(
                chosen, lat_bf, (((1,), (1,)), ((), ())), preferred_element_type=jnp.float32
            ).astype(jnp.bfloat16)
            weight = m_ref[(2 * a + e) * TILE : (2 * a + e + 1) * TILE]
            projected = projected + jnp.dot(patch, weight, preferred_element_type=jnp.float32)

    even = lax.broadcasted_iota(jnp.int32, (tokens, HD), 1) % 2 == 0
    cosine = jnp.concatenate([rope_ref[:16]] * clips, axis=0)
    sine = jnp.concatenate([rope_ref[16:]] * clips, axis=0)

    def turn(vectors, gain):
        square = jnp.mean(vectors * vectors, axis=-1, keepdims=True)
        vectors = vectors * lax.rsqrt(square + norm_eps) * gain
        swapped = jnp.where(even, pltpu.roll(vectors, HD - 1, 1), pltpu.roll(vectors, 1, 1))
        return vectors * cosine + swapped * sine

    def keep(ref, head, value):
        value = value.reshape(tokens // 8, 8, HD).astype(jnp.bfloat16)
        ref[:, :, head * HD : (head + 1) * HD] = value

    for head in range(heads):
        at = 3 * HD * head
        keep(q_ref, head, turn(projected[:, at : at + HD], table_ref[48:49]))
        keep(k_ref, head, turn(projected[:, at + HD : at + 2 * HD], table_ref[49:50]))
        keep(v_ref, head, projected[:, at + 2 * HD : at + 3 * HD])


def rope_freqs():
    freqs = []
    for dims in (time_dims, row_dims, row_dims):
        freqs.append(rope_base ** (-np.arange(0, dims, 2, dtype=np.float64) / dims))
    return np.repeat(np.concatenate(freqs), 2)[None].astype(np.float32)


def vmem(count):
    return [pl.BlockSpec(memory_space=pltpu.VMEM)] * count


def grouped(
    clip_inputs,
    conv_in_weight,
    group_gain,
    group_bias,
    conv_out_weight,
    out_bias,
    patch_weight,
    patch_bias,
    qkv_weight,
    qkv_bias,
    q_gain,
    k_gain,
    frame_pos,
    row_pos,
):
    plane_axes = ("tm", "height")
    clips = lax.axis_size("dp")
    steps = lax.axis_size("tm")
    plane = steps * lax.axis_size("height")
    channels = clip_inputs.shape[4]
    depth = conv_in_weight.shape[0]

    width = -(-depth // LANES) * LANES + LANES
    hbm = pl.BlockSpec(memory_space=pltpu.HBM)
    wide = pltpu.CompilerParams(vmem_limit_bytes=60 * 1024 * 1024)
    limit = pltpu.CompilerParams(vmem_limit_bytes=32 * 1024 * 1024)
    small = pl.CostEstimate(flops=10**6, bytes_accessed=10**6, transcendentals=0)
    with jax.named_scope("weight_by_group"):
        weight_block = jax.ShapeDtypeStruct((4 * GROUP, width), jnp.bfloat16)
        own_block = jax.ShapeDtypeStruct((4 * GROUP, width + LANES), jnp.bfloat16)
        small_arrays = (group_gain, group_bias, out_bias, qkv_bias, q_gain, k_gain)
        small_arrays += (frame_pos,)
        *packed, scale, table = pl.pallas_call(
            pack_kernel,
            out_shape=(own_block,)
            + (weight_block,) * 3
            + (
                jax.ShapeDtypeStruct((4 * GROUP, 2), jnp.float32),
                jax.ShapeDtypeStruct((56, LANES), jnp.float32),
            ),
            in_specs=[hbm] * 12,
            out_specs=(hbm,) * 6,
            scratch_shapes=[
                pltpu.VMEM(conv_in_weight.shape, jnp.bfloat16),
                pltpu.VMEM(qkv_weight.shape, jnp.bfloat16),
                pltpu.VMEM((patch_weight.shape[0], qkv_weight.shape[0]), jnp.bfloat16),
                pltpu.VMEM(patch_bias.shape, jnp.bfloat16),
                *[pltpu.VMEM(array.shape, array.dtype) for array in small_arrays],
                pltpu.VMEM((1, HD), jnp.float32),
                pltpu.VMEM((patch_bias.shape[0] // LANES, LANES), jnp.float32),
                pltpu.VMEM((8 * GROUP, depth), jnp.bfloat16),
                pltpu.VMEM((patch_weight.shape[0], qkv_weight.shape[1]), jnp.float32),
                pltpu.VMEM((4, 4 * GROUP, width), jnp.bfloat16),
                pltpu.VMEM((16, LANES), jnp.bfloat16),
                pltpu.VMEM((4 * GROUP, 2), jnp.float32),
                pltpu.VMEM((56, LANES), jnp.float32),
                pltpu.SemaphoreType.DMA((20,)),
            ],
            compiler_params=wide,
            cost_estimate=pl.CostEstimate(flops=10**8, bytes_accessed=10**6, transcendentals=0),
            name="pack_weights",
        )(
            rope_freqs(),
            conv_in_weight,
            qkv_weight,
            patch_weight,
            patch_bias,
            *small_arrays,
        )
        blocks = [packed[0]]
        for flip, block in zip((1, 4, 5), packed[1:]):
            blocks.append(lax.ppermute(block, plane_axes, [(i, i ^ flip) for i in range(plane)]))
    with jax.named_scope("gather_clips"):
        own = clip_inputs.reshape(64, channels)
        layers = []
        for step in (3, 0, 2, 1):
            pairs = []
            for layer in range(clips):
                for tm in range(steps):
                    to = (layer // 2 * 2 + tm % 2 + step) % clips
                    pair = (layer * steps + tm, to * steps + tm // 2 * 2 + layer % 2)
                    if pair[0] != pair[1]:
                        pairs.append(pair)
            layers.append(lax.ppermute(own, ("dp", "tm"), pairs))
    with jax.named_scope("spread_clips"):
        keep, send = pl.pallas_call(
            arrange_kernel,
            out_shape=(jax.ShapeDtypeStruct((2, 64, channels), jnp.bfloat16),) * 2,
            in_specs=vmem(5),
            out_specs=tuple(vmem(2)),
            scratch_shapes=[pltpu.VMEM((4, 64, channels), jnp.bfloat16)],
            compiler_params=limit,
            cost_estimate=small,
            name="arrange_clips",
        )(*layers, own)
        pieces = [keep]
        for flip in (1, 4, 5):
            pairs = [(i, i ^ flip) for i in range(plane)]
            pieces.append(lax.ppermute(send if flip % 2 else keep, plane_axes, pairs))
    with jax.named_scope("small_weights"):
        first = lax.axis_index("tm") // 2 * (4 * GROUP)
        weight_out = lax.dynamic_slice_in_dim(conv_out_weight, first, 4 * GROUP, axis=1)
        weight_out = weight_out.transpose(0, 2, 1).reshape(TAPS * TILE, 4 * GROUP)
    with jax.named_scope("join_weights"):
        height = len(core_taps(0)) * 4 * GROUP
        joined = pl.pallas_call(
            join_kernel,
            out_shape=jax.ShapeDtypeStruct((height + 32, channels), jnp.bfloat16),
            in_specs=vmem(4),
            out_specs=vmem(1)[0],
            scratch_shapes=[pltpu.VMEM((4, 4 * GROUP, width), jnp.bfloat16)],
            compiler_params=limit,
            cost_estimate=small,
            name="join_weights",
        )(*blocks)
        joined_pair = lax.ppermute(joined, "tm", [(i, i ^ 1) for i in range(steps)])
    with jax.named_scope("merged_projection"):
        share = joined[height:].astype(jnp.float32) + joined_pair[height:].astype(jnp.float32)
        share = share.astype(jnp.bfloat16)
        shares = [share]
        for flip in (1, 4, 5):
            pairs = [(i, i ^ flip) for i in range(plane)]
            shares.append(lax.ppermute(share, plane_axes, pairs))

        merged, base, rope = pl.pallas_call(
            share_kernel,
            out_shape=(
                jax.ShapeDtypeStruct((64, 6 * HD), jnp.bfloat16),
                jax.ShapeDtypeStruct((1, 6 * HD), jnp.float32),
                jax.ShapeDtypeStruct((32, LANES), jnp.float32),
            ),
            in_specs=vmem(5) + [pl.BlockSpec(memory_space=pltpu.SMEM)],
            out_specs=tuple(vmem(3)),
            scratch_shapes=[pltpu.VMEM((4, 16, 6 * HD), jnp.float32)],
            compiler_params=limit,
            cost_estimate=small,
            name="share_rows",
        )(*shares, table, row_pos)

    flops = 4 * height * steps * LANES * channels
    clip = pl.pallas_call(
        place_kernel,
        out_shape=jax.ShapeDtypeStruct((plane, 64, channels), jnp.bfloat16),
        in_specs=vmem(4),
        out_specs=vmem(1)[0],
        compiler_params=limit,
        cost_estimate=pl.CostEstimate(flops=4 * 10**10, bytes_accessed=10**6, transcendentals=0),
        name="place_clip",
    )(*pieces)
    partial = pl.pallas_call(
        conv_kernel,
        out_shape=jax.ShapeDtypeStruct((clips * plane, 8, LANES), jnp.float32),
        in_specs=vmem(5),
        out_specs=vmem(1)[0],
        scratch_shapes=[
            pltpu.VMEM((2, height, steps * LANES), jnp.float32),
        ],
        compiler_params=limit,
        cost_estimate=pl.CostEstimate(flops=flops, bytes_accessed=10**6, transcendentals=0),
        name="convolutions",
    )(clip, joined, joined_pair, scale, weight_out)

    with jax.named_scope("sum_latents"):
        partials = lax.all_to_all(partial, ("dp",) + plane_axes, 0, 0, tiled=True)

    heads = qkv_weight.shape[1] // (3 * HD)
    frames = clip_inputs.shape[1]
    tokens = jax.ShapeDtypeStruct((clips * frames, 8, heads * HD), jnp.bfloat16)
    latents, query, key, value = pl.pallas_call(
        token_kernel,
        out_shape=(jax.ShapeDtypeStruct((1, 2, 2, 256), jnp.float32), tokens, tokens, tokens),
        in_specs=vmem(5),
        out_specs=tuple(vmem(4)),
        compiler_params=limit,
        cost_estimate=pl.CostEstimate(flops=10**8, bytes_accessed=10**6, transcendentals=0),
        name="tokens",
    )(
        partials,
        merged,
        base,
        rope,
        table,
    )
    full = (clips, frames, 1, 8, heads * HD)
    return latents, query.reshape(full), key.reshape(full), value.reshape(full)


def pick(mesh, *arrays):
    if one_group_each(mesh, arrays[0], arrays[1], arrays[4], arrays[8]):
        return grouped(*arrays)
    return shards(*arrays)


def solution(mesh):
    placed = (
        P("dp", "tm", "height", None, None),
        P(("tm", "height"), "dp"),
        P("dp"),
        P("dp"),
        P(None, "dp", None),
        P(),
        P(),
        P(),
        P(("tm", "height"), "dp"),
        P("dp"),
        P(),
        P(),
        P("tm"),
        P("height"),
    )
    return jax.shard_map(
        functools.partial(pick, mesh),
        mesh=mesh,
        in_specs=placed,
        out_specs=(
            P("dp", "tm", "height", None),
            P(None, "tm", "height", None, "dp"),
            P(None, "tm", "height", None, "dp"),
            P(None, "tm", "height", None, "dp"),
        ),
        check_vma=False,
    )
```
